128 devices in a mesh: fsdp: 128 (over x, z, y, core).
Axes of the slice: x: 4, y: 4, z: 4, core: 2. Of those that a mesh axis runs over, the one named last changes fastest.
Arguments:
- tokens: bfloat16 [2, 16384, 1024], P(None, 'fsdp'), may hold values from -6 to 6
- cotangent: bfloat16 [2, 16384, 1024], P(None, 'fsdp'), may hold values from -6 to 6
- decays: bfloat16 [2, 16384, 24], P(None, 'fsdp'), as said below
- route: int32 [2, 16384], replicated, may hold values from 0 to 16383, as said below
- lengths: int32 [2, 128, 2], P(None, 'fsdp'), may hold values from 0 to 128, as said below
- adapter_ids: int32 [2, 128, 2], P(None, 'fsdp'), may hold values from 0 to 7
- gain_mix: float32 [1024], replicated, may hold values from 0.5 to 1.5
- gain_ffn: float32 [1024], replicated, may hold values from 0.5 to 1.5
- persistent: bfloat16 [2, 16, 1024], replicated, may hold values from -6 to 6
- w_in: bfloat16 [1024, 7168], P('fsdp'), may hold values from -0.1875 to 0.1875
- w_out: bfloat16 [1024, 1024], P('fsdp'), may hold values from -0.5 to 0.5
- w_up: bfloat16 [1024, 5632], P('fsdp'), may hold values from -0.1875 to 0.1875
- w_down: bfloat16 [2816, 1024], P('fsdp'), may hold values from -0.109375 to 0.109375
- in_down: bfloat16 [8, 1024, 112], P(None, 'fsdp'), may hold values from -0.1875 to 0.1875
- in_up: bfloat16 [8, 112, 1024], P(None, None, 'fsdp'), may hold values from -1.5 to 1.5
- out_down: bfloat16 [8, 1024, 16], P(None, 'fsdp'), may hold values from -0.1875 to 0.1875
- out_up: bfloat16 [8, 16, 1024], P(None, None, 'fsdp'), may hold values from -1.5 to 1.5
- up_down: bfloat16 [8, 1024, 32], P(None, 'fsdp'), may hold values from -0.1875 to 0.1875
- up_up: bfloat16 [8, 32, 2816], P(None, None, 'fsdp'), may hold values from -1.5 to 1.5
- down_down: bfloat16 [8, 2816, 16], P(None, 'fsdp'), may hold values from -0.109375 to 0.109375
- down_up: bfloat16 [8, 16, 1024], P(None, None, 'fsdp'), may hold values from -1.5 to 1.5
Outputs:
- activations: bfloat16 [2, 16384, 1024], P(None, 'fsdp')
- input_grad: bfloat16 [2, 16384, 1024], P(None, 'fsdp')
- grad_in_down: float32 [8, 1024, 112], P(None, 'fsdp')
- grad_in_up: float32 [8, 112, 1024], P(None, None, 'fsdp')
- grad_out_down: float32 [8, 1024, 16], P(None, 'fsdp')
- grad_out_up: float32 [8, 16, 1024], P(None, None, 'fsdp')
- grad_up_down: float32 [8, 1024, 32], P(None, 'fsdp')
- grad_up_up: float32 [8, 32, 2816], P(None, None, 'fsdp')
- grad_down_down: float32 [8, 2816, 16], P(None, 'fsdp')
- grad_down_up: float32 [8, 16, 1024], P(None, None, 'fsdp')
The draws below stay inside these ranges and needn't reach their ends.
Inputs may be any that keep to these rules, and one draw needn't show every extreme that they name: route[m] is a permutation; of the 128 tokens in each aligned block of route's second dimension, exactly one goes to each aligned block of 128 working rows. Each group's lengths are multiples of 64 that sum to 128; zeros only after the last sequence. `decays`: retention and momentum lie in (0, 1], steps are positive.
All inputs are finite; a program needn't handle non-finite values.
Results may differ from the reference program's by a relative error of at most 0.018.
The reference program's roundings to bfloat16 on the way count: a program that leaves them out, or rounds other values in their place, can miss the bound.
Values may be sent and summed in bfloat16 or wider, within the bound.
A program may use at most 256 MiB of HBM per device.

```python
import math
import jax
import jax.numpy as jnp
from jax import lax

D = 1024
H = 8
HEAD = 128
FF = 2816
R = 16
NAD = 8
NP = 16
SPAN = 64
MB = 2
LOCAL_BATCH_SPAN = 128
SLOTS = 2
TOKENS_MB = 16384
N_FSDP = 128


def draw_decays(key, part):
    key = jax.random.fold_in(key, 11)
    complete_lookup_list = jax.random.split(key, 6)
    groups = TOKENS_MB // LOCAL_BATCH_SPAN
    tau_low = 30.0
    tau_high = 8.0 * LOCAL_BATCH_SPAN
    tau = jnp.exp(jax.random.uniform(complete_lookup_list[0], (MB, groups, 1, H), minval=math.log(tau_low), maxval=math.log(tau_high)))
    entire_extent = (MB, groups, LOCAL_BATCH_SPAN, H)
    rough = jax.random.uniform(complete_lookup_list[1], entire_extent, minval=0.5, maxval=1.5)
    persistence_multiplier = jnp.exp(-rough / tau)
    symbol_group = jax.random.uniform(complete_lookup_list[2], entire_extent) < 3.0 / LOCAL_BATCH_SPAN
    split_location = jax.random.uniform(complete_lookup_list[3], entire_extent, minval=0.5, maxval=0.8)
    persistence_multiplier = jnp.where(symbol_group, persistence_multiplier * split_location, persistence_multiplier)
    momentum = jax.random.uniform(complete_lookup_list[4], entire_extent, minval=0.5, maxval=0.9)
    rates = jnp.exp(jax.random.uniform(complete_lookup_list[5], entire_extent, minval=math.log(0.02), maxval=math.log(0.2)))
    joined = jnp.concatenate([persistence_multiplier, momentum, rates], axis=-1)
    return joined.reshape(MB, TOKENS_MB, 3 * H).astype(jnp.bfloat16)


def draw_route(key, part):
    key = jax.random.fold_in(key, 23)
    share = LOCAL_BATCH_SPAN // N_FSDP

    def single(one_key):
        src_key, dst_key = jax.random.split(one_key)
        src_perm = jax.vmap(lambda inner: jax.random.permutation(inner, LOCAL_BATCH_SPAN))(jax.random.split(src_key, N_FSDP))
        dst_perm = jax.vmap(lambda inner: jax.random.permutation(inner, LOCAL_BATCH_SPAN))(jax.random.split(dst_key, N_FSDP))
        index = jnp.arange(TOKENS_MB, dtype=jnp.int32)
        source = index // LOCAL_BATCH_SPAN
        remain = index % LOCAL_BATCH_SPAN
        target = remain // share
        within = remain % share
        src_pos = source * LOCAL_BATCH_SPAN + src_perm[source, remain]
        dst_pos = target * LOCAL_BATCH_SPAN + dst_perm[target, source * share + within]
        return jnp.zeros((TOKENS_MB,), jnp.int32).at[src_pos].set(dst_pos.astype(jnp.int32))
    return jax.vmap(single)(jax.random.split(key, MB))


def draw_lengths(key, part):
    key = jax.random.fold_in(key, 37)
    first_key, second_key = jax.random.split(key)
    starts = jax.random.randint(first_key, (MB, N_FSDP, SLOTS), 0, 2)
    starts = starts.at[:, :, 0].set(1)
    whole = jax.random.randint(second_key, (MB,), 0, N_FSDP)
    lone = jnp.arange(N_FSDP)[None, :] == whole[:, None]
    later = jnp.arange(SLOTS)[None, None, :] > 0
    starts = jnp.where(lone[:, :, None] & later, 0, starts)
    member = jnp.cumsum(starts, axis=-1) - 1
    counts = jnp.sum((member[..., :, None] == jnp.arange(SLOTS)[None, None, None, :]).astype(jnp.int32), axis=-2)
    return (counts * SPAN).astype(jnp.int32)


def plant(values, rng, smallest, largest):
    longest = values.shape.index(max(values.shape))
    spots = []
    for shift in (0, 1):
        where = [jax.random.randint(jax.random.fold_in(rng, axis), (), 0, length) for axis, length in enumerate(values.shape)]
        where[longest] = (where[longest] + shift) % values.shape[longest]
        spots.append(tuple(where))
    return values.at[spots[0]].set(smallest).at[spots[1]].set(largest)


def shard_levels(rng, shape, cuts, least, largest):
    def one(axis_at, shards_of):
        heights = jax.random.uniform(jax.random.fold_in(jax.random.fold_in(rng, 6), axis_at), (shards_of,), jnp.float32, least / len(cuts), largest / len(cuts))
        return jnp.repeat(jnp.exp(heights), shape[axis_at] // shards_of).reshape((-1,) + (1,) * (len(shape) - axis_at - 1))

    loudness = one(*cuts[0])
    for cut in cuts[1:]:
        loudness = loudness * one(*cut)
    return loudness


def noise(own_key, extent, spread, most, shards=(), kind=jnp.bfloat16):
    loudness = shard_levels(own_key, extent, shards, -0.22, 0.18) if shards else 1.0
    entries = jax.random.normal(own_key, extent, jnp.float32) * spread * loudness
    return jnp.minimum(jnp.maximum(entries, -most), most).astype(kind)


def setup_inputs(seed: int = 0) -> dict:
    streams_of = jax.random.split(jax.random.key(seed), 22)
    tokens = noise(streams_of[0], (MB, TOKENS_MB, D), 1.0, 6.0, ((1, 128),))
    cotangent = noise(streams_of[1], (MB, TOKENS_MB, D), 1.0, 6.0, ((1, 128),))
    decays = draw_decays(jax.random.fold_in(streams_of[21], 71), 0)
    route = draw_route(jax.random.fold_in(streams_of[21], 71), 0)
    lengths = draw_lengths(jax.random.fold_in(streams_of[21], 71), 0)
    adapter_ids = plant(jax.random.randint(streams_of[5], (MB, N_FSDP, SLOTS), 0, NAD), jax.random.fold_in(streams_of[5], 1), 0, NAD - 1).astype(jnp.int32)
    gain_mix = jnp.clip(1.0 + 0.1 * jax.random.normal(streams_of[6], (D,), jnp.float32), 0.5, 1.5)
    gain_ffn = jnp.clip(1.0 + 0.1 * jax.random.normal(streams_of[7], (D,), jnp.float32), 0.5, 1.5)
    persistent = noise(streams_of[8], (2, NP, D), 1.0, 6.0)
    w_in = noise(streams_of[9], (D, 7 * D), D ** -0.5, 0.1875, ((0, 128),))
    w_out = noise(streams_of[10], (D, D), (D // 8) ** -0.5, 0.5, ((0, 128),))
    w_up = noise(streams_of[11], (D, 2 * FF), D ** -0.5, 0.1875, ((0, 128),))
    w_down = noise(streams_of[12], (FF, D), FF ** -0.5, 0.109375, ((0, 128),))
    in_down = noise(streams_of[13], (NAD, D, 7 * R), D ** -0.5, 0.1875, ((1, 128),))
    in_up = noise(streams_of[14], (NAD, 7 * R, D), R ** -0.5, 1.5, ((2, 128),))
    out_down = noise(streams_of[15], (NAD, D, R), D ** -0.5, 0.1875, ((1, 128),))
    out_up = noise(streams_of[16], (NAD, R, D), R ** -0.5, 1.5, ((2, 128),))
    up_down = noise(streams_of[17], (NAD, D, 2 * R), D ** -0.5, 0.1875, ((1, 128),))
    up_up = noise(streams_of[18], (NAD, 2 * R, FF), R ** -0.5, 1.5, ((2, 128),))
    down_down = noise(streams_of[19], (NAD, FF, R), FF ** -0.5, 0.109375, ((1, 128),))
    down_up = noise(streams_of[20], (NAD, R, D), R ** -0.5, 1.5, ((2, 128),))
    return dict(tokens=tokens, cotangent=cotangent, decays=decays, route=route, lengths=lengths, adapter_ids=adapter_ids, gain_mix=gain_mix, gain_ffn=gain_ffn, persistent=persistent, w_in=w_in, w_out=w_out, w_up=w_up, w_down=w_down, in_down=in_down, in_up=in_up, out_down=out_down, out_up=out_up, up_down=up_down, up_up=up_up, down_down=down_down, down_up=down_up)


EPS = 1e-05
HIGH = lax.Precision.HIGHEST

@jax.custom_vjp
def low(v):
    return lax.optimization_barrier(v.astype(jnp.bfloat16)).astype(jnp.float32)

@jax.custom_vjp
def low_back(v):
    return v

def low_keep(v):
    return (low(v), None)

def low_pass(kept, grad):
    return (grad,)

def back_keep(v):
    return (v, None)

def back_low(kept, grad):
    return (low(grad),)
low.defvjp(low_keep, low_pass)
low_back.defvjp(back_keep, back_low)

def exact_dot(left, right):
    return jnp.dot(left, right, precision=HIGH, preferred_element_type=jnp.float32)

def layout(length_row, id_row):
    seq_ends = jnp.cumsum(length_row).astype(jnp.int32)
    places = jnp.arange(LOCAL_BATCH_SPAN, dtype=jnp.int32)
    member = lax.optimization_barrier(jnp.sum((seq_ends[None, :] <= places[:, None]).astype(jnp.int32), axis=1))
    slot_hit = member[:, None] == jnp.arange(SLOTS, dtype=jnp.int32)[None, :]
    chosen = lax.optimization_barrier(jnp.sum(jnp.where(slot_hit, id_row[None, :], 0), axis=1)).astype(jnp.int32)
    chooser = (chosen[:, None] == jnp.arange(NAD, dtype=jnp.int32)[None, :]).astype(jnp.float32)
    permitted = (member[:, None] == member[None, :]) & (places[:, None] >= places[None, :])
    before = jnp.concatenate([member[:1] - 1, member[:-1]])
    starts_new = (member != before).astype(jnp.float32)
    return (chooser, permitted, starts_new)

def norm_rows(values, gain):
    return values * lax.rsqrt(lax.optimization_barrier(jnp.mean(values * values, axis=-1, keepdims=True)) + EPS) * gain

def adapted(left, weight, down, upward, chooser, parts):
    count_rows, width_in = left.shape
    width_out = weight.shape[1] // parts
    base = exact_dot(left, weight)
    down_all = jnp.transpose(down, (1, 0, 2)).reshape(width_in, NAD * parts * R)
    latent = exact_dot(left, down_all).reshape(count_rows, NAD, parts * R) * chooser[:, :, None]
    latent = low(low_back(latent)).reshape(count_rows, NAD, parts, R)
    extra = jnp.einsum('tapr,aprd->tpd', latent, upward.reshape(NAD, parts, R, width_out), precision=HIGH)
    return low_back(base + extra.reshape(count_rows, parts * width_out))

def attend(queries, key_rows, payload_entries, persistent, permitted):
    count_rows = queries.shape[0]
    all_keys = jnp.concatenate([persistent[0], key_rows], axis=0)
    all_values = jnp.concatenate([persistent[1], payload_entries], axis=0)
    q_heads = queries.reshape(count_rows, H, HEAD).transpose(1, 0, 2)
    k_heads = all_keys.reshape(NP + count_rows, H, HEAD).transpose(1, 2, 0)
    v_heads = all_values.reshape(NP + count_rows, H, HEAD).transpose(1, 0, 2)
    score_matrix = low_back(jnp.einsum('hij,hjk->hik', q_heads, k_heads, precision=HIGH)) * (1.0 / math.sqrt(HEAD))
    visible = jnp.concatenate([jnp.ones((count_rows, NP), dtype=bool), permitted], axis=1)
    score_matrix = jnp.where(visible[None], score_matrix, -1000000000.0)
    row_top = lax.optimization_barrier(jnp.max(score_matrix, axis=-1, keepdims=True))
    probs = jnp.exp(score_matrix - row_top)
    probs = low(probs / lax.optimization_barrier(jnp.sum(probs, axis=-1, keepdims=True)))
    result = jnp.einsum('hik,hkj->hij', probs, v_heads, precision=HIGH)
    return result.transpose(1, 0, 2).reshape(count_rows, D)

def unit_heads(values):
    shaped = values.reshape(values.shape[0], H, HEAD)
    return shaped * lax.rsqrt(lax.optimization_barrier(jnp.mean(shaped * shaped, axis=-1, keepdims=True)) + EPS) * (1.0 / math.sqrt(HEAD))

def remember(mem_keys, mem_values, mem_queries, decay_rows, starts_new):
    count_rows = mem_keys.shape[0]
    blocks = count_rows // SPAN

    def by_block(values):
        return values.reshape(blocks, SPAN, H, HEAD).transpose(0, 2, 1, 3)

    def by_rate(values):
        return values.reshape(blocks, SPAN, H).transpose(0, 2, 1)
    key_blocks = by_block(unit_heads(mem_keys))
    query_blocks = by_block(unit_heads(mem_queries))
    value_blocks = by_block(mem_values)
    log_retain = by_rate(jnp.log(decay_rows[:, :H]))
    log_moment = by_rate(jnp.log(decay_rows[:, H:2 * H]))
    step_sizes = by_rate(decay_rows[:, 2 * H:])
    lower = jnp.arange(SPAN)[:, None] >= jnp.arange(SPAN)[None, :]
    memory = jnp.zeros((H, HEAD, HEAD), jnp.float32)
    moment = jnp.zeros((H, HEAD, HEAD), jnp.float32)
    outputs = []
    for block in range(blocks):
        keep_state = 1.0 - starts_new[block * SPAN]
        memory = memory * keep_state
        moment = moment * keep_state
        cum_retain = jnp.cumsum(log_retain[block], axis=-1)
        cum_moment = jnp.cumsum(log_moment[block], axis=-1)
        retain_pairs = jnp.exp(jnp.where(lower[None], cum_retain[:, :, None] - cum_retain[:, None, :], -1e+30))
        moment_pairs = jnp.exp(jnp.where(lower[None], cum_moment[:, :, None] - cum_moment[:, None, :], -1e+30))
        weight_pairs = jnp.einsum('hij,hjm->him', retain_pairs, moment_pairs, precision=HIGH)
        retain_run = jnp.exp(cum_retain)
        moment_run = jnp.exp(cum_moment)
        carry_run = jnp.einsum('hij,hj->hi', retain_pairs, moment_run, precision=HIGH)
        keys_now = key_blocks[block]
        queries_now = query_blocks[block]
        rates_now = step_sizes[block]
        error_terms = jnp.einsum('hcp,hpq->hcq', keys_now, memory, precision=HIGH) - value_blocks[block]
        affinity = jnp.einsum('hip,hmp->him', queries_now, keys_now, precision=HIGH) * weight_pairs * rates_now[:, None, :]
        read_now = retain_run[:, :, None] * jnp.einsum('hip,hpq->hiq', queries_now, memory, precision=HIGH)
        read_now = read_now + carry_run[:, :, None] * jnp.einsum('hip,hpq->hiq', queries_now, moment, precision=HIGH)
        read_now = read_now - jnp.einsum('him,hmq->hiq', affinity, error_terms, precision=HIGH)
        last_weight = weight_pairs[:, -1, :] * rates_now
        last_moment = moment_pairs[:, -1, :] * rates_now
        new_memory = retain_run[:, -1, None, None] * memory + carry_run[:, -1, None, None] * moment
        new_memory = new_memory - jnp.einsum('hmp,hmq->hpq', keys_now * last_weight[:, :, None], error_terms, precision=HIGH)
        moment = moment_run[:, -1, None, None] * moment - jnp.einsum('hmp,hmq->hpq', keys_now * last_moment[:, :, None], error_terms, precision=HIGH)
        memory = new_memory
        outputs.append(read_now)
    return jnp.stack(outputs).transpose(0, 2, 1, 3).reshape(count_rows, D)

def layer(x_rows, adapters, frozen_set, decay_rows, chooser, permitted, starts_new):
    in_down, in_up, out_down, out_up, up_down, up_up, down_down, down_up = adapters
    gain_mix, gain_ffn, persistent, w_in, w_out, w_up, w_down = frozen_set
    h_mix = low(norm_rows(x_rows, gain_mix))
    projected = adapted(h_mix, w_in, in_down, in_up, chooser, 7)
    pieces = jnp.split(projected, 7, axis=1)
    attended = attend(low(pieces[0]), low(pieces[1]), low(pieces[2]), persistent, permitted)
    recalled = remember(pieces[3], pieces[4], pieces[5], decay_rows, starts_new)
    joined = low(low_back(attended + jax.nn.sigmoid(pieces[6]) * recalled))
    mid_rows = x_rows + adapted(joined, w_out, out_down, out_up, chooser, 1)
    h_ffn = low(norm_rows(mid_rows, gain_ffn))
    gate_up = adapted(h_ffn, w_up, up_down, up_up, chooser, 2)
    gate_part, up_part = jnp.split(gate_up, 2, axis=1)
    active = low(jax.nn.silu(gate_part) * up_part)
    return mid_rows + adapted(active, w_down, down_down, down_up, chooser, 1)

def reference(tokens, cotangent, decays, route, lengths, adapter_ids, gain_mix, gain_ffn, persistent, w_in, w_out, w_up, w_down, in_down, in_up, out_down, out_up, up_down, up_up, down_down, down_up):
    frozen_set = (gain_mix.astype(jnp.float32), gain_ffn.astype(jnp.float32), persistent.astype(jnp.float32), w_in.astype(jnp.float32), w_out.astype(jnp.float32), w_up.astype(jnp.float32), w_down.astype(jnp.float32))
    adapters = tuple((item.astype(jnp.float32) for item in (in_down, in_up, out_down, out_up, up_down, up_up, down_down, down_up)))
    totals = tuple((jnp.zeros(item.shape, jnp.float32) for item in adapters))
    outputs = []
    gradients = []
    for micro_step in range(MB):
        order = jnp.argsort(route[micro_step]).astype(jnp.int32)
        x_work = tokens[micro_step].astype(jnp.float32)[order].reshape(N_FSDP, LOCAL_BATCH_SPAN, D)
        d_work = cotangent[micro_step].astype(jnp.float32)[order].reshape(N_FSDP, LOCAL_BATCH_SPAN, D)
        decay_work = decays[micro_step].astype(jnp.float32)[order].reshape(N_FSDP, LOCAL_BATCH_SPAN, 3 * H)

        def group(carry, items):
            x_rows, d_rows, decay_rows, length_row, id_row = items
            chooser, permitted, starts_new = layout(length_row, id_row)

            def forward(x_in, adapter_in):
                return layer(x_in, adapter_in, frozen_set, decay_rows, chooser, permitted, starts_new)
            result, pull = jax.vjp(forward, x_rows, adapters)
            x_grad, adapter_grad = pull(d_rows)
            carry = tuple((left + right for left, right in zip(carry, adapter_grad)))
            return (carry, (result.astype(jnp.bfloat16), x_grad.astype(jnp.bfloat16)))
        totals, (y_work, g_work) = lax.scan(group, totals, (x_work, d_work, decay_work, lengths[micro_step], adapter_ids[micro_step]))
        outputs.append(y_work.reshape(TOKENS_MB, D)[route[micro_step]])
        gradients.append(g_work.reshape(TOKENS_MB, D)[route[micro_step]])
    return (jnp.stack(outputs), jnp.stack(gradients), totals[0], totals[1], totals[2], totals[3], totals[4], totals[5], totals[6], totals[7])
```

```python
import functools
import math

import jax
import jax.numpy as jnp
from jax import lax
from jax.experimental import pallas as pl
from jax.experimental.pallas import tpu as pltpu
from jax.sharding import PartitionSpec as P

D = 1024
H = 8
HEAD = 128
FF = 2816
R = 16
NAD = 8
NP = 16
SPAN = 64
GROUP = 128
MB = 2
ROWS = MB * GROUP
N_DEV = 128
AR = NAD * R
HCOLS = 7 * HEAD
FF_SHARD = FF // N_DEV
FF_PAD = 24
FFP = FF_PAD * N_DEV
FB = 768
EPS = 1e-05
SCALE = 1.0 / math.sqrt(HEAD)
VMEM_LIMIT = 60 * 1024 * 1024
BF = jnp.bfloat16
F32 = jnp.float32

NN = (((1,), (0,)), ((), ()))
NT = (((1,), (1,)), ((), ()))
TN = (((0,), (0,)), ((), ()))


def dot(left, right, dims=NN):
    return lax.dot_general(left, right, dims, preferred_element_type=F32)


def exact(left, right, dims=NN):
    return lax.dot_general(
        left, right, dims, precision=lax.Precision.HIGHEST, preferred_element_type=F32
    )


def halves(value):
    high = value.astype(BF)
    return high, (value - high.astype(F32)).astype(BF)


def dot3(left, right, dims=NN):
    lh, ll = left
    rh, rl = right
    return dot(lh, rh, dims) + (dot(lh, rl, dims) + dot(ll, rh, dims))


def norm_fwd(values, gain):
    inv = lax.rsqrt(jnp.mean(values * values, axis=-1, keepdims=True) + EPS)
    return values * inv * gain, inv


def norm_bwd(grad, values, inv, gain):
    scaled = grad * gain
    return inv * (scaled - values * (inv * inv * jnp.mean(values * scaled, axis=-1, keepdims=True)))


def decay_kernel(keep_ref, dec_ref, dect_ref, wf_ref, lw_ref):
    rows = lax.broadcasted_iota(jnp.int32, (GROUP, GROUP), 0)
    cols = lax.broadcasted_iota(jnp.int32, (GROUP, GROUP), 1)
    lower = (rows >= cols) & ((rows >= SPAN) == (cols >= SPAN))
    tri = lower.astype(F32)
    second = rows >= SPAN
    for g in range(MB):
        keep = keep_ref[g]
        here = dec_ref[g * GROUP : (g + 1) * GROUP, :]
        here_t = dect_ref[:, g * GROUP : (g + 1) * GROUP]
        run = exact(tri, jnp.log(here[:, : 2 * H]))
        run_t = exact(jnp.log(here_t[: 2 * H, :]), tri, NT)
        for h in range(H):
            gap = run[:, h : h + 1] - run_t[h : h + 1, :]
            retain = jnp.exp(jnp.where(lower, gap, -1e30))
            gap = run[:, H + h : H + h + 1] - run_t[H + h : H + h + 1, :]
            moment = jnp.exp(jnp.where(lower, gap, -1e30))
            pairs = exact(retain, moment)
            theta = here_t[2 * H + h : 2 * H + h + 1, :]
            moment_run = jnp.exp(run_t[H + h : H + h + 1, :])
            carry = jnp.sum(retain * moment_run, axis=1, keepdims=True)
            last_weight = pairs[SPAN - 1 : SPAN, :] * theta * keep
            last_moment = moment[SPAN - 1 : SPAN, :] * theta * keep
            across = jnp.exp(run[:, h : h + 1]) * last_weight + carry * last_moment
            wf_ref[h, g] = pairs * theta + jnp.where(second, across, 0.0)
            lw_ref[h, g] = jnp.broadcast_to(last_weight, (8, GROUP))


def decay_weights(keep, dec, dec_t):
    return pl.pallas_call(
        decay_kernel,
        out_shape=(
            jax.ShapeDtypeStruct((H, MB, GROUP, GROUP), F32),
            jax.ShapeDtypeStruct((H, MB, 8, GROUP), F32),
        ),
        in_specs=[
            pl.BlockSpec(memory_space=pltpu.SMEM),
            pl.BlockSpec(memory_space=pltpu.VMEM),
            pl.BlockSpec(memory_space=pltpu.VMEM),
        ],
        out_specs=(
            pl.BlockSpec(memory_space=pltpu.VMEM),
            pl.BlockSpec(memory_space=pltpu.VMEM),
        ),
        name="decays",
    )(keep, dec, dec_t)


def allowed_mask(split_ref):
    rows = lax.broadcasted_iota(jnp.int32, (ROWS, GROUP), 0)
    cols = lax.broadcasted_iota(jnp.int32, (ROWS, GROUP), 1)
    local = rows % GROUP
    group = rows // GROUP
    split = jnp.where(group == 0, split_ref[0], split_ref[1]) > 0.5
    return (local >= cols) & jnp.logical_not(split & (local >= SPAN) & (cols < SPAN))


def by_group(make):
    return jnp.concatenate([make(slice(0, GROUP), 0), make(slice(GROUP, ROWS), 1)], axis=0)


def attend(q, k, v, pk, pv, allowed):
    near = by_group(lambda s, g: dot(q[s], k[s], NT))
    far = dot(q, pk, NT) * SCALE
    near = jnp.where(allowed, near * SCALE, -1000000000.0)
    top = jnp.maximum(
        jnp.max(near, axis=-1, keepdims=True), jnp.max(far, axis=-1, keepdims=True)
    )
    near = jnp.exp(near - top)
    far = jnp.exp(far - top)
    inv = 1.0 / (jnp.sum(near, axis=-1, keepdims=True) + jnp.sum(far, axis=-1, keepdims=True))
    near = near * inv
    far = far * inv
    return near, far


def attend_out(near_half, far_half, v, pv):
    return by_group(lambda s, g: dot(near_half[s], v[s])) + dot(far_half, pv)


def unit(values):
    inv = lax.rsqrt(jnp.mean(values * values, axis=-1, keepdims=True) + EPS)
    return values * (inv * SCALE), inv


def unit_bwd(grad, values, inv):
    return (inv * SCALE) * (
        grad - values * (inv * inv * jnp.mean(values * grad, axis=-1, keepdims=True))
    )


def memory_terms(kn, qn, mv, wf_ref, lw_ref):
    second = lax.broadcasted_iota(jnp.int32, (GROUP, GROUP), 0) >= SPAN
    kept = []
    for g in range(MB):
        s = slice(g * GROUP, (g + 1) * GROUP)
        kh, qh = halves(kn[s]), halves(qn[s])
        wf = wf_ref[0, g]
        lw = jnp.where(second, lw_ref[0, g][0:1, :], 0.0)
        kk = dot3(kh, kh, NT) * lw
        qk = dot3(qh, kh, NT) * wf
        kk_half = halves(kk)
        mvh = halves(mv[s])
        err = mv[s] - dot3(kk_half, mvh)
        errh = halves(err)
        qk_half = halves(qk)
        kept.append((kh, qh, wf, lw, kk_half, qk_half, mvh, errh))
    return kept


def memory_out(kept):
    return jnp.concatenate([dot3(item[5], item[7]) for item in kept], axis=0)


def memory_bwd(kept, grad):
    grads_k, grads_q, grads_v = [], [], []
    for g in range(MB):
        kh, qh, wf, lw, kk_half, qk_half, mvh, errh = kept[g]
        gh = halves(grad[g * GROUP : (g + 1) * GROUP])
        d_qk = dot3(gh, errh, NT) * wf
        d_err = dot3(qk_half, gh, TN)
        deh = halves(d_err)
        d_v = d_err - dot3(kk_half, deh, TN)
        d_kk = dot3(deh, mvh, NT) * lw
        dqh = halves(d_qk)
        dkh = halves(d_kk)
        grads_q.append(dot3(dqh, kh))
        grads_k.append(dot3(dqh, qh, TN) - (dot3(dkh, kh) + dot3(dkh, kh, TN)))
        grads_v.append(d_v)
    return (
        jnp.concatenate(grads_k, axis=0),
        jnp.concatenate(grads_q, axis=0),
        jnp.concatenate(grads_v, axis=0),
    )


def heads_fwd_kernel(
    split_ref, x_ref, gain_ref, mask_ref, w_ref, down_ref, up_ref, pers_ref, wf_ref, lw_ref,
    proj_ref, z_ref, h1_ref, lat_ref,
):
    @pl.when(pl.program_id(0) == 0)
    def _():
        normed, _ = norm_fwd(x_ref[...].astype(F32), gain_ref[...])
        h1_ref[...] = normed.astype(BF)
        latent = dot(h1_ref[...], down_ref[0])
        mask = mask_ref[...]
        for part in range(7):
            s = slice(part * AR, (part + 1) * AR)
            lat_ref[:, s] = (latent[:, s] * mask).astype(BF)

    base = dot(h1_ref[...], w_ref[0])
    pieces = []
    for part in range(7):
        s = slice(part * AR, (part + 1) * AR)
        piece = base[:, part * HEAD : (part + 1) * HEAD] + dot(lat_ref[:, s], up_ref[0, :, s], NT)
        proj_ref[:, part * HEAD : (part + 1) * HEAD] = piece
        pieces.append(piece)
    q, k, v = (pieces[i].astype(BF) for i in range(3))
    near, far = attend(q, k, v, pers_ref[0], pers_ref[1], allowed_mask(split_ref))
    att = attend_out(near.astype(BF), far.astype(BF), v, pers_ref[1])
    kn, _ = unit(pieces[3])
    qn, _ = unit(pieces[5])
    mem = memory_out(memory_terms(kn, qn, pieces[4], wf_ref, lw_ref))
    z_ref[...] = (att + jax.nn.sigmoid(pieces[6]) * mem).astype(BF)


def heads_fwd(split, x, gain, mask, a1, persistent, wf, lw):
    return pl.pallas_call(
        heads_fwd_kernel,
        grid=(H,),
        out_shape=(
            jax.ShapeDtypeStruct((ROWS, 7 * D), F32),
            jax.ShapeDtypeStruct((ROWS, D), BF),
            jax.ShapeDtypeStruct((ROWS, D), BF),
            jax.ShapeDtypeStruct((ROWS, 7 * AR), BF),
        ),
        in_specs=[
            pl.BlockSpec(memory_space=pltpu.SMEM),
            pl.BlockSpec((ROWS, D), lambda h: (0, 0)),
            pl.BlockSpec((1, D), lambda h: (0, 0)),
            pl.BlockSpec((ROWS, AR), lambda h: (0, 0)),
            pl.BlockSpec((1, D, HCOLS), lambda h: (h // 4, 0, h % 4)),
            pl.BlockSpec((1, D, HCOLS), lambda h: (0, 0, 4)),
            pl.BlockSpec((1, HEAD, HCOLS), lambda h: (1, h, 4)),
            pl.BlockSpec((2, NP, HEAD), lambda h: (0, 0, h)),
            pl.BlockSpec((1, MB, GROUP, GROUP), lambda h: (h, 0, 0, 0)),
            pl.BlockSpec((1, MB, 8, GROUP), lambda h: (h, 0, 0, 0)),
        ],
        out_specs=(
            pl.BlockSpec((ROWS, HCOLS), lambda h: (0, h)),
            pl.BlockSpec((ROWS, HEAD), lambda h: (0, h)),
            pl.BlockSpec((ROWS, D), lambda h: (0, 0)),
            pl.BlockSpec((ROWS, 7 * AR), lambda h: (0, 0)),
        ),
        compiler_params=pltpu.CompilerParams(vmem_limit_bytes=VMEM_LIMIT),
        name="heads_fwd",
    )(split, x, gain, mask, a1, a1, a1, persistent, wf, lw)


def ffn_kernel(
    x_ref, d_ref, z_ref, gain_ref, mask_ref, place_ref, w_out_ref, small_ref, w_up_ref, wd0_ref, wd1_ref,
    back_ref, dz_ref, dmid_ref, grads_ref,
    x2_ref, h2_ref, inv_ref, lat_out_ref, lat_up_ref, dl_down_ref, acc_ref, lat_acc_ref, dh_ref, dlat_ref,
):
    step = pl.program_id(0)
    out_down = lambda: small_ref[0, :, 0:128]
    out_up = lambda: small_ref[0, :, 128:256]
    up_down = lambda: small_ref[0, :, 256:512]
    down_up = lambda: small_ref[0, :, 512:640]

    @pl.when(step == 0)
    def _():
        mask = mask_ref[...]
        z = z_ref[...]
        lat_out_ref[...] = (dot(z, out_down()) * mask).astype(BF)
        x2 = x_ref[...].astype(F32) + (dot(z, w_out_ref[0]) + dot(lat_out_ref[...], out_up(), NT))
        x2_ref[...] = x2
        normed, inv = norm_fwd(x2, gain_ref[...])
        inv_ref[...] = jnp.broadcast_to(inv, inv_ref.shape)
        h2_ref[...] = normed.astype(BF)
        latent = dot(h2_ref[...], up_down())
        lat_up_ref[:, :AR] = (latent[:, :AR] * mask).astype(BF)
        lat_up_ref[:, AR:] = (latent[:, AR:] * mask).astype(BF)
        dl_down_ref[...] = (dot(d_ref[...], down_up()) * mask).astype(BF)
        acc_ref[...] = jnp.zeros_like(acc_ref)
        lat_acc_ref[...] = jnp.zeros_like(lat_acc_ref)
        dh_ref[...] = jnp.zeros_like(dh_ref)
        dlat_ref[...] = jnp.zeros_like(dlat_ref)

    h2 = h2_ref[...]
    d = d_ref[...]
    w_gate, w_lift = w_up_ref[0, :, :FB], w_up_ref[0, :, FB:]
    lat0, lat1 = lat_up_ref[:, :AR], lat_up_ref[:, AR:]
    uu0, uu1 = wd1_ref[0, :, 256:384], wd1_ref[0, :, 384:512]
    dd = wd1_ref[0, :, 512:640]
    wda, wdb = wd0_ref[0], wd1_ref[0, :, :256]
    gate = dot(h2, w_gate) + dot(lat0, uu0, NT)
    lift = dot(h2, w_lift) + dot(lat1, uu1, NT)
    sig = jax.nn.sigmoid(gate)
    silu = gate * sig
    act = (silu * lift).astype(BF)
    acc_ref[:, :768] += dot(act, wda)
    acc_ref[:, 768:] += dot(act, wdb)
    lat_acc_ref[...] += dot(act, dd)
    d_act = dot(d[:, :768], wda, NT) + dot(d[:, 768:], wdb, NT) + dot(dl_down_ref[...], dd, NT)
    d_gate = (d_act * lift * (sig * (1.0 + gate * (1.0 - sig)))).astype(BF)
    d_lift = (d_act * silu).astype(BF)
    dh_ref[...] += dot(d_gate, w_gate, NT) + dot(d_lift, w_lift, NT)
    dlat_ref[:, :AR] += dot(d_gate, uu0)
    dlat_ref[:, AR:] += dot(d_lift, uu1)
    chips = FB // 48
    first = pl.multiple_of(step * chips, chips)
    for place, term in (
        (0, dot(d_gate, lat0, TN)),
        (1, dot(d_lift, lat1, TN)),
        (2, dot(act, dl_down_ref[...], TN)),
    ):
        shaped = term.reshape(chips, 3, 16, AR).astype(BF)
        for k in range(3):
            if place < 2:
                at = k * 256 + place * AR
                grads_ref[0, pl.ds(first, chips), :, at : at + AR] = shaped[:, k]
            else:
                grads_ref[1, pl.ds(first, chips), :, k * AR : (k + 1) * AR] = shaped[:, k]

    @pl.when(step == pl.num_programs(0) - 1)
    def _():
        mask = mask_ref[...]
        lat_down = (lat_acc_ref[...] * mask).astype(BF)
        out = (x2_ref[...] + acc_ref[...] + dot(lat_down, down_up(), NT)).astype(BF)
        for m in range(MB):
            s = slice(m * GROUP, (m + 1) * GROUP)
            back_ref[:, m * D : (m + 1) * D] = dot(place_ref[m], out[s], TN).astype(BF)
        d = d_ref[...]
        h2 = h2_ref[...]
        z = z_ref[...]

        def put(half, at, value):
            grads_ref[half, :, :, at : at + AR] = value.reshape(64, 16, AR).astype(BF)

        put(0, 768, dot(d, lat_down, TN))
        dlu0 = (dlat_ref[:, :AR] * mask).astype(BF)
        dlu1 = (dlat_ref[:, AR:] * mask).astype(BF)
        put(1, 640, dot(h2, dlu0, TN))
        put(1, 768, dot(h2, dlu1, TN))
        ud = up_down()
        dh = dh_ref[...] + (dot(dlu0, ud[:, :AR], NT) + dot(dlu1, ud[:, AR:], NT))
        dmid = d.astype(F32) + norm_bwd(dh, x2_ref[...], inv_ref[:, :1], gain_ref[...])
        dmid_ref[...] = dmid
        dmb = dmid.astype(BF)
        dlo = (dot(dmb, out_up()) * mask).astype(BF)
        put(1, 384, dot(z, dlo, TN))
        put(1, 512, dot(dmb, lat_out_ref[...], TN))
        dz_ref[...] = (dot(dmb, w_out_ref[0], NT) + dot(dlo, out_down(), NT)).astype(BF)


def ffn(x, d, z, gain, mask, place, a2, a3):
    whole = lambda *shape: pl.BlockSpec(shape, lambda j: (0,) * len(shape))
    return pl.pallas_call(
        ffn_kernel,
        grid=(FFP // FB,),
        out_shape=(
            jax.ShapeDtypeStruct((GROUP, MB * D), BF),
            jax.ShapeDtypeStruct((ROWS, D), BF),
            jax.ShapeDtypeStruct((ROWS, D), F32),
            jax.ShapeDtypeStruct((2, 64, 16, 896), BF),
        ),
        in_specs=[
            whole(ROWS, D),
            whole(ROWS, D),
            whole(ROWS, D),
            whole(1, D),
            whole(ROWS, AR),
            whole(MB, GROUP, GROUP),
            pl.BlockSpec((1, D, D), lambda j: (1, 0, 3)),
            pl.BlockSpec((1, D, D), lambda j: (0, 0, 3)),
            pl.BlockSpec((1, D, 2 * FB), lambda j: (j // 2, 0, j % 2)),
            pl.BlockSpec((1, FB, 768), lambda j: (0, j, 0)),
            pl.BlockSpec((1, FB, 768), lambda j: (1, j, 0)),
        ],
        out_specs=(
            whole(GROUP, MB * D),
            whole(ROWS, D),
            whole(ROWS, D),
            whole(2, 64, 16, 896),
        ),
        scratch_shapes=[
            pltpu.VMEM((ROWS, D), F32),
            pltpu.VMEM((ROWS, D), BF),
            pltpu.VMEM((ROWS, 128), F32),
            pltpu.VMEM((ROWS, AR), BF),
            pltpu.VMEM((ROWS, 2 * AR), BF),
            pltpu.VMEM((ROWS, AR), BF),
            pltpu.VMEM((ROWS, D), F32),
            pltpu.VMEM((ROWS, AR), F32),
            pltpu.VMEM((ROWS, D), F32),
            pltpu.VMEM((ROWS, 2 * AR), F32),
        ],
        compiler_params=pltpu.CompilerParams(vmem_limit_bytes=VMEM_LIMIT),
        name="ffn",
    )(x, d, z, gain, mask, place, a2, a2, a2, a3, a3)


def heads_bwd_kernel(
    split_ref, x_ref, gain_ref, mask_ref, place_ref, proj_ref, dz_ref, dmid_ref, h1_ref, lat_ref,
    w_ref, down_ref, up_ref, pers_ref, wf_ref, lw_ref,
    back_ref, grads_ref,
    dh_ref, dlat_ref,
):
    step = pl.program_id(0)

    @pl.when(step == 0)
    def _():
        dh_ref[...] = jnp.zeros_like(dh_ref)
        dlat_ref[...] = jnp.zeros_like(dlat_ref)

    pieces = [proj_ref[:, p * HEAD : (p + 1) * HEAD] for p in range(7)]
    q, k, v = (pieces[i].astype(BF) for i in range(3))
    pk, pv = pers_ref[0], pers_ref[1]
    near, far = attend(q, k, v, pk, pv, allowed_mask(split_ref))
    near_half = near.astype(BF)
    dz = dz_ref[...]
    d_near = by_group(lambda s, g: dot(dz[s], v[s], NT))
    d_far = dot(dz, pv, NT)
    d_v = by_group(lambda s, g: dot(near_half[s], dz[s], TN))
    total = jnp.sum(d_near * near, axis=-1, keepdims=True) + jnp.sum(
        d_far * far, axis=-1, keepdims=True
    )
    ds_near = (near * (d_near - total) * SCALE).astype(BF)
    ds_far = (far * (d_far - total) * SCALE).astype(BF)
    d_q = by_group(lambda s, g: dot(ds_near[s], k[s])) + dot(ds_far, pk)
    d_k = by_group(lambda s, g: dot(ds_near[s], q[s], TN))

    dzf = dz.astype(F32)
    opening = jax.nn.sigmoid(pieces[6])
    kn, k_inv = unit(pieces[3])
    qn, q_inv = unit(pieces[5])
    kept = memory_terms(kn, qn, pieces[4], wf_ref, lw_ref)
    mem = memory_out(kept)
    d_open = dzf * mem * (opening * (1.0 - opening))
    d_kn, d_qn, d_mv = memory_bwd(kept, dzf * opening)
    d_mk = unit_bwd(d_kn, pieces[3], k_inv)
    d_mq = unit_bwd(d_qn, pieces[5], q_inv)
    dy = [item.astype(BF) for item in (d_q, d_k, d_v, d_mk, d_mv, d_mq, d_open)]
    dh_ref[...] += dot(jnp.concatenate(dy, axis=1), w_ref[0], NT)
    first = pl.multiple_of(step * 8, 8)
    for part in range(7):
        s = slice(part * AR, (part + 1) * AR)
        dlat_ref[:, s] += dot(dy[part], up_ref[0, :, s])
        grads_ref[1, pl.ds(first, 8), :, s] = (
            dot(dy[part], lat_ref[:, s], TN).reshape(8, 16, AR).astype(BF)
        )

    @pl.when(step == pl.num_programs(0) - 1)
    def _():
        mask = mask_ref[...]
        dlat = jnp.concatenate(
            [(dlat_ref[:, p * AR : (p + 1) * AR] * mask).astype(BF) for p in range(7)], axis=1
        )
        grads_ref[0] = dot(h1_ref[...], dlat, TN).reshape(64, 16, 7 * AR).astype(BF)
        dh = dh_ref[...] + dot(dlat, down_ref[0], NT)
        x = x_ref[...].astype(F32)
        inv = lax.rsqrt(jnp.mean(x * x, axis=-1, keepdims=True) + EPS)
        dx = (dmid_ref[...] + norm_bwd(dh, x, inv, gain_ref[...])).astype(BF)
        for m in range(MB):
            s = slice(m * GROUP, (m + 1) * GROUP)
            back_ref[:, m * D : (m + 1) * D] = dot(place_ref[m], dx[s], TN).astype(BF)


def heads_bwd(split, x, gain, mask, place, proj, dz, dmid, h1, lat, a1, persistent, wf, lw):
    whole = lambda *shape: pl.BlockSpec(shape, lambda h: (0,) * len(shape))
    return pl.pallas_call(
        heads_bwd_kernel,
        grid=(H,),
        out_shape=(
            jax.ShapeDtypeStruct((GROUP, MB * D), BF),
            jax.ShapeDtypeStruct((2, 64, 16, 896), BF),
        ),
        in_specs=[
            pl.BlockSpec(memory_space=pltpu.SMEM),
            whole(ROWS, D),
            whole(1, D),
            whole(ROWS, AR),
            whole(MB, GROUP, GROUP),
            pl.BlockSpec((ROWS, HCOLS), lambda h: (0, h)),
            pl.BlockSpec((ROWS, HEAD), lambda h: (0, h)),
            whole(ROWS, D),
            whole(ROWS, D),
            whole(ROWS, 7 * AR),
            pl.BlockSpec((1, D, HCOLS), lambda h: (h // 4, 0, h % 4)),
            pl.BlockSpec((1, D, HCOLS), lambda h: (0, 0, 4)),
            pl.BlockSpec((1, HEAD, HCOLS), lambda h: (1, h, 4)),
            pl.BlockSpec((2, NP, HEAD), lambda h: (0, 0, h)),
            pl.BlockSpec((1, MB, GROUP, GROUP), lambda h: (h, 0, 0, 0)),
            pl.BlockSpec((1, MB, 8, GROUP), lambda h: (h, 0, 0, 0)),
        ],
        out_specs=(whole(GROUP, MB * D), whole(2, 64, 16, 896)),
        scratch_shapes=[pltpu.VMEM((ROWS, D), F32), pltpu.VMEM((ROWS, 7 * AR), F32)],
        compiler_params=pltpu.CompilerParams(vmem_limit_bytes=VMEM_LIMIT),
        name="heads_bwd",
    )(split, x, gain, mask, place, proj, dz, dmid, h1, lat, a1, a1, a1, persistent, wf, lw)


def by_rank(value, parts):
    rows = value.shape[1]
    return value.reshape(NAD, rows, parts, R).transpose(1, 2, 0, 3).reshape(rows, parts * AR)


def by_rank_t(value, parts):
    cols = value.shape[2]
    return value.reshape(NAD, parts, R, cols).transpose(3, 1, 0, 2).reshape(cols, parts * AR)


def pack_shards(w_in, w_out, w_up, w_down, in_down, in_up, out_down, out_up, up_down, up_up, down_down, down_up):
    rows = w_in.shape[0]
    heads = w_in.reshape(rows, 7, H, HEAD).transpose(0, 2, 1, 3).reshape(rows, 2, 4 * HCOLS)
    a1 = jnp.stack(
        [
            jnp.concatenate([heads[:, 0], by_rank(in_down, 7)], axis=1),
            jnp.concatenate([heads[:, 1], by_rank_t(in_up, 7)], axis=1),
        ]
    )
    up = w_up.reshape(rows, 2, N_DEV, FF_SHARD)
    up = jnp.pad(up, ((0, 0), (0, 0), (0, 0), (0, FF_PAD - FF_SHARD)))
    up = up.reshape(rows, 2, FFP // FB, FB).transpose(0, 2, 1, 3).reshape(rows, 2, 4 * FB)
    small = jnp.concatenate(
        [by_rank(out_down, 1), by_rank_t(out_up, 1), by_rank(up_down, 2), by_rank_t(down_up, 1)], axis=1
    )
    small = jnp.pad(small, ((0, 0), (0, D - small.shape[1])))
    a2 = jnp.stack(
        [jnp.concatenate([up[:, 0], small], axis=1), jnp.concatenate([up[:, 1], w_out], axis=1)]
    )
    rest = jnp.concatenate([w_down[:, 768:], by_rank_t(up_up, 2), by_rank(down_down, 1)], axis=1)
    rest = jnp.pad(rest, ((0, 0), (0, 128)))
    a3 = jnp.stack([w_down[:, :768], rest])
    a3 = jnp.pad(a3, ((0, 0), (0, FF_PAD - FF_SHARD), (0, 0)))
    return a1, a2, a3


def un_rank(value, parts):
    rows = value.shape[0]
    return value.reshape(rows, parts, NAD, R).transpose(2, 0, 1, 3).reshape(NAD, rows, parts * R)


def un_rank_t(value, parts):
    cols = value.shape[0]
    return value.reshape(cols, parts, NAD, R).transpose(2, 1, 3, 0).reshape(NAD, parts * R, cols)


def unpack_grads(ffn_chip, heads_chip, core):
    def rows8(value):
        return lax.dynamic_slice_in_dim(value, core * 8, 8, axis=0)

    grad_id = un_rank(rows8(heads_chip[0]), 7)
    grad_iu = un_rank_t(rows8(heads_chip[1]), 7)
    tall = lambda value, width: value.reshape(16, 3, width).transpose(1, 0, 2).reshape(48, width)

    def rows22(value):
        return lax.dynamic_slice_in_dim(value, core * FF_PAD, FF_PAD, axis=0)[:FF_SHARD]

    grad_uu = un_rank_t(rows22(tall(ffn_chip[0, :, :768], 256)), 2)
    grad_dd = un_rank(rows22(tall(ffn_chip[1, :, :384], AR)), 1)
    grad_du = un_rank_t(rows8(ffn_chip[0, :, 768:]), 1)
    grad_od = un_rank(rows8(ffn_chip[1, :, 384:512]), 1)
    grad_ou = un_rank_t(rows8(ffn_chip[1, :, 512:640]), 1)
    grad_ud = un_rank(rows8(ffn_chip[1, :, 640:896]), 2)
    return grad_id, grad_iu, grad_od, grad_ou, grad_ud, grad_uu, grad_dd, grad_du


def local_layer(x, d, dec, dec_t, lengths, ids, gain_mix, gain_ffn, persistent, place, a1, a2, a3):
    split = (lengths[:, 0] < GROUP).astype(F32)
    row_ids = jnp.where(
        (jnp.arange(GROUP)[None, :] >= lengths[:, :1]), ids[:, 1:], ids[:, :1]
    ).reshape(ROWS)
    mask = (row_ids[:, None] == (jnp.arange(AR) // R)[None, :]).astype(F32)
    gain_mix, gain_ffn = gain_mix[None, :], gain_ffn[None, :]
    wf, lw = decay_weights(1.0 - split, dec, dec_t)
    proj, z, h1, lat = heads_fwd(split, x, gain_mix, mask, a1, persistent, wf, lw)
    back, dz, dmid, grads_ffn = ffn(x, d, z, gain_ffn, mask, place, a2, a3)
    back_grad, grads_heads = heads_bwd(
        split, x, gain_mix, mask, place, proj, dz, dmid, h1, lat, a1, persistent, wf, lw
    )
    return back, back_grad, grads_ffn, grads_heads
MESH = pl.DeviceIdType.MESH


def position():
    me = lax.axis_index("fsdp")
    chip = me // 2
    return me % 2, (chip // 16, (chip // 4) % 4, chip % 4)


def device(core, spot):
    return (((spot[0] * 4 + spot[1]) * 4 + spot[2]) * 2 + core,)


def moved(spot, axis, by):
    return tuple((v + by + 4) % 4 if i == axis else v for i, v in enumerate(spot))


def cut(lanes, count):
    base, extra = divmod(lanes, count)
    runs, at = [], 0
    for i in range(count):
        size = base + (1 if i < extra else 0)
        runs.append((at * 128, size * 128))
        at += size
    return runs


class Sends:
    def __init__(self, send_sem, recv_sem):
        self.send_sem, self.recv_sem = send_sem, recv_sem
        self.slots, self.open = {}, []

    def copy(self, name, src, dst, target):
        slot = self.slots.setdefault(name, len(self.slots))
        return pltpu.make_async_remote_copy(
            src_ref=src, dst_ref=dst, send_sem=self.send_sem.at[slot], recv_sem=self.recv_sem.at[slot],
            device_id=target, device_id_type=MESH,
        )

    def start(self, name, src, dst, target):
        copy = self.copy(name, src, dst, target)
        copy.start()
        self.open.append(copy)

    def arrived(self, name, ref, target):
        self.copy(name, ref, ref, target).wait_recv()

    def drain(self):
        for copy in self.open:
            copy.wait_send()
        self.open = []


def greet(targets):
    barrier = pltpu.get_barrier_semaphore()
    for target in targets:
        pl.semaphore_signal(barrier, inc=1, device_id=target, device_id_type=MESH)
    pl.semaphore_wait(barrier, len(targets))


def gather_kernel(shapes, *refs):
    n = len(shapes)
    mine, outs = refs[:n], refs[n : 2 * n]
    inc, stage = refs[2 * n : 3 * n], refs[3 * n : 4 * n]
    send_sem, recv_sem, local_sem = refs[4 * n :]
    core, spot = position()
    sibling = device(1 - core, spot)
    sends = Sends(send_sem, recv_sem)
    greet([sibling] + [device(core, moved(spot, a, by)) for a in range(3) for by in (1, -1)])

    for i in range(n):
        sends.start(("pair", i), mine[i].at[1 - core], inc[i], sibling)
    for i in range(n):
        sends.arrived(("pair", i), inc[i], sibling)
        own, other = mine[i][core], inc[i][...]
        first = jnp.where(core == 0, own, other)
        last = jnp.where(core == 0, other, own)
        stage[i][...] = jnp.concatenate([first, last], axis=0).astype(BF)
        pltpu.make_async_copy(
            stage[i], outs[i].at[core, spot[0], spot[1], spot[2]], local_sem.at[i]
        ).start()
    for i in range(n):
        pltpu.make_async_copy(
            stage[i], outs[i].at[core, spot[0], spot[1], spot[2]], local_sem.at[i]
        ).wait()

    def block(i, whole_axes, spot_at, cols, half=None):
        index = [
            pl.ds(0, 4) if a in whole_axes else pl.ds(spot_at[a], 1) for a in range(3)
        ]
        half = core if half is None else half
        return outs[i].at[half, index[0], index[1], index[2], :, pl.ds(cols[0], cols[1])]

    jobs = [
        (i, part, cols)
        for i in range(n)
        for part, cols in enumerate(cut(shapes[i][1] // 128, 3))
    ]

    def two(cols):
        runs = cut(cols[1] // 128, 2)
        return [(cols[0] + at, size) for at, size in runs]

    forwards = []

    def forward(name, i, whole_axes, spot_at, cols):
        ref = block(i, whole_axes, spot_at, cols)
        sends.start(name, ref, ref, sibling)
        forwards.append((name, i, whole_axes, spot_at, cols))

    for phase in range(3):
        for i, part, cols in jobs:
            axis = (part + phase) % 3
            done = [(part + p) % 3 for p in range(phase)]
            right, left = device(core, moved(spot, axis, 1)), device(core, moved(spot, axis, -1))
            parts = two(cols)
            for step, (to_right, to_left) in enumerate(((0, 1), (1, 0))):
                ref = block(i, done, spot, parts[to_right])
                sends.start((i, part, phase, "r", step), ref, ref, right)
                ref = block(i, done, spot, parts[to_left])
                sends.start((i, part, phase, "l", step), ref, ref, left)
            if phase == 2:
                forward((i, part, "f"), i, done, spot, cols)
        for i, part, cols in jobs:
            axis = (part + phase) % 3
            done = [(part + p) % 3 for p in range(phase)]
            right, left = device(core, moved(spot, axis, 1)), device(core, moved(spot, axis, -1))
            at_left, at_right = moved(spot, axis, -1), moved(spot, axis, 1)
            parts = two(cols)
            ref = block(i, done, at_left, parts[0])
            sends.arrived((i, part, phase, "r", 0), ref, left)
            sends.start((i, part, phase, "r", 2), ref, ref, right)
            if phase == 2:
                forward((i, part, "f", 0), i, done, at_left, parts[0])
            ref = block(i, done, at_right, parts[1])
            sends.arrived((i, part, phase, "l", 0), ref, right)
            sends.start((i, part, phase, "l", 2), ref, ref, left)
            if phase == 2:
                forward((i, part, "f", 1), i, done, at_right, parts[1])
        for i, part, cols in jobs:
            axis = (part + phase) % 3
            done = [(part + p) % 3 for p in range(phase)]
            right, left = device(core, moved(spot, axis, 1)), device(core, moved(spot, axis, -1))
            at_left, at_right = moved(spot, axis, -1), moved(spot, axis, 1)
            far = moved(spot, axis, 2)
            parts = two(cols)
            for k, (name, at, cc, source) in enumerate(
                (
                    (("r", 1), at_left, parts[1], left),
                    (("l", 1), at_right, parts[0], right),
                    (("r", 2), far, parts[0], left),
                    (("l", 2), far, parts[1], right),
                )
            ):
                sends.arrived((i, part, phase) + name, block(i, done, at, cc), source)
                if phase == 2:
                    forward((i, part, "f", 2 + k), i, done, at, cc)
    for name, i, whole_axes, spot_at, cols in forwards:
        sends.arrived(name, block(i, whole_axes, spot_at, cols, 1 - core), sibling)
    sends.drain()


def gather(mine, collective_id):
    shapes = [(m.shape[1], m.shape[2]) for m in mine]
    n = len(shapes)
    slots = n * (1 + 3 * (3 * 6 + 7))
    return pl.pallas_call(
        functools.partial(gather_kernel, shapes),
        out_shape=tuple(
            jax.ShapeDtypeStruct((2, 4, 4, 4, 2 * r, c), BF) for r, c in shapes
        ),
        in_specs=[pl.BlockSpec(memory_space=pltpu.VMEM)] * n,
        out_specs=tuple(pl.BlockSpec(memory_space=pl.ANY) for _ in shapes),
        scratch_shapes=[pltpu.VMEM((r, c), F32) for r, c in shapes]
        + [pltpu.VMEM((2 * r, c), BF) for r, c in shapes]
        + [
            pltpu.SemaphoreType.DMA((slots,)),
            pltpu.SemaphoreType.DMA((slots,)),
            pltpu.SemaphoreType.DMA((n,)),
        ],
        compiler_params=pltpu.CompilerParams(
            collective_id=collective_id, has_side_effects=True, vmem_limit_bytes=VMEM_LIMIT
        ),
        name="gather",
    )(*mine)


def scatter_kernel(count, *refs):
    g_refs, out_refs = refs[:count], refs[count : 2 * count]
    inc0, total, inc1, inc2, inc3, t1, t2 = refs[2 * count : 2 * count + 7]
    send_sem, recv_sem = refs[2 * count + 7 :]
    core, spot = position()
    sibling = device(1 - core, spot)
    sends = Sends(send_sem, recv_sem)
    peers = [(a, by) for a in range(3) for by in (1, 3, 2)]
    greet([sibling] + [device(core, moved(spot, a, by)) for a, by in peers])
    parts = cut(7, 3)
    for i in range(count):
        for x in range(4):
            sends.start((i, "pair", x), g_refs[i].at[1 - core, pl.ds(16 * x, 16)], inc0.at[i, x], sibling)
    for i in range(count):
        for x in range(4):
            sends.arrived((i, "pair", x), inc0.at[i, x], sibling)
            both = g_refs[i][core, pl.ds(16 * x, 16)].astype(F32) + inc0[i, x].astype(F32)
            total[i, x] = both.reshape(4, 4, 16, 896).astype(BF)

    def index(done, axis, at):
        return tuple(
            spot[a] if a in done else (at if a == axis else slice(None)) for a in range(3)
        )

    def squeeze(done, axis, a_order):
        return [a for a in range(3) if a not in done and a != axis]

    jobs = [(i, part, cols) for i in range(count) for part, cols in enumerate(parts)]
    for i, part, cols in jobs:
        axis = part
        cs = pl.ds(cols[0], cols[1])
        for k, by in enumerate((2, 1, 3)):
            to = moved(spot, axis, by)
            idx = index((), axis, to[axis])
            sends.start((i, part, 1, by), total.at[(i,) + idx + (slice(None), cs)], inc1.at[i, k, :, :, :, cs], device(core, to))
    for i, part, cols in jobs:
        axis = part
        cs = pl.ds(cols[0], cols[1])
        idx = index((), axis, spot[axis])
        acc = total[(i,) + idx + (slice(None), cs)].astype(F32)
        for k, by in enumerate((2, 1, 3)):
            frm = moved(spot, axis, -by)
            sends.arrived((i, part, 1, by), inc1.at[i, k, :, :, :, cs], device(core, frm))
            acc = acc + inc1[i, k, :, :, :, cs].astype(F32)
        t1[i, :, :, :, cs] = acc.astype(BF)
        axis2 = (part + 1) % 3
        rest = [a for a in range(3) if a != axis]
        for k, by in enumerate((2, 1, 3)):
            to = moved(spot, axis2, by)
            src = t1.at[i, to[axis2], :, :, cs] if rest[0] == axis2 else t1.at[i, :, to[axis2], :, cs]
            sends.start((i, part, 2, by), src, inc2.at[i, k, :, :, cs], device(core, to))
    for i, part, cols in jobs:
        axis2, axis3 = (part + 1) % 3, (part + 2) % 3
        rest = [a for a in range(3) if a != part]
        cs = pl.ds(cols[0], cols[1])
        own = spot[axis2]
        acc = (t1[i, own, :, :, cs] if rest[0] == axis2 else t1[i, :, own, :, cs]).astype(F32)
        for k, by in enumerate((2, 1, 3)):
            frm = moved(spot, axis2, -by)
            sends.arrived((i, part, 2, by), inc2.at[i, k, :, :, cs], device(core, frm))
            acc = acc + inc2[i, k, :, :, cs].astype(F32)
        t2[i, :, :, cs] = acc.astype(BF)
        for k, by in enumerate((2, 1, 3)):
            to = moved(spot, axis3, by)
            sends.start((i, part, 3, by), t2.at[i, to[axis3], :, cs], inc3.at[i, k, :, cs], device(core, to))
    for i, part, cols in jobs:
        axis3 = (part + 2) % 3
        cs = pl.ds(cols[0], cols[1])
        acc = t2[i, spot[axis3], :, cs].astype(F32)
        for k, by in enumerate((2, 1, 3)):
            frm = moved(spot, axis3, -by)
            sends.arrived((i, part, 3, by), inc3.at[i, k, :, cs], device(core, frm))
            acc = acc + inc3[i, k, :, cs].astype(F32)
        out_refs[i][core, :, cs] = acc
    for i in range(count):
        sends.start((i, "last"), out_refs[i].at[core], out_refs[i].at[core], sibling)
    for i in range(count):
        sends.arrived((i, "last"), out_refs[i].at[1 - core], sibling)
    sends.drain()


def scatter(grads, collective_id):
    n = len(grads)
    slots = n * (4 + 3 * 9 + 1)
    return pl.pallas_call(
        functools.partial(scatter_kernel, n),
        out_shape=tuple(jax.ShapeDtypeStruct((2, 16, 896), F32) for _ in grads),
        in_specs=[pl.BlockSpec(memory_space=pltpu.VMEM)] * n,
        out_specs=tuple(pl.BlockSpec(memory_space=pltpu.VMEM) for _ in grads),
        scratch_shapes=[
            pltpu.VMEM((n, 4, 16, 16, 896), BF),
            pltpu.VMEM((n, 4, 4, 4, 16, 896), BF),
            pltpu.VMEM((n, 3, 4, 4, 16, 896), BF),
            pltpu.VMEM((n, 3, 4, 16, 896), BF),
            pltpu.VMEM((n, 3, 16, 896), BF),
            pltpu.VMEM((n, 4, 4, 16, 896), BF),
            pltpu.VMEM((n, 4, 16, 896), BF),
            pltpu.SemaphoreType.DMA((slots,)),
            pltpu.SemaphoreType.DMA((slots,)),
        ],
        compiler_params=pltpu.CompilerParams(
            collective_id=collective_id, has_side_effects=True, vmem_limit_bytes=VMEM_LIMIT
        ),
        name="scatter",
    )(*grads)


def body(
    tokens, cotangent, decays, route, lengths, adapter_ids, gain_mix, gain_ffn, persistent,
    w_in, w_out, w_up, w_down, in_down, in_up, out_down, out_up, up_down, up_up, down_down, down_up,
):
    me = lax.axis_index("fsdp")
    packed = pack_shards(
        w_in, w_out, w_up, w_down, in_down, in_up, out_down, out_up, up_down, up_up, down_down, down_up
    )
    a1, a2, a3 = gather([item.astype(F32) for item in packed], 0)
    a1 = a1.reshape(2, D, a1.shape[-1])
    a2 = a2.reshape(2, D, a2.shape[-1])
    a3 = a3.reshape(2, FFP, a3.shape[-1])

    spots = jnp.arange(GROUP, dtype=jnp.int32)
    own = lax.dynamic_slice_in_dim(route, me * GROUP, GROUP, axis=1)
    send = (own[:, None, :] // GROUP == spots[None, :, None]).astype(BF)
    blocks = route.reshape(MB, N_DEV, GROUP)
    landing = jnp.sum(jnp.where(blocks // GROUP == me, blocks % GROUP, 0), axis=2)
    place = (landing[:, None, :] == spots[None, :, None]).astype(BF)

    def permute(onehot, values):
        return jnp.einsum("mij,mjd->mid", onehot, values, preferred_element_type=F32).astype(BF)

    def exchange(values):
        return lax.all_to_all(values, "fsdp", split_axis=0, concat_axis=0, tiled=True)

    out_x = permute(send, tokens)
    out_d = permute(send, cotangent)
    out_r = permute(send, decays)
    sent = jnp.concatenate(
        [out_x[0], out_x[1], out_d[0], out_d[1], out_r[0], out_r[1], jnp.zeros((GROUP, 80), BF)], axis=1
    )
    got = exchange(sent)
    at = lambda lo, width: jnp.stack([got[:, lo : lo + width], got[:, lo + width : lo + 2 * width]])
    x = permute(place, at(0, D)).reshape(ROWS, D)
    d = permute(place, at(2 * D, D)).reshape(ROWS, D)
    dec = permute(place, at(4 * D, 3 * H)).astype(F32).reshape(ROWS, 3 * H)
    back, back_grad, grads_ffn, grads_heads = local_layer(
        x, d, dec, dec.T, lengths[:, 0], adapter_ids[:, 0], gain_mix, gain_ffn, persistent, place, a1, a2, a3
    )

    def home(values):
        values = exchange(values)
        return jnp.einsum(
            "mij,mid->mjd", send, values.reshape(GROUP, MB, D).transpose(1, 0, 2), preferred_element_type=F32
        ).astype(BF)

    ffn_chip, heads_chip = scatter([grads_ffn, grads_heads], 1)
    return (home(back), home(back_grad)) + unpack_grads(ffn_chip, heads_chip, me % 2)


def solution(mesh):
    rows, cols = P(None, "fsdp", None), P(None, None, "fsdp")
    weight = P("fsdp", None)
    return jax.shard_map(
        body,
        mesh=mesh,
        in_specs=(rows, rows, rows, P(), rows, rows, P(), P(), P())
        + (weight,) * 4
        + (rows, cols) * 4,
        out_specs=(rows, rows) + (rows, cols) * 4,
        check_vma=False,
    )
```

```python
import functools
import math

import jax
import jax.numpy as jnp
from jax import lax
from jax.experimental import pallas as pl
from jax.experimental.pallas import tpu as pltpu
from jax.sharding import PartitionSpec as P

D = 1024
H = 8
HEAD = 128
FF = 2816
R = 16
NAD = 8
NP = 16
SPAN = 64
GROUP = 128
MB = 2
ROWS = MB * GROUP
N_DEV = 128
AR = NAD * R
HCOLS = 7 * HEAD
FF_SHARD = FF // N_DEV
FF_PAD = 24
FFP = FF_PAD * N_DEV
FB = 768
EPS = 1e-05
SCALE = 1.0 / math.sqrt(HEAD)
VMEM_LIMIT = 60 * 1024 * 1024
BF = jnp.bfloat16
F32 = jnp.float32

NN = (((1,), (0,)), ((), ()))
NT = (((1,), (1,)), ((), ()))
TN = (((0,), (0,)), ((), ()))


def dot(left, right, dims=NN):
    return lax.dot_general(left, right, dims, preferred_element_type=F32)


def exact(left, right, dims=NN):
    return lax.dot_general(
        left, right, dims, precision=lax.Precision.HIGHEST, preferred_element_type=F32
    )


def halves(value):
    high = value.astype(BF)
    return high, (value - high.astype(F32)).astype(BF)


def dot3(left, right, dims=NN):
    lh, ll = left
    rh, rl = right
    return dot(lh, rh, dims) + (dot(lh, rl, dims) + dot(ll, rh, dims))


def norm_fwd(values, gain):
    inv = lax.rsqrt(jnp.mean(values * values, axis=-1, keepdims=True) + EPS)
    return values * inv * gain, inv


def norm_bwd(grad, values, inv, gain):
    scaled = grad * gain
    return inv * (scaled - values * (inv * inv * jnp.mean(values * scaled, axis=-1, keepdims=True)))


def decay_kernel(split_ref, dec_ref, dect_ref, wf_ref, lw_ref):
    rows = lax.broadcasted_iota(jnp.int32, (GROUP, GROUP), 0)
    cols = lax.broadcasted_iota(jnp.int32, (GROUP, GROUP), 1)
    lower = (rows >= cols) & ((rows >= SPAN) == (cols >= SPAN))
    tri = lower.astype(F32)
    second = rows >= SPAN
    for g in range(MB):
        keep = 1.0 - split_ref[g]
        here = dec_ref[g * GROUP : (g + 1) * GROUP, :]
        here_t = dect_ref[:, g * GROUP : (g + 1) * GROUP]
        run = exact(tri, jnp.log(here[:, : 2 * H]))
        run_t = exact(jnp.log(here_t[: 2 * H, :]), tri, NT)
        for h in range(H):
            gap = run[:, h : h + 1] - run_t[h : h + 1, :]
            retain = jnp.exp(jnp.where(lower, gap, -1e30))
            gap = run[:, H + h : H + h + 1] - run_t[H + h : H + h + 1, :]
            moment = jnp.exp(jnp.where(lower, gap, -1e30))
            pairs = exact(retain, moment)
            theta = here_t[2 * H + h : 2 * H + h + 1, :]
            moment_run = jnp.exp(run_t[H + h : H + h + 1, :])
            carry = jnp.sum(retain * moment_run, axis=1, keepdims=True)
            last_weight = pairs[SPAN - 1 : SPAN, :] * theta * keep
            last_moment = moment[SPAN - 1 : SPAN, :] * theta * keep
            across = jnp.exp(run[:, h : h + 1]) * last_weight + carry * last_moment
            wf_ref[h, g] = pairs * theta + jnp.where(second, across, 0.0)
            lw_ref[h, g] = jnp.broadcast_to(last_weight, (8, GROUP))


def allowed_mask(split_ref):
    rows = lax.broadcasted_iota(jnp.int32, (ROWS, GROUP), 0)
    cols = lax.broadcasted_iota(jnp.int32, (ROWS, GROUP), 1)
    local = rows % GROUP
    group = rows // GROUP
    split = jnp.where(group == 0, split_ref[0], split_ref[1]) > 0.5
    return (local >= cols) & jnp.logical_not(split & (local >= SPAN) & (cols < SPAN))


def by_group(make):
    return jnp.concatenate([make(slice(0, GROUP), 0), make(slice(GROUP, ROWS), 1)], axis=0)


def attend(q, k, v, pk, pv, allowed):
    near = by_group(lambda s, g: dot(q[s], k[s], NT))
    far = dot(q, pk, NT) * SCALE
    near = jnp.where(allowed, near * SCALE, -1000000000.0)
    top = jnp.maximum(
        jnp.max(near, axis=-1, keepdims=True), jnp.max(far, axis=-1, keepdims=True)
    )
    near = jnp.exp(near - top)
    far = jnp.exp(far - top)
    inv = 1.0 / (jnp.sum(near, axis=-1, keepdims=True) + jnp.sum(far, axis=-1, keepdims=True))
    near = near * inv
    far = far * inv
    return near, far


def attend_out(near_half, far_half, v, pv):
    return by_group(lambda s, g: dot(near_half[s], v[s])) + dot(far_half, pv)


def unit(values):
    inv = lax.rsqrt(jnp.mean(values * values, axis=-1, keepdims=True) + EPS)
    return values * (inv * SCALE), inv


def unit_bwd(grad, values, inv):
    return (inv * SCALE) * (
        grad - values * (inv * inv * jnp.mean(values * grad, axis=-1, keepdims=True))
    )


def memory_terms(kn, qn, mv, wf_ref, lw_ref):
    second = lax.broadcasted_iota(jnp.int32, (GROUP, GROUP), 0) >= SPAN
    kept = []
    for g in range(MB):
        s = slice(g * GROUP, (g + 1) * GROUP)
        kh, qh = halves(kn[s]), halves(qn[s])
        wf = wf_ref[0, g]
        lw = jnp.where(second, lw_ref[0, g][0:1, :], 0.0)
        kk = dot3(kh, kh, NT) * lw
        qk = dot3(qh, kh, NT) * wf
        kk_half = halves(kk)
        mvh = halves(mv[s])
        err = mv[s] - dot3(kk_half, mvh)
        errh = halves(err)
        qk_half = halves(qk)
        kept.append((kh, qh, wf, lw, kk_half, qk_half, mvh, errh))
    return kept


def memory_out(kept):
    return jnp.concatenate([dot3(item[5], item[7]) for item in kept], axis=0)


def memory_bwd(kept, grad):
    grads_k, grads_q, grads_v = [], [], []
    for g in range(MB):
        kh, qh, wf, lw, kk_half, qk_half, mvh, errh = kept[g]
        gh = halves(grad[g * GROUP : (g + 1) * GROUP])
        d_qk = dot3(gh, errh, NT) * wf
        d_err = dot3(qk_half, gh, TN)
        deh = halves(d_err)
        d_v = d_err - dot3(kk_half, deh, TN)
        d_kk = dot3(deh, mvh, NT) * lw
        dqh = halves(d_qk)
        dkh = halves(d_kk)
        grads_q.append(dot3(dqh, kh))
        grads_k.append(dot3(dqh, qh, TN) - (dot3(dkh, kh) + dot3(dkh, kh, TN)))
        grads_v.append(d_v)
    return (
        jnp.concatenate(grads_k, axis=0),
        jnp.concatenate(grads_q, axis=0),
        jnp.concatenate(grads_v, axis=0),
    )


AXES = ("x", "z", "y")
MESH = pl.DeviceIdType.MESH


def position():
    me = lax.axis_index("fsdp")
    chip = me // 2
    return me % 2, (chip // 16, (chip // 4) % 4, chip % 4)


def device(core, spot):
    return (((spot[0] * 4 + spot[1]) * 4 + spot[2]) * 2 + core,)


def moved(spot, axis, by):
    return tuple((v + by + 4) % 4 if i == axis else v for i, v in enumerate(spot))


def cut(lanes, count):
    base, extra = divmod(lanes, count)
    runs, at = [], 0
    for i in range(count):
        size = base + (1 if i < extra else 0)
        runs.append((at * 128, size * 128))
        at += size
    return runs


def neighbours(core, spot):
    found = {}
    for axis in range(3):
        for by in (1, 2, 3):
            there = moved(spot, axis, by)
            found[axis, by] = (there, device(core, there))
    return found


class Sends:
    def __init__(self, send_sem, recv_sem):
        self.send_sem, self.recv_sem = send_sem, recv_sem
        self.slots, self.open = {}, []

    def copy(self, name, src, dst, target):
        slot = self.slots.setdefault(name, len(self.slots))
        return pltpu.make_async_remote_copy(
            src_ref=src, dst_ref=dst, send_sem=self.send_sem.at[slot], recv_sem=self.recv_sem.at[slot],
            device_id=target, device_id_type=MESH,
        )

    def start(self, name, make):
        self.copy(name, *make()).start()
        self.open.append((name, make))

    def arrived(self, name, ref, target):
        self.copy(name, ref, ref, target).wait_recv()

    def drain(self):
        for name, make in self.open:
            self.copy(name, *make()).wait_send()
        self.open = []


def greet(targets):
    barrier = pltpu.get_barrier_semaphore()
    for target in targets:
        pl.semaphore_signal(barrier, inc=1, device_id=target, device_id_type=MESH)
    pl.semaphore_wait(barrier, len(targets))


class Gather:
    def __init__(self, sends, outs, widths):
        self.sends, self.outs = sends, outs
        self.core, self.spot = position()
        self.other = 1 - self.core
        self.sibling = device(1 - self.core, self.spot)
        self.near = neighbours(self.core, self.spot)
        self.jobs = [
            [(i, part, cols) for part, cols in enumerate(cut(width // 128, 3))] for i, width in enumerate(widths)
        ]
        self.forwards = [[] for _ in widths]

    def peers(self):
        return [self.sibling] + [self.near[a, by][1] for a in range(3) for by in (1, 3)]

    def block(self, i, whole_axes, at, cols, half=None):
        index = [pl.ds(0, 4) if a in whole_axes else pl.ds(at[a], 1) for a in range(3)]
        half = self.core if half is None else half
        return self.outs[i].at[half, index[0], index[1], index[2], :, pl.ds(cols[0], cols[1])]

    def push(self, name, target, *where):
        def make():
            ref = self.block(*where)
            return ref, ref, target

        self.sends.start(name, make)

    def forward(self, name, *where):
        self.push(name, self.sibling, *where)
        self.forwards[where[0]].append((name, where))

    def plan(self, item, phase):
        for i, part, cols in self.jobs[item]:
            axis = (part + phase) % 3
            done = [(part + p) % 3 for p in range(phase)]
            sides = [self.near[axis, by] for by in (1, 3, 2)]
            halves_of = [(cols[0] + at, size) for at, size in cut(cols[1] // 128, 2)]
            yield i, part, cols, done, sides, halves_of

    def begin(self, item, phase):
        for i, part, cols, done, (right, left, _), two in self.plan(item, phase):
            for step, (a, b) in enumerate(((0, 1), (1, 0))):
                self.push((i, part, phase, "r", step), right[1], i, done, self.spot, two[a])
                self.push((i, part, phase, "l", step), left[1], i, done, self.spot, two[b])
            if phase == 2:
                self.forward((i, part, "f"), i, done, self.spot, cols)

    def relay(self, item, phase):
        for i, part, cols, done, (right, left, _), two in self.plan(item, phase):
            for side, source, target, cc in (("r", left, right, two[0]), ("l", right, left, two[1])):
                where = (i, done, source[0], cc)
                self.sends.arrived((i, part, phase, side, 0), self.block(*where), source[1])
                self.push((i, part, phase, side, 2), target[1], *where)
                if phase == 2:
                    self.forward((i, part, "f", side, 0), *where)

    def finish(self, item, phase):
        for i, part, cols, done, (right, left, far), two in self.plan(item, phase):
            for side, step, at, cc, source in (
                ("r", 1, left, two[1], left),
                ("l", 1, right, two[0], right),
                ("r", 2, far, two[0], left),
                ("l", 2, far, two[1], right),
            ):
                where = (i, done, at[0], cc)
                self.sends.arrived((i, part, phase, side, step), self.block(*where), source[1])
                if phase == 2:
                    self.forward((i, part, "f", side, step), *where)

    def received(self, item):
        for name, (i, done, at, cc) in self.forwards[item]:
            self.sends.arrived(name, self.block(i, done, at, cc, self.other), self.sibling)


W1 = 4 * HCOLS + 7 * AR
W2 = 4 * FB + D + 3 * 768
FSTEPS = H
JSTEPS = FFP // FB


def forward_kernel(
    split_ref, x_ref, d_ref, gain1_ref, gain2_ref, mask_ref, place_ref, dec_ref, dect_ref, pers_ref, mine0, mine1,
    a1_ref, a23_ref, proj_ref, h1_ref, lat_ref, wf_ref, lw_ref, back_ref, dz_ref, dmid_ref, grads_ref,
    inc0, inc1, stage0, stage1, w_buf, up_buf, down_buf, z_ref, wup_buf, wd_buf, wout_buf, small_buf,
    x2_ref, h2_ref, inv_ref, lat_out_ref, lat_up_ref, dl_down_ref, acc_ref, lat_acc_ref, dh_ref, dlat_ref,
    send_sem, recv_sem, local_sem, w_sem, j_sem,
):
    step = pl.program_id(0)
    mine, inc, stage, outs = (mine0, mine1), (inc0, inc1), (stage0, stage1), (a1_ref, a23_ref)
    sends = Sends(send_sem, recv_sem)
    ring = Gather(sends, outs, (W1, W2))
    core, spot = ring.core, ring.spot
    other = 1 - core

    def head_loads(h, slot):
        half, place = h // 4, pl.multiple_of((h % 4) * HCOLS, 128)
        return (
            pltpu.make_async_copy(
                a1_ref.at[half, :, :, :, :, pl.ds(place, HCOLS)], w_buf.at[slot], w_sem.at[slot, 0]
            ),
            pltpu.make_async_copy(
                a1_ref.at[1, h // 2, pl.ds(2 * (h % 2), 2), :, :, pl.ds(4 * HCOLS, HCOLS)],
                up_buf.at[slot],
                w_sem.at[slot, 1],
            ),
        )

    def down_load():
        return pltpu.make_async_copy(
            a1_ref.at[0, :, :, :, :, pl.ds(4 * HCOLS, HCOLS)], down_buf, local_sem.at[0]
        )

    def block_loads(j, slot):
        place = pl.multiple_of((j % 2) * 2 * FB, 128)
        return (
            pltpu.make_async_copy(
                a23_ref.at[j // 2, :, :, :, :, pl.ds(place, 2 * FB)], wup_buf.at[slot], j_sem.at[slot, 0]
            ),
            pltpu.make_async_copy(
                a23_ref.at[:, j, :, :, :, pl.ds(4 * FB + D, 3 * 768)], wd_buf.at[slot], j_sem.at[slot, 1]
            ),
        )

    def side_loads():
        return (
            pltpu.make_async_copy(a23_ref.at[1, :, :, :, :, pl.ds(4 * FB, D)], wout_buf, local_sem.at[0]),
            pltpu.make_async_copy(a23_ref.at[0, :, :, :, :, pl.ds(4 * FB, D)], small_buf, local_sem.at[1]),
        )

    @pl.when(step == 0)
    def _():
        greet(ring.peers())
        for i in range(2):
            sends.start(("pair", i), lambda i=i: (mine[i].at[other], inc[i], ring.sibling))
        own_copy = lambda i: pltpu.make_async_copy(
            stage[i], outs[i].at[core, spot[0], spot[1], spot[2]], local_sem.at[i]
        )
        for i in range(2):
            sends.arrived(("pair", i), inc[i], ring.sibling)
            own, theirs = mine[i][core], inc[i][...]
            first = jnp.where(core == 0, own, theirs)
            last = jnp.where(core == 0, theirs, own)
            stage[i][...] = jnp.concatenate([first, last], axis=0).astype(BF)
            own_copy(i).start()
        for i in range(2):
            own_copy(i).wait()
            ring.begin(i, 0)
        decay_kernel(split_ref, dec_ref, dect_ref, wf_ref, lw_ref)
        normed, _ = norm_fwd(x_ref[...].astype(F32), gain1_ref[...])
        h1_ref[...] = normed.astype(BF)
        ring.relay(0, 0)
        ring.relay(1, 0)
        ring.finish(0, 0)
        ring.begin(0, 1)
        ring.finish(1, 0)
        ring.relay(0, 1)
        ring.finish(0, 1)
        ring.begin(0, 2)
        ring.begin(1, 1)
        ring.relay(0, 2)
        ring.relay(1, 1)
        ring.finish(0, 2)
        ring.received(0)
        for copy in head_loads(0, 0):
            copy.start()
        down_load().start()
        ring.finish(1, 1)
        ring.begin(1, 2)
        down_load().wait()
        latent = dot(h1_ref[...], down_buf[...].reshape(D, HCOLS))
        mask = mask_ref[...]
        for part in range(7):
            s = slice(part * AR, (part + 1) * AR)
            lat_ref[:, s] = (latent[:, s] * mask).astype(BF)

    @pl.when(step == RELAY_STEP)
    def _():
        ring.relay(1, 2)

    @pl.when(step < FSTEPS)
    def _():
        slot = step % 2
        for copy in head_loads(step, slot):
            copy.wait()

        @pl.when(step + 1 < FSTEPS)
        def _():
            for copy in head_loads(step + 1, 1 - slot):
                copy.start()

        base = dot(h1_ref[...], w_buf[slot].reshape(D, HCOLS))
        up = up_buf[slot].reshape(HEAD, HCOLS)
        pieces = []
        for part in range(7):
            s = slice(part * AR, (part + 1) * AR)
            piece = base[:, part * HEAD : (part + 1) * HEAD] + dot(lat_ref[:, s], up[:, s], NT)
            proj_ref[:, part * HEAD : (part + 1) * HEAD] = piece
            pieces.append(piece)
        q, k, v = (pieces[i].astype(BF) for i in range(3))
        pk, pv = pers_ref[0, :, pl.ds(pl.multiple_of(step * HEAD, HEAD), HEAD)], pers_ref[
            1, :, pl.ds(pl.multiple_of(step * HEAD, HEAD), HEAD)
        ]
        near, far = attend(q, k, v, pk, pv, allowed_mask(split_ref))
        att = attend_out(near.astype(BF), far.astype(BF), v, pv)
        kn, _ = unit(pieces[3])
        qn, _ = unit(pieces[5])
        here = pl.ds(step, 1)
        mem = memory_out(memory_terms(kn, qn, pieces[4], wf_ref.at[here], lw_ref.at[here]))
        z_ref[:, pl.ds(pl.multiple_of(step * HEAD, HEAD), HEAD)] = (
            att + jax.nn.sigmoid(pieces[6]) * mem
        ).astype(BF)

    small = lambda lo, hi: small_buf[:, :, :, :, lo:hi].reshape(D, hi - lo)
    out_down = lambda: small(0, 128)
    out_up = lambda: small(128, 256)
    up_down = lambda: small(256, 512)
    down_up = lambda: small(512, 640)

    @pl.when(step == FSTEPS)
    def _():
        ring.finish(1, 2)
        ring.received(1)
        for copy in side_loads() + block_loads(0, 0):
            copy.start()
        for copy in side_loads():
            copy.wait()
        mask = mask_ref[...]
        z = z_ref[...]
        lat_out_ref[...] = (dot(z, out_down()) * mask).astype(BF)
        x2 = x_ref[...].astype(F32) + (
            dot(z, wout_buf[...].reshape(D, D)) + dot(lat_out_ref[...], out_up(), NT)
        )
        x2_ref[...] = x2
        normed, inv = norm_fwd(x2, gain2_ref[...])
        inv_ref[...] = jnp.broadcast_to(inv, inv_ref.shape)
        h2_ref[...] = normed.astype(BF)
        latent = dot(h2_ref[...], up_down())
        lat_up_ref[:, :AR] = (latent[:, :AR] * mask).astype(BF)
        lat_up_ref[:, AR:] = (latent[:, AR:] * mask).astype(BF)
        dl_down_ref[...] = (dot(d_ref[...], down_up()) * mask).astype(BF)
        acc_ref[...] = jnp.zeros_like(acc_ref)
        lat_acc_ref[...] = jnp.zeros_like(lat_acc_ref)
        dh_ref[...] = jnp.zeros_like(dh_ref)
        dlat_ref[...] = jnp.zeros_like(dlat_ref)

    @pl.when(step >= FSTEPS)
    def _():
        j = step - FSTEPS
        slot = j % 2
        for copy in block_loads(j, slot):
            copy.wait()

        @pl.when(j + 1 < JSTEPS)
        def _():
            for copy in block_loads(j + 1, 1 - slot):
                copy.start()

        h2 = h2_ref[...]
        d = d_ref[...]
        w_gate = wup_buf[slot, :, :, :, :, :FB].reshape(D, FB)
        w_lift = wup_buf[slot, :, :, :, :, FB:].reshape(D, FB)
        lat0, lat1 = lat_up_ref[:, :AR], lat_up_ref[:, AR:]

        def tall(half, lo, hi):
            return jnp.concatenate(
                [wd_buf[slot, half, :, :, :, k * 768 + lo : k * 768 + hi].reshape(256, hi - lo) for k in range(3)],
                axis=0,
            )

        wda, wdb = tall(0, 0, 768), tall(1, 0, 256)
        uu0, uu1, dd = tall(1, 256, 384), tall(1, 384, 512), tall(1, 512, 640)
        gate = dot(h2, w_gate) + dot(lat0, uu0, NT)
        lift = dot(h2, w_lift) + dot(lat1, uu1, NT)
        sig = jax.nn.sigmoid(gate)
        silu = gate * sig
        act = (silu * lift).astype(BF)
        acc_ref[:, :768] += dot(act, wda)
        acc_ref[:, 768:] += dot(act, wdb)
        lat_acc_ref[...] += dot(act, dd)
        d_act = dot(d[:, :768], wda, NT) + dot(d[:, 768:], wdb, NT) + dot(dl_down_ref[...], dd, NT)
        d_gate = (d_act * lift * (sig * (1.0 + gate * (1.0 - sig)))).astype(BF)
        d_lift = (d_act * silu).astype(BF)
        dh_ref[...] += dot(d_gate, w_gate, NT) + dot(d_lift, w_lift, NT)
        dlat_ref[:, :AR] += dot(d_gate, uu0)
        dlat_ref[:, AR:] += dot(d_lift, uu1)
        first = pl.multiple_of(j * 16, 16)
        for place, term in (
            (0, dot(d_gate, lat0, TN)),
            (1, dot(d_lift, lat1, TN)),
            (2, dot(act, dl_down_ref[...], TN)),
        ):
            shaped = term.reshape(3, 16, 16, AR).astype(BF)
            for k in range(3):
                if place < 2:
                    at = k * 256 + place * AR
                    grads_ref[0, pl.ds(first, 16), :, at : at + AR] = shaped[k]
                else:
                    grads_ref[1, pl.ds(first, 16), :, k * AR : (k + 1) * AR] = shaped[k]

    @pl.when(step == FSTEPS + JSTEPS - 1)
    def _():
        mask = mask_ref[...]
        lat_down = (lat_acc_ref[...] * mask).astype(BF)
        out = (x2_ref[...] + acc_ref[...] + dot(lat_down, down_up(), NT)).astype(BF)
        for m in range(MB):
            s = slice(m * GROUP, (m + 1) * GROUP)
            back_ref[:, m * D : (m + 1) * D] = dot(place_ref[m], out[s], TN).astype(BF)
        d = d_ref[...]
        h2 = h2_ref[...]
        z = z_ref[...]

        def put(half, at, value):
            grads_ref[half, :, :, at : at + AR] = value.reshape(64, 16, AR).astype(BF)

        put(0, 768, dot(d, lat_down, TN))
        dlu0 = (dlat_ref[:, :AR] * mask).astype(BF)
        dlu1 = (dlat_ref[:, AR:] * mask).astype(BF)
        put(1, 640, dot(h2, dlu0, TN))
        put(1, 768, dot(h2, dlu1, TN))
        ud = up_down()
        dh = dh_ref[...] + (dot(dlu0, ud[:, :AR], NT) + dot(dlu1, ud[:, AR:], NT))
        dmid = d.astype(F32) + norm_bwd(dh, x2_ref[...], inv_ref[:, :1], gain2_ref[...])
        dmid_ref[...] = dmid
        dmb = dmid.astype(BF)
        dlo = (dot(dmb, out_up()) * mask).astype(BF)
        put(1, 384, dot(z, dlo, TN))
        put(1, 512, dot(dmb, lat_out_ref[...], TN))
        dz_ref[...] = (dot(dmb, wout_buf[...].reshape(D, D), NT) + dot(dlo, out_down(), NT)).astype(BF)
        sends.drain()


RELAY_STEP = 3


def forward_call(split, x, d, gain1, gain2, mask, place, dec, dec_t, persistent, mine0, mine1):
    whole = lambda *shape: pl.BlockSpec(shape, lambda s: (0,) * len(shape))
    hbm = pl.BlockSpec(memory_space=pl.ANY)
    slots = 2 * (1 + 3 * (3 * 6 + 7))
    return pl.pallas_call(
        forward_kernel,
        grid=(FSTEPS + JSTEPS,),
        out_shape=(
            jax.ShapeDtypeStruct((2, 4, 4, 4, 16, W1), BF),
            jax.ShapeDtypeStruct((2, 4, 4, 4, 16, W2), BF),
            jax.ShapeDtypeStruct((ROWS, 7 * D), F32),
            jax.ShapeDtypeStruct((ROWS, D), BF),
            jax.ShapeDtypeStruct((ROWS, 7 * AR), BF),
            jax.ShapeDtypeStruct((H, MB, GROUP, GROUP), F32),
            jax.ShapeDtypeStruct((H, MB, 8, GROUP), F32),
            jax.ShapeDtypeStruct((GROUP, MB * D), BF),
            jax.ShapeDtypeStruct((ROWS, D), BF),
            jax.ShapeDtypeStruct((ROWS, D), F32),
            jax.ShapeDtypeStruct((2, 64, 16, 896), BF),
        ),
        in_specs=[
            pl.BlockSpec(memory_space=pltpu.SMEM),
            whole(ROWS, D),
            whole(ROWS, D),
            whole(1, D),
            whole(1, D),
            whole(ROWS, AR),
            whole(MB, GROUP, GROUP),
            whole(ROWS, 3 * H),
            whole(3 * H, ROWS),
            whole(2, NP, D),
            whole(2, 8, W1),
            whole(2, 8, W2),
        ],
        out_specs=(
            hbm,
            hbm,
            pl.BlockSpec((ROWS, HCOLS), lambda s: (0, jnp.minimum(s, FSTEPS - 1))),
            whole(ROWS, D),
            whole(ROWS, 7 * AR),
            whole(H, MB, GROUP, GROUP),
            whole(H, MB, 8, GROUP),
            whole(GROUP, MB * D),
            whole(ROWS, D),
            whole(ROWS, D),
            whole(2, 64, 16, 896),
        ),
        scratch_shapes=[
            pltpu.VMEM((8, W1), F32),
            pltpu.VMEM((8, W2), F32),
            pltpu.VMEM((16, W1), BF),
            pltpu.VMEM((16, W2), BF),
            pltpu.VMEM((2, 4, 4, 4, 16, HCOLS), BF),
            pltpu.VMEM((2, 2, 4, 16, HCOLS), BF),
            pltpu.VMEM((4, 4, 4, 16, HCOLS), BF),
            pltpu.VMEM((ROWS, D), BF),
            pltpu.VMEM((2, 4, 4, 4, 16, 2 * FB), BF),
            pltpu.VMEM((2, 2, 4, 4, 16, 3 * 768), BF),
            pltpu.VMEM((4, 4, 4, 16, D), BF),
            pltpu.VMEM((4, 4, 4, 16, D), BF),
            pltpu.VMEM((ROWS, D), F32),
            pltpu.VMEM((ROWS, D), BF),
            pltpu.VMEM((ROWS, 128), F32),
            pltpu.VMEM((ROWS, AR), BF),
            pltpu.VMEM((ROWS, 2 * AR), BF),
            pltpu.VMEM((ROWS, AR), BF),
            pltpu.VMEM((ROWS, D), F32),
            pltpu.VMEM((ROWS, AR), F32),
            pltpu.VMEM((ROWS, D), F32),
            pltpu.VMEM((ROWS, 2 * AR), F32),
            pltpu.SemaphoreType.DMA((slots,)),
            pltpu.SemaphoreType.DMA((slots,)),
            pltpu.SemaphoreType.DMA((2,)),
            pltpu.SemaphoreType.DMA((2, 2)),
            pltpu.SemaphoreType.DMA((2, 2)),
        ],
        compiler_params=pltpu.CompilerParams(
            collective_id=0, has_side_effects=True, vmem_limit_bytes=VMEM_LIMIT
        ),
        name="gather_forward",
    )(split, x, d, gain1, gain2, mask, place, dec, dec_t, persistent, mine0, mine1)


class Scatter:
    def __init__(self, sends, key, grads, out, inc0, total, inc1, inc2, inc3, t1, t2):
        self.sends, self.key, self.grads, self.out = sends, key, grads, out
        self.inc0, self.total, self.inc = inc0, total, (None, inc1, inc2, inc3)
        self.t1, self.t2 = t1, t2
        self.core, self.spot = position()
        self.other = 1 - self.core
        self.sibling = device(1 - self.core, self.spot)
        self.near = neighbours(self.core, self.spot)
        self.parts = [(part, pl.ds(*cols)) for part, cols in enumerate(cut(7, 3))]

    def peers(self):
        return [self.sibling] + [there[1] for there in self.near.values()]

    def pair(self):
        for x in range(4):
            self.sends.start(
                (self.key, "pair", x),
                lambda x=x: (
                    self.grads.at[self.other, pl.ds(16 * x, 16)],
                    self.inc0.at[x],
                    self.sibling,
                ),
            )

    def source(self, phase, part, at):
        axis = (part + phase - 1) % 3
        cs = self.parts[part][1]
        if phase == 1:
            index = tuple(at if a == axis else slice(None) for a in range(3))
            return self.total, index + (slice(None), cs)
        rest = [a for a in range(3) if a != part]
        if phase == 2:
            index = (at, slice(None)) if rest[0] == axis else (slice(None), at)
            return self.t1, index + (slice(None), cs)
        return self.t2, (at, slice(None), cs)

    def landing(self, phase, part, k):
        return (k,) + (slice(None),) * (4 - phase) + (self.parts[part][1],)

    def send(self, phase):
        for part, _ in self.parts:
            axis = (part + phase - 1) % 3
            for k, by in enumerate((2, 1, 3)):
                to = self.near[axis, by]

                def make(part=part, axis=axis, to=to, k=k):
                    ref, index = self.source(phase, part, to[0][axis])
                    return ref.at[index], self.inc[phase].at[self.landing(phase, part, k)], to[1]

                self.sends.start((self.key, part, phase, by), make)

    def add(self, phase):
        for part, cs in self.parts:
            axis = (part + phase - 1) % 3
            ref, index = self.source(phase, part, self.spot[axis])
            acc = ref[index].astype(F32)
            for k, by in enumerate((2, 1, 3)):
                here = self.landing(phase, part, k)
                source = self.near[axis, 4 - by][1]
                self.sends.arrived((self.key, part, phase, by), self.inc[phase].at[here], source)
                acc = acc + self.inc[phase][here].astype(F32)
            if phase == 1:
                self.t1[:, :, :, cs] = acc.astype(BF)
            elif phase == 2:
                self.t2[:, :, cs] = acc.astype(BF)
            else:
                self.out[self.core, :, cs] = acc

    def add_pair(self):
        for x in range(4):
            self.sends.arrived((self.key, "pair", x), self.inc0.at[x], self.sibling)
            both = self.grads[self.core, pl.ds(16 * x, 16)].astype(F32) + self.inc0[x].astype(F32)
            self.total[x] = both.reshape(4, 4, 16, 896).astype(BF)

    def swap(self):
        self.sends.start(
            (self.key, "last"), lambda: (self.out.at[self.core], self.out.at[self.core], self.sibling)
        )

    def swapped(self):
        self.sends.arrived((self.key, "last"), self.out.at[self.other], self.sibling)


def backward_kernel(
    split_ref, x_ref, gain_ref, mask_ref, place_ref, proj_ref, dz_ref, dmid_ref, h1_ref, lat_ref,
    w_ref, down_ref, up_ref, pers_ref, wf_ref, lw_ref, ffn_ref,
    back_ref, ffn_out, heads_out,
    dh_ref, dlat_ref, grads_ref, *rest,
):
    step = pl.program_id(0)
    send_sem, recv_sem = rest[-2:]
    sends = Sends(send_sem, recv_sem)
    first_sums = Scatter(sends, 0, ffn_ref, *rest[:8])
    last_sums = Scatter(sends, 1, grads_ref, *rest[8:16])

    @pl.when(step == 0)
    def _():
        greet(first_sums.peers())
        first_sums.pair()
        dh_ref[...] = jnp.zeros_like(dh_ref)
        dlat_ref[...] = jnp.zeros_like(dlat_ref)

    @pl.when(step == 2)
    def _():
        first_sums.add_pair()
        first_sums.send(1)

    @pl.when(step == 5)
    def _():
        first_sums.add(1)
        first_sums.send(2)

    @pl.when(step == 6)
    def _():
        first_sums.add(2)
        first_sums.send(3)

    @pl.when(step == 7)
    def _():
        first_sums.add(3)
        first_sums.swap()

    pieces = [proj_ref[:, p * HEAD : (p + 1) * HEAD] for p in range(7)]
    q, k, v = (pieces[i].astype(BF) for i in range(3))
    pk, pv = pers_ref[0], pers_ref[1]
    near, far = attend(q, k, v, pk, pv, allowed_mask(split_ref))
    near_half = near.astype(BF)
    dz = dz_ref[...]
    d_near = by_group(lambda s, g: dot(dz[s], v[s], NT))
    d_far = dot(dz, pv, NT)
    d_v = by_group(lambda s, g: dot(near_half[s], dz[s], TN))
    total = jnp.sum(d_near * near, axis=-1, keepdims=True) + jnp.sum(
        d_far * far, axis=-1, keepdims=True
    )
    ds_near = (near * (d_near - total) * SCALE).astype(BF)
    ds_far = (far * (d_far - total) * SCALE).astype(BF)
    d_q = by_group(lambda s, g: dot(ds_near[s], k[s])) + dot(ds_far, pk)
    d_k = by_group(lambda s, g: dot(ds_near[s], q[s], TN))

    dzf = dz.astype(F32)
    opening = jax.nn.sigmoid(pieces[6])
    kn, k_inv = unit(pieces[3])
    qn, q_inv = unit(pieces[5])
    kept = memory_terms(kn, qn, pieces[4], wf_ref, lw_ref)
    mem = memory_out(kept)
    d_open = dzf * mem * (opening * (1.0 - opening))
    d_kn, d_qn, d_mv = memory_bwd(kept, dzf * opening)
    d_mk = unit_bwd(d_kn, pieces[3], k_inv)
    d_mq = unit_bwd(d_qn, pieces[5], q_inv)
    dy = [item.astype(BF) for item in (d_q, d_k, d_v, d_mk, d_mv, d_mq, d_open)]
    dh_ref[...] += dot(jnp.concatenate(dy, axis=1), w_ref[0], NT)
    first = pl.multiple_of(step * 8, 8)
    for part in range(7):
        s = slice(part * AR, (part + 1) * AR)
        dlat_ref[:, s] += dot(dy[part], up_ref[0, :, s])
        grads_ref[1, pl.ds(first, 8), :, s] = (
            dot(dy[part], lat_ref[:, s], TN).reshape(8, 16, AR).astype(BF)
        )

    @pl.when(step == pl.num_programs(0) - 1)
    def _():
        mask = mask_ref[...]
        dlat = jnp.concatenate(
            [(dlat_ref[:, p * AR : (p + 1) * AR] * mask).astype(BF) for p in range(7)], axis=1
        )
        grads_ref[0] = dot(h1_ref[...], dlat, TN).reshape(64, 16, 7 * AR).astype(BF)
        last_sums.pair()
        dh = dh_ref[...] + dot(dlat, down_ref[0], NT)
        x = x_ref[...].astype(F32)
        inv = lax.rsqrt(jnp.mean(x * x, axis=-1, keepdims=True) + EPS)
        dx = (dmid_ref[...] + norm_bwd(dh, x, inv, gain_ref[...])).astype(BF)
        for m in range(MB):
            s = slice(m * GROUP, (m + 1) * GROUP)
            back_ref[:, m * D : (m + 1) * D] = dot(place_ref[m], dx[s], TN).astype(BF)
        last_sums.add_pair()
        last_sums.send(1)
        first_sums.swapped()
        last_sums.add(1)
        last_sums.send(2)
        last_sums.add(2)
        last_sums.send(3)
        last_sums.add(3)
        last_sums.swap()
        last_sums.swapped()
        ffn_out[...] = first_sums.out[...]
        heads_out[...] = last_sums.out[...]
        sends.drain()


def backward_call(split, x, gain, mask, place, proj, dz, dmid, h1, lat, a1, persistent, wf, lw, grads_ffn):
    whole = lambda *shape: pl.BlockSpec(shape, lambda h: (0,) * len(shape))
    buffers = [
        pltpu.VMEM((2, 16, 896), F32),
        pltpu.VMEM((4, 16, 16, 896), BF),
        pltpu.VMEM((4, 4, 4, 16, 896), BF),
        pltpu.VMEM((3, 4, 4, 16, 896), BF),
        pltpu.VMEM((3, 4, 16, 896), BF),
        pltpu.VMEM((3, 16, 896), BF),
        pltpu.VMEM((4, 4, 16, 896), BF),
        pltpu.VMEM((4, 16, 896), BF),
    ]
    slots = 2 * (4 + 3 * 9 + 1)
    return pl.pallas_call(
        backward_kernel,
        grid=(H,),
        out_shape=(
            jax.ShapeDtypeStruct((GROUP, MB * D), BF),
            jax.ShapeDtypeStruct((2, 16, 896), F32),
            jax.ShapeDtypeStruct((2, 16, 896), F32),
        ),
        in_specs=[
            pl.BlockSpec(memory_space=pltpu.SMEM),
            whole(ROWS, D),
            whole(1, D),
            whole(ROWS, AR),
            whole(MB, GROUP, GROUP),
            pl.BlockSpec((ROWS, HCOLS), lambda h: (0, h)),
            pl.BlockSpec((ROWS, HEAD), lambda h: (0, h)),
            whole(ROWS, D),
            whole(ROWS, D),
            whole(ROWS, 7 * AR),
            pl.BlockSpec((1, D, HCOLS), lambda h: (h // 4, 0, h % 4)),
            pl.BlockSpec((1, D, HCOLS), lambda h: (0, 0, 4)),
            pl.BlockSpec((1, HEAD, HCOLS), lambda h: (1, h, 4)),
            pl.BlockSpec((2, NP, HEAD), lambda h: (0, 0, h)),
            pl.BlockSpec((1, MB, GROUP, GROUP), lambda h: (h, 0, 0, 0)),
            pl.BlockSpec((1, MB, 8, GROUP), lambda h: (h, 0, 0, 0)),
            pl.BlockSpec(memory_space=pltpu.VMEM),
        ],
        out_specs=(
            whole(GROUP, MB * D),
            pl.BlockSpec(memory_space=pltpu.VMEM),
            pl.BlockSpec(memory_space=pltpu.VMEM),
        ),
        scratch_shapes=[
            pltpu.VMEM((ROWS, D), F32),
            pltpu.VMEM((ROWS, 7 * AR), F32),
            pltpu.VMEM((2, 64, 16, 896), BF),
        ]
        + buffers * 2
        + [pltpu.SemaphoreType.DMA((slots,)), pltpu.SemaphoreType.DMA((slots,))],
        compiler_params=pltpu.CompilerParams(
            collective_id=1, has_side_effects=True, vmem_limit_bytes=VMEM_LIMIT
        ),
        name="backward_scatter",
    )(split, x, gain, mask, place, proj, dz, dmid, h1, lat, a1, a1, a1, persistent, wf, lw, grads_ffn)


def by_rank(value, parts):
    rows = value.shape[1]
    return value.reshape(NAD, rows, parts, R).transpose(1, 2, 0, 3).reshape(rows, parts * AR)


def by_rank_t(value, parts):
    cols = value.shape[2]
    return value.reshape(NAD, parts, R, cols).transpose(3, 1, 0, 2).reshape(cols, parts * AR)


def pack_shards(w_in, w_out, w_up, w_down, in_down, in_up, out_down, out_up, up_down, up_up, down_down, down_up):
    rows = w_in.shape[0]
    heads = w_in.reshape(rows, 7, H, HEAD).transpose(0, 2, 1, 3).reshape(rows, 2, 4 * HCOLS)
    first = jnp.stack(
        [
            jnp.concatenate([heads[:, 0], by_rank(in_down, 7)], axis=1),
            jnp.concatenate([heads[:, 1], by_rank_t(in_up, 7)], axis=1),
        ]
    )
    up = w_up.reshape(rows, 2, N_DEV, FF_SHARD)
    up = jnp.pad(up, ((0, 0), (0, 0), (0, 0), (0, FF_PAD - FF_SHARD)))
    up = up.reshape(rows, 2, 4, 32, 3, 8).transpose(0, 2, 1, 4, 3, 5).reshape(rows, 2, 4 * FB)
    small = jnp.concatenate(
        [by_rank(out_down, 1), by_rank_t(out_up, 1), by_rank(up_down, 2), by_rank_t(down_up, 1)], axis=1
    )
    small = jnp.pad(small, ((0, 0), (0, D - small.shape[1])))
    rest = jnp.concatenate([w_down[:, 768:], by_rank_t(up_up, 2), by_rank(down_down, 1)], axis=1)
    rest = jnp.pad(rest, ((0, 0), (0, 128)))
    tall = jnp.pad(jnp.stack([w_down[:, :768], rest]), ((0, 0), (0, FF_PAD - FF_SHARD), (0, 0)))
    tall = tall.reshape(2, 3, 8, 768).transpose(0, 2, 1, 3).reshape(2, 8, 3 * 768)
    second = jnp.stack(
        [
            jnp.concatenate([up[:, 0], small, tall[0]], axis=1),
            jnp.concatenate([up[:, 1], w_out, tall[1]], axis=1),
        ]
    )
    return first, second


def un_rank(value, parts):
    rows = value.shape[0]
    return value.reshape(rows, parts, NAD, R).transpose(2, 0, 1, 3).reshape(NAD, rows, parts * R)


def un_rank_t(value, parts):
    cols = value.shape[0]
    return value.reshape(cols, parts, NAD, R).transpose(2, 1, 3, 0).reshape(NAD, parts * R, cols)


def unpack_grads(ffn_chip, heads_chip, core):
    def rows8(value):
        return lax.dynamic_slice_in_dim(value, core * 8, 8, axis=0)

    grad_id = un_rank(rows8(heads_chip[0]), 7)
    grad_iu = un_rank_t(rows8(heads_chip[1]), 7)

    def rows22(value, width):
        value = rows8(value).reshape(8, 3, width).transpose(1, 0, 2)
        return value.reshape(FF_PAD, width)[:FF_SHARD]

    grad_uu = un_rank_t(rows22(ffn_chip[0, :, :768], 256), 2)
    grad_dd = un_rank(rows22(ffn_chip[1, :, :384], AR), 1)
    grad_du = un_rank_t(rows8(ffn_chip[0, :, 768:]), 1)
    grad_od = un_rank(rows8(ffn_chip[1, :, 384:512]), 1)
    grad_ou = un_rank_t(rows8(ffn_chip[1, :, 512:640]), 1)
    grad_ud = un_rank(rows8(ffn_chip[1, :, 640:896]), 2)
    return grad_id, grad_iu, grad_od, grad_ou, grad_ud, grad_uu, grad_dd, grad_du


def body(
    tokens, cotangent, decays, route, lengths, adapter_ids, gain_mix, gain_ffn, persistent,
    w_in, w_out, w_up, w_down, in_down, in_up, out_down, out_up, up_down, up_up, down_down, down_up,
):
    me = lax.axis_index("fsdp")
    packed = pack_shards(
        w_in, w_out, w_up, w_down, in_down, in_up, out_down, out_up, up_down, up_up, down_down, down_up
    )
    first, second = (item.astype(F32) for item in packed)

    spots = jnp.arange(GROUP, dtype=jnp.int32)
    own = lax.dynamic_slice_in_dim(route, me * GROUP, GROUP, axis=1)
    send = (own[:, None, :] // GROUP == spots[None, :, None]).astype(BF)
    blocks = route.reshape(MB, N_DEV, GROUP)
    landing = jnp.sum(jnp.where(blocks // GROUP == me, blocks % GROUP, 0), axis=2)
    place = (landing[:, None, :] == spots[None, :, None]).astype(BF)

    def permute(onehot, values):
        return jnp.einsum("mij,mjd->mid", onehot, values, preferred_element_type=F32).astype(BF)

    def exchange(values):
        return lax.all_to_all(values, "fsdp", split_axis=0, concat_axis=0, tiled=True)

    out_x = permute(send, tokens)
    out_d = permute(send, cotangent)
    out_r = permute(send, decays)
    sent = jnp.concatenate(
        [out_x[0], out_x[1], out_d[0], out_d[1], out_r[0], out_r[1], jnp.zeros((GROUP, 80), BF)], axis=1
    )
    got = exchange(sent)
    at = lambda lo, width: jnp.stack([got[:, lo : lo + width], got[:, lo + width : lo + 2 * width]])
    x = permute(place, at(0, D)).reshape(ROWS, D)
    d = permute(place, at(2 * D, D)).reshape(ROWS, D)
    dec = permute(place, at(4 * D, 3 * H)).astype(F32).reshape(ROWS, 3 * H)
    lengths, ids = lengths[:, 0], adapter_ids[:, 0]
    split = (lengths[:, 0] < GROUP).astype(F32)
    row_ids = jnp.where(spots[None, :] >= lengths[:, :1], ids[:, 1:], ids[:, :1]).reshape(ROWS)
    mask = (row_ids[:, None] == (jnp.arange(AR) // R)[None, :]).astype(F32)
    gain_mix, gain_ffn = gain_mix[None, :], gain_ffn[None, :]
    a1, _, proj, h1, lat, wf, lw, back, dz, dmid, grads_ffn = forward_call(
        split, x, d, gain_mix, gain_ffn, mask, place, dec, dec.T, persistent, first, second
    )
    back_grad, ffn_chip, heads_chip = backward_call(
        split, x, gain_mix, mask, place, proj, dz, dmid, h1, lat, a1.reshape(2, D, W1), persistent, wf, lw, grads_ffn
    )

    def home(values):
        values = exchange(values)
        return jnp.einsum(
            "mij,mid->mjd", send, values.reshape(GROUP, MB, D).transpose(1, 0, 2), preferred_element_type=F32
        ).astype(BF)

    return (home(back), home(back_grad)) + unpack_grads(ffn_chip, heads_chip, me % 2)


def solution(mesh):
    rows, cols = P(None, "fsdp", None), P(None, None, "fsdp")
    weight = P("fsdp", None)
    return jax.shard_map(
        body,
        mesh=mesh,
        in_specs=(rows, rows, rows, P(), rows, rows, P(), P(), P())
        + (weight,) * 4
        + (rows, cols) * 4,
        out_specs=(rows, rows) + (rows, cols) * 4,
        check_vma=False,
    )
```

```python
import functools
import math

import jax
import jax.numpy as jnp
from jax import lax
from jax.experimental import pallas as pl
from jax.experimental.pallas import tpu as pltpu
from jax.sharding import PartitionSpec as P

D = 1024
H = 8
HEAD = 128
FF = 2816
R = 16
NAD = 8
NP = 16
SPAN = 64
GROUP = 128
MB = 2
ROWS = MB * GROUP
N_DEV = 128
AR = NAD * R
HCOLS = 7 * HEAD
FF_SHARD = FF // N_DEV
FF_PAD = 24
FFP = FF_PAD * N_DEV
FB = 1024
EPS = 1e-05
SCALE = 1.0 / math.sqrt(HEAD)
VMEM_LIMIT = 60 * 1024 * 1024
BF = jnp.bfloat16
F32 = jnp.float32

NN = (((1,), (0,)), ((), ()))
NT = (((1,), (1,)), ((), ()))
TN = (((0,), (0,)), ((), ()))


def dot(left, right, dims=NN):
    return lax.dot_general(left, right, dims, preferred_element_type=F32)


def exact(left, right, dims=NN):
    return lax.dot_general(
        left, right, dims, precision=lax.Precision.HIGHEST, preferred_element_type=F32
    )


def halves(value):
    high = value.astype(BF)
    return high, (value - high.astype(F32)).astype(BF)


def dot3(left, right, dims=NN):
    lh, ll = left
    rh, rl = right
    return dot(lh, rh, dims) + (dot(lh, rl, dims) + dot(ll, rh, dims))


def transposed(onehot):
    rows = lax.broadcasted_iota(jnp.int32, onehot.shape, 0)
    cols = lax.broadcasted_iota(jnp.int32, onehot.shape, 1)
    return dot((rows == cols).astype(BF), onehot, NT).astype(BF)


def norm_fwd(values, gain):
    inv = lax.rsqrt(jnp.mean(values * values, axis=-1, keepdims=True) + EPS)
    return values * inv * gain, inv


def norm_bwd(grad, values, inv, gain):
    scaled = grad * gain
    return inv * (scaled - values * (inv * inv * jnp.mean(values * scaled, axis=-1, keepdims=True)))


def decay_kernel(split_ref, dec_ref, dect_ref, wf_ref, lw_ref):
    rows = lax.broadcasted_iota(jnp.int32, (GROUP, GROUP), 0)
    cols = lax.broadcasted_iota(jnp.int32, (GROUP, GROUP), 1)
    lower = (rows >= cols) & ((rows >= SPAN) == (cols >= SPAN))
    tri = lower.astype(F32)
    second = rows >= SPAN
    for g in range(MB):
        keep = 1.0 - split_ref[g]
        here = dec_ref[g * GROUP : (g + 1) * GROUP, :]
        here_t = dect_ref[:, g * GROUP : (g + 1) * GROUP]
        run = exact(tri, jnp.log(here[:, : 2 * H]))
        run_t = exact(jnp.log(here_t[: 2 * H, :]), tri, NT)
        for h in range(H):
            gap = run[:, h : h + 1] - run_t[h : h + 1, :]
            retain = jnp.exp(jnp.where(lower, gap, -1e30))
            gap = run[:, H + h : H + h + 1] - run_t[H + h : H + h + 1, :]
            moment = jnp.exp(jnp.where(lower, gap, -1e30))
            pairs = exact(retain, moment)
            theta = here_t[2 * H + h : 2 * H + h + 1, :]
            moment_run = jnp.exp(run_t[H + h : H + h + 1, :])
            carry = jnp.sum(retain * moment_run, axis=1, keepdims=True)
            last_weight = pairs[SPAN - 1 : SPAN, :] * theta * keep
            last_moment = moment[SPAN - 1 : SPAN, :] * theta * keep
            across = jnp.exp(run[:, h : h + 1]) * last_weight + carry * last_moment
            wf_ref[h, g] = pairs * theta + jnp.where(second, across, 0.0)
            lw_ref[h, g] = jnp.broadcast_to(last_weight, (8, GROUP))


def allowed_mask(split_ref):
    rows = lax.broadcasted_iota(jnp.int32, (ROWS, GROUP), 0)
    cols = lax.broadcasted_iota(jnp.int32, (ROWS, GROUP), 1)
    local = rows % GROUP
    group = rows // GROUP
    split = jnp.where(group == 0, split_ref[0], split_ref[1]) > 0.5
    return (local >= cols) & jnp.logical_not(split & (local >= SPAN) & (cols < SPAN))


def by_group(make):
    return jnp.concatenate([make(slice(0, GROUP), 0), make(slice(GROUP, ROWS), 1)], axis=0)


def attend(q, k, v, pk, pv, allowed):
    near = by_group(lambda s, g: dot(q[s], k[s], NT))
    far = dot(q, pk, NT) * SCALE
    near = jnp.where(allowed, near * SCALE, -1000000000.0)
    top = jnp.maximum(
        jnp.max(near, axis=-1, keepdims=True), jnp.max(far, axis=-1, keepdims=True)
    )
    near = jnp.exp(near - top)
    far = jnp.exp(far - top)
    inv = 1.0 / (jnp.sum(near, axis=-1, keepdims=True) + jnp.sum(far, axis=-1, keepdims=True))
    near = near * inv
    far = far * inv
    return near, far


def attend_out(near_half, far_half, v, pv):
    return by_group(lambda s, g: dot(near_half[s], v[s])) + dot(far_half, pv)


def unit(values):
    inv = lax.rsqrt(jnp.mean(values * values, axis=-1, keepdims=True) + EPS)
    return values * (inv * SCALE), inv


def unit_bwd(grad, values, inv):
    return (inv * SCALE) * (
        grad - values * (inv * inv * jnp.mean(values * grad, axis=-1, keepdims=True))
    )


def memory_terms(kn, qn, mv, wf_ref, lw_ref):
    second = lax.broadcasted_iota(jnp.int32, (GROUP, GROUP), 0) >= SPAN
    kept = []
    for g in range(MB):
        s = slice(g * GROUP, (g + 1) * GROUP)
        kh, qh = halves(kn[s]), halves(qn[s])
        wf = wf_ref[0, g]
        lw = jnp.where(second, lw_ref[0, g][0:1, :], 0.0)
        kk = dot3(kh, kh, NT) * lw
        qk = dot3(qh, kh, NT) * wf
        kk_half = halves(kk)
        mvh = halves(mv[s])
        err = mv[s] - dot3(kk_half, mvh)
        errh = halves(err)
        qk_half = halves(qk)
        kept.append((kh, qh, wf, lw, kk_half, qk_half, mvh, errh))
    return kept


def memory_out(kept):
    return jnp.concatenate([dot3(item[5], item[7]) for item in kept], axis=0)


def memory_bwd(kept, grad):
    grads_k, grads_q, grads_v = [], [], []
    for g in range(MB):
        kh, qh, wf, lw, kk_half, qk_half, mvh, errh = kept[g]
        gh = halves(grad[g * GROUP : (g + 1) * GROUP])
        d_qk = dot3(gh, errh, NT) * wf
        d_err = dot3(qk_half, gh, TN)
        deh = halves(d_err)
        d_v = d_err - dot3(kk_half, deh, TN)
        d_kk = dot3(deh, mvh, NT) * lw
        dqh = halves(d_qk)
        dkh = halves(d_kk)
        grads_q.append(dot3(dqh, kh))
        grads_k.append(dot3(dqh, qh, TN) - (dot3(dkh, kh) + dot3(dkh, kh, TN)))
        grads_v.append(d_v)
    return (
        jnp.concatenate(grads_k, axis=0),
        jnp.concatenate(grads_q, axis=0),
        jnp.concatenate(grads_v, axis=0),
    )


AXES = ("x", "z", "y")
MESH = pl.DeviceIdType.MESH


def position():
    me = lax.axis_index("fsdp")
    chip = me // 2
    return me % 2, (chip // 16, (chip // 4) % 4, chip % 4)


def device(core, spot):
    return (((spot[0] * 4 + spot[1]) * 4 + spot[2]) * 2 + core,)


def moved(spot, axis, by):
    return tuple((v + by + 4) % 4 if i == axis else v for i, v in enumerate(spot))


def cut(lanes, count):
    base, extra = divmod(lanes, count)
    runs, at = [], 0
    for i in range(count):
        size = base + (1 if i < extra else 0)
        runs.append((at * 128, size * 128))
        at += size
    return runs


def neighbours(core, spot):
    found = {}
    for axis in range(3):
        for by in (1, 2, 3):
            there = moved(spot, axis, by)
            found[axis, by] = (there, device(core, there))
    return found


class Sends:
    def __init__(self, send_sem, recv_sem):
        self.send_sem, self.recv_sem = send_sem, recv_sem
        self.slots, self.open = {}, []

    def copy(self, name, src, dst, target):
        slot = self.slots.setdefault(name, len(self.slots))
        return pltpu.make_async_remote_copy(
            src_ref=src, dst_ref=dst, send_sem=self.send_sem.at[slot], recv_sem=self.recv_sem.at[slot],
            device_id=target, device_id_type=MESH,
        )

    def start(self, name, make):
        self.copy(name, *make()).start()
        self.open.append((name, make))

    def arrived(self, name, ref, target):
        self.copy(name, ref, ref, target).wait_recv()

    def drain(self):
        for name, make in self.open:
            self.copy(name, *make()).wait_send()
        self.open = []


def greet(targets):
    barrier = pltpu.get_barrier_semaphore()
    for target in targets:
        pl.semaphore_signal(barrier, inc=1, device_id=target, device_id_type=MESH)
    pl.semaphore_wait(barrier, len(targets))


class Gather:
    def __init__(self, sends, outs, widths):
        self.sends, self.outs = sends, outs
        self.core, self.spot = position()
        self.other = 1 - self.core
        self.sibling = device(1 - self.core, self.spot)
        self.near = neighbours(self.core, self.spot)
        self.jobs = [
            [(i, part, cols) for part, cols in enumerate(cut(width // 128, 3))] for i, width in enumerate(widths)
        ]
        self.forwards = [[] for _ in widths]

    def peers(self):
        return [self.sibling] + [self.near[a, by][1] for a in range(3) for by in (1, 3)]

    def block(self, i, whole_axes, at, cols, half=None):
        index = [pl.ds(0, 4) if a in whole_axes else pl.ds(at[a], 1) for a in range(3)]
        half = self.core if half is None else half
        return self.outs[i].at[half, index[0], index[1], index[2], :, pl.ds(cols[0], cols[1])]

    def push(self, name, target, *where):
        def make():
            ref = self.block(*where)
            return ref, ref, target

        self.sends.start(name, make)

    def forward(self, name, *where):
        self.push(name, self.sibling, *where)
        self.forwards[where[0]].append((name, where))

    def plan(self, item, phase):
        for i, part, cols in self.jobs[item]:
            axis = (part + phase) % 3
            done = [(part + p) % 3 for p in range(phase)]
            sides = [self.near[axis, by] for by in (1, 3, 2)]
            halves_of = [(cols[0] + at, size) for at, size in cut(cols[1] // 128, 2)]
            yield i, part, cols, done, sides, halves_of

    def begin(self, item, phase):
        for i, part, cols, done, (right, left, _), two in self.plan(item, phase):
            for step, (a, b) in enumerate(((0, 1), (1, 0))):
                self.push((i, part, phase, "r", step), right[1], i, done, self.spot, two[a])
                self.push((i, part, phase, "l", step), left[1], i, done, self.spot, two[b])
            if phase == 2:
                self.forward((i, part, "f"), i, done, self.spot, cols)

    def relay(self, item, phase):
        for i, part, cols, done, (right, left, _), two in self.plan(item, phase):
            for side, source, target, cc in (("r", left, right, two[0]), ("l", right, left, two[1])):
                where = (i, done, source[0], cc)
                self.sends.arrived((i, part, phase, side, 0), self.block(*where), source[1])
                self.push((i, part, phase, side, 2), target[1], *where)
                if phase == 2:
                    self.forward((i, part, "f", side, 0), *where)

    def finish(self, item, phase):
        for i, part, cols, done, (right, left, far), two in self.plan(item, phase):
            for side, step, at, cc, source in (
                ("r", 1, left, two[1], left),
                ("l", 1, right, two[0], right),
                ("r", 2, far, two[0], left),
                ("l", 2, far, two[1], right),
            ):
                where = (i, done, at[0], cc)
                self.sends.arrived((i, part, phase, side, step), self.block(*where), source[1])
                if phase == 2:
                    self.forward((i, part, "f", side, step), *where)

    def received(self, item):
        for name, (i, done, at, cc) in self.forwards[item]:
            self.sends.arrived(name, self.block(i, done, at, cc, self.other), self.sibling)


class Exchange:
    RADIX = {"x": 4, "z": 4, "y": 4, "c": 2}
    NATURAL = ("x", "z", "y", "c")

    def __init__(self, sends, key, lanes, src, dst):
        self.sends, self.key, self.src, self.dst = sends, key, src, dst
        self.core, self.spot = position()
        self.other = 1 - self.core
        self.sibling = device(self.other, self.spot)
        self.near = neighbours(self.core, self.spot)
        self.parts = list(enumerate(cut(lanes, 3)))

    def source(self, stage):
        return self.src.at[stage] if stage < 2 else self.dst.at[stage - 2]

    def order(self, stage, part):
        lead = "c" if stage == 0 else AXES[(part + stage - 1) % 3]
        return (lead,) + tuple(name for name in self.NATURAL if name != lead)

    def shuffle(self, new, old):
        rest = lax.broadcasted_iota(jnp.int32, (N_DEV, N_DEV), 0)
        digit = {}
        for name in reversed(new):
            digit[name] = rest % self.RADIX[name]
            rest = rest // self.RADIX[name]
        index = 0
        for name in old:
            index = index * self.RADIX[name] + digit[name]
        return (index == lax.broadcasted_iota(jnp.int32, (N_DEV, N_DEV), 1)).astype(BF)

    def load(self, lo, onehot, value):
        first = self.shuffle(self.order(0, 0), self.NATURAL)
        onehot = first if onehot is None else dot(first, onehot).astype(BF)
        width = value.shape[1]
        self.src[0, :, :, lo : lo + width] = dot(onehot, value).astype(BF).reshape(4, 32, width)

    def launch(self, stage):
        if stage == 0:
            self.sends.start(
                (self.key, 0),
                lambda: (
                    self.src.at[0, pl.ds(2 * self.other, 2)],
                    self.dst.at[0, pl.ds(2 * self.core, 2)],
                    self.sibling,
                ),
            )
            return
        for part, (lo, width) in self.parts:
            before = self.order(stage - 1, part)
            onehot = self.shuffle(self.order(stage, part), before)
            rows = self.dst[stage - 1, :, :, lo : lo + width].reshape(N_DEV, width)
            self.source(stage)[:, :, lo : lo + width] = dot(onehot, rows).astype(BF).reshape(4, 32, width)
            axis = (part + stage - 1) % 3
            for by in (2, 1, 3):
                there, target = self.near[axis, by]
                self.sends.start(
                    (self.key, stage, part, by),
                    lambda lo=lo, width=width, axis=axis, there=there, target=target: (
                        self.source(stage).at[there[axis], :, pl.ds(lo, width)],
                        self.dst.at[stage, self.spot[axis], :, pl.ds(lo, width)],
                        target,
                    ),
                )

    def land(self, stage):
        if stage == 0:
            here = pl.ds(2 * self.core, 2)
            self.dst[0, here] = self.src[0, here]
            self.sends.arrived((self.key, 0), self.dst.at[0, pl.ds(2 * self.other, 2)], self.sibling)
            return
        for part, (lo, width) in self.parts:
            axis = (part + stage - 1) % 3
            cs = pl.ds(lo, width)
            self.dst[stage, self.spot[axis], :, cs] = self.source(stage)[self.spot[axis], :, cs]
            for by in (2, 1, 3):
                there, source = self.near[axis, 4 - by]
                self.sends.arrived((self.key, stage, part, by), self.dst.at[stage, there[axis], :, cs], source)

    def rows(self):
        return jnp.concatenate(
            [
                dot(
                    self.shuffle(self.NATURAL, self.order(3, part)),
                    self.dst[3, :, :, lo : lo + width].reshape(N_DEV, width),
                ).astype(BF)
                for part, (lo, width) in self.parts
            ],
            axis=1,
        )


XLANES = 33
DLANES = 16
EX_SLOTS = 1 + 3 * 9

WALL = 768
WIDTHS = (4 * HCOLS + 7 * AR, D + FB + WALL, FB + WALL, FB + WALL)
FSTEPS = H
BLOCKS = FFP // FB


def forward_kernel(
    split_ref, tok_ref, cot_ref, rates_ref, gain1_ref, gain2_ref, mask_ref, to_ref, place_ref, pers_ref,
    mine0, mine1, mine2, mine3,
    g0_ref, g1_ref, g2_ref, g3_ref, proj_ref, x_ref, h1_ref, lat_ref, wf_ref, lw_ref, back_ref, dz_ref, dmid_ref,
    grads_ref,
    xsrc, xdst, d_ref, dec_ref, dect_ref, inc0, inc1, inc2, inc3, stage0, stage1, stage2, stage3,
    w_buf, up_buf, down_buf, z_ref, wup_buf, wd_buf, lead_buf,
    x2_ref, h2_ref, inv_ref, lat_out_ref, lat_up_ref, dl_down_ref, acc_ref, lat_acc_ref, dh_ref, dlat_ref,
    send_sem, recv_sem, local_sem, w_sem, j_sem,
):
    step = pl.program_id(0)
    mine, inc = (mine0, mine1, mine2, mine3), (inc0, inc1, inc2, inc3)
    stage, outs = (stage0, stage1, stage2, stage3), (g0_ref, g1_ref, g2_ref, g3_ref)
    sends = Sends(send_sem, recv_sem)
    ring = Gather(sends, outs, WIDTHS)
    core, spot = ring.core, ring.spot
    other = 1 - core
    swap = Exchange(sends, "x", XLANES, xsrc, xdst)
    items = range(4)

    def head_loads(h, slot):
        half, place = h // 4, pl.multiple_of((h % 4) * HCOLS, 128)
        return (
            pltpu.make_async_copy(
                g0_ref.at[half, :, :, :, :, pl.ds(place, HCOLS)], w_buf.at[slot], w_sem.at[slot, 0]
            ),
            pltpu.make_async_copy(
                g0_ref.at[1, h // 2, pl.ds(2 * (h % 2), 2), :, :, pl.ds(4 * HCOLS, HCOLS)],
                up_buf.at[slot],
                w_sem.at[slot, 1],
            ),
        )

    def down_load():
        return pltpu.make_async_copy(
            g0_ref.at[0, :, :, :, :, pl.ds(4 * HCOLS, HCOLS)], down_buf, local_sem.at[0]
        )

    def lead_load():
        return pltpu.make_async_copy(g1_ref.at[:, :, :, :, :, pl.ds(0, D)], lead_buf, local_sem.at[0])

    def up_load(k):
        at = D if k == 0 else 0
        return pltpu.make_async_copy(
            outs[k + 1].at[:, :, :, :, :, pl.ds(at, FB)], wup_buf.at[k % 2], j_sem.at[k % 2, 0]
        )

    def wall_load(k):
        at = D + FB if k == 0 else FB
        return pltpu.make_async_copy(
            outs[k + 1].at[:, :, :, :, :, pl.ds(at, WALL)], wd_buf.at[k % 2], j_sem.at[k % 2, 1]
        )

    @pl.when(step == 0)
    def _():
        greet([ring.sibling] + [there[1] for there in ring.near.values()])
        for i in items:
            sends.start(("pair", i), lambda i=i: (mine[i].at[other], inc[i], ring.sibling))
        for m in range(MB):
            swap.load(m * D, to_ref[m], tok_ref[m])
            swap.load((MB + m) * D, to_ref[m], cot_ref[m])
        swap.load(2 * MB * D, None, rates_ref[...])
        swap.launch(0)
        own_copy = lambda i: pltpu.make_async_copy(
            stage[i], outs[i].at[core, spot[0], spot[1], spot[2]], local_sem.at[i]
        )
        for i in items:
            sends.arrived(("pair", i), inc[i], ring.sibling)
            own, theirs = mine[i][core], inc[i][...]
            first = jnp.where(core == 0, own, theirs)
            last = jnp.where(core == 0, theirs, own)
            stage[i][...] = jnp.concatenate([first, last], axis=0).astype(BF)
            own_copy(i).start()
        for i in items:
            own_copy(i).wait()
            ring.begin(i, 0)
        swap.land(0)
        swap.launch(1)
        for i in items:
            ring.relay(i, 0)
        for i in items:
            ring.finish(i, 0)
            ring.begin(i, 1)
        swap.land(1)
        swap.launch(2)
        for i in items:
            ring.relay(i, 1)
        swap.land(2)
        swap.launch(3)
        ring.finish(0, 1)
        ring.begin(0, 2)
        for i in items[1:]:
            ring.finish(i, 1)
        swap.land(3)
        got = swap.rows()
        for m in range(MB):
            s = slice(m * GROUP, (m + 1) * GROUP)
            x_ref[s, :] = dot(place_ref[m], got[:, m * D : (m + 1) * D]).astype(BF)
            d_ref[s, :] = dot(place_ref[m], got[:, (MB + m) * D : (MB + m + 1) * D]).astype(BF)
            sent = got[:, 2 * MB * D + m * 3 * H : 2 * MB * D + (m + 1) * 3 * H]
            dec_ref[s, :] = dot(place_ref[m], sent)
            dect_ref[:, s] = lax.dot_general(
                sent, place_ref[m], (((0,), (1,)), ((), ())), preferred_element_type=F32
            )
        decay_kernel(split_ref, dec_ref, dect_ref, wf_ref, lw_ref)
        normed, _ = norm_fwd(x_ref[...].astype(F32), gain1_ref[...])
        h1_ref[...] = normed.astype(BF)
        ring.relay(0, 2)
        ring.begin(1, 2)
        ring.finish(0, 2)
        ring.received(0)
        for copy in head_loads(0, 0):
            copy.start()
        down_load().start()
        down_load().wait()
        latent = dot(h1_ref[...], down_buf[...].reshape(D, HCOLS))
        mask = mask_ref[...]
        for part in range(7):
            s = slice(part * AR, (part + 1) * AR)
            lat_ref[:, s] = (latent[:, s] * mask).astype(BF)

    @pl.when(step == 3)
    def _():
        ring.relay(1, 2)
        ring.begin(2, 2)

    @pl.when(step < FSTEPS)
    def _():
        slot = step % 2
        for copy in head_loads(step, slot):
            copy.wait()

        @pl.when(step + 1 < FSTEPS)
        def _():
            for copy in head_loads(step + 1, 1 - slot):
                copy.start()

        base = dot(h1_ref[...], w_buf[slot].reshape(D, HCOLS))
        up = up_buf[slot].reshape(HEAD, HCOLS)
        pieces = []
        for part in range(7):
            s = slice(part * AR, (part + 1) * AR)
            piece = base[:, part * HEAD : (part + 1) * HEAD] + dot(lat_ref[:, s], up[:, s], NT)
            proj_ref[:, part * HEAD : (part + 1) * HEAD] = piece
            pieces.append(piece)
        q, k, v = (pieces[i].astype(BF) for i in range(3))
        pk, pv = pers_ref[0, :, pl.ds(pl.multiple_of(step * HEAD, HEAD), HEAD)], pers_ref[
            1, :, pl.ds(pl.multiple_of(step * HEAD, HEAD), HEAD)
        ]
        near, far = attend(q, k, v, pk, pv, allowed_mask(split_ref))
        att = attend_out(near.astype(BF), far.astype(BF), v, pv)
        kn, _ = unit(pieces[3])
        qn, _ = unit(pieces[5])
        here = pl.ds(step, 1)
        mem = memory_out(memory_terms(kn, qn, pieces[4], wf_ref.at[here], lw_ref.at[here]))
        z_ref[:, pl.ds(pl.multiple_of(step * HEAD, HEAD), HEAD)] = (
            att + jax.nn.sigmoid(pieces[6]) * mem
        ).astype(BF)

    lead = lambda half, lo, hi: lead_buf[half, :, :, :, :, lo:hi].reshape(D, hi - lo)
    out_down = lambda: lead(0, 0, 128)
    out_up = lambda: lead(0, 128, 256)
    up_down = lambda: lead(0, 256, 512)
    down_up = lambda: lead(0, 512, 640)
    w_out = lambda: lead(1, 0, D)

    @pl.when(step == FSTEPS)
    def _():
        ring.finish(1, 2)
        ring.received(1)
        for copy in (lead_load(), up_load(0), wall_load(0)):
            copy.start()
        ring.relay(2, 2)
        ring.begin(3, 2)
        lead_load().wait()
        mask = mask_ref[...]
        z = z_ref[...]
        lat_out_ref[...] = (dot(z, out_down()) * mask).astype(BF)
        x2 = x_ref[...].astype(F32) + (dot(z, w_out()) + dot(lat_out_ref[...], out_up(), NT))
        x2_ref[...] = x2
        normed, inv = norm_fwd(x2, gain2_ref[...])
        inv_ref[...] = jnp.broadcast_to(inv, inv_ref.shape)
        h2_ref[...] = normed.astype(BF)
        latent = dot(h2_ref[...], up_down())
        lat_up_ref[:, :AR] = (latent[:, :AR] * mask).astype(BF)
        lat_up_ref[:, AR:] = (latent[:, AR:] * mask).astype(BF)
        dl_down_ref[...] = (dot(d_ref[...], down_up()) * mask).astype(BF)
        for ref in (acc_ref, lat_acc_ref, dh_ref, dlat_ref):
            ref[...] = jnp.zeros_like(ref)

    @pl.when(step >= FSTEPS)
    def _():
        k = step - FSTEPS
        slot = k % 2
        h2 = h2_ref[...]
        d = d_ref[...]
        lat0, lat1 = lat_up_ref[:, :AR], lat_up_ref[:, AR:]
        wall = lambda half, lo, hi: wd_buf[slot, half, :, :, :, :, lo:hi].reshape(FB, hi - lo)
        pltpu.make_async_copy(wup_buf.at[slot], wup_buf.at[slot], j_sem.at[slot, 0]).wait()
        pltpu.make_async_copy(wd_buf.at[slot], wd_buf.at[slot], j_sem.at[slot, 1]).wait()
        w_gate, w_lift = (wup_buf[slot, half].reshape(D, FB) for half in range(2))
        wda, wdb = wall(0, 0, 768), wall(1, 0, 256)
        uu0, uu1, dd = wall(1, 256, 384), wall(1, 384, 512), wall(1, 512, 640)
        gate = dot(h2, w_gate) + dot(lat0, uu0, NT)
        lift = dot(h2, w_lift) + dot(lat1, uu1, NT)
        sig = jax.nn.sigmoid(gate)
        silu = gate * sig
        act = (silu * lift).astype(BF)
        d_act = dot(d[:, :768], wda, NT) + dot(d[:, 768:], wdb, NT) + dot(dl_down_ref[...], dd, NT)
        d_gate = (d_act * lift * (sig * (1.0 + gate * (1.0 - sig)))).astype(BF)
        d_lift = (d_act * silu).astype(BF)
        acc_ref[:, :768] += dot(act, wda)
        acc_ref[:, 768:] += dot(act, wdb)
        lat_acc_ref[...] += dot(act, dd)
        dh_ref[...] += dot(d_gate, w_gate, NT) + dot(d_lift, w_lift, NT)
        dlat_ref[:, :AR] += dot(d_gate, uu0)
        dlat_ref[:, AR:] += dot(d_lift, uu1)
        for half, at, term in (
            (0, k * 256, dot(d_gate, lat0, TN)),
            (0, k * 256 + AR, dot(d_lift, lat1, TN)),
            (1, k * AR, dot(act, dl_down_ref[...], TN)),
        ):
            at = pl.ds(pl.multiple_of(at, AR), AR)
            grads_ref[half, :, :, at] = term.reshape(64, 16, AR).astype(BF)

        for j in range(1, BLOCKS):

            @pl.when(k == j - 1)
            def _():
                ring.finish(j + 1, 2)
                ring.received(j + 1)
                up_load(j).start()
                wall_load(j).start()
                if j + 1 < BLOCKS:
                    ring.relay(j + 2, 2)

    @pl.when(step == FSTEPS + BLOCKS - 1)
    def _():
        mask = mask_ref[...]
        lat_down = (lat_acc_ref[...] * mask).astype(BF)
        out = (x2_ref[...] + acc_ref[...] + dot(lat_down, down_up(), NT)).astype(BF)
        for m in range(MB):
            s = slice(m * GROUP, (m + 1) * GROUP)
            back_ref[:, m * D : (m + 1) * D] = dot(place_ref[m], out[s], TN).astype(BF)
        d = d_ref[...]
        h2 = h2_ref[...]
        z = z_ref[...]

        def put(half, at, value):
            grads_ref[half, :, :, at : at + AR] = value.reshape(64, 16, AR).astype(BF)

        put(0, 768, dot(d, lat_down, TN))
        dlu0 = (dlat_ref[:, :AR] * mask).astype(BF)
        dlu1 = (dlat_ref[:, AR:] * mask).astype(BF)
        put(1, 640, dot(h2, dlu0, TN))
        put(1, 768, dot(h2, dlu1, TN))
        ud = up_down()
        dh = dh_ref[...] + (dot(dlu0, ud[:, :AR], NT) + dot(dlu1, ud[:, AR:], NT))
        dmid = d.astype(F32) + norm_bwd(dh, x2_ref[...], inv_ref[:, :1], gain2_ref[...])
        dmid_ref[...] = dmid
        dmb = dmid.astype(BF)
        dlo = (dot(dmb, out_up()) * mask).astype(BF)
        put(1, 384, dot(z, dlo, TN))
        put(1, 512, dot(dmb, lat_out_ref[...], TN))
        dz_ref[...] = (dot(dmb, w_out(), NT) + dot(dlo, out_down(), NT)).astype(BF)
        sends.drain()


def forward_call(split, tokens, cotangent, rates, gain1, gain2, mask, to, place, persistent, mine):
    once = pl.Buffered(1)
    whole = lambda *shape: pl.BlockSpec(shape, lambda s: (0,) * len(shape), pipeline_mode=once)
    hbm = pl.BlockSpec(memory_space=pl.ANY)
    slots = 4 * (1 + 3 * (3 * 6 + 7)) + EX_SLOTS
    return pl.pallas_call(
        forward_kernel,
        grid=(FSTEPS + BLOCKS,),
        out_shape=tuple(jax.ShapeDtypeStruct((2, 4, 4, 4, 16, width), BF) for width in WIDTHS)
        + (
            jax.ShapeDtypeStruct((ROWS, 7 * D), F32),
            jax.ShapeDtypeStruct((ROWS, D), BF),
            jax.ShapeDtypeStruct((ROWS, D), BF),
            jax.ShapeDtypeStruct((ROWS, 7 * AR), BF),
            jax.ShapeDtypeStruct((H, MB, GROUP, GROUP), F32),
            jax.ShapeDtypeStruct((H, MB, 8, GROUP), F32),
            jax.ShapeDtypeStruct((GROUP, MB * D), BF),
            jax.ShapeDtypeStruct((ROWS, D), BF),
            jax.ShapeDtypeStruct((ROWS, D), F32),
            jax.ShapeDtypeStruct((2, 64, 16, 896), BF),
        ),
        in_specs=[
            pl.BlockSpec(memory_space=pltpu.SMEM),
            whole(MB, GROUP, D),
            whole(MB, GROUP, D),
            whole(GROUP, 128),
            whole(1, D),
            whole(1, D),
            whole(ROWS, AR),
            whole(MB, GROUP, GROUP),
            whole(MB, GROUP, GROUP),
            whole(2, NP, D),
        ]
        + [whole(2, 8, width) for width in WIDTHS],
        out_specs=(hbm,) * 4
        + (
            pl.BlockSpec((ROWS, HCOLS), lambda s: (0, jnp.minimum(s, FSTEPS - 1))),
            whole(ROWS, D),
            whole(ROWS, D),
            whole(ROWS, 7 * AR),
            whole(H, MB, GROUP, GROUP),
            whole(H, MB, 8, GROUP),
            whole(GROUP, MB * D),
            whole(ROWS, D),
            whole(ROWS, D),
            whole(2, 64, 16, 896),
        ),
        scratch_shapes=[
            pltpu.VMEM((2, 4, 32, XLANES * 128), BF),
            pltpu.VMEM((4, 4, 32, XLANES * 128), BF),
            pltpu.VMEM((ROWS, D), BF),
            pltpu.VMEM((ROWS, 3 * H), F32),
            pltpu.VMEM((3 * H, ROWS), F32),
        ]
        + [pltpu.VMEM((8, width), F32) for width in WIDTHS]
        + [pltpu.VMEM((16, width), BF) for width in WIDTHS]
        + [
            pltpu.VMEM((2, 4, 4, 4, 16, HCOLS), BF),
            pltpu.VMEM((2, 2, 4, 16, HCOLS), BF),
            pltpu.VMEM((4, 4, 4, 16, HCOLS), BF),
            pltpu.VMEM((ROWS, D), BF),
            pltpu.VMEM((2, 2, 4, 4, 4, 16, FB), BF),
            pltpu.VMEM((2, 2, 4, 4, 4, 16, WALL), BF),
            pltpu.VMEM((2, 4, 4, 4, 16, D), BF),
            pltpu.VMEM((ROWS, D), F32),
            pltpu.VMEM((ROWS, D), BF),
            pltpu.VMEM((ROWS, 128), F32),
            pltpu.VMEM((ROWS, AR), BF),
            pltpu.VMEM((ROWS, 2 * AR), BF),
            pltpu.VMEM((ROWS, AR), BF),
            pltpu.VMEM((ROWS, D), F32),
            pltpu.VMEM((ROWS, AR), F32),
            pltpu.VMEM((ROWS, D), F32),
            pltpu.VMEM((ROWS, 2 * AR), F32),
            pltpu.SemaphoreType.DMA((slots,)),
            pltpu.SemaphoreType.DMA((slots,)),
            pltpu.SemaphoreType.DMA((4,)),
            pltpu.SemaphoreType.DMA((2, 2)),
            pltpu.SemaphoreType.DMA((2, 2)),
        ],
        compiler_params=pltpu.CompilerParams(
            collective_id=0, has_side_effects=True, vmem_limit_bytes=VMEM_LIMIT
        ),
        name="gather_forward",
    )(split, tokens, cotangent, rates, gain1, gain2, mask, to, place, persistent, *mine)


class Scatter:
    def __init__(self, sends, key, grads, out, inc0, total, inc1, inc2, inc3, t1, t2):
        self.sends, self.key, self.grads, self.out = sends, key, grads, out
        self.inc0, self.total, self.inc = inc0, total, (None, inc1, inc2, inc3)
        self.t1, self.t2 = t1, t2
        self.core, self.spot = position()
        self.other = 1 - self.core
        self.sibling = device(1 - self.core, self.spot)
        self.near = neighbours(self.core, self.spot)
        self.parts = [(part, pl.ds(*cols)) for part, cols in enumerate(cut(7, 3))]

    def peers(self):
        return [self.sibling] + [there[1] for there in self.near.values()]

    def pair(self):
        for x in range(4):
            self.sends.start(
                (self.key, "pair", x),
                lambda x=x: (
                    self.grads.at[self.other, pl.ds(16 * x, 16)],
                    self.inc0.at[x],
                    self.sibling,
                ),
            )

    def source(self, phase, part, at):
        axis = (part + phase - 1) % 3
        cs = self.parts[part][1]
        if phase == 1:
            index = tuple(at if a == axis else slice(None) for a in range(3))
            return self.total, index + (slice(None), cs)
        rest = [a for a in range(3) if a != part]
        if phase == 2:
            index = (at, slice(None)) if rest[0] == axis else (slice(None), at)
            return self.t1, index + (slice(None), cs)
        return self.t2, (at, slice(None), cs)

    def landing(self, phase, part, k):
        return (k,) + (slice(None),) * (4 - phase) + (self.parts[part][1],)

    def send(self, phase):
        for part, _ in self.parts:
            axis = (part + phase - 1) % 3
            for k, by in enumerate((2, 1, 3)):
                to = self.near[axis, by]

                def make(part=part, axis=axis, to=to, k=k):
                    ref, index = self.source(phase, part, to[0][axis])
                    return ref.at[index], self.inc[phase].at[self.landing(phase, part, k)], to[1]

                self.sends.start((self.key, part, phase, by), make)

    def add(self, phase):
        for part, cs in self.parts:
            axis = (part + phase - 1) % 3
            ref, index = self.source(phase, part, self.spot[axis])
            acc = ref[index].astype(F32)
            for k, by in enumerate((2, 1, 3)):
                here = self.landing(phase, part, k)
                source = self.near[axis, 4 - by][1]
                self.sends.arrived((self.key, part, phase, by), self.inc[phase].at[here], source)
                acc = acc + self.inc[phase][here].astype(F32)
            if phase == 1:
                self.t1[:, :, :, cs] = acc.astype(BF)
            elif phase == 2:
                self.t2[:, :, cs] = acc.astype(BF)
            else:
                self.out[self.core, :, cs] = acc

    def add_pair(self):
        for x in range(4):
            self.sends.arrived((self.key, "pair", x), self.inc0.at[x], self.sibling)
            both = self.grads[self.core, pl.ds(16 * x, 16)].astype(F32) + self.inc0[x].astype(F32)
            self.total[x] = both.reshape(4, 4, 16, 896).astype(BF)

    def swap(self):
        self.sends.start(
            (self.key, "last"), lambda: (self.out.at[self.core], self.out.at[self.core], self.sibling)
        )

    def swapped(self):
        self.sends.arrived((self.key, "last"), self.out.at[self.other], self.sibling)


def backward_kernel(
    split_ref, x_ref, gain_ref, mask_ref, to_ref, place_ref, proj_ref, dz_ref, dmid_ref, h1_ref, lat_ref,
    w_ref, down_ref, up_ref, pers_ref, wf_ref, lw_ref, ffn_ref, back_ref,
    act_out, grad_out, ffn_out, heads_out,
    dh_ref, dlat_ref, dlat_half, dy_ref, grads_ref, *rest,
):
    step = pl.program_id(0)
    send_sem, recv_sem = rest[-2:]
    sends = Sends(send_sem, recv_sem)
    first_sums = Scatter(sends, 0, ffn_ref, *rest[:8])
    last_sums = Scatter(sends, 1, grads_ref, *rest[8:16])
    ex_act = Exchange(sends, "a", DLANES, *rest[16:18])
    ex_grad = Exchange(sends, "g", DLANES, *rest[18:20])

    def home(exchange, out_ref):
        got = exchange.rows()
        for m in range(MB):
            out_ref[m] = dot(to_ref[m], got[:, m * D : (m + 1) * D], TN).astype(BF)

    def one_head():
        pieces = [proj_ref[:, p * HEAD : (p + 1) * HEAD] for p in range(7)]
        q, k, v = (pieces[i].astype(BF) for i in range(3))
        pk, pv = pers_ref[0], pers_ref[1]
        near, far = attend(q, k, v, pk, pv, allowed_mask(split_ref))
        near_half = near.astype(BF)
        dz = dz_ref[...]
        d_near = by_group(lambda s, g: dot(dz[s], v[s], NT))
        d_far = dot(dz, pv, NT)
        d_v = by_group(lambda s, g: dot(near_half[s], dz[s], TN))
        total = jnp.sum(d_near * near, axis=-1, keepdims=True) + jnp.sum(
            d_far * far, axis=-1, keepdims=True
        )
        ds_near = (near * (d_near - total) * SCALE).astype(BF)
        ds_far = (far * (d_far - total) * SCALE).astype(BF)
        d_q = by_group(lambda s, g: dot(ds_near[s], k[s])) + dot(ds_far, pk)
        d_k = by_group(lambda s, g: dot(ds_near[s], q[s], TN))

        dzf = dz.astype(F32)
        opening = jax.nn.sigmoid(pieces[6])
        kn, k_inv = unit(pieces[3])
        qn, q_inv = unit(pieces[5])
        kept = memory_terms(kn, qn, pieces[4], wf_ref, lw_ref)
        mem = memory_out(kept)
        d_open = dzf * mem * (opening * (1.0 - opening))
        d_kn, d_qn, d_mv = memory_bwd(kept, dzf * opening)
        d_mk = unit_bwd(d_kn, pieces[3], k_inv)
        d_mq = unit_bwd(d_qn, pieces[5], q_inv)
        dy = [item.astype(BF) for item in (d_q, d_k, d_v, d_mk, d_mv, d_mq, d_open)]
        dy_ref[step] = jnp.concatenate(dy, axis=1)
        first = pl.multiple_of(step * 8, 8)
        for part in range(7):
            s = slice(part * AR, (part + 1) * AR)
            dlat_ref[:, s] += dot(dy[part], up_ref[0, :, s])
            grads_ref[1, pl.ds(first, 8), :, s] = (
                dot(dy[part], lat_ref[:, s], TN).reshape(8, 16, AR).astype(BF)
            )

    @pl.when(step == 0)
    def _():
        greet(first_sums.peers())
        ex_act.load(0, None, back_ref[...])
        ex_act.launch(0)
        first_sums.pair()
        dlat_ref[...] = jnp.zeros_like(dlat_ref)

    @pl.when(step == 1)
    def _():
        ex_act.land(0)
        ex_act.launch(1)

    @pl.when(step == 2)
    def _():
        first_sums.add_pair()
        first_sums.send(1)

    @pl.when(step == 3)
    def _():
        ex_act.land(1)
        ex_act.launch(2)

    @pl.when(step == 5)
    def _():
        first_sums.add(1)
        first_sums.send(2)
        ex_act.land(2)
        ex_act.launch(3)

    @pl.when(step == 6)
    def _():
        first_sums.add(2)
        first_sums.send(3)

    @pl.when(step == 7)
    def _():
        first_sums.add(3)
        first_sums.swap()
        ex_act.land(3)
        home(ex_act, act_out)

    @pl.when(step < H)
    def _():
        one_head()

    @pl.when(step == H)
    def _():
        mask = mask_ref[...]
        for p in range(7):
            s = slice(p * AR, (p + 1) * AR)
            dlat_half[:, s] = (dlat_ref[:, s] * mask).astype(BF)
        grads_ref[0] = dot(h1_ref[...], dlat_half[...], TN).reshape(64, 16, 7 * AR).astype(BF)
        last_sums.pair()
        dh_ref[...] = dot(dlat_half[...], down_ref[0], NT)

    @pl.when(step == H + 3)
    def _():
        last_sums.add_pair()
        last_sums.send(1)

    @pl.when(step >= H)
    def _():
        dh_ref[...] += dot(dy_ref[step - H], w_ref[0], NT)

    @pl.when(step == 2 * H - 1)
    def _():
        x = x_ref[...].astype(F32)
        inv = lax.rsqrt(jnp.mean(x * x, axis=-1, keepdims=True) + EPS)
        dx = (dmid_ref[...] + norm_bwd(dh_ref[...], x, inv, gain_ref[...])).astype(BF)
        for m in range(MB):
            s = slice(m * GROUP, (m + 1) * GROUP)
            ex_grad.load(m * D, transposed(place_ref[m]), dx[s])
        ex_grad.launch(0)
        first_sums.swapped()
        ffn_out[...] = first_sums.out[...]
        ex_grad.land(0)
        ex_grad.launch(1)
        last_sums.add(1)
        last_sums.send(2)
        ex_grad.land(1)
        ex_grad.launch(2)
        last_sums.add(2)
        last_sums.send(3)
        ex_grad.land(2)
        ex_grad.launch(3)
        last_sums.add(3)
        last_sums.swap()
        ex_grad.land(3)
        home(ex_grad, grad_out)
        last_sums.swapped()
        heads_out[...] = last_sums.out[...]
        sends.drain()


def backward_call(split, x, gain, mask, to, place, proj, dz, dmid, h1, lat, a1, persistent, wf, lw, grads_ffn, back):
    once = pl.Buffered(1)
    whole = lambda *shape: pl.BlockSpec(shape, lambda s: (0,) * len(shape), pipeline_mode=once)
    head = lambda s: jnp.minimum(s, H - 1)
    late = lambda s: jnp.maximum(s - H, 0)
    buffers = [
        pltpu.VMEM((2, 16, 896), F32),
        pltpu.VMEM((4, 16, 16, 896), BF),
        pltpu.VMEM((4, 4, 4, 16, 896), BF),
        pltpu.VMEM((3, 4, 4, 16, 896), BF),
        pltpu.VMEM((3, 4, 16, 896), BF),
        pltpu.VMEM((3, 16, 896), BF),
        pltpu.VMEM((4, 4, 16, 896), BF),
        pltpu.VMEM((4, 16, 896), BF),
    ]
    slots = 2 * (4 + 3 * 9 + 1) + 2 * EX_SLOTS
    return pl.pallas_call(
        backward_kernel,
        grid=(2 * H,),
        out_shape=(
            jax.ShapeDtypeStruct((MB, GROUP, D), BF),
            jax.ShapeDtypeStruct((MB, GROUP, D), BF),
            jax.ShapeDtypeStruct((2, 16, 896), F32),
            jax.ShapeDtypeStruct((2, 16, 896), F32),
        ),
        in_specs=[
            pl.BlockSpec(memory_space=pltpu.SMEM),
            whole(ROWS, D),
            whole(1, D),
            whole(ROWS, AR),
            whole(MB, GROUP, GROUP),
            whole(MB, GROUP, GROUP),
            pl.BlockSpec((ROWS, HCOLS), lambda s: (0, head(s))),
            pl.BlockSpec((ROWS, HEAD), lambda s: (0, head(s))),
            whole(ROWS, D),
            whole(ROWS, D),
            whole(ROWS, 7 * AR),
            pl.BlockSpec((1, D, HCOLS), lambda s: (late(s) // 4, 0, late(s) % 4)),
            pl.BlockSpec((1, D, HCOLS), lambda s: (0, 0, 4), pipeline_mode=once),
            pl.BlockSpec((1, HEAD, HCOLS), lambda s: (1, head(s), 4)),
            pl.BlockSpec((2, NP, HEAD), lambda s: (0, 0, head(s))),
            pl.BlockSpec((1, MB, GROUP, GROUP), lambda s: (head(s), 0, 0, 0)),
            pl.BlockSpec((1, MB, 8, GROUP), lambda s: (head(s), 0, 0, 0)),
            pl.BlockSpec(memory_space=pltpu.VMEM),
            pl.BlockSpec(memory_space=pltpu.VMEM),
        ],
        out_specs=(
            whole(MB, GROUP, D),
            whole(MB, GROUP, D),
            pl.BlockSpec(memory_space=pltpu.VMEM),
            pl.BlockSpec(memory_space=pltpu.VMEM),
        ),
        scratch_shapes=[
            pltpu.VMEM((ROWS, D), F32),
            pltpu.VMEM((ROWS, 7 * AR), F32),
            pltpu.VMEM((ROWS, 7 * AR), BF),
            pltpu.VMEM((H, ROWS, HCOLS), BF),
            pltpu.VMEM((2, 64, 16, 896), BF),
        ]
        + buffers * 2
        + [pltpu.VMEM((rows, 4, 32, DLANES * 128), BF) for rows in (2, 4, 2, 4)]
        + [pltpu.SemaphoreType.DMA((slots,)), pltpu.SemaphoreType.DMA((slots,))],
        compiler_params=pltpu.CompilerParams(
            collective_id=1, has_side_effects=True, vmem_limit_bytes=VMEM_LIMIT
        ),
        name="backward_scatter",
    )(split, x, gain, mask, to, place, proj, dz, dmid, h1, lat, a1, a1, a1, persistent, wf, lw, grads_ffn, back)


def by_rank(value, parts):
    rows = value.shape[1]
    return value.reshape(NAD, rows, parts, R).transpose(1, 2, 0, 3).reshape(rows, parts * AR)


def by_rank_t(value, parts):
    cols = value.shape[2]
    return value.reshape(NAD, parts, R, cols).transpose(3, 1, 0, 2).reshape(cols, parts * AR)


def pack_shards(w_in, w_out, w_up, w_down, in_down, in_up, out_down, out_up, up_down, up_up, down_down, down_up):
    rows = w_in.shape[0]
    heads = w_in.reshape(rows, 7, H, HEAD).transpose(0, 2, 1, 3).reshape(rows, 2, 4 * HCOLS)
    items = [
        jnp.stack(
            [
                jnp.concatenate([heads[:, 0], by_rank(in_down, 7)], axis=1),
                jnp.concatenate([heads[:, 1], by_rank_t(in_up, 7)], axis=1),
            ]
        )
    ]
    up = w_up.reshape(rows, 2, N_DEV, FF_SHARD)
    up = jnp.pad(up, ((0, 0), (0, 0), (0, 0), (0, FF_PAD - FF_SHARD)))
    up = up.reshape(rows, 2, N_DEV, 3, 8).transpose(3, 1, 0, 2, 4).reshape(3, 2, rows, FB)
    small = jnp.concatenate(
        [by_rank(out_down, 1), by_rank_t(out_up, 1), by_rank(up_down, 2), by_rank_t(down_up, 1)], axis=1
    )
    small = jnp.pad(small, ((0, 0), (0, D - small.shape[1])))
    rest = jnp.concatenate([w_down[:, 768:], by_rank_t(up_up, 2), by_rank(down_down, 1)], axis=1)
    rest = jnp.pad(rest, ((0, 0), (0, 128)))
    tall = jnp.pad(jnp.stack([w_down[:, :768], rest]), ((0, 0), (0, FF_PAD - FF_SHARD), (0, 0)))
    tall = tall.reshape(2, 3, 8, 768)
    lead = jnp.stack([small, w_out])
    for k in range(3):
        parts = [up[k], tall[:, k]]
        items.append(jnp.concatenate([lead] + parts if k == 0 else parts, axis=2))
    return items


def un_rank(value, parts):
    rows = value.shape[0]
    return value.reshape(rows, parts, NAD, R).transpose(2, 0, 1, 3).reshape(NAD, rows, parts * R)


def un_rank_t(value, parts):
    cols = value.shape[0]
    return value.reshape(cols, parts, NAD, R).transpose(2, 1, 3, 0).reshape(NAD, parts * R, cols)


def unpack_grads(ffn_chip, heads_chip, core):
    def rows8(value):
        return lax.dynamic_slice_in_dim(value, core * 8, 8, axis=0)

    grad_id = un_rank(rows8(heads_chip[0]), 7)
    grad_iu = un_rank_t(rows8(heads_chip[1]), 7)

    def rows22(value, width):
        value = rows8(value).reshape(8, 3, width).transpose(1, 0, 2)
        return value.reshape(FF_PAD, width)[:FF_SHARD]

    grad_uu = un_rank_t(rows22(ffn_chip[0, :, :768], 256), 2)
    grad_dd = un_rank(rows22(ffn_chip[1, :, :384], AR), 1)
    grad_du = un_rank_t(rows8(ffn_chip[0, :, 768:]), 1)
    grad_od = un_rank(rows8(ffn_chip[1, :, 384:512]), 1)
    grad_ou = un_rank_t(rows8(ffn_chip[1, :, 512:640]), 1)
    grad_ud = un_rank(rows8(ffn_chip[1, :, 640:896]), 2)
    return grad_id, grad_iu, grad_od, grad_ou, grad_ud, grad_uu, grad_dd, grad_du


def body(
    tokens, cotangent, decays, route, lengths, adapter_ids, gain_mix, gain_ffn, persistent,
    w_in, w_out, w_up, w_down, in_down, in_up, out_down, out_up, up_down, up_up, down_down, down_up,
):
    me = lax.axis_index("fsdp")
    packed = pack_shards(
        w_in, w_out, w_up, w_down, in_down, in_up, out_down, out_up, up_down, up_up, down_down, down_up
    )
    items = [item.astype(F32) for item in packed]

    spots = jnp.arange(GROUP, dtype=jnp.int32)
    own = lax.dynamic_slice_in_dim(route, me * GROUP, GROUP, axis=1)
    send = (own[:, None, :] // GROUP == spots[None, :, None]).astype(BF)
    blocks = route.reshape(MB, N_DEV, GROUP)
    landing = jnp.sum(jnp.where(blocks // GROUP == me, blocks % GROUP, 0), axis=2)
    place = (landing[:, None, :] == spots[None, :, None]).astype(BF)

    rates = jnp.einsum("mij,mjd->mid", send, decays, preferred_element_type=F32).astype(BF)
    rates = jnp.concatenate([rates[0], rates[1], jnp.zeros((GROUP, 128 - MB * 3 * H), BF)], axis=1)
    lengths, ids = lengths[:, 0], adapter_ids[:, 0]
    split = (lengths[:, 0] < GROUP).astype(F32)
    row_ids = jnp.where(spots[None, :] >= lengths[:, :1], ids[:, 1:], ids[:, :1]).reshape(ROWS)
    mask = (row_ids[:, None] == (jnp.arange(AR) // R)[None, :]).astype(F32)
    gain_mix, gain_ffn = gain_mix[None, :], gain_ffn[None, :]
    a1, _, _, _, proj, x, h1, lat, wf, lw, back, dz, dmid, grads_ffn = forward_call(
        split, tokens, cotangent, rates, gain_mix, gain_ffn, mask, send, place, persistent, items
    )
    out, grad, ffn_chip, heads_chip = backward_call(
        split, x, gain_mix, mask, send, place, proj, dz, dmid, h1, lat, a1.reshape(2, D, WIDTHS[0]), persistent, wf, lw,
        grads_ffn, back,
    )
    return (out, grad) + unpack_grads(ffn_chip, heads_chip, me % 2)


def solution(mesh):
    rows, cols = P(None, "fsdp", None), P(None, None, "fsdp")
    weight = P("fsdp", None)
    return jax.shard_map(
        body,
        mesh=mesh,
        in_specs=(rows, rows, rows, P(), rows, rows, P(), P(), P())
        + (weight,) * 4
        + (rows, cols) * 4,
        out_specs=(rows, rows) + (rows, cols) * 4,
        check_vma=False,
    )
```

```python
import functools
import math

import jax
import jax.numpy as jnp
from jax import lax
from jax.experimental import pallas as pl
from jax.experimental.pallas import tpu as pltpu
from jax.sharding import PartitionSpec as P

D = 1024
H = 8
HEAD = 128
FF = 2816
R = 16
NAD = 8
NP = 16
SPAN = 64
GROUP = 128
MB = 2
ROWS = MB * GROUP
N_DEV = 128
AR = NAD * R
HCOLS = 7 * HEAD
FF_SHARD = FF // N_DEV
FF_PAD = 24
FFP = FF_PAD * N_DEV
FB = 1024
EPS = 1e-05
SCALE = 1.0 / math.sqrt(HEAD)
VMEM_LIMIT = 60 * 1024 * 1024
BF = jnp.bfloat16
F32 = jnp.float32

NN = (((1,), (0,)), ((), ()))
NT = (((1,), (1,)), ((), ()))
TN = (((0,), (0,)), ((), ()))


def dot(left, right, dims=NN):
    return lax.dot_general(left, right, dims, preferred_element_type=F32)


def exact(left, right, dims=NN):
    return lax.dot_general(
        left, right, dims, precision=lax.Precision.HIGHEST, preferred_element_type=F32
    )


def halves(value):
    high = value.astype(BF)
    return high, (value - high.astype(F32)).astype(BF)


def dot3(left, right, dims=NN):
    lh, ll = left
    rh, rl = right
    return dot(lh, rh, dims) + (dot(lh, rl, dims) + dot(ll, rh, dims))


def norm_fwd(values, gain):
    inv = lax.rsqrt(jnp.mean(values * values, axis=-1, keepdims=True) + EPS)
    return values * inv * gain, inv


def norm_bwd(grad, values, inv, gain):
    scaled = grad * gain
    return inv * (scaled - values * (inv * inv * jnp.mean(values * scaled, axis=-1, keepdims=True)))


def decay_kernel(split_ref, dec_ref, dect_ref, wf_ref, lw_ref):
    rows = lax.broadcasted_iota(jnp.int32, (GROUP, GROUP), 0)
    cols = lax.broadcasted_iota(jnp.int32, (GROUP, GROUP), 1)
    lower = (rows >= cols) & ((rows >= SPAN) == (cols >= SPAN))
    tri = lower.astype(F32)
    second = rows >= SPAN
    for g in range(MB):
        keep = 1.0 - split_ref[g]
        here = dec_ref[g * GROUP : (g + 1) * GROUP, :]
        here_t = dect_ref[:, g * GROUP : (g + 1) * GROUP]
        run = exact(tri, jnp.log(here[:, : 2 * H]))
        run_t = exact(jnp.log(here_t[: 2 * H, :]), tri, NT)
        for h in range(H):
            gap = run[:, h : h + 1] - run_t[h : h + 1, :]
            retain = jnp.exp(jnp.where(lower, gap, -1e30))
            gap = run[:, H + h : H + h + 1] - run_t[H + h : H + h + 1, :]
            moment = jnp.exp(jnp.where(lower, gap, -1e30))
            pairs = exact(retain, moment)
            theta = here_t[2 * H + h : 2 * H + h + 1, :]
            moment_run = jnp.exp(run_t[H + h : H + h + 1, :])
            carry = jnp.sum(retain * moment_run, axis=1, keepdims=True)
            last_weight = pairs[SPAN - 1 : SPAN, :] * theta * keep
            last_moment = moment[SPAN - 1 : SPAN, :] * theta * keep
            across = jnp.exp(run[:, h : h + 1]) * last_weight + carry * last_moment
            wf_ref[h, g] = pairs * theta + jnp.where(second, across, 0.0)
            lw_ref[h, g] = jnp.broadcast_to(last_weight, (8, GROUP))


def allowed_mask(split_ref):
    rows = lax.broadcasted_iota(jnp.int32, (ROWS, GROUP), 0)
    cols = lax.broadcasted_iota(jnp.int32, (ROWS, GROUP), 1)
    local = rows % GROUP
    group = rows // GROUP
    split = jnp.where(group == 0, split_ref[0], split_ref[1]) > 0.5
    return (local >= cols) & jnp.logical_not(split & (local >= SPAN) & (cols < SPAN))


def by_group(make):
    return jnp.concatenate([make(slice(0, GROUP), 0), make(slice(GROUP, ROWS), 1)], axis=0)


def attend(q, k, v, pk, pv, allowed):
    near = by_group(lambda s, g: dot(q[s], k[s], NT))
    far = dot(q, pk, NT) * SCALE
    near = jnp.where(allowed, near * SCALE, -1000000000.0)
    top = jnp.maximum(
        jnp.max(near, axis=-1, keepdims=True), jnp.max(far, axis=-1, keepdims=True)
    )
    near = jnp.exp(near - top)
    far = jnp.exp(far - top)
    inv = 1.0 / (jnp.sum(near, axis=-1, keepdims=True) + jnp.sum(far, axis=-1, keepdims=True))
    near = near * inv
    far = far * inv
    return near, far


def attend_out(near_half, far_half, v, pv):
    return by_group(lambda s, g: dot(near_half[s], v[s])) + dot(far_half, pv)


def unit(values):
    inv = lax.rsqrt(jnp.mean(values * values, axis=-1, keepdims=True) + EPS)
    return values * (inv * SCALE), inv


def unit_bwd(grad, values, inv):
    return (inv * SCALE) * (
        grad - values * (inv * inv * jnp.mean(values * grad, axis=-1, keepdims=True))
    )


def plain(value):
    return (value.astype(BF),)


def dot1(left, right, dims=NN):
    return dot(left[0], right[0], dims)


def memory_terms(kn, qn, mv, wf_ref, lw_ref, halves=halves, dot3=dot3):
    second = lax.broadcasted_iota(jnp.int32, (GROUP, GROUP), 0) >= SPAN
    kept = []
    for g in range(MB):
        s = slice(g * GROUP, (g + 1) * GROUP)
        kh, qh = halves(kn[s]), halves(qn[s])
        wf = wf_ref[0, g]
        lw = jnp.where(second, lw_ref[0, g][0:1, :], 0.0)
        kk = dot3(kh, kh, NT) * lw
        qk = dot3(qh, kh, NT) * wf
        kk_half = halves(kk)
        mvh = halves(mv[s])
        err = mv[s] - dot3(kk_half, mvh)
        errh = halves(err)
        qk_half = halves(qk)
        kept.append((kh, qh, wf, lw, kk_half, qk_half, mvh, errh))
    return kept


def memory_out(kept, dot3=dot3):
    return jnp.concatenate([dot3(item[5], item[7]) for item in kept], axis=0)


def memory_bwd(kept, grad, halves=plain, dot3=dot1):
    grads_k, grads_q, grads_v = [], [], []
    for g in range(MB):
        kh, qh, wf, lw, kk_half, qk_half, mvh, errh = kept[g]
        gh = halves(grad[g * GROUP : (g + 1) * GROUP])
        d_qk = dot3(gh, errh, NT) * wf
        d_err = dot3(qk_half, gh, TN)
        deh = halves(d_err)
        d_v = d_err - dot3(kk_half, deh, TN)
        d_kk = dot3(deh, mvh, NT) * lw
        dqh = halves(d_qk)
        dkh = halves(d_kk)
        grads_q.append(dot3(dqh, kh))
        grads_k.append(dot3(dqh, qh, TN) - (dot3(dkh, kh) + dot3(dkh, kh, TN)))
        grads_v.append(d_v)
    return (
        jnp.concatenate(grads_k, axis=0),
        jnp.concatenate(grads_q, axis=0),
        jnp.concatenate(grads_v, axis=0),
    )


AXES = ("x", "z", "y")
MESH = pl.DeviceIdType.MESH


def position():
    me = lax.axis_index("fsdp")
    chip = me // 2
    return me % 2, (chip // 16, (chip // 4) % 4, chip % 4)


def device(core, spot):
    return (((spot[0] * 4 + spot[1]) * 4 + spot[2]) * 2 + core,)


def moved(spot, axis, by):
    return tuple((v + by + 4) % 4 if i == axis else v for i, v in enumerate(spot))


def cut(lanes, count):
    base, extra = divmod(lanes, count)
    runs, at = [], 0
    for i in range(count):
        size = base + (1 if i < extra else 0)
        runs.append((at * 128, size * 128))
        at += size
    return runs


def neighbours(core, spot):
    found = {}
    for axis in range(3):
        for by in (1, 2, 3):
            there = moved(spot, axis, by)
            found[axis, by] = (there, device(core, there))
    return found


class Sends:
    def __init__(self, send_sem, recv_sem):
        self.send_sem, self.recv_sem = send_sem, recv_sem
        self.slots, self.open = {}, []

    def copy(self, name, src, dst, target):
        slot = self.slots.setdefault(name, len(self.slots))
        return pltpu.make_async_remote_copy(
            src_ref=src, dst_ref=dst, send_sem=self.send_sem.at[slot], recv_sem=self.recv_sem.at[slot],
            device_id=target, device_id_type=MESH,
        )

    def start(self, name, make):
        self.copy(name, *make()).start()
        self.open.append((name, make))

    def arrived(self, name, ref, target):
        self.copy(name, ref, ref, target).wait_recv()

    def drain(self):
        for name, make in self.open:
            self.copy(name, *make()).wait_send()
        self.open = []


def greet(targets):
    barrier = pltpu.get_barrier_semaphore()
    for target in targets:
        pl.semaphore_signal(barrier, inc=1, device_id=target, device_id_type=MESH)
    pl.semaphore_wait(barrier, len(targets))


class Gather:
    def __init__(self, sends, outs, widths):
        self.sends, self.outs = sends, outs
        self.core, self.spot = position()
        self.other = 1 - self.core
        self.sibling = device(1 - self.core, self.spot)
        self.near = neighbours(self.core, self.spot)
        self.jobs = [
            [(i, part, cols) for part, cols in enumerate(cut(width // 128, 3))] for i, width in enumerate(widths)
        ]
        self.forwards = [[] for _ in widths]

    def peers(self):
        return [self.sibling] + [self.near[a, by][1] for a in range(3) for by in (1, 3)]

    def block(self, i, whole_axes, at, cols, half=None):
        index = [pl.ds(0, 4) if a in whole_axes else pl.ds(at[a], 1) for a in range(3)]
        half = self.core if half is None else half
        return self.outs[i].at[half, index[0], index[1], index[2], :, pl.ds(cols[0], cols[1])]

    def push(self, name, target, *where):
        def make():
            ref = self.block(*where)
            return ref, ref, target

        self.sends.start(name, make)

    def forward(self, name, *where):
        self.push(name, self.sibling, *where)
        self.forwards[where[0]].append((name, where))

    def plan(self, item, phase):
        for i, part, cols in self.jobs[item]:
            axis = (part + phase) % 3
            done = [(part + p) % 3 for p in range(phase)]
            sides = [self.near[axis, by] for by in (1, 3, 2)]
            halves_of = [(cols[0] + at, size) for at, size in cut(cols[1] // 128, 2)]
            yield i, part, cols, done, sides, halves_of

    def begin(self, item, phase):
        for i, part, cols, done, (right, left, _), two in self.plan(item, phase):
            for step, (a, b) in enumerate(((0, 1), (1, 0))):
                self.push((i, part, phase, "r", step), right[1], i, done, self.spot, two[a])
                self.push((i, part, phase, "l", step), left[1], i, done, self.spot, two[b])
            if phase == 2:
                self.forward((i, part, "f"), i, done, self.spot, cols)

    def relay(self, item, phase):
        for i, part, cols, done, (right, left, _), two in self.plan(item, phase):
            for side, source, target, cc in (("r", left, right, two[0]), ("l", right, left, two[1])):
                where = (i, done, source[0], cc)
                self.sends.arrived((i, part, phase, side, 0), self.block(*where), source[1])
                self.push((i, part, phase, side, 2), target[1], *where)
                if phase == 2:
                    self.forward((i, part, "f", side, 0), *where)

    def finish(self, item, phase):
        for i, part, cols, done, (right, left, far), two in self.plan(item, phase):
            for side, step, at, cc, source in (
                ("r", 1, left, two[1], left),
                ("l", 1, right, two[0], right),
                ("r", 2, far, two[0], left),
                ("l", 2, far, two[1], right),
            ):
                where = (i, done, at[0], cc)
                self.sends.arrived((i, part, phase, side, step), self.block(*where), source[1])
                if phase == 2:
                    self.forward((i, part, "f", side, step), *where)

    def received(self, item):
        for name, (i, done, at, cc) in self.forwards[item]:
            self.sends.arrived(name, self.block(i, done, at, cc, self.other), self.sibling)


class Exchange:
    def __init__(self, sends, key, bufs, lanes, jobs):
        self.sends, self.key, self.bufs, self.lanes, self.jobs = sends, key, bufs, lanes, jobs
        self.core, self.spot = position()
        self.other = 1 - self.core
        self.mine, self.theirs = (
            [pl.ds(pl.multiple_of(lane * 256 + core * 128, 128), 128) for lane in range(lanes)]
            for core in (self.core, self.other)
        )
        self.sibling = device(self.other, self.spot)
        self.near = neighbours(self.core, self.spot)

    def index(self, cols, axis=None, where=None):
        return tuple(pl.ds(where, 1) if a == axis else pl.ds(0, 4) for a in range(3)) + (slice(None), cols)

    def moves(self, stage, which):
        before, after = self.bufs[stage], self.bufs[stage + 1]
        away, stay = [], []
        if stage == 0:
            for lane in range(self.lanes):
                mine, theirs = self.index(self.mine[lane]), self.index(self.theirs[lane])
                away.append(((self.key, 0, lane), theirs, mine, self.sibling, theirs, self.sibling))
                stay.append(mine)
            return before, after, away, stay
        for number, (lo, width, first) in enumerate(self.jobs):
            if which is not None and number not in which:
                continue
            axis = (first + stage - 1) % 3
            cols = pl.ds(lo, width)
            here = self.index(cols, axis, self.spot[axis])
            for by in (2, 1, 3):
                there, target = self.near[axis, by]
                behind, source = self.near[axis, 4 - by]
                away.append(
                    (
                        (self.key, stage, number, by),
                        self.index(cols, axis, there[axis]),
                        here,
                        target,
                        self.index(cols, axis, behind[axis]),
                        source,
                    )
                )
            stay.append(here)
        return before, after, away, stay

    def launch(self, stage, which=None):
        before, after, away, stay = self.moves(stage, which)
        for name, src, dst, target, _, _ in away:
            self.sends.start(name, lambda src=src, dst=dst, target=target: (before.at[src], after.at[dst], target))
        for here in stay:
            after[here] = before[here]

    def land(self, stage, which=None):
        _, after, away, _ = self.moves(stage, which)
        for name, _, _, _, landing, source in away:
            self.sends.arrived(name, after.at[landing], source)

    def fill(self, lane, scratch, values):
        row = 0
        for value in values:
            for j in range(value.shape[1] // 128):
                scratch[pl.ds(row, N_DEV, stride=16), :] = value[:, j * 128 : (j + 1) * 128].astype(F32)
                row += 1
        blocks = scratch[...].reshape(4, 4, 4, 2, 16, 128)
        for core in range(2):
            at = lane * 256 + core * 128
            self.bufs[0][:, :, :, :, at : at + 128] = blocks[:, :, :, core].astype(BF)


BY_CORE = [(0, 128, 0), (128, 128, 1)]


WALL = 768
TOKEN_ROWS = 48
WIDTHS = (4 * HCOLS + 7 * AR, D + FB + WALL, FB + WALL, FB + WALL)
FSTEPS = H
BLOCKS = FFP // FB


def forward_kernel(
    split_ref, got_ref, gain1_ref, gain2_ref, mask_ref, place_ref, pers_ref,
    mine0, mine1, mine2, mine3,
    g0_ref, g1_ref, g2_ref, g3_ref, proj_ref, x_ref, h1_ref, lat_ref, wf_ref, lw_ref, back_ref, dz_ref, dmid_ref,
    grads_ref,
    flat, d_ref, dec_ref, dect_ref, inc0, inc1, inc2, inc3, stage0, stage1, stage2, stage3,
    w_buf, up_buf, down_buf, z_ref, wup_buf, wd_buf, lead_buf,
    x2_ref, h2_ref, inv_ref, lat_out_ref, lat_up_ref, dl_down_ref, acc_ref, lat_acc_ref, dh_ref, dlat_ref,
    send_sem, recv_sem, local_sem, w_sem, j_sem,
):
    step = pl.program_id(0)
    mine, inc = (mine0, mine1, mine2, mine3), (inc0, inc1, inc2, inc3)
    stage, outs = (stage0, stage1, stage2, stage3), (g0_ref, g1_ref, g2_ref, g3_ref)
    sends = Sends(send_sem, recv_sem)
    ring = Gather(sends, outs, WIDTHS)
    core, spot = ring.core, ring.spot
    other = 1 - core
    items = range(4)

    def head_loads(h, slot):
        half, place = h // 4, pl.multiple_of((h % 4) * HCOLS, 128)
        return (
            pltpu.make_async_copy(
                g0_ref.at[half, :, :, :, :, pl.ds(place, HCOLS)], w_buf.at[slot], w_sem.at[slot, 0]
            ),
            pltpu.make_async_copy(
                g0_ref.at[1, h // 2, pl.ds(2 * (h % 2), 2), :, :, pl.ds(4 * HCOLS, HCOLS)],
                up_buf.at[slot],
                w_sem.at[slot, 1],
            ),
        )

    def down_load():
        return pltpu.make_async_copy(
            g0_ref.at[0, :, :, :, :, pl.ds(4 * HCOLS, HCOLS)], down_buf, local_sem.at[0]
        )

    def lead_load():
        return pltpu.make_async_copy(g1_ref.at[:, :, :, :, :, pl.ds(0, D)], lead_buf, local_sem.at[0])

    def up_load(k):
        at = D if k == 0 else 0
        return pltpu.make_async_copy(
            outs[k + 1].at[:, :, :, :, :, pl.ds(at, FB)], wup_buf.at[k % 2], j_sem.at[k % 2, 0]
        )

    def wall_load(k):
        at = D + FB if k == 0 else FB
        return pltpu.make_async_copy(
            outs[k + 1].at[:, :, :, :, :, pl.ds(at, WALL)], wd_buf.at[k % 2], j_sem.at[k % 2, 1]
        )

    @pl.when(step == 0)
    def _():
        greet([ring.sibling] + [there[1] for there in ring.near.values()])
        for i in items:
            sends.start(("pair", i), lambda i=i: (mine[i].at[other], inc[i], ring.sibling))
        own_copy = lambda i: pltpu.make_async_copy(
            stage[i], outs[i].at[core, spot[0], spot[1], spot[2]], local_sem.at[i]
        )
        for i in items:
            sends.arrived(("pair", i), inc[i], ring.sibling)
            own, theirs = mine[i][core], inc[i][...]
            first = jnp.where(core == 0, own, theirs)
            last = jnp.where(core == 0, theirs, own)
            stage[i][...] = jnp.concatenate([first, last], axis=0).astype(BF)
            own_copy(i).start()
        for i in items:
            own_copy(i).wait()
            ring.begin(i, 0)
        flat[...] = got_ref[...].astype(F32).reshape(N_DEV * TOKEN_ROWS, 128)

        def columns(first, count):
            return jnp.concatenate(
                [flat[pl.ds(first + c, N_DEV, stride=TOKEN_ROWS), :].astype(BF) for c in range(count)], axis=1
            )

        for i in items:
            ring.relay(i, 0)
        for i in items:
            ring.finish(i, 0)
            ring.begin(i, 1)
        for i in items:
            ring.relay(i, 1)
        ring.finish(0, 1)
        ring.begin(0, 2)
        for i in items[1:]:
            ring.finish(i, 1)
        rates = columns(4 * D // 128, 1)
        for m in range(MB):
            s = slice(m * GROUP, (m + 1) * GROUP)
            x_ref[s, :] = dot(place_ref[m], columns(m * D // 128, D // 128), TN).astype(BF)
            d_ref[s, :] = dot(place_ref[m], columns((MB + m) * D // 128, D // 128), TN).astype(BF)
            sent = rates[:, m * 3 * H : (m + 1) * 3 * H]
            dec_ref[s, :] = dot(place_ref[m], sent, TN)
            dect_ref[:, s] = dot(sent, place_ref[m], TN)
        decay_kernel(split_ref, dec_ref, dect_ref, wf_ref, lw_ref)
        normed, _ = norm_fwd(x_ref[...].astype(F32), gain1_ref[...])
        h1_ref[...] = normed.astype(BF)
        ring.relay(0, 2)
        ring.begin(1, 2)
        ring.finish(0, 2)
        ring.received(0)
        for copy in head_loads(0, 0):
            copy.start()
        down_load().start()
        down_load().wait()
        latent = dot(h1_ref[...], down_buf[...].reshape(D, HCOLS))
        mask = mask_ref[...]
        for part in range(7):
            s = slice(part * AR, (part + 1) * AR)
            lat_ref[:, s] = (latent[:, s] * mask).astype(BF)

    @pl.when(step == 3)
    def _():
        ring.relay(1, 2)
        ring.begin(2, 2)

    @pl.when(step == FSTEPS - 1)
    def _():
        ring.finish(1, 2)
        ring.received(1)
        for copy in (lead_load(), up_load(0), wall_load(0)):
            copy.start()
        ring.relay(2, 2)
        ring.begin(3, 2)

    @pl.when(step < FSTEPS)
    def _():
        slot = step % 2
        for copy in head_loads(step, slot):
            copy.wait()

        @pl.when(step + 1 < FSTEPS)
        def _():
            for copy in head_loads(step + 1, 1 - slot):
                copy.start()

        base = dot(h1_ref[...], w_buf[slot].reshape(D, HCOLS))
        up = up_buf[slot].reshape(HEAD, HCOLS)
        pieces = []
        for part in range(7):
            s = slice(part * AR, (part + 1) * AR)
            piece = base[:, part * HEAD : (part + 1) * HEAD] + dot(lat_ref[:, s], up[:, s], NT)
            proj_ref[:, part * HEAD : (part + 1) * HEAD] = piece
            pieces.append(piece)
        q, k, v = (pieces[i].astype(BF) for i in range(3))
        pk, pv = pers_ref[0, :, pl.ds(pl.multiple_of(step * HEAD, HEAD), HEAD)], pers_ref[
            1, :, pl.ds(pl.multiple_of(step * HEAD, HEAD), HEAD)
        ]
        near, far = attend(q, k, v, pk, pv, allowed_mask(split_ref))
        att = attend_out(near.astype(BF), far.astype(BF), v, pv)
        kn, _ = unit(pieces[3])
        qn, _ = unit(pieces[5])
        here = pl.ds(step, 1)
        mem = memory_out(memory_terms(kn, qn, pieces[4], wf_ref.at[here], lw_ref.at[here]))
        z_ref[:, pl.ds(pl.multiple_of(step * HEAD, HEAD), HEAD)] = (
            att + jax.nn.sigmoid(pieces[6]) * mem
        ).astype(BF)

    lead = lambda half, lo, hi: lead_buf[half, :, :, :, :, lo:hi].reshape(D, hi - lo)
    out_down = lambda: lead(0, 0, 128)
    up_down = lambda: lead(0, 128, 384)
    out_up = lambda: lead(0, 384, 512)
    down_up = lambda: lead(0, 512, 640)
    w_out = lambda: lead(1, 0, D)

    @pl.when(step == FSTEPS)
    def _():
        lead_load().wait()
        mask = mask_ref[...]
        z = z_ref[...]
        lat_out_ref[...] = (dot(z, out_down()) * mask).astype(BF)
        x2 = x_ref[...].astype(F32) + (dot(z, w_out()) + dot(lat_out_ref[...], out_up(), NT))
        x2_ref[...] = x2
        normed, inv = norm_fwd(x2, gain2_ref[...])
        inv_ref[...] = jnp.broadcast_to(inv, inv_ref.shape)
        h2_ref[...] = normed.astype(BF)
        latent = dot(h2_ref[...], up_down())
        lat_up_ref[:, :AR] = (latent[:, :AR] * mask).astype(BF)
        lat_up_ref[:, AR:] = (latent[:, AR:] * mask).astype(BF)
        dl_down_ref[...] = (dot(d_ref[...], down_up()) * mask).astype(BF)
        for ref in (acc_ref, lat_acc_ref, dh_ref, dlat_ref):
            ref[...] = jnp.zeros_like(ref)

    @pl.when(step == FSTEPS)
    def _():
        ring.finish(2, 2)
        ring.received(2)
        up_load(1).start()
        wall_load(1).start()

    @pl.when(step >= FSTEPS)
    def _():
        k = step - FSTEPS
        slot = k % 2
        h2 = h2_ref[...]
        d = d_ref[...]
        lat0, lat1 = lat_up_ref[:, :AR], lat_up_ref[:, AR:]
        wall = lambda half, lo, hi: wd_buf[slot, half, :, :, :, :, lo:hi].reshape(FB, hi - lo)
        pltpu.make_async_copy(wup_buf.at[slot], wup_buf.at[slot], j_sem.at[slot, 0]).wait()
        pltpu.make_async_copy(wd_buf.at[slot], wd_buf.at[slot], j_sem.at[slot, 1]).wait()
        w_gate, w_lift = (wup_buf[slot, half].reshape(D, FB) for half in range(2))
        wda, wdb = wall(0, 0, 768), wall(1, 0, 256)
        uu0, uu1, dd = wall(1, 256, 384), wall(1, 384, 512), wall(1, 512, 640)
        gate = dot(h2, w_gate) + dot(lat0, uu0, NT)
        lift = dot(h2, w_lift) + dot(lat1, uu1, NT)
        sig = jax.nn.sigmoid(gate)
        silu = gate * sig
        act = (silu * lift).astype(BF)
        d_act = dot(d[:, :768], wda, NT) + dot(d[:, 768:], wdb, NT) + dot(dl_down_ref[...], dd, NT)
        d_gate = (d_act * lift * (sig * (1.0 + gate * (1.0 - sig)))).astype(BF)
        d_lift = (d_act * silu).astype(BF)
        acc_ref[:, :768] += dot(act, wda)
        acc_ref[:, 768:] += dot(act, wdb)
        lat_acc_ref[...] += dot(act, dd)
        dh_ref[...] += dot(d_gate, w_gate, NT) + dot(d_lift, w_lift, NT)
        dlat_ref[:, :AR] += dot(d_gate, uu0)
        dlat_ref[:, AR:] += dot(d_lift, uu1)
        for half, at, term in (
            (0, k * 256, dot(d_gate, lat0, TN)),
            (0, k * 256 + AR, dot(d_lift, lat1, TN)),
            (1, k * AR, dot(act, dl_down_ref[...], TN)),
        ):
            at = pl.ds(pl.multiple_of(at, AR), AR)
            grads_ref[half, :, :, at] = term.reshape(64, 16, AR).astype(BF)

        @pl.when(k == 0)
        def _():
            ring.relay(3, 2)

        @pl.when(k == 1)
        def _():
            ring.finish(3, 2)
            ring.received(3)
            up_load(2).start()
            wall_load(2).start()

    @pl.when(step == FSTEPS + BLOCKS - 1)
    def _():
        mask = mask_ref[...]
        lat_down = (lat_acc_ref[...] * mask).astype(BF)
        out = (x2_ref[...] + acc_ref[...] + dot(lat_down, down_up(), NT)).astype(BF)
        for m in range(MB):
            s = slice(m * GROUP, (m + 1) * GROUP)
            back_ref[:, m * D : (m + 1) * D] = dot(place_ref[m], out[s]).astype(BF)
        d = d_ref[...]
        h2 = h2_ref[...]
        z = z_ref[...]

        def put(half, at, value):
            grads_ref[half, :, :, at : at + AR] = value.reshape(64, 16, AR).astype(BF)

        put(0, 768, dot(d, lat_down, TN))
        dlu0 = (dlat_ref[:, :AR] * mask).astype(BF)
        dlu1 = (dlat_ref[:, AR:] * mask).astype(BF)
        put(1, 640, dot(h2, dlu0, TN))
        put(1, 768, dot(h2, dlu1, TN))
        ud = up_down()
        dh = dh_ref[...] + (dot(dlu0, ud[:, :AR], NT) + dot(dlu1, ud[:, AR:], NT))
        dmid = d.astype(F32) + norm_bwd(dh, x2_ref[...], inv_ref[:, :1], gain2_ref[...])
        dmid_ref[...] = dmid
        dmb = dmid.astype(BF)
        dlo = (dot(dmb, out_up()) * mask).astype(BF)
        put(1, 384, dot(z, dlo, TN))
        put(1, 512, dot(dmb, lat_out_ref[...], TN))
        dz_ref[...] = (dot(dmb, w_out(), NT) + dot(dlo, out_down(), NT)).astype(BF)
        sends.drain()


def forward_call(split, got, gain1, gain2, mask, place, persistent, mine):
    once = pl.Buffered(1)
    whole = lambda *shape: pl.BlockSpec(shape, lambda s: (0,) * len(shape), pipeline_mode=once)
    hbm = pl.BlockSpec(memory_space=pl.ANY)
    slots = 4 * (1 + 3 * (3 * 6 + 7))
    return pl.pallas_call(
        forward_kernel,
        grid=(FSTEPS + BLOCKS,),
        out_shape=tuple(jax.ShapeDtypeStruct((2, 4, 4, 4, 16, width), BF) for width in WIDTHS)
        + (
            jax.ShapeDtypeStruct((ROWS, 7 * D), F32),
            jax.ShapeDtypeStruct((ROWS, D), BF),
            jax.ShapeDtypeStruct((ROWS, D), BF),
            jax.ShapeDtypeStruct((ROWS, 7 * AR), BF),
            jax.ShapeDtypeStruct((H, MB, GROUP, GROUP), F32),
            jax.ShapeDtypeStruct((H, MB, 8, GROUP), F32),
            jax.ShapeDtypeStruct((GROUP, MB * D), BF),
            jax.ShapeDtypeStruct((ROWS, D), BF),
            jax.ShapeDtypeStruct((ROWS, D), F32),
            jax.ShapeDtypeStruct((2, 64, 16, 896), BF),
        ),
        in_specs=[
            pl.BlockSpec(memory_space=pltpu.SMEM),
            whole(N_DEV, TOKEN_ROWS, 128),
            whole(1, D),
            whole(1, D),
            whole(ROWS, AR),
            whole(MB, GROUP, GROUP),
            whole(2, NP, D),
        ]
        + [whole(2, 8, width) for width in WIDTHS],
        out_specs=(hbm,) * 4
        + (
            pl.BlockSpec((ROWS, HCOLS), lambda s: (0, jnp.minimum(s, FSTEPS - 1))),
            whole(ROWS, D),
            whole(ROWS, D),
            whole(ROWS, 7 * AR),
            whole(H, MB, GROUP, GROUP),
            whole(H, MB, 8, GROUP),
            whole(GROUP, MB * D),
            whole(ROWS, D),
            whole(ROWS, D),
            whole(2, 64, 16, 896),
        ),
        scratch_shapes=[
            pltpu.VMEM((N_DEV * TOKEN_ROWS, 128), F32),
            pltpu.VMEM((ROWS, D), BF),
            pltpu.VMEM((ROWS, 3 * H), F32),
            pltpu.VMEM((3 * H, ROWS), F32),
        ]
        + [pltpu.VMEM((8, width), F32) for width in WIDTHS]
        + [pltpu.VMEM((16, width), BF) for width in WIDTHS]
        + [
            pltpu.VMEM((2, 4, 4, 4, 16, HCOLS), BF),
            pltpu.VMEM((2, 2, 4, 16, HCOLS), BF),
            pltpu.VMEM((4, 4, 4, 16, HCOLS), BF),
            pltpu.VMEM((ROWS, D), BF),
            pltpu.VMEM((2, 2, 4, 4, 4, 16, FB), BF),
            pltpu.VMEM((2, 2, 4, 4, 4, 16, WALL), BF),
            pltpu.VMEM((2, 4, 4, 4, 16, D), BF),
            pltpu.VMEM((ROWS, D), F32),
            pltpu.VMEM((ROWS, D), BF),
            pltpu.VMEM((ROWS, 128), F32),
            pltpu.VMEM((ROWS, AR), BF),
            pltpu.VMEM((ROWS, 2 * AR), BF),
            pltpu.VMEM((ROWS, AR), BF),
            pltpu.VMEM((ROWS, D), F32),
            pltpu.VMEM((ROWS, AR), F32),
            pltpu.VMEM((ROWS, D), F32),
            pltpu.VMEM((ROWS, 2 * AR), F32),
            pltpu.SemaphoreType.DMA((slots,)),
            pltpu.SemaphoreType.DMA((slots,)),
            pltpu.SemaphoreType.DMA((4,)),
            pltpu.SemaphoreType.DMA((2, 2)),
            pltpu.SemaphoreType.DMA((2, 2)),
        ],
        compiler_params=pltpu.CompilerParams(
            collective_id=0, has_side_effects=True, vmem_limit_bytes=VMEM_LIMIT
        ),
        name="gather_forward",
    )(split, got, gain1, gain2, mask, place, persistent, *mine)


class Scatter:
    def __init__(self, sends, key, grads, out, inc0, total, inc1, inc2, inc3, t1, t2):
        self.sends, self.key, self.grads, self.out = sends, key, grads, out
        self.inc0, self.total, self.inc = inc0, total, (None, inc1, inc2, inc3)
        self.t1, self.t2 = t1, t2
        self.core, self.spot = position()
        self.other = 1 - self.core
        self.sibling = device(1 - self.core, self.spot)
        self.near = neighbours(self.core, self.spot)
        self.parts = [(part, pl.ds(*cols)) for part, cols in enumerate(cut(7, 3))]

    def peers(self):
        return [self.sibling] + [there[1] for there in self.near.values()]

    def pair(self):
        for x in range(4):
            self.sends.start(
                (self.key, "pair", x),
                lambda x=x: (
                    self.grads.at[self.other, pl.ds(16 * x, 16)],
                    self.inc0.at[x],
                    self.sibling,
                ),
            )

    def source(self, phase, part, at):
        axis = (part + phase - 1) % 3
        cs = self.parts[part][1]
        if phase == 1:
            index = tuple(at if a == axis else slice(None) for a in range(3))
            return self.total, index + (slice(None), cs)
        rest = [a for a in range(3) if a != part]
        if phase == 2:
            index = (at, slice(None)) if rest[0] == axis else (slice(None), at)
            return self.t1, index + (slice(None), cs)
        return self.t2, (at, slice(None), cs)

    def landing(self, phase, part, k):
        return (k,) + (slice(None),) * (4 - phase) + (self.parts[part][1],)

    def send(self, phase):
        for part, _ in self.parts:
            axis = (part + phase - 1) % 3
            for k, by in enumerate((2, 1, 3)):
                to = self.near[axis, by]

                def make(part=part, axis=axis, to=to, k=k):
                    ref, index = self.source(phase, part, to[0][axis])
                    return ref.at[index], self.inc[phase].at[self.landing(phase, part, k)], to[1]

                self.sends.start((self.key, part, phase, by), make)

    def add(self, phase):
        for part, cs in self.parts:
            axis = (part + phase - 1) % 3
            ref, index = self.source(phase, part, self.spot[axis])
            acc = ref[index].astype(F32)
            for k, by in enumerate((2, 1, 3)):
                here = self.landing(phase, part, k)
                source = self.near[axis, 4 - by][1]
                self.sends.arrived((self.key, part, phase, by), self.inc[phase].at[here], source)
                acc = acc + self.inc[phase][here].astype(F32)
            if phase == 1:
                self.t1[:, :, :, cs] = acc.astype(BF)
            elif phase == 2:
                self.t2[:, :, cs] = acc.astype(BF)
            else:
                self.out[self.core, :, cs] = acc

    def add_pair(self):
        for x in range(4):
            self.sends.arrived((self.key, "pair", x), self.inc0.at[x], self.sibling)
            both = self.grads[self.core, pl.ds(16 * x, 16)].astype(F32) + self.inc0[x].astype(F32)
            self.total[x] = both.reshape(4, 4, 16, 896).astype(BF)

    def swap(self):
        self.sends.start(
            (self.key, "last"), lambda: (self.out.at[self.core], self.out.at[self.core], self.sibling)
        )

    def swapped(self):
        self.sends.arrived((self.key, "last"), self.out.at[self.other], self.sibling)


def backward_kernel(
    split_ref, x_ref, gain_ref, mask_ref, place_ref, proj_ref, dz_ref, dmid_ref, h1_ref, lat_ref,
    w_ref, down_ref, up_ref, pers_ref, wf_ref, lw_ref, ffn_ref, back_ref,
    act_out, grad_out, ffn_out, heads_out,
    dh_ref, dlat_ref, dlat_half, dy_ref, grads_ref, *rest,
):
    step = pl.program_id(0)
    send_sem, recv_sem = rest[-2:]
    sends = Sends(send_sem, recv_sem)
    first_sums = Scatter(sends, 0, ffn_ref, *rest[:8])
    last_sums = Scatter(sends, 1, grads_ref, *rest[8:16])
    flat = rest[26]
    ex_act = Exchange(sends, "a", rest[16:21], 1, BY_CORE)
    ex_grad = Exchange(sends, "g", rest[21:26], 1, BY_CORE)

    def one_head():
        pieces = [proj_ref[:, p * HEAD : (p + 1) * HEAD] for p in range(7)]
        q, k, v = (pieces[i].astype(BF) for i in range(3))
        pk, pv = pers_ref[0], pers_ref[1]
        near, far = attend(q, k, v, pk, pv, allowed_mask(split_ref))
        near_half = near.astype(BF)
        dz = dz_ref[...]
        d_near = by_group(lambda s, g: dot(dz[s], v[s], NT))
        d_far = dot(dz, pv, NT)
        d_v = by_group(lambda s, g: dot(near_half[s], dz[s], TN))
        total = jnp.sum(d_near * near, axis=-1, keepdims=True) + jnp.sum(
            d_far * far, axis=-1, keepdims=True
        )
        ds_near = (near * (d_near - total) * SCALE).astype(BF)
        ds_far = (far * (d_far - total) * SCALE).astype(BF)
        d_q = by_group(lambda s, g: dot(ds_near[s], k[s])) + dot(ds_far, pk)
        d_k = by_group(lambda s, g: dot(ds_near[s], q[s], TN))

        dzf = dz.astype(F32)
        opening = jax.nn.sigmoid(pieces[6])
        kn, k_inv = unit(pieces[3])
        qn, q_inv = unit(pieces[5])
        kept = memory_terms(kn, qn, pieces[4], wf_ref, lw_ref, plain, dot1)
        mem = memory_out(kept, dot1)
        d_open = dzf * mem * (opening * (1.0 - opening))
        d_kn, d_qn, d_mv = memory_bwd(kept, dzf * opening)
        d_mk = unit_bwd(d_kn, pieces[3], k_inv)
        d_mq = unit_bwd(d_qn, pieces[5], q_inv)
        dy = [item.astype(BF) for item in (d_q, d_k, d_v, d_mk, d_mv, d_mq, d_open)]
        dy_ref[step] = jnp.concatenate(dy, axis=1)
        first = pl.multiple_of(step * 8, 8)
        for part in range(7):
            s = slice(part * AR, (part + 1) * AR)
            dlat_ref[:, s] += dot(dy[part], up_ref[0, :, s])
            grads_ref[1, pl.ds(first, 8), :, s] = (
                dot(dy[part], lat_ref[:, s], TN).reshape(8, 16, AR).astype(BF)
            )

    @pl.when(step == 0)
    def _():
        greet(first_sums.peers())
        ex_act.fill(0, flat, [back_ref[...]])
        ex_act.launch(0)
        first_sums.pair()
        dlat_ref[...] = jnp.zeros_like(dlat_ref)

    @pl.when(step == 1)
    def _():
        ex_act.land(0)
        ex_act.launch(1)

    @pl.when(step == 2)
    def _():
        first_sums.add_pair()
        first_sums.send(1)

    @pl.when(step == 3)
    def _():
        ex_act.land(1)
        ex_act.launch(2)

    @pl.when(step == 5)
    def _():
        first_sums.add(1)
        first_sums.send(2)
        ex_act.land(2)
        ex_act.launch(3)

    @pl.when(step == 6)
    def _():
        first_sums.add(2)
        first_sums.send(3)

    @pl.when(step == 7)
    def _():
        first_sums.add(3)
        first_sums.swap()
        ex_act.land(3)
        act_out[...] = ex_act.bufs[4][...]

    @pl.when(step < H)
    def _():
        one_head()

    @pl.when(step == H)
    def _():
        mask = mask_ref[...]
        for p in range(7):
            s = slice(p * AR, (p + 1) * AR)
            dlat_half[:, s] = (dlat_ref[:, s] * mask).astype(BF)
        grads_ref[0] = dot(h1_ref[...], dlat_half[...], TN).reshape(64, 16, 7 * AR).astype(BF)
        last_sums.pair()
        dh_ref[...] = dot(dlat_half[...], down_ref[0], NT)

    @pl.when(step == H + 2)
    def _():
        last_sums.add_pair()
        last_sums.send(1)

    @pl.when(step >= H)
    def _():
        dh_ref[...] += dot(dy_ref[step - H], w_ref[0], NT)

    @pl.when(step == 2 * H - 1)
    def _():
        x = x_ref[...].astype(F32)
        inv = lax.rsqrt(jnp.mean(x * x, axis=-1, keepdims=True) + EPS)
        dx = (dmid_ref[...] + norm_bwd(dh_ref[...], x, inv, gain_ref[...])).astype(BF)
        ex_grad.fill(
            0, flat, [dot(place_ref[m], dx[m * GROUP : (m + 1) * GROUP]) for m in range(MB)]
        )
        ex_grad.launch(0)
        first_sums.swapped()
        ffn_out[...] = first_sums.out[...]
        ex_grad.land(0)
        ex_grad.launch(1)
        last_sums.add(1)
        last_sums.send(2)
        ex_grad.land(1)
        ex_grad.launch(2)
        last_sums.add(2)
        last_sums.send(3)
        ex_grad.land(2)
        ex_grad.launch(3)
        last_sums.add(3)
        last_sums.swap()
        ex_grad.land(3)
        grad_out[...] = ex_grad.bufs[4][...]
        last_sums.swapped()
        heads_out[...] = last_sums.out[...]
        sends.drain()


def backward_call(split, x, gain, mask, place, proj, dz, dmid, h1, lat, a1, persistent, wf, lw, grads_ffn, back):
    once = pl.Buffered(1)
    whole = lambda *shape: pl.BlockSpec(shape, lambda s: (0,) * len(shape), pipeline_mode=once)
    head = lambda s: jnp.minimum(s, H - 1)
    late = lambda s: jnp.maximum(s - H, 0)
    buffers = [
        pltpu.VMEM((2, 16, 896), F32),
        pltpu.VMEM((4, 16, 16, 896), BF),
        pltpu.VMEM((4, 4, 4, 16, 896), BF),
        pltpu.VMEM((3, 4, 4, 16, 896), BF),
        pltpu.VMEM((3, 4, 16, 896), BF),
        pltpu.VMEM((3, 16, 896), BF),
        pltpu.VMEM((4, 4, 16, 896), BF),
        pltpu.VMEM((4, 16, 896), BF),
    ]
    slots = 2 * (4 + 3 * 9 + 1) + 2 * (1 + 3 * 6)
    return pl.pallas_call(
        backward_kernel,
        grid=(2 * H,),
        out_shape=(
            jax.ShapeDtypeStruct((4, 4, 4, 16, 256), BF),
            jax.ShapeDtypeStruct((4, 4, 4, 16, 256), BF),
            jax.ShapeDtypeStruct((2, 16, 896), F32),
            jax.ShapeDtypeStruct((2, 16, 896), F32),
        ),
        in_specs=[
            pl.BlockSpec(memory_space=pltpu.SMEM),
            whole(ROWS, D),
            whole(1, D),
            whole(ROWS, AR),
            whole(MB, GROUP, GROUP),
            pl.BlockSpec((ROWS, HCOLS), lambda s: (0, head(s))),
            pl.BlockSpec((ROWS, HEAD), lambda s: (0, head(s))),
            whole(ROWS, D),
            whole(ROWS, D),
            whole(ROWS, 7 * AR),
            pl.BlockSpec((1, D, HCOLS), lambda s: (late(s) // 4, 0, late(s) % 4)),
            pl.BlockSpec((1, D, HCOLS), lambda s: (0, 0, 4), pipeline_mode=once),
            pl.BlockSpec((1, HEAD, HCOLS), lambda s: (1, head(s), 4)),
            pl.BlockSpec((2, NP, HEAD), lambda s: (0, 0, head(s))),
            pl.BlockSpec((1, MB, GROUP, GROUP), lambda s: (head(s), 0, 0, 0)),
            pl.BlockSpec((1, MB, 8, GROUP), lambda s: (head(s), 0, 0, 0)),
            pl.BlockSpec(memory_space=pltpu.VMEM),
            pl.BlockSpec(memory_space=pltpu.VMEM),
        ],
        out_specs=(
            whole(4, 4, 4, 16, 256),
            whole(4, 4, 4, 16, 256),
            pl.BlockSpec(memory_space=pltpu.VMEM),
            pl.BlockSpec(memory_space=pltpu.VMEM),
        ),
        scratch_shapes=[
            pltpu.VMEM((ROWS, D), F32),
            pltpu.VMEM((ROWS, 7 * AR), F32),
            pltpu.VMEM((ROWS, 7 * AR), BF),
            pltpu.VMEM((H, ROWS, HCOLS), BF),
            pltpu.VMEM((2, 64, 16, 896), BF),
        ]
        + buffers * 2
        + [pltpu.VMEM((4, 4, 4, 16, 256), BF)] * 10
        + [pltpu.VMEM((16 * N_DEV, 128), F32)]
        + [pltpu.SemaphoreType.DMA((slots,)), pltpu.SemaphoreType.DMA((slots,))],
        compiler_params=pltpu.CompilerParams(
            collective_id=1, has_side_effects=True, vmem_limit_bytes=VMEM_LIMIT
        ),
        name="backward_scatter",
    )(split, x, gain, mask, place, proj, dz, dmid, h1, lat, a1, a1, a1, persistent, wf, lw, grads_ffn, back)


def selector(parts):
    rows = lax.broadcasted_iota(jnp.int32, (parts * R, parts * AR), 0)
    cols = lax.broadcasted_iota(jnp.int32, (parts * R, parts * AR), 1)
    return (rows // R == cols // AR) & (rows % R == cols % R)


def adapter_of(shape):
    return (lax.broadcasted_iota(jnp.int32, shape, len(shape) - 1) % AR) // R


def pack_kernel(
    lengths_ref, ids_ref, route_ref, tok_ref, cot_ref, decays_ref,
    w_in, w_out, w_up, w_down, in_down, in_up, out_down, out_up, up_down, up_up, down_down, down_up,
    got_ref, item0, item1, item2, item3, to_ref, place_ref, mask_ref, split_ref,
    flat, wide, sent, send_sem, recv_sem, own_sem,
):
    me = lax.axis_index("fsdp")
    barrier = pltpu.get_barrier_semaphore()

    def signal(k, carry):
        pl.semaphore_signal(barrier, inc=1, device_id=((me + k) % N_DEV,), device_id_type=MESH)
        return carry

    lax.fori_loop(1, N_DEV, signal, 0)

    below = lax.broadcasted_iota(jnp.int32, (GROUP, GROUP), 0)
    along = lax.broadcasted_iota(jnp.int32, (GROUP, GROUP), 1)
    for m in range(MB):
        to = (below == route_ref[m, pl.ds(me, 1), :] // GROUP).astype(BF)
        to_ref[m] = to
        for ref, first in ((tok_ref, m * 8), (cot_ref, (MB + m) * 8)):
            value = dot(to, ref[m])
            for j in range(8):
                flat[pl.ds(first + j, N_DEV, stride=TOKEN_ROWS), :] = value[:, j * 128 : (j + 1) * 128]
    rates = [dot(to_ref[m], decays_ref[m], NT) for m in range(MB)]
    rates = jnp.concatenate(rates + [jnp.zeros((GROUP, 128 - MB * 3 * H), F32)], axis=1)
    flat[pl.ds(4 * D // 128, N_DEV, stride=TOKEN_ROWS), :] = rates
    for j in range(4 * D // 128 + 1, TOKEN_ROWS):
        flat[pl.ds(j, N_DEV, stride=TOKEN_ROWS), :] = jnp.zeros((N_DEV, 128), F32)
    sent[...] = flat[...].reshape(N_DEV, TOKEN_ROWS, 128).astype(BF)

    def copy(k):
        target = (me + k) % N_DEV
        return pltpu.make_async_remote_copy(
            src_ref=sent.at[target], dst_ref=got_ref.at[me], send_sem=send_sem.at[k], recv_sem=recv_sem.at[k],
            device_id=(target,), device_id_type=MESH,
        )

    def begin(k, carry):
        copy(k).start()
        return carry

    def end(k, carry):
        copy(k).wait()
        return carry

    pl.semaphore_wait(barrier, N_DEV - 1)
    lax.fori_loop(1, N_DEV, begin, 0)
    own = pltpu.make_async_copy(sent.at[me], got_ref.at[me], own_sem)
    own.start()
    for m in range(MB):
        blocks = route_ref[m]
        landing = jnp.sum(jnp.where(blocks // GROUP == me, blocks % GROUP, 0), axis=1, keepdims=True)
        place_ref[m] = (landing == along).astype(BF)
        early = lengths_ref[m, 0]
        row = lax.broadcasted_iota(jnp.int32, (GROUP, AR), 0)
        adapter = jnp.where(row < early, ids_ref[m, 0], ids_ref[m, 1])
        mask_ref[m * GROUP : (m + 1) * GROUP, :] = (adapter == adapter_of((GROUP, AR))).astype(F32)
        split_ref[m] = jnp.where(early < GROUP, 1.0, 0.0)

    select = selector(7).astype(BF)
    items = (item1, item2, item3)

    def ranks(ref, parts):
        cut_to = select[: parts * R, : parts * AR]
        rows = ref.shape[1]
        out = jnp.zeros((rows, parts * AR), F32)
        for a in range(NAD):
            out = out + jnp.where(adapter_of(out.shape) == a, dot(ref[a], cut_to), 0.0)
        return out

    def ranks_t(ref, parts):
        cut_to = select[: parts * R, : parts * AR]
        cols = ref.shape[2]
        out = jnp.zeros((cols, parts * AR), F32)
        for a in range(NAD):
            out = out + jnp.where(adapter_of(out.shape) == a, dot(ref[a], cut_to, TN), 0.0)
        return out

    def ranks_mid(ref, parts):
        rows = ref.shape[0]
        value = ref[...].astype(F32).reshape(rows * NAD, parts * R).astype(BF)
        value = dot(value, select[: parts * R, : parts * AR]).reshape(rows, NAD, parts * AR)
        mine = adapter_of(value.shape) == lax.broadcasted_iota(jnp.int32, value.shape, 1)
        return jnp.sum(jnp.where(mine, value, 0.0), axis=1)

    def tall(value):
        return jnp.concatenate([value, jnp.zeros((FF_PAD - FF_SHARD, value.shape[1]), F32)], axis=0)

    for h in range(H):
        for part in range(7):
            at = (h % 4) * HCOLS + part * HEAD
            item0[h // 4, :, at : at + HEAD] = w_in[:, part * D + h * HEAD : part * D + (h + 1) * HEAD].astype(F32)
    item0[0, :, 4 * HCOLS :] = ranks(in_down, 7)
    item0[1, :, 4 * HCOLS :] = ranks(in_up, 7)

    item1[0, :, 0:128] = ranks(out_down, 1)
    item1[0, :, 128:384] = ranks(up_down, 2)
    item1[0, :, 384:512] = ranks(out_up, 1)
    item1[0, :, 512:640] = ranks(down_up, 1)
    item1[0, :, 640:D] = jnp.zeros((8, D - 640), F32)
    item1[1, :, 0:D] = w_out[...].astype(F32)

    wide[...] = w_up[...].astype(F32)
    span = 8 * FF_SHARD
    rows = lax.broadcasted_iota(jnp.int32, (span, 3 * 64), 0)
    cols = lax.broadcasted_iota(jnp.int32, (span, 3 * 64), 1)
    unit_at = (cols // 64) * 8 + cols % 8
    spread = ((rows == (cols % 64) // 8 * FF_SHARD + unit_at) & (unit_at < FF_SHARD)).astype(BF)
    pieces = [wide[:, c * span : (c + 1) * span] for c in range(32)]
    moved_up = dot(jnp.concatenate(pieces, axis=0).astype(BF), spread)
    for c in range(32):
        half, chunk = c // 16, c % 16
        for k in range(3):
            at = (D if k == 0 else 0) + chunk * 64
            items[k][half, :, at : at + 64] = moved_up[c * 8 : (c + 1) * 8, k * 64 : (k + 1) * 64]
    down = tall(w_down[...].astype(F32))
    uu, dd = tall(ranks_mid(up_up, 2)), tall(ranks_t(down_down, 1))
    for k in range(3):
        at = (D if k == 0 else 0) + FB
        s = slice(k * 8, (k + 1) * 8)
        items[k][0, :, at : at + 768] = down[s, :768]
        items[k][1, :, at : at + 256] = down[s, 768:]
        items[k][1, :, at + 256 : at + 512] = uu[s]
        items[k][1, :, at + 512 : at + 640] = dd[s]
        items[k][1, :, at + 640 : at + 768] = jnp.zeros((8, 128), F32)

    own.wait()
    lax.fori_loop(1, N_DEV, end, 0)


def pack_call(lengths, ids, route, tokens, cotangent, decays, weights):
    smem, vmem = pl.BlockSpec(memory_space=pltpu.SMEM), pl.BlockSpec(memory_space=pltpu.VMEM)
    return pl.pallas_call(
        pack_kernel,
        out_shape=(jax.ShapeDtypeStruct((N_DEV, TOKEN_ROWS, 128), BF),)
        + tuple(jax.ShapeDtypeStruct((2, 8, width), F32) for width in WIDTHS)
        + (
            jax.ShapeDtypeStruct((MB, GROUP, GROUP), BF),
            jax.ShapeDtypeStruct((MB, GROUP, GROUP), BF),
            jax.ShapeDtypeStruct((ROWS, AR), F32),
            jax.ShapeDtypeStruct((MB,), F32),
        ),
        in_specs=[smem] * 2 + [vmem] * (4 + len(weights)),
        out_specs=(pl.BlockSpec(memory_space=pl.ANY),) + (vmem,) * 7 + (smem,),
        scratch_shapes=[
            pltpu.VMEM((N_DEV * TOKEN_ROWS, 128), F32),
            pltpu.VMEM((8, 2 * FF), F32),
            pltpu.VMEM((N_DEV, TOKEN_ROWS, 128), BF),
            pltpu.SemaphoreType.DMA((N_DEV,)),
            pltpu.SemaphoreType.DMA((N_DEV,)),
            pltpu.SemaphoreType.DMA,
        ],
        compiler_params=pltpu.CompilerParams(
            collective_id=2, has_side_effects=True, vmem_limit_bytes=VMEM_LIMIT
        ),
        name="pack",
    )(lengths, ids, route, tokens, cotangent, decays, *weights)


def unpack_kernel(
    core_ref, to_ref, act_ref, grad_ref, ffn_ref, heads_ref,
    out_ref, back_ref, in_down, in_up, out_down, out_up, up_down, up_up, down_down, down_up,
    flat,
):
    core = core_ref[0]
    for source, target in ((act_ref, out_ref), (grad_ref, back_ref)):
        got = [source[:, :, :, :, c * 128 : (c + 1) * 128].astype(F32) for c in range(2)]
        flat[...] = jnp.stack(got, axis=3).reshape(16 * N_DEV, 128)
        for m in range(MB):
            value = jnp.concatenate(
                [flat[pl.ds(m * 8 + j, N_DEV, stride=16), :].astype(BF) for j in range(8)], axis=1
            )
            target[m] = dot(to_ref[m], value, TN).astype(BF)
    own = pl.ds(pl.multiple_of(core * 8, 8), 8)
    heads = [heads_ref[half, own, :] for half in range(2)]
    ffn = [ffn_ref[half, own, :] for half in range(2)]
    select = selector(7).astype(F32)

    def tall(value, width):
        return jnp.concatenate([value[:, k * width : (k + 1) * width] for k in range(3)], axis=0)

    def put(ref, value, parts):
        rows, width = value.shape
        shape = (NAD, rows, width)
        mine = adapter_of(shape) == lax.broadcasted_iota(jnp.int32, shape, 0)
        apart = jnp.where(mine, value[None], 0.0).reshape(NAD * rows, width)
        ref[...] = exact(apart, select[: parts * R, :width], NT).reshape(NAD, rows, parts * R)

    put(in_down, heads[0], 7)
    put(in_up, heads[1], 7)
    put(out_down, ffn[1][:, 384:512], 1)
    put(out_up, ffn[1][:, 512:640], 1)
    put(up_down, ffn[1][:, 640:896], 2)
    put(down_up, ffn[0][:, 768:], 1)
    value = tall(ffn[0][:, :768], 256)
    shape = (FF_PAD, NAD, 2 * AR)
    mine = adapter_of(shape) == lax.broadcasted_iota(jnp.int32, shape, 1)
    apart = jnp.where(mine, jnp.broadcast_to(value[:, None, :], shape), 0.0).reshape(FF_PAD * NAD, 2 * AR)
    up_up[...] = exact(apart, select[: 2 * R, : 2 * AR], NT).reshape(FF_PAD, NAD, 2 * R)[:FF_SHARD]
    value = tall(ffn[1][:, :384], AR)
    for a in range(NAD):
        mine = jnp.where(adapter_of(value.shape) == a, value, 0.0)
        down_down[a] = exact(select[:R, :AR], mine, NT)[:, :FF_SHARD]


def unpack_call(core, to, act, grad, ffn_sums, heads_sums, shapes):
    smem, vmem = pl.BlockSpec(memory_space=pltpu.SMEM), pl.BlockSpec(memory_space=pltpu.VMEM)
    return pl.pallas_call(
        unpack_kernel,
        out_shape=(jax.ShapeDtypeStruct((MB, GROUP, D), BF),) * 2
        + tuple(jax.ShapeDtypeStruct(shape, F32) for shape in shapes),
        in_specs=[smem] + [vmem] * 5,
        out_specs=(vmem,) * (2 + len(shapes)),
        scratch_shapes=[pltpu.VMEM((16 * N_DEV, 128), F32)],
        compiler_params=pltpu.CompilerParams(vmem_limit_bytes=VMEM_LIMIT),
        name="unpack",
    )(core, to, act, grad, ffn_sums, heads_sums)


def body(
    tokens, cotangent, decays, route, lengths, adapter_ids, gain_mix, gain_ffn, persistent,
    w_in, w_out, w_up, w_down, in_down, in_up, out_down, out_up, up_down, up_up, down_down, down_up,
):
    me = lax.axis_index("fsdp").astype(jnp.int32)
    weights = (
        w_in, w_out, w_up, w_down, in_down, in_up, out_down, out_up, up_down, up_up, down_down, down_up,
    )
    turned = lambda value: jnp.swapaxes(value, 1, 2)
    views = (None,) * 5 + (turned, None, turned, None, lambda value: value.transpose(2, 0, 1), turned, turned)
    back_views = views[:9] + (lambda value: value.transpose(1, 2, 0), turned, turned)
    viewed = [item if view is None else view(item) for item, view in zip(weights, views)]
    got, *items, to, place, mask, split = pack_call(
        lengths[:, 0], adapter_ids[:, 0], route.reshape(MB, N_DEV, GROUP), tokens, cotangent, turned(decays), viewed
    )
    gain_mix, gain_ffn = gain_mix[None, :], gain_ffn[None, :]
    a1, _, _, _, proj, x, h1, lat, wf, lw, back, dz, dmid, grads_ffn = forward_call(
        split, got, gain_mix, gain_ffn, mask, place, persistent, items
    )
    act, grad, ffn_sums, heads_sums = backward_call(
        split, x, gain_mix, mask, place, proj, dz, dmid, h1, lat, a1.reshape(2, D, WIDTHS[0]), persistent, wf, lw,
        grads_ffn, back,
    )
    outs = unpack_call((me % 2)[None], to, act, grad, ffn_sums, heads_sums, [item.shape for item in viewed[4:]])
    grads = [item if view is None else view(item) for item, view in zip(outs[2:], back_views[4:])]
    return tuple(outs[:2]) + tuple(grads)


def solution(mesh):
    rows, cols = P(None, "fsdp", None), P(None, None, "fsdp")
    weight = P("fsdp", None)
    return jax.shard_map(
        body,
        mesh=mesh,
        in_specs=(rows, rows, rows, P(), rows, rows, P(), P(), P())
        + (weight,) * 4
        + (rows, cols) * 4,
        out_specs=(rows, rows) + (rows, cols) * 4,
        check_vma=False,
    )
```

```python
import functools
import math

import jax
import jax.numpy as jnp
from jax import lax
from jax.experimental import pallas as pl
from jax.experimental.pallas import tpu as pltpu
from jax.sharding import PartitionSpec as P

D = 1024
H = 8
HEAD = 128
FF = 2816
R = 16
NAD = 8
NP = 16
SPAN = 64
GROUP = 128
MB = 2
ROWS = MB * GROUP
N_DEV = 128
AR = NAD * R
HCOLS = 7 * HEAD
FF_SHARD = FF // N_DEV
FF_PAD = 24
FFP = FF_PAD * N_DEV
FB = 1024
EPS = 1e-05
SCALE = 1.0 / math.sqrt(HEAD)
VMEM_LIMIT = 60 * 1024 * 1024
BF = jnp.bfloat16
F32 = jnp.float32

NN = (((1,), (0,)), ((), ()))
NT = (((1,), (1,)), ((), ()))
TN = (((0,), (0,)), ((), ()))


def dot(left, right, dims=NN):
    return lax.dot_general(left, right, dims, preferred_element_type=F32)


def exact(left, right, dims=NN):
    return lax.dot_general(
        left, right, dims, precision=lax.Precision.HIGHEST, preferred_element_type=F32
    )


def halves(value):
    high = value.astype(BF)
    return high, (value - high.astype(F32)).astype(BF)


def dot3(left, right, dims=NN):
    lh, ll = left
    rh, rl = right
    return dot(lh, rh, dims) + (dot(lh, rl, dims) + dot(ll, rh, dims))


def norm_fwd(values, gain):
    inv = lax.rsqrt(jnp.mean(values * values, axis=-1, keepdims=True) + EPS)
    return values * inv * gain, inv


def norm_bwd(grad, values, inv, gain):
    scaled = grad * gain
    return inv * (scaled - values * (inv * inv * jnp.mean(values * scaled, axis=-1, keepdims=True)))


def decay_kernel(split_ref, dec_ref, dect_ref, wf_ref, lw_ref):
    rows = lax.broadcasted_iota(jnp.int32, (GROUP, GROUP), 0)
    cols = lax.broadcasted_iota(jnp.int32, (GROUP, GROUP), 1)
    lower = (rows >= cols) & ((rows >= SPAN) == (cols >= SPAN))
    tri = lower.astype(F32)
    second = rows >= SPAN
    for g in range(MB):
        keep = 1.0 - split_ref[g]
        here = dec_ref[g * GROUP : (g + 1) * GROUP, :]
        here_t = dect_ref[:, g * GROUP : (g + 1) * GROUP]
        run = exact(tri, jnp.log(here[:, : 2 * H]))
        run_t = exact(jnp.log(here_t[: 2 * H, :]), tri, NT)
        for h in range(H):
            gap = run[:, h : h + 1] - run_t[h : h + 1, :]
            retain = jnp.exp(jnp.where(lower, gap, -1e30))
            gap = run[:, H + h : H + h + 1] - run_t[H + h : H + h + 1, :]
            moment = jnp.exp(jnp.where(lower, gap, -1e30))
            pairs = exact(retain, moment)
            theta = here_t[2 * H + h : 2 * H + h + 1, :]
            moment_run = jnp.exp(run_t[H + h : H + h + 1, :])
            carry = jnp.sum(retain * moment_run, axis=1, keepdims=True)
            last_weight = pairs[SPAN - 1 : SPAN, :] * theta * keep
            last_moment = moment[SPAN - 1 : SPAN, :] * theta * keep
            across = jnp.exp(run[:, h : h + 1]) * last_weight + carry * last_moment
            wf_ref[h, g] = pairs * theta + jnp.where(second, across, 0.0)
            lw_ref[h, g] = jnp.broadcast_to(last_weight, (8, GROUP))


def allowed_mask(split_ref):
    rows = lax.broadcasted_iota(jnp.int32, (ROWS, GROUP), 0)
    cols = lax.broadcasted_iota(jnp.int32, (ROWS, GROUP), 1)
    local = rows % GROUP
    group = rows // GROUP
    split = jnp.where(group == 0, split_ref[0], split_ref[1]) > 0.5
    return (local >= cols) & jnp.logical_not(split & (local >= SPAN) & (cols < SPAN))


def by_group(make):
    return jnp.concatenate([make(slice(0, GROUP), 0), make(slice(GROUP, ROWS), 1)], axis=0)


def attend(q, k, v, pk, pv, allowed):
    near = by_group(lambda s, g: dot(q[s], k[s], NT))
    far = dot(q, pk, NT) * SCALE
    near = jnp.where(allowed, near * SCALE, -1000000000.0)
    top = jnp.maximum(
        jnp.max(near, axis=-1, keepdims=True), jnp.max(far, axis=-1, keepdims=True)
    )
    near = jnp.exp(near - top)
    far = jnp.exp(far - top)
    inv = 1.0 / (jnp.sum(near, axis=-1, keepdims=True) + jnp.sum(far, axis=-1, keepdims=True))
    near = near * inv
    far = far * inv
    return near, far


def attend_out(near_half, far_half, v, pv):
    return by_group(lambda s, g: dot(near_half[s], v[s])) + dot(far_half, pv)


def unit(values):
    inv = lax.rsqrt(jnp.mean(values * values, axis=-1, keepdims=True) + EPS)
    return values * (inv * SCALE), inv


def unit_bwd(grad, values, inv):
    return (inv * SCALE) * (
        grad - values * (inv * inv * jnp.mean(values * grad, axis=-1, keepdims=True))
    )


def plain(value):
    return (value.astype(BF),)


def dot1(left, right, dims=NN):
    return dot(left[0], right[0], dims)


def memory_terms(kn, qn, mv, wf_ref, lw_ref, halves=halves, dot3=dot3):
    second = lax.broadcasted_iota(jnp.int32, (GROUP, GROUP), 0) >= SPAN
    kept = []
    for g in range(MB):
        s = slice(g * GROUP, (g + 1) * GROUP)
        kh, qh = halves(kn[s]), halves(qn[s])
        wf = wf_ref[0, g]
        lw = jnp.where(second, lw_ref[0, g][0:1, :], 0.0)
        kk = dot3(kh, kh, NT) * lw
        qk = dot3(qh, kh, NT) * wf
        kk_half = halves(kk)
        mvh = halves(mv[s])
        err = mv[s] - dot3(kk_half, mvh)
        errh = halves(err)
        qk_half = halves(qk)
        kept.append((kh, qh, wf, lw, kk_half, qk_half, mvh, errh))
    return kept


def memory_out(kept, dot3=dot3):
    return jnp.concatenate([dot3(item[5], item[7]) for item in kept], axis=0)


def memory_bwd(kept, grad, halves=plain, dot3=dot1):
    grads_k, grads_q, grads_v = [], [], []
    for g in range(MB):
        kh, qh, wf, lw, kk_half, qk_half, mvh, errh = kept[g]
        gh = halves(grad[g * GROUP : (g + 1) * GROUP])
        d_qk = dot3(gh, errh, NT) * wf
        d_err = dot3(qk_half, gh, TN)
        deh = halves(d_err)
        d_v = d_err - dot3(kk_half, deh, TN)
        d_kk = dot3(deh, mvh, NT) * lw
        dqh = halves(d_qk)
        dkh = halves(d_kk)
        grads_q.append(dot3(dqh, kh))
        grads_k.append(dot3(dqh, qh, TN) - (dot3(dkh, kh) + dot3(dkh, kh, TN)))
        grads_v.append(d_v)
    return (
        jnp.concatenate(grads_k, axis=0),
        jnp.concatenate(grads_q, axis=0),
        jnp.concatenate(grads_v, axis=0),
    )


AXES = ("x", "z", "y")
MESH = pl.DeviceIdType.MESH


def position():
    me = lax.axis_index("fsdp")
    chip = me // 2
    return me % 2, (chip // 16, (chip // 4) % 4, chip % 4)


def device(core, spot):
    return (((spot[0] * 4 + spot[1]) * 4 + spot[2]) * 2 + core,)


def moved(spot, axis, by):
    return tuple((v + by + 4) % 4 if i == axis else v for i, v in enumerate(spot))


def cut(lanes, count, first=0):
    base, extra = divmod(lanes, count)
    runs, at = [], 0
    for i in range(count):
        size = base + (1 if (i - first) % count < extra else 0)
        runs.append((at * 128, size * 128))
        at += size
    return runs


def neighbours(core, spot):
    found = {}
    for axis in range(3):
        for by in (1, 2, 3):
            there = moved(spot, axis, by)
            found[axis, by] = (there, device(core, there))
    return found


class Sends:
    def __init__(self, send_sem, recv_sem):
        self.send_sem, self.recv_sem = send_sem, recv_sem
        self.slots, self.open = {}, []

    def copy(self, name, src, dst, target):
        slot = self.slots.setdefault(name, len(self.slots))
        return pltpu.make_async_remote_copy(
            src_ref=src, dst_ref=dst, send_sem=self.send_sem.at[slot], recv_sem=self.recv_sem.at[slot],
            device_id=target, device_id_type=MESH,
        )

    def start(self, name, make):
        self.copy(name, *make()).start()
        self.open.append((name, make))

    def arrived(self, name, ref, target):
        self.copy(name, ref, ref, target).wait_recv()

    def drain(self):
        for name, make in self.open:
            self.copy(name, *make()).wait_send()
        self.open = []


def greet(targets):
    barrier = pltpu.get_barrier_semaphore()
    for target in targets:
        pl.semaphore_signal(barrier, inc=1, device_id=target, device_id_type=MESH)
    pl.semaphore_wait(barrier, len(targets))


LONGER = (0, 2, 2, 1)
TURNED = {(2, 0), (2, 2), (3, 1)}


class Gather:
    def __init__(self, sends, outs, widths):
        self.sends, self.outs = sends, outs
        self.core, self.spot = position()
        self.other = 1 - self.core
        self.sibling = device(1 - self.core, self.spot)
        self.near = neighbours(self.core, self.spot)
        self.jobs = [
            [(i, part, cols) for part, cols in enumerate(cut(width // 128, 3, LONGER[i]))]
            for i, width in enumerate(widths)
        ]
        self.forwards = [[] for _ in widths]

    def peers(self):
        return [self.sibling] + [self.near[a, by][1] for a in range(3) for by in (1, 3)]

    def block(self, i, whole_axes, at, cols, half=None):
        index = [pl.ds(0, 4) if a in whole_axes else pl.ds(at[a], 1) for a in range(3)]
        half = self.core if half is None else half
        return self.outs[i].at[half, index[0], index[1], index[2], :, pl.ds(cols[0], cols[1])]

    def push(self, name, target, *where):
        def make():
            ref = self.block(*where)
            return ref, ref, target

        self.sends.start(name, make)

    def forward(self, name, *where):
        self.push(name, self.sibling, *where)
        self.forwards[where[0]].append((name, where))

    def plan(self, item, phase):
        for i, part, cols in self.jobs[item]:
            axis = (part + phase) % 3
            done = [(part + p) % 3 for p in range(phase)]
            sides = [self.near[axis, by] for by in (1, 3, 2)]
            halves_of = [(cols[0] + at, size) for at, size in cut(cols[1] // 128, 2, (i, part) in TURNED)]
            yield i, part, cols, done, sides, halves_of

    def begin(self, item, phase):
        for i, part, cols, done, (right, left, far), two in self.plan(item, phase):
            if phase == 0:
                for side, there in (("f", far), ("r", right), ("l", left)):
                    self.push((i, part, phase, side), there[1], i, done, self.spot, cols)
                continue
            for step, (a, b) in enumerate(((0, 1), (1, 0))):
                self.push((i, part, phase, "r", step), right[1], i, done, self.spot, two[a])
                self.push((i, part, phase, "l", step), left[1], i, done, self.spot, two[b])
            if phase == 2:
                self.forward((i, part, "f"), i, done, self.spot, cols)

    def relay(self, item, phase):
        for i, part, cols, done, (right, left, _), two in self.plan(item, phase):
            for side, source, target, cc in (("r", left, right, two[0]), ("l", right, left, two[1])):
                where = (i, done, source[0], cc)
                self.sends.arrived((i, part, phase, side, 0), self.block(*where), source[1])
                self.push((i, part, phase, side, 2), target[1], *where)
                if phase == 2:
                    self.forward((i, part, "f", side, 0), *where)

    def finish(self, item, phase):
        for i, part, cols, done, (right, left, far), two in self.plan(item, phase):
            if phase == 0:
                for side, source in (("r", left), ("l", right), ("f", far)):
                    self.sends.arrived((i, part, phase, side), self.block(i, done, source[0], cols), source[1])
                continue
            for side, step, at, cc, source in (
                ("r", 1, left, two[1], left),
                ("l", 1, right, two[0], right),
                ("r", 2, far, two[0], left),
                ("l", 2, far, two[1], right),
            ):
                where = (i, done, at[0], cc)
                self.sends.arrived((i, part, phase, side, step), self.block(*where), source[1])
                if phase == 2:
                    self.forward((i, part, "f", side, step), *where)

    def received(self, item):
        for name, (i, done, at, cc) in self.forwards[item]:
            self.sends.arrived(name, self.block(i, done, at, cc, self.other), self.sibling)


class Exchange:
    def __init__(self, sends, key, bufs, lanes, jobs):
        self.sends, self.key, self.bufs, self.lanes, self.jobs = sends, key, bufs, lanes, jobs
        self.core, self.spot = position()
        self.other = 1 - self.core
        self.mine, self.theirs = (
            [pl.ds(pl.multiple_of(lane * 256 + core * 128, 128), 128) for lane in range(lanes)]
            for core in (self.core, self.other)
        )
        self.sibling = device(self.other, self.spot)
        self.near = neighbours(self.core, self.spot)

    def index(self, cols, axis=None, where=None):
        return tuple(pl.ds(where, 1) if a == axis else pl.ds(0, 4) for a in range(3)) + (slice(None), cols)

    def moves(self, stage, which):
        before, after = self.bufs[stage], self.bufs[stage + 1]
        away, stay = [], []
        if stage == 0:
            for lane in range(self.lanes):
                mine, theirs = self.index(self.mine[lane]), self.index(self.theirs[lane])
                away.append(((self.key, 0, lane), theirs, mine, self.sibling, theirs, self.sibling))
                stay.append(mine)
            return before, after, away, stay
        for number, (lo, width, first) in enumerate(self.jobs):
            if which is not None and number not in which:
                continue
            axis = (first + stage - 1) % 3
            cols = pl.ds(lo, width)
            here = self.index(cols, axis, self.spot[axis])
            for by in (2, 1, 3):
                there, target = self.near[axis, by]
                behind, source = self.near[axis, 4 - by]
                away.append(
                    (
                        (self.key, stage, number, by),
                        self.index(cols, axis, there[axis]),
                        here,
                        target,
                        self.index(cols, axis, behind[axis]),
                        source,
                    )
                )
            stay.append(here)
        return before, after, away, stay

    def launch(self, stage, which=None):
        before, after, away, stay = self.moves(stage, which)
        for name, src, dst, target, _, _ in away:
            self.sends.start(name, lambda src=src, dst=dst, target=target: (before.at[src], after.at[dst], target))
        for here in stay:
            after[here] = before[here]

    def land(self, stage, which=None):
        _, after, away, _ = self.moves(stage, which)
        for name, _, _, _, landing, source in away:
            self.sends.arrived(name, after.at[landing], source)

    def fill(self, lane, scratch, values):
        row = 0
        for value in values:
            for j in range(value.shape[1] // 128):
                scratch[pl.ds(row, N_DEV, stride=16), :] = value[:, j * 128 : (j + 1) * 128].astype(F32)
                row += 1
        blocks = scratch[...].reshape(4, 4, 4, 2, 16, 128)
        for core in range(2):
            at = lane * 256 + core * 128
            self.bufs[0][:, :, :, :, at : at + 128] = blocks[:, :, :, core].astype(BF)


BY_CORE = [(0, 128, 0), (128, 128, 1)]


WALL = 768
TOKEN_ROWS = 48
WIDTHS = (4 * HCOLS + 7 * AR, D + FB + WALL, FB + WALL, FB + WALL)
FSTEPS = H
BLOCKS = FFP // FB


def forward_kernel(
    split_ref, sent_ref, gain1_ref, gain2_ref, mask_ref, place_ref, pers_ref,
    mine0, mine1, mine2, mine3,
    g0_ref, g1_ref, g2_ref, g3_ref, proj_ref, x_ref, h1_ref, lat_ref, wf_ref, lw_ref, back_ref, dz_ref, dmid_ref,
    grads_ref,
    got, flat, d_ref, dec_ref, dect_ref, inc0, inc1, inc2, inc3, stage0, stage1, stage2, stage3,
    w_buf, up_buf, down_buf, z_ref, wup_buf, wd_buf, lead_buf,
    x2_ref, h2_ref, inv_ref, lat_out_ref, lat_up_ref, dl_down_ref, acc_ref, lat_acc_ref, dh_ref, dlat_ref,
    send_sem, recv_sem, local_sem, w_sem, j_sem, token_send, token_recv,
):
    step = pl.program_id(0)
    mine, inc = (mine0, mine1, mine2, mine3), (inc0, inc1, inc2, inc3)
    stage, outs = (stage0, stage1, stage2, stage3), (g0_ref, g1_ref, g2_ref, g3_ref)
    sends = Sends(send_sem, recv_sem)
    ring = Gather(sends, outs, WIDTHS)
    core, spot = ring.core, ring.spot
    other = 1 - core
    items = range(4)
    me = lax.axis_index("fsdp")

    def token_copy(k):
        target = (me + k) % N_DEV
        return pltpu.make_async_remote_copy(
            src_ref=sent_ref.at[target], dst_ref=got.at[me], send_sem=token_send.at[k], recv_sem=token_recv.at[k],
            device_id=(target,), device_id_type=MESH,
        )

    def head_loads(h, slot):
        half, place = h // 4, pl.multiple_of((h % 4) * HCOLS, 128)
        return (
            pltpu.make_async_copy(
                g0_ref.at[half, :, :, :, :, pl.ds(place, HCOLS)], w_buf.at[slot], w_sem.at[slot, 0]
            ),
            pltpu.make_async_copy(
                g0_ref.at[1, h // 2, pl.ds(2 * (h % 2), 2), :, :, pl.ds(4 * HCOLS, HCOLS)],
                up_buf.at[slot],
                w_sem.at[slot, 1],
            ),
        )

    def down_load():
        return pltpu.make_async_copy(
            g0_ref.at[0, :, :, :, :, pl.ds(4 * HCOLS, HCOLS)], down_buf, local_sem.at[0]
        )

    def lead_load():
        return pltpu.make_async_copy(g1_ref.at[:, :, :, :, :, pl.ds(0, D)], lead_buf, local_sem.at[0])

    def up_load(k):
        at = D if k == 0 else 0
        return pltpu.make_async_copy(
            outs[k + 1].at[:, :, :, :, :, pl.ds(at, FB)], wup_buf.at[k % 2], j_sem.at[k % 2, 0]
        )

    def wall_load(k):
        at = D + FB if k == 0 else FB
        return pltpu.make_async_copy(
            outs[k + 1].at[:, :, :, :, :, pl.ds(at, WALL)], wd_buf.at[k % 2], j_sem.at[k % 2, 1]
        )

    @pl.when(step == 0)
    def _():
        barrier = pltpu.get_barrier_semaphore()

        def signal(k, carry):
            pl.semaphore_signal(barrier, inc=1, device_id=((me + k) % N_DEV,), device_id_type=MESH)
            return carry

        lax.fori_loop(1, N_DEV, signal, 0)
        pl.semaphore_wait(barrier, N_DEV - 1)
        for i in items:
            sends.start(("pair", i), lambda i=i: (mine[i].at[other], inc[i], ring.sibling))
        own_copy = lambda i: pltpu.make_async_copy(
            stage[i], outs[i].at[core, spot[0], spot[1], spot[2]], local_sem.at[i]
        )
        for i in items:
            sends.arrived(("pair", i), inc[i], ring.sibling)
            own, theirs = mine[i][core], inc[i][...]
            first = jnp.where(core == 0, own, theirs)
            last = jnp.where(core == 0, theirs, own)
            stage[i][...] = jnp.concatenate([first, last], axis=0).astype(BF)
            own_copy(i).start()
        for i in items:
            own_copy(i).wait()
            ring.begin(i, 0)
        def columns(first, count):
            return jnp.concatenate(
                [flat[pl.ds(first + c, N_DEV, stride=TOKEN_ROWS), :].astype(BF) for c in range(count)], axis=1
            )

        ring.finish(0, 0)
        ring.begin(0, 1)

        def send_tokens(k, carry):
            token_copy(k).start()
            return carry

        def take_tokens(k, carry):
            token_copy(k).wait()
            return carry

        lax.fori_loop(1, N_DEV, send_tokens, 0)
        got[me] = sent_ref[me]
        for i in items[1:]:
            ring.finish(i, 0)
        ring.relay(0, 1)
        ring.finish(0, 1)
        ring.begin(0, 2)
        ring.begin(1, 1)
        lax.fori_loop(1, N_DEV, take_tokens, 0)
        flat[...] = got[...].astype(F32).reshape(N_DEV * TOKEN_ROWS, 128)
        rates = columns(4 * D // 128, 1)
        for m in range(MB):
            s = slice(m * GROUP, (m + 1) * GROUP)
            x_ref[s, :] = dot(place_ref[m], columns(m * D // 128, D // 128), TN).astype(BF)
            d_ref[s, :] = dot(place_ref[m], columns((MB + m) * D // 128, D // 128), TN).astype(BF)
            sent = rates[:, m * 3 * H : (m + 1) * 3 * H]
            dec_ref[s, :] = dot(place_ref[m], sent, TN)
            dect_ref[:, s] = dot(sent, place_ref[m], TN)
        decay_kernel(split_ref, dec_ref, dect_ref, wf_ref, lw_ref)
        normed, _ = norm_fwd(x_ref[...].astype(F32), gain1_ref[...])
        h1_ref[...] = normed.astype(BF)
        ring.relay(0, 2)
        ring.relay(1, 1)
        for i in items[2:]:
            ring.begin(i, 1)
        ring.finish(0, 2)
        ring.finish(1, 1)
        ring.begin(1, 2)
        ring.received(0)
        for copy in head_loads(0, 0):
            copy.start()
        down_load().start()
        down_load().wait()
        latent = dot(h1_ref[...], down_buf[...].reshape(D, HCOLS))
        mask = mask_ref[...]
        for part in range(7):
            s = slice(part * AR, (part + 1) * AR)
            lat_ref[:, s] = (latent[:, s] * mask).astype(BF)

    @pl.when(step == 1)
    def _():
        for i in items[2:]:
            ring.relay(i, 1)

    @pl.when(step == 3)
    def _():
        ring.relay(1, 2)

    @pl.when(step == 6)
    def _():
        ring.finish(2, 1)
        ring.begin(2, 2)
        ring.finish(3, 1)

    @pl.when(step < FSTEPS)
    def _():
        slot = step % 2
        for copy in head_loads(step, slot):
            copy.wait()

        @pl.when(step + 1 < FSTEPS)
        def _():
            for copy in head_loads(step + 1, 1 - slot):
                copy.start()

        base = dot(h1_ref[...], w_buf[slot].reshape(D, HCOLS))
        up = up_buf[slot].reshape(HEAD, HCOLS)
        pieces = []
        for part in range(7):
            s = slice(part * AR, (part + 1) * AR)
            piece = base[:, part * HEAD : (part + 1) * HEAD] + dot(lat_ref[:, s], up[:, s], NT)
            proj_ref[:, part * HEAD : (part + 1) * HEAD] = piece
            pieces.append(piece)
        q, k, v = (pieces[i].astype(BF) for i in range(3))
        pk, pv = pers_ref[0, :, pl.ds(pl.multiple_of(step * HEAD, HEAD), HEAD)], pers_ref[
            1, :, pl.ds(pl.multiple_of(step * HEAD, HEAD), HEAD)
        ]
        near, far = attend(q, k, v, pk, pv, allowed_mask(split_ref))
        att = attend_out(near.astype(BF), far.astype(BF), v, pv)
        kn, _ = unit(pieces[3])
        qn, _ = unit(pieces[5])
        here = pl.ds(step, 1)
        mem = memory_out(memory_terms(kn, qn, pieces[4], wf_ref.at[here], lw_ref.at[here]))
        z_ref[:, pl.ds(pl.multiple_of(step * HEAD, HEAD), HEAD)] = (
            att + jax.nn.sigmoid(pieces[6]) * mem
        ).astype(BF)

    lead = lambda half, lo, hi: lead_buf[half, :, :, :, :, lo:hi].reshape(D, hi - lo)
    out_down = lambda: lead(0, 0, 128)
    up_down = lambda: lead(0, 128, 384)
    out_up = lambda: lead(0, 384, 512)
    down_up = lambda: lead(0, 512, 640)
    w_out = lambda: lead(1, 0, D)

    @pl.when(step == FSTEPS)
    def _():
        ring.finish(1, 2)
        ring.received(1)
        for copy in (lead_load(), up_load(0), wall_load(0)):
            copy.start()
        lead_load().wait()
        ring.relay(2, 2)
        ring.begin(3, 2)
        mask = mask_ref[...]
        z = z_ref[...]
        lat_out_ref[...] = (dot(z, out_down()) * mask).astype(BF)
        x2 = x_ref[...].astype(F32) + (dot(z, w_out()) + dot(lat_out_ref[...], out_up(), NT))
        x2_ref[...] = x2
        normed, inv = norm_fwd(x2, gain2_ref[...])
        inv_ref[...] = jnp.broadcast_to(inv, inv_ref.shape)
        h2_ref[...] = normed.astype(BF)
        latent = dot(h2_ref[...], up_down())
        lat_up_ref[:, :AR] = (latent[:, :AR] * mask).astype(BF)
        lat_up_ref[:, AR:] = (latent[:, AR:] * mask).astype(BF)
        dl_down_ref[...] = (dot(d_ref[...], down_up()) * mask).astype(BF)
        for ref in (acc_ref, lat_acc_ref, dh_ref, dlat_ref):
            ref[...] = jnp.zeros_like(ref)

    @pl.when(step == FSTEPS)
    def _():
        ring.finish(2, 2)
        ring.received(2)
        up_load(1).start()
        wall_load(1).start()

    @pl.when(step >= FSTEPS)
    def _():
        k = step - FSTEPS
        slot = k % 2
        h2 = h2_ref[...]
        d = d_ref[...]
        lat0, lat1 = lat_up_ref[:, :AR], lat_up_ref[:, AR:]
        wall = lambda half, lo, hi: wd_buf[slot, half, :, :, :, :, lo:hi].reshape(FB, hi - lo)
        pltpu.make_async_copy(wup_buf.at[slot], wup_buf.at[slot], j_sem.at[slot, 0]).wait()
        pltpu.make_async_copy(wd_buf.at[slot], wd_buf.at[slot], j_sem.at[slot, 1]).wait()
        w_gate, w_lift = (wup_buf[slot, half].reshape(D, FB) for half in range(2))
        wda, wdb = wall(0, 0, 768), wall(1, 0, 256)
        uu0, uu1, dd = wall(1, 256, 384), wall(1, 384, 512), wall(1, 512, 640)
        gate = dot(h2, w_gate) + dot(lat0, uu0, NT)
        lift = dot(h2, w_lift) + dot(lat1, uu1, NT)
        sig = jax.nn.sigmoid(gate)
        silu = gate * sig
        act = (silu * lift).astype(BF)
        d_act = dot(d[:, :768], wda, NT) + dot(d[:, 768:], wdb, NT) + dot(dl_down_ref[...], dd, NT)
        d_gate = (d_act * lift * (sig * (1.0 + gate * (1.0 - sig)))).astype(BF)
        d_lift = (d_act * silu).astype(BF)
        acc_ref[:, :768] += dot(act, wda)
        acc_ref[:, 768:] += dot(act, wdb)
        lat_acc_ref[...] += dot(act, dd)
        dh_ref[...] += dot(d_gate, w_gate, NT) + dot(d_lift, w_lift, NT)
        dlat_ref[:, :AR] += dot(d_gate, uu0)
        dlat_ref[:, AR:] += dot(d_lift, uu1)
        for half, at, term in (
            (0, k * 256, dot(d_gate, lat0, TN)),
            (0, k * 256 + AR, dot(d_lift, lat1, TN)),
            (1, k * AR, dot(act, dl_down_ref[...], TN)),
        ):
            at = pl.ds(pl.multiple_of(at, AR), AR)
            grads_ref[half, :, :, at] = term.reshape(64, 16, AR).astype(BF)

        @pl.when(k == 0)
        def _():
            ring.relay(3, 2)

        @pl.when(k == 1)
        def _():
            ring.finish(3, 2)
            ring.received(3)
            up_load(2).start()
            wall_load(2).start()

    @pl.when(step == FSTEPS + BLOCKS - 1)
    def _():
        mask = mask_ref[...]
        lat_down = (lat_acc_ref[...] * mask).astype(BF)
        out = (x2_ref[...] + acc_ref[...] + dot(lat_down, down_up(), NT)).astype(BF)
        for m in range(MB):
            s = slice(m * GROUP, (m + 1) * GROUP)
            back_ref[:, m * D : (m + 1) * D] = dot(place_ref[m], out[s]).astype(BF)
        d = d_ref[...]
        h2 = h2_ref[...]
        z = z_ref[...]

        def put(half, at, value):
            grads_ref[half, :, :, at : at + AR] = value.reshape(64, 16, AR).astype(BF)

        put(0, 768, dot(d, lat_down, TN))
        dlu0 = (dlat_ref[:, :AR] * mask).astype(BF)
        dlu1 = (dlat_ref[:, AR:] * mask).astype(BF)
        put(1, 640, dot(h2, dlu0, TN))
        put(1, 768, dot(h2, dlu1, TN))
        ud = up_down()
        dh = dh_ref[...] + (dot(dlu0, ud[:, :AR], NT) + dot(dlu1, ud[:, AR:], NT))
        dmid = d.astype(F32) + norm_bwd(dh, x2_ref[...], inv_ref[:, :1], gain2_ref[...])
        dmid_ref[...] = dmid
        dmb = dmid.astype(BF)
        dlo = (dot(dmb, out_up()) * mask).astype(BF)
        put(1, 384, dot(z, dlo, TN))
        put(1, 512, dot(dmb, lat_out_ref[...], TN))
        dz_ref[...] = (dot(dmb, w_out(), NT) + dot(dlo, out_down(), NT)).astype(BF)
        sends.drain()


def forward_call(split, sent, gain1, gain2, mask, place, persistent, mine):
    once = pl.Buffered(1)
    whole = lambda *shape: pl.BlockSpec(shape, lambda s: (0,) * len(shape), pipeline_mode=once)
    hbm = pl.BlockSpec(memory_space=pl.ANY)
    slots = 4 * (1 + 3 * (3 + 2 * 6 + 7))
    return pl.pallas_call(
        forward_kernel,
        grid=(FSTEPS + BLOCKS,),
        out_shape=tuple(jax.ShapeDtypeStruct((2, 4, 4, 4, 16, width), BF) for width in WIDTHS)
        + (
            jax.ShapeDtypeStruct((ROWS, 7 * D), F32),
            jax.ShapeDtypeStruct((ROWS, D), BF),
            jax.ShapeDtypeStruct((ROWS, D), BF),
            jax.ShapeDtypeStruct((ROWS, 7 * AR), BF),
            jax.ShapeDtypeStruct((H, MB, GROUP, GROUP), F32),
            jax.ShapeDtypeStruct((H, MB, 8, GROUP), F32),
            jax.ShapeDtypeStruct((GROUP, MB * D), BF),
            jax.ShapeDtypeStruct((ROWS, D), BF),
            jax.ShapeDtypeStruct((ROWS, D), F32),
            jax.ShapeDtypeStruct((2, 64, 16, 896), BF),
        ),
        in_specs=[
            pl.BlockSpec(memory_space=pltpu.SMEM),
            whole(N_DEV, TOKEN_ROWS, 128),
            whole(1, D),
            whole(1, D),
            whole(ROWS, AR),
            whole(MB, GROUP, GROUP),
            whole(2, NP, D),
        ]
        + [whole(2, 8, width) for width in WIDTHS],
        out_specs=(hbm,) * 4
        + (
            pl.BlockSpec((ROWS, HCOLS), lambda s: (0, jnp.minimum(s, FSTEPS - 1))),
            whole(ROWS, D),
            whole(ROWS, D),
            whole(ROWS, 7 * AR),
            whole(H, MB, GROUP, GROUP),
            whole(H, MB, 8, GROUP),
            whole(GROUP, MB * D),
            whole(ROWS, D),
            whole(ROWS, D),
            whole(2, 64, 16, 896),
        ),
        scratch_shapes=[
            pltpu.VMEM((N_DEV, TOKEN_ROWS, 128), BF),
            pltpu.VMEM((N_DEV * TOKEN_ROWS, 128), F32),
            pltpu.VMEM((ROWS, D), BF),
            pltpu.VMEM((ROWS, 3 * H), F32),
            pltpu.VMEM((3 * H, ROWS), F32),
        ]
        + [pltpu.VMEM((8, width), F32) for width in WIDTHS]
        + [pltpu.VMEM((16, width), BF) for width in WIDTHS]
        + [
            pltpu.VMEM((2, 4, 4, 4, 16, HCOLS), BF),
            pltpu.VMEM((2, 2, 4, 16, HCOLS), BF),
            pltpu.VMEM((4, 4, 4, 16, HCOLS), BF),
            pltpu.VMEM((ROWS, D), BF),
            pltpu.VMEM((2, 2, 4, 4, 4, 16, FB), BF),
            pltpu.VMEM((2, 2, 4, 4, 4, 16, WALL), BF),
            pltpu.VMEM((2, 4, 4, 4, 16, D), BF),
            pltpu.VMEM((ROWS, D), F32),
            pltpu.VMEM((ROWS, D), BF),
            pltpu.VMEM((ROWS, 128), F32),
            pltpu.VMEM((ROWS, AR), BF),
            pltpu.VMEM((ROWS, 2 * AR), BF),
            pltpu.VMEM((ROWS, AR), BF),
            pltpu.VMEM((ROWS, D), F32),
            pltpu.VMEM((ROWS, AR), F32),
            pltpu.VMEM((ROWS, D), F32),
            pltpu.VMEM((ROWS, 2 * AR), F32),
            pltpu.SemaphoreType.DMA((slots,)),
            pltpu.SemaphoreType.DMA((slots,)),
            pltpu.SemaphoreType.DMA((4,)),
            pltpu.SemaphoreType.DMA((2, 2)),
            pltpu.SemaphoreType.DMA((2, 2)),
            pltpu.SemaphoreType.DMA((N_DEV,)),
            pltpu.SemaphoreType.DMA((N_DEV,)),
        ],
        compiler_params=pltpu.CompilerParams(
            collective_id=0, has_side_effects=True, vmem_limit_bytes=VMEM_LIMIT
        ),
        name="gather_forward",
    )(split, sent, gain1, gain2, mask, place, persistent, *mine)


class Scatter:
    def __init__(self, sends, key, grads, out, inc0, total, inc1, inc2, inc3, t1, t2):
        self.sends, self.key, self.grads, self.out = sends, key, grads, out
        self.inc0, self.total, self.inc = inc0, total, (None, inc1, inc2, inc3)
        self.t1, self.t2 = t1, t2
        self.core, self.spot = position()
        self.other = 1 - self.core
        self.sibling = device(1 - self.core, self.spot)
        self.near = neighbours(self.core, self.spot)
        self.parts = [(part, pl.ds(*cols)) for part, cols in enumerate(cut(7, 3))]

    def peers(self):
        return [self.sibling] + [there[1] for there in self.near.values()]

    def pair(self):
        for x in range(4):
            self.sends.start(
                (self.key, "pair", x),
                lambda x=x: (
                    self.grads.at[self.other, pl.ds(16 * x, 16)],
                    self.inc0.at[x],
                    self.sibling,
                ),
            )

    def source(self, phase, part, at):
        axis = (part + phase - 1) % 3
        cs = self.parts[part][1]
        if phase == 1:
            index = tuple(at if a == axis else slice(None) for a in range(3))
            return self.total, index + (slice(None), cs)
        rest = [a for a in range(3) if a != part]
        if phase == 2:
            index = (at, slice(None)) if rest[0] == axis else (slice(None), at)
            return self.t1, index + (slice(None), cs)
        return self.t2, (at, slice(None), cs)

    def landing(self, phase, part, k):
        return (k,) + (slice(None),) * (4 - phase) + (self.parts[part][1],)

    def send(self, phase):
        for part, _ in self.parts:
            axis = (part + phase - 1) % 3
            for k, by in enumerate((2, 1, 3)):
                to = self.near[axis, by]

                def make(part=part, axis=axis, to=to, k=k):
                    ref, index = self.source(phase, part, to[0][axis])
                    return ref.at[index], self.inc[phase].at[self.landing(phase, part, k)], to[1]

                self.sends.start((self.key, part, phase, by), make)

    def add(self, phase):
        for part, cs in self.parts:
            axis = (part + phase - 1) % 3
            ref, index = self.source(phase, part, self.spot[axis])
            acc = ref[index].astype(F32)
            for k, by in enumerate((2, 1, 3)):
                here = self.landing(phase, part, k)
                source = self.near[axis, 4 - by][1]
                self.sends.arrived((self.key, part, phase, by), self.inc[phase].at[here], source)
                acc = acc + self.inc[phase][here].astype(F32)
            if phase == 1:
                self.t1[:, :, :, cs] = acc.astype(BF)
            elif phase == 2:
                self.t2[:, :, cs] = acc.astype(BF)
            else:
                self.out[self.core, :, cs] = acc

    def add_pair(self):
        for x in range(4):
            self.sends.arrived((self.key, "pair", x), self.inc0.at[x], self.sibling)
            both = self.grads[self.core, pl.ds(16 * x, 16)].astype(F32) + self.inc0[x].astype(F32)
            self.total[x] = both.reshape(4, 4, 16, 896).astype(BF)

    def swap(self):
        self.sends.start(
            (self.key, "last"), lambda: (self.out.at[self.core], self.out.at[self.core], self.sibling)
        )

    def swapped(self):
        self.sends.arrived((self.key, "last"), self.out.at[self.other], self.sibling)


def backward_kernel(
    split_ref, x_ref, gain_ref, mask_ref, place_ref, proj_ref, dz_ref, dmid_ref, h1_ref, lat_ref,
    w_ref, down_ref, up_ref, pers_ref, wf_ref, lw_ref, ffn_ref, back_ref,
    act_out, grad_out, ffn_out, heads_out,
    dh_ref, dlat_ref, dlat_half, grads_ref, *rest,
):
    step = pl.program_id(0)
    send_sem, recv_sem = rest[-2:]
    sends = Sends(send_sem, recv_sem)
    first_sums = Scatter(sends, 0, ffn_ref, *rest[:8])
    last_sums = Scatter(sends, 1, grads_ref, *rest[8:16])
    flat = rest[26]
    ex_act = Exchange(sends, "a", rest[16:21], 1, BY_CORE)
    ex_grad = Exchange(sends, "g", rest[21:26], 1, BY_CORE)

    def one_head():
        pieces = [proj_ref[:, p * HEAD : (p + 1) * HEAD] for p in range(7)]
        q, k, v = (pieces[i].astype(BF) for i in range(3))
        pk, pv = pers_ref[0], pers_ref[1]
        near, far = attend(q, k, v, pk, pv, allowed_mask(split_ref))
        near_half = near.astype(BF)
        dz = dz_ref[...]
        d_near = by_group(lambda s, g: dot(dz[s], v[s], NT))
        d_far = dot(dz, pv, NT)
        d_v = by_group(lambda s, g: dot(near_half[s], dz[s], TN))
        total = jnp.sum(d_near * near, axis=-1, keepdims=True) + jnp.sum(
            d_far * far, axis=-1, keepdims=True
        )
        ds_near = (near * (d_near - total) * SCALE).astype(BF)
        ds_far = (far * (d_far - total) * SCALE).astype(BF)
        d_q = by_group(lambda s, g: dot(ds_near[s], k[s])) + dot(ds_far, pk)
        d_k = by_group(lambda s, g: dot(ds_near[s], q[s], TN))

        dzf = dz.astype(F32)
        opening = jax.nn.sigmoid(pieces[6])
        kn, k_inv = unit(pieces[3])
        qn, q_inv = unit(pieces[5])
        kept = memory_terms(kn, qn, pieces[4], wf_ref, lw_ref, plain, dot1)
        mem = memory_out(kept, dot1)
        d_open = dzf * mem * (opening * (1.0 - opening))
        d_kn, d_qn, d_mv = memory_bwd(kept, dzf * opening)
        d_mk = unit_bwd(d_kn, pieces[3], k_inv)
        d_mq = unit_bwd(d_qn, pieces[5], q_inv)
        dy = [item.astype(BF) for item in (d_q, d_k, d_v, d_mk, d_mv, d_mq, d_open)]
        dh_ref[...] += dot(jnp.concatenate(dy, axis=1), w_ref[0], NT)
        first = pl.multiple_of(step * 8, 8)
        for part in range(7):
            s = slice(part * AR, (part + 1) * AR)
            dlat_ref[:, s] += dot(dy[part], up_ref[0, :, s])
            grads_ref[1, pl.ds(first, 8), :, s] = (
                dot(dy[part], lat_ref[:, s], TN).reshape(8, 16, AR).astype(BF)
            )

    @pl.when(step == 0)
    def _():
        greet(first_sums.peers())
        ex_act.fill(0, flat, [back_ref[...]])
        ex_act.launch(0)
        first_sums.pair()
        dh_ref[...] = jnp.zeros_like(dh_ref)
        dlat_ref[...] = jnp.zeros_like(dlat_ref)

    @pl.when(step == 1)
    def _():
        ex_act.land(0)
        ex_act.launch(1)

    @pl.when(step == 2)
    def _():
        first_sums.add_pair()
        first_sums.send(1)

    @pl.when(step == 3)
    def _():
        ex_act.land(1)
        ex_act.launch(2)

    @pl.when(step == 5)
    def _():
        first_sums.add(1)
        first_sums.send(2)
        ex_act.land(2)
        ex_act.launch(3)

    @pl.when(step == 6)
    def _():
        first_sums.add(2)
        first_sums.send(3)

    @pl.when(step == 7)
    def _():
        first_sums.add(3)
        first_sums.swap()
        ex_act.land(3)
        act_out[...] = ex_act.bufs[4][...]

    one_head()

    @pl.when(step == H - 1)
    def _():
        mask = mask_ref[...]
        for p in range(7):
            s = slice(p * AR, (p + 1) * AR)
            dlat_half[:, s] = (dlat_ref[:, s] * mask).astype(BF)
        grads_ref[0] = dot(h1_ref[...], dlat_half[...], TN).reshape(64, 16, 7 * AR).astype(BF)
        last_sums.pair()
        dh = dh_ref[...] + dot(dlat_half[...], down_ref[0], NT)
        x = x_ref[...].astype(F32)
        inv = lax.rsqrt(jnp.mean(x * x, axis=-1, keepdims=True) + EPS)
        dx = (dmid_ref[...] + norm_bwd(dh, x, inv, gain_ref[...])).astype(BF)
        ex_grad.fill(
            0, flat, [dot(place_ref[m], dx[m * GROUP : (m + 1) * GROUP]) for m in range(MB)]
        )
        ex_grad.launch(0)
        last_sums.add_pair()
        ex_grad.land(0)
        ex_grad.launch(1)
        last_sums.send(1)
        first_sums.swapped()
        ffn_out[...] = first_sums.out[...]
        ex_grad.land(1)
        ex_grad.launch(2)
        last_sums.add(1)
        last_sums.send(2)
        ex_grad.land(2)
        ex_grad.launch(3)
        last_sums.add(2)
        last_sums.send(3)
        ex_grad.land(3)
        grad_out[...] = ex_grad.bufs[4][...]
        last_sums.add(3)
        last_sums.swap()
        last_sums.swapped()
        heads_out[...] = last_sums.out[...]
        sends.drain()


def backward_call(split, x, gain, mask, place, proj, dz, dmid, h1, lat, a1, persistent, wf, lw, grads_ffn, back):
    once = pl.Buffered(1)
    whole = lambda *shape: pl.BlockSpec(shape, lambda s: (0,) * len(shape), pipeline_mode=once)
    head = lambda s: s
    buffers = [
        pltpu.VMEM((2, 16, 896), F32),
        pltpu.VMEM((4, 16, 16, 896), BF),
        pltpu.VMEM((4, 4, 4, 16, 896), BF),
        pltpu.VMEM((3, 4, 4, 16, 896), BF),
        pltpu.VMEM((3, 4, 16, 896), BF),
        pltpu.VMEM((3, 16, 896), BF),
        pltpu.VMEM((4, 4, 16, 896), BF),
        pltpu.VMEM((4, 16, 896), BF),
    ]
    slots = 2 * (4 + 3 * 9 + 1) + 2 * (1 + 3 * 6)
    return pl.pallas_call(
        backward_kernel,
        grid=(H,),
        out_shape=(
            jax.ShapeDtypeStruct((4, 4, 4, 16, 256), BF),
            jax.ShapeDtypeStruct((4, 4, 4, 16, 256), BF),
            jax.ShapeDtypeStruct((2, 16, 896), F32),
            jax.ShapeDtypeStruct((2, 16, 896), F32),
        ),
        in_specs=[
            pl.BlockSpec(memory_space=pltpu.SMEM),
            whole(ROWS, D),
            whole(1, D),
            whole(ROWS, AR),
            whole(MB, GROUP, GROUP),
            pl.BlockSpec((ROWS, HCOLS), lambda s: (0, head(s))),
            pl.BlockSpec((ROWS, HEAD), lambda s: (0, head(s))),
            whole(ROWS, D),
            whole(ROWS, D),
            whole(ROWS, 7 * AR),
            pl.BlockSpec((1, D, HCOLS), lambda s: (s // 4, 0, s % 4)),
            pl.BlockSpec((1, D, HCOLS), lambda s: (0, 0, 4), pipeline_mode=once),
            pl.BlockSpec((1, HEAD, HCOLS), lambda s: (1, head(s), 4)),
            pl.BlockSpec((2, NP, HEAD), lambda s: (0, 0, head(s))),
            pl.BlockSpec((1, MB, GROUP, GROUP), lambda s: (head(s), 0, 0, 0)),
            pl.BlockSpec((1, MB, 8, GROUP), lambda s: (head(s), 0, 0, 0)),
            pl.BlockSpec(memory_space=pltpu.VMEM),
            pl.BlockSpec(memory_space=pltpu.VMEM),
        ],
        out_specs=(
            whole(4, 4, 4, 16, 256),
            whole(4, 4, 4, 16, 256),
            pl.BlockSpec(memory_space=pltpu.VMEM),
            pl.BlockSpec(memory_space=pltpu.VMEM),
        ),
        scratch_shapes=[
            pltpu.VMEM((ROWS, D), F32),
            pltpu.VMEM((ROWS, 7 * AR), F32),
            pltpu.VMEM((ROWS, 7 * AR), BF),
            pltpu.VMEM((2, 64, 16, 896), BF),
        ]
        + buffers * 2
        + [pltpu.VMEM((4, 4, 4, 16, 256), BF)] * 10
        + [pltpu.VMEM((16 * N_DEV, 128), F32)]
        + [pltpu.SemaphoreType.DMA((slots,)), pltpu.SemaphoreType.DMA((slots,))],
        compiler_params=pltpu.CompilerParams(
            collective_id=1, has_side_effects=True, vmem_limit_bytes=VMEM_LIMIT
        ),
        name="backward_scatter",
    )(split, x, gain, mask, place, proj, dz, dmid, h1, lat, a1, a1, a1, persistent, wf, lw, grads_ffn, back)


def selector(parts):
    rows = lax.broadcasted_iota(jnp.int32, (parts * R, parts * AR), 0)
    cols = lax.broadcasted_iota(jnp.int32, (parts * R, parts * AR), 1)
    return (rows // R == cols // AR) & (rows % R == cols % R)


def adapter_of(shape):
    return (lax.broadcasted_iota(jnp.int32, shape, len(shape) - 1) % AR) // R


def pack_kernel(
    lengths_ref, ids_ref, route_ref, tok_ref, cot_ref, decays_ref,
    w_in, w_out, w_up, w_down, in_down, in_up, out_down, out_up, up_down, up_up, down_down, down_up,
    sent, item0, item1, item2, item3, to_ref, place_ref, mask_ref, split_ref,
    flat, wide,
):
    me = lax.axis_index("fsdp")

    below = lax.broadcasted_iota(jnp.int32, (GROUP, GROUP), 0)
    along = lax.broadcasted_iota(jnp.int32, (GROUP, GROUP), 1)
    for m in range(MB):
        to = (below == route_ref[m, pl.ds(me, 1), :] // GROUP).astype(BF)
        to_ref[m] = to
        for ref, first in ((tok_ref, m * 8), (cot_ref, (MB + m) * 8)):
            value = dot(to, ref[m])
            for j in range(8):
                flat[pl.ds(first + j, N_DEV, stride=TOKEN_ROWS), :] = value[:, j * 128 : (j + 1) * 128]
    rates = [dot(to_ref[m], decays_ref[m], NT) for m in range(MB)]
    rates = jnp.concatenate(rates + [jnp.zeros((GROUP, 128 - MB * 3 * H), F32)], axis=1)
    flat[pl.ds(4 * D // 128, N_DEV, stride=TOKEN_ROWS), :] = rates
    for j in range(4 * D // 128 + 1, TOKEN_ROWS):
        flat[pl.ds(j, N_DEV, stride=TOKEN_ROWS), :] = jnp.zeros((N_DEV, 128), F32)
    sent[...] = flat[...].reshape(N_DEV, TOKEN_ROWS, 128).astype(BF)

    for m in range(MB):
        blocks = route_ref[m]
        landing = jnp.sum(jnp.where(blocks // GROUP == me, blocks % GROUP, 0), axis=1, keepdims=True)
        place_ref[m] = (landing == along).astype(BF)
        early = lengths_ref[m, 0]
        row = lax.broadcasted_iota(jnp.int32, (GROUP, AR), 0)
        adapter = jnp.where(row < early, ids_ref[m, 0], ids_ref[m, 1])
        mask_ref[m * GROUP : (m + 1) * GROUP, :] = (adapter == adapter_of((GROUP, AR))).astype(F32)
        split_ref[m] = jnp.where(early < GROUP, 1.0, 0.0)

    select = selector(7).astype(BF)
    items = (item1, item2, item3)

    def ranks(ref, parts):
        cut_to = select[: parts * R, : parts * AR]
        rows = ref.shape[1]
        out = jnp.zeros((rows, parts * AR), F32)
        for a in range(NAD):
            out = out + jnp.where(adapter_of(out.shape) == a, dot(ref[a], cut_to), 0.0)
        return out

    def ranks_t(ref, parts):
        cut_to = select[: parts * R, : parts * AR]
        cols = ref.shape[2]
        out = jnp.zeros((cols, parts * AR), F32)
        for a in range(NAD):
            out = out + jnp.where(adapter_of(out.shape) == a, dot(ref[a], cut_to, TN), 0.0)
        return out

    def ranks_mid(ref, parts):
        rows = ref.shape[0]
        value = ref[...].astype(F32).reshape(rows * NAD, parts * R).astype(BF)
        value = dot(value, select[: parts * R, : parts * AR]).reshape(rows, NAD, parts * AR)
        mine = adapter_of(value.shape) == lax.broadcasted_iota(jnp.int32, value.shape, 1)
        return jnp.sum(jnp.where(mine, value, 0.0), axis=1)

    def tall(value):
        return jnp.concatenate([value, jnp.zeros((FF_PAD - FF_SHARD, value.shape[1]), F32)], axis=0)

    for h in range(H):
        for part in range(7):
            at = (h % 4) * HCOLS + part * HEAD
            item0[h // 4, :, at : at + HEAD] = w_in[:, part * D + h * HEAD : part * D + (h + 1) * HEAD].astype(F32)
    item0[0, :, 4 * HCOLS :] = ranks(in_down, 7)
    item0[1, :, 4 * HCOLS :] = ranks(in_up, 7)

    item1[0, :, 0:128] = ranks(out_down, 1)
    item1[0, :, 128:384] = ranks(up_down, 2)
    item1[0, :, 384:512] = ranks(out_up, 1)
    item1[0, :, 512:640] = ranks(down_up, 1)
    item1[0, :, 640:D] = jnp.zeros((8, D - 640), F32)
    item1[1, :, 0:D] = w_out[...].astype(F32)

    wide[...] = w_up[...].astype(F32)
    span = 8 * FF_SHARD
    rows = lax.broadcasted_iota(jnp.int32, (span, 3 * 64), 0)
    cols = lax.broadcasted_iota(jnp.int32, (span, 3 * 64), 1)
    unit_at = (cols // 64) * 8 + cols % 8
    spread = ((rows == (cols % 64) // 8 * FF_SHARD + unit_at) & (unit_at < FF_SHARD)).astype(BF)
    pieces = [wide[:, c * span : (c + 1) * span] for c in range(32)]
    moved_up = dot(jnp.concatenate(pieces, axis=0).astype(BF), spread)
    for c in range(32):
        half, chunk = c // 16, c % 16
        for k in range(3):
            at = (D if k == 0 else 0) + chunk * 64
            items[k][half, :, at : at + 64] = moved_up[c * 8 : (c + 1) * 8, k * 64 : (k + 1) * 64]
    down = tall(w_down[...].astype(F32))
    uu, dd = tall(ranks_mid(up_up, 2)), tall(ranks_t(down_down, 1))
    for k in range(3):
        at = (D if k == 0 else 0) + FB
        s = slice(k * 8, (k + 1) * 8)
        items[k][0, :, at : at + 768] = down[s, :768]
        items[k][1, :, at : at + 256] = down[s, 768:]
        items[k][1, :, at + 256 : at + 512] = uu[s]
        items[k][1, :, at + 512 : at + 640] = dd[s]
        items[k][1, :, at + 640 : at + 768] = jnp.zeros((8, 128), F32)


def pack_call(lengths, ids, route, tokens, cotangent, decays, weights):
    smem, vmem = pl.BlockSpec(memory_space=pltpu.SMEM), pl.BlockSpec(memory_space=pltpu.VMEM)
    return pl.pallas_call(
        pack_kernel,
        out_shape=(jax.ShapeDtypeStruct((N_DEV, TOKEN_ROWS, 128), BF),)
        + tuple(jax.ShapeDtypeStruct((2, 8, width), F32) for width in WIDTHS)
        + (
            jax.ShapeDtypeStruct((MB, GROUP, GROUP), BF),
            jax.ShapeDtypeStruct((MB, GROUP, GROUP), BF),
            jax.ShapeDtypeStruct((ROWS, AR), F32),
            jax.ShapeDtypeStruct((MB,), F32),
        ),
        in_specs=[smem] * 2 + [vmem] * (4 + len(weights)),
        out_specs=(vmem,) * 8 + (smem,),
        scratch_shapes=[
            pltpu.VMEM((N_DEV * TOKEN_ROWS, 128), F32),
            pltpu.VMEM((8, 2 * FF), F32),
        ],
        compiler_params=pltpu.CompilerParams(vmem_limit_bytes=VMEM_LIMIT),
        name="pack",
    )(lengths, ids, route, tokens, cotangent, decays, *weights)


def unpack_kernel(
    core_ref, to_ref, act_ref, grad_ref, ffn_ref, heads_ref,
    out_ref, back_ref, in_down, in_up, out_down, out_up, up_down, up_up, down_down, down_up,
    flat,
):
    core = core_ref[0]
    for source, target in ((act_ref, out_ref), (grad_ref, back_ref)):
        got = [source[:, :, :, :, c * 128 : (c + 1) * 128].astype(F32) for c in range(2)]
        flat[...] = jnp.stack(got, axis=3).reshape(16 * N_DEV, 128)
        for m in range(MB):
            value = jnp.concatenate(
                [flat[pl.ds(m * 8 + j, N_DEV, stride=16), :].astype(BF) for j in range(8)], axis=1
            )
            target[m] = dot(to_ref[m], value, TN).astype(BF)
    own = pl.ds(pl.multiple_of(core * 8, 8), 8)
    heads = [heads_ref[half, own, :] for half in range(2)]
    ffn = [ffn_ref[half, own, :] for half in range(2)]
    select = selector(7).astype(F32)

    def tall(value, width):
        return jnp.concatenate([value[:, k * width : (k + 1) * width] for k in range(3)], axis=0)

    def put(ref, value, parts):
        rows, width = value.shape
        shape = (NAD, rows, width)
        mine = adapter_of(shape) == lax.broadcasted_iota(jnp.int32, shape, 0)
        apart = jnp.where(mine, value[None], 0.0).reshape(NAD * rows, width)
        ref[...] = exact(apart, select[: parts * R, :width], NT).reshape(NAD, rows, parts * R)

    put(in_down, heads[0], 7)
    put(in_up, heads[1], 7)
    put(out_down, ffn[1][:, 384:512], 1)
    put(out_up, ffn[1][:, 512:640], 1)
    put(up_down, ffn[1][:, 640:896], 2)
    put(down_up, ffn[0][:, 768:], 1)
    value = tall(ffn[0][:, :768], 256)
    shape = (FF_PAD, NAD, 2 * AR)
    mine = adapter_of(shape) == lax.broadcasted_iota(jnp.int32, shape, 1)
    apart = jnp.where(mine, jnp.broadcast_to(value[:, None, :], shape), 0.0).reshape(FF_PAD * NAD, 2 * AR)
    up_up[...] = exact(apart, select[: 2 * R, : 2 * AR], NT).reshape(FF_PAD, NAD, 2 * R)[:FF_SHARD]
    value = tall(ffn[1][:, :384], AR)
    for a in range(NAD):
        mine = jnp.where(adapter_of(value.shape) == a, value, 0.0)
        down_down[a] = exact(select[:R, :AR], mine, NT)[:, :FF_SHARD]


def unpack_call(core, to, act, grad, ffn_sums, heads_sums, shapes):
    smem, vmem = pl.BlockSpec(memory_space=pltpu.SMEM), pl.BlockSpec(memory_space=pltpu.VMEM)
    return pl.pallas_call(
        unpack_kernel,
        out_shape=(jax.ShapeDtypeStruct((MB, GROUP, D), BF),) * 2
        + tuple(jax.ShapeDtypeStruct(shape, F32) for shape in shapes),
        in_specs=[smem] + [vmem] * 5,
        out_specs=(vmem,) * (2 + len(shapes)),
        scratch_shapes=[pltpu.VMEM((16 * N_DEV, 128), F32)],
        compiler_params=pltpu.CompilerParams(vmem_limit_bytes=VMEM_LIMIT),
        name="unpack",
    )(core, to, act, grad, ffn_sums, heads_sums)


def body(
    tokens, cotangent, decays, route, lengths, adapter_ids, gain_mix, gain_ffn, persistent,
    w_in, w_out, w_up, w_down, in_down, in_up, out_down, out_up, up_down, up_up, down_down, down_up,
):
    me = lax.axis_index("fsdp").astype(jnp.int32)
    weights = (
        w_in, w_out, w_up, w_down, in_down, in_up, out_down, out_up, up_down, up_up, down_down, down_up,
    )
    turned = lambda value: jnp.swapaxes(value, 1, 2)
    views = (None,) * 5 + (turned, None, turned, None, lambda value: value.transpose(2, 0, 1), turned, turned)
    back_views = views[:9] + (lambda value: value.transpose(1, 2, 0), turned, turned)
    viewed = [item if view is None else view(item) for item, view in zip(weights, views)]
    sent, *items, to, place, mask, split = pack_call(
        lengths[:, 0], adapter_ids[:, 0], route.reshape(MB, N_DEV, GROUP), tokens, cotangent, turned(decays), viewed
    )
    gain_mix, gain_ffn = gain_mix[None, :], gain_ffn[None, :]
    a1, _, _, _, proj, x, h1, lat, wf, lw, back, dz, dmid, grads_ffn = forward_call(
        split, sent, gain_mix, gain_ffn, mask, place, persistent, items
    )
    act, grad, ffn_sums, heads_sums = backward_call(
        split, x, gain_mix, mask, place, proj, dz, dmid, h1, lat, a1.reshape(2, D, WIDTHS[0]), persistent, wf, lw,
        grads_ffn, back,
    )
    outs = unpack_call((me % 2)[None], to, act, grad, ffn_sums, heads_sums, [item.shape for item in viewed[4:]])
    grads = [item if view is None else view(item) for item, view in zip(outs[2:], back_views[4:])]
    return tuple(outs[:2]) + tuple(grads)


def solution(mesh):
    rows, cols = P(None, "fsdp", None), P(None, None, "fsdp")
    weight = P("fsdp", None)
    return jax.shard_map(
        body,
        mesh=mesh,
        in_specs=(rows, rows, rows, P(), rows, rows, P(), P(), P())
        + (weight,) * 4
        + (rows, cols) * 4,
        out_specs=(rows, rows) + (rows, cols) * 4,
        check_vma=False,
    )
```

```python
import functools
import math

import jax
import jax.numpy as jnp
from jax import lax
from jax.experimental import pallas as pl
from jax.experimental.pallas import tpu as pltpu
from jax.sharding import PartitionSpec as P

D = 1024
H = 8
HEAD = 128
FF = 2816
R = 16
NAD = 8
NP = 16
SPAN = 64
GROUP = 128
MB = 2
ROWS = MB * GROUP
N_DEV = 128
AR = NAD * R
HCOLS = 7 * HEAD
FF_SHARD = FF // N_DEV
FF_PAD = 24
FFP = FF_PAD * N_DEV
FB = 1024
EPS = 1e-05
SCALE = 1.0 / math.sqrt(HEAD)
VMEM_LIMIT = 60 * 1024 * 1024
BF = jnp.bfloat16
F32 = jnp.float32

NN = (((1,), (0,)), ((), ()))
NT = (((1,), (1,)), ((), ()))
TN = (((0,), (0,)), ((), ()))


def dot(left, right, dims=NN):
    return lax.dot_general(left, right, dims, preferred_element_type=F32)


def exact(left, right, dims=NN):
    return lax.dot_general(
        left, right, dims, precision=lax.Precision.HIGHEST, preferred_element_type=F32
    )


def halves(value):
    high = value.astype(BF)
    return high, (value - high.astype(F32)).astype(BF)


def dot3(left, right, dims=NN):
    lh, ll = left
    rh, rl = right
    return dot(lh, rh, dims) + (dot(lh, rl, dims) + dot(ll, rh, dims))


def norm_fwd(values, gain):
    inv = lax.rsqrt(jnp.mean(values * values, axis=-1, keepdims=True) + EPS)
    return values * inv * gain, inv


def norm_bwd(grad, values, inv, gain):
    scaled = grad * gain
    return inv * (scaled - values * (inv * inv * jnp.mean(values * scaled, axis=-1, keepdims=True)))


def decay_kernel(split_ref, dec_ref, dect_ref, wf_ref, lw_ref):
    rows = lax.broadcasted_iota(jnp.int32, (GROUP, GROUP), 0)
    cols = lax.broadcasted_iota(jnp.int32, (GROUP, GROUP), 1)
    lower = (rows >= cols) & ((rows >= SPAN) == (cols >= SPAN))
    tri = lower.astype(F32)
    second = rows >= SPAN
    for g in range(MB):
        keep = 1.0 - split_ref[g]
        here = dec_ref[g * GROUP : (g + 1) * GROUP, :]
        here_t = dect_ref[:, g * GROUP : (g + 1) * GROUP]
        run = exact(tri, jnp.log(here[:, : 2 * H]))
        run_t = exact(jnp.log(here_t[: 2 * H, :]), tri, NT)
        for h in range(H):
            gap = run[:, h : h + 1] - run_t[h : h + 1, :]
            retain = jnp.exp(jnp.where(lower, gap, -1e30))
            gap = run[:, H + h : H + h + 1] - run_t[H + h : H + h + 1, :]
            moment = jnp.exp(jnp.where(lower, gap, -1e30))
            pairs = exact(retain, moment)
            theta = here_t[2 * H + h : 2 * H + h + 1, :]
            moment_run = jnp.exp(run_t[H + h : H + h + 1, :])
            carry = jnp.sum(retain * moment_run, axis=1, keepdims=True)
            last_weight = pairs[SPAN - 1 : SPAN, :] * theta * keep
            last_moment = moment[SPAN - 1 : SPAN, :] * theta * keep
            across = jnp.exp(run[:, h : h + 1]) * last_weight + carry * last_moment
            wf_ref[h, g] = pairs * theta + jnp.where(second, across, 0.0)
            lw_ref[h, g] = jnp.broadcast_to(last_weight, (8, GROUP))


def allowed_mask(split_ref):
    rows = lax.broadcasted_iota(jnp.int32, (ROWS, GROUP), 0)
    cols = lax.broadcasted_iota(jnp.int32, (ROWS, GROUP), 1)
    local = rows % GROUP
    group = rows // GROUP
    split = jnp.where(group == 0, split_ref[0], split_ref[1]) > 0.5
    return (local >= cols) & jnp.logical_not(split & (local >= SPAN) & (cols < SPAN))


def by_group(make):
    return jnp.concatenate([make(slice(0, GROUP), 0), make(slice(GROUP, ROWS), 1)], axis=0)


def attend(q, k, v, pk, pv, allowed):
    near = by_group(lambda s, g: dot(q[s], k[s], NT))
    far = dot(q, pk, NT) * SCALE
    near = jnp.where(allowed, near * SCALE, -1000000000.0)
    top = jnp.maximum(
        jnp.max(near, axis=-1, keepdims=True), jnp.max(far, axis=-1, keepdims=True)
    )
    near = jnp.exp(near - top)
    far = jnp.exp(far - top)
    inv = 1.0 / (jnp.sum(near, axis=-1, keepdims=True) + jnp.sum(far, axis=-1, keepdims=True))
    near = near * inv
    far = far * inv
    return near, far


def attend_out(near_half, far_half, v, pv):
    return by_group(lambda s, g: dot(near_half[s], v[s])) + dot(far_half, pv)


def unit(values):
    inv = lax.rsqrt(jnp.mean(values * values, axis=-1, keepdims=True) + EPS)
    return values * (inv * SCALE), inv


def unit_bwd(grad, values, inv):
    return (inv * SCALE) * (
        grad - values * (inv * inv * jnp.mean(values * grad, axis=-1, keepdims=True))
    )


def plain(value):
    return (value.astype(BF),)


def dot1(left, right, dims=NN):
    return dot(left[0], right[0], dims)


def memory_terms(kn, qn, mv, wf_ref, lw_ref, halves=halves, dot3=dot3):
    second = lax.broadcasted_iota(jnp.int32, (GROUP, GROUP), 0) >= SPAN
    kept = []
    for g in range(MB):
        s = slice(g * GROUP, (g + 1) * GROUP)
        kh, qh = halves(kn[s]), halves(qn[s])
        wf = wf_ref[0, g]
        lw = jnp.where(second, lw_ref[0, g][0:1, :], 0.0)
        kk = dot3(kh, kh, NT) * lw
        qk = dot3(qh, kh, NT) * wf
        kk_half = halves(kk)
        mvh = halves(mv[s])
        err = mv[s] - dot3(kk_half, mvh)
        errh = halves(err)
        qk_half = halves(qk)
        kept.append((kh, qh, wf, lw, kk_half, qk_half, mvh, errh))
    return kept


def memory_out(kept, dot3=dot3):
    return jnp.concatenate([dot3(item[5], item[7]) for item in kept], axis=0)


def memory_bwd(kept, grad, halves=plain, dot3=dot1):
    grads_k, grads_q, grads_v = [], [], []
    for g in range(MB):
        kh, qh, wf, lw, kk_half, qk_half, mvh, errh = kept[g]
        gh = halves(grad[g * GROUP : (g + 1) * GROUP])
        d_qk = dot3(gh, errh, NT) * wf
        d_err = dot3(qk_half, gh, TN)
        deh = halves(d_err)
        d_v = d_err - dot3(kk_half, deh, TN)
        d_kk = dot3(deh, mvh, NT) * lw
        dqh = halves(d_qk)
        dkh = halves(d_kk)
        grads_q.append(dot3(dqh, kh))
        grads_k.append(dot3(dqh, qh, TN) - (dot3(dkh, kh) + dot3(dkh, kh, TN)))
        grads_v.append(d_v)
    return (
        jnp.concatenate(grads_k, axis=0),
        jnp.concatenate(grads_q, axis=0),
        jnp.concatenate(grads_v, axis=0),
    )


AXES = ("x", "z", "y")
MESH = pl.DeviceIdType.MESH


def position():
    me = lax.axis_index("fsdp")
    chip = me // 2
    return me % 2, (chip // 16, (chip // 4) % 4, chip % 4)


def device(core, spot):
    return (((spot[0] * 4 + spot[1]) * 4 + spot[2]) * 2 + core,)


def moved(spot, axis, by):
    return tuple((v + by + 4) % 4 if i == axis else v for i, v in enumerate(spot))


def cut(lanes, count, first=0):
    base, extra = divmod(lanes, count)
    runs, at = [], 0
    for i in range(count):
        size = base + (1 if (i - first) % count < extra else 0)
        runs.append((at * 128, size * 128))
        at += size
    return runs


def neighbours(core, spot):
    found = {}
    for axis in range(3):
        for by in (1, 2, 3):
            there = moved(spot, axis, by)
            found[axis, by] = (there, device(core, there))
    return found


class Sends:
    def __init__(self, send_sem, recv_sem):
        self.send_sem, self.recv_sem = send_sem, recv_sem
        self.slots, self.open = {}, []

    def copy(self, name, src, dst, target):
        slot = self.slots.setdefault(name, len(self.slots))
        return pltpu.make_async_remote_copy(
            src_ref=src, dst_ref=dst, send_sem=self.send_sem.at[slot], recv_sem=self.recv_sem.at[slot],
            device_id=target, device_id_type=MESH,
        )

    def start(self, name, make):
        self.copy(name, *make()).start()
        self.open.append((name, make))

    def arrived(self, name, ref, target):
        self.copy(name, ref, ref, target).wait_recv()

    def drain(self):
        for name, make in self.open:
            self.copy(name, *make()).wait_send()
        self.open = []


def greet(targets):
    barrier = pltpu.get_barrier_semaphore()
    for target in targets:
        pl.semaphore_signal(barrier, inc=1, device_id=target, device_id_type=MESH)
    pl.semaphore_wait(barrier, len(targets))


LONGER = (0, 2, 2, 1)
TURNED = {(2, 0), (2, 2), (3, 1)}


class Gather:
    def __init__(self, sends, outs, widths):
        self.sends, self.outs = sends, outs
        self.core, self.spot = position()
        self.other = 1 - self.core
        self.sibling = device(1 - self.core, self.spot)
        self.near = neighbours(self.core, self.spot)
        self.jobs = [
            [(i, part, cols) for part, cols in enumerate(cut(width // 128, 3, LONGER[i]))]
            for i, width in enumerate(widths)
        ]
        self.forwards = [[] for _ in widths]

    def peers(self):
        return [self.sibling] + [self.near[a, by][1] for a in range(3) for by in (1, 3)]

    def block(self, i, whole_axes, at, cols, half=None):
        index = [pl.ds(0, 4) if a in whole_axes else pl.ds(at[a], 1) for a in range(3)]
        half = self.core if half is None else half
        return self.outs[i].at[half, index[0], index[1], index[2], :, pl.ds(cols[0], cols[1])]

    def push(self, name, target, *where):
        def make():
            ref = self.block(*where)
            return ref, ref, target

        self.sends.start(name, make)

    def forward(self, name, *where):
        self.push(name, self.sibling, *where)
        self.forwards[where[0]].append((name, where))

    def plan(self, item, phase):
        for i, part, cols in self.jobs[item]:
            axis = (part + phase) % 3
            done = [(part + p) % 3 for p in range(phase)]
            sides = [self.near[axis, by] for by in (1, 3, 2)]
            halves_of = [(cols[0] + at, size) for at, size in cut(cols[1] // 128, 2, (i, part) in TURNED)]
            yield i, part, cols, done, sides, halves_of

    def begin(self, item, phase):
        for i, part, cols, done, (right, left, far), two in self.plan(item, phase):
            if phase == 0:
                for side, there in (("f", far), ("r", right), ("l", left)):
                    self.push((i, part, phase, side), there[1], i, done, self.spot, cols)
                continue
            for step, (a, b) in enumerate(((0, 1), (1, 0))):
                self.push((i, part, phase, "r", step), right[1], i, done, self.spot, two[a])
                self.push((i, part, phase, "l", step), left[1], i, done, self.spot, two[b])
            if phase == 2:
                self.forward((i, part, "f"), i, done, self.spot, cols)

    def relay(self, item, phase):
        for i, part, cols, done, (right, left, _), two in self.plan(item, phase):
            for side, source, target, cc in (("r", left, right, two[0]), ("l", right, left, two[1])):
                where = (i, done, source[0], cc)
                self.sends.arrived((i, part, phase, side, 0), self.block(*where), source[1])
                self.push((i, part, phase, side, 2), target[1], *where)
                if phase == 2:
                    self.forward((i, part, "f", side, 0), *where)

    def finish(self, item, phase):
        for i, part, cols, done, (right, left, far), two in self.plan(item, phase):
            if phase == 0:
                for side, source in (("r", left), ("l", right), ("f", far)):
                    self.sends.arrived((i, part, phase, side), self.block(i, done, source[0], cols), source[1])
                continue
            for side, step, at, cc, source in (
                ("r", 1, left, two[1], left),
                ("l", 1, right, two[0], right),
                ("r", 2, far, two[0], left),
                ("l", 2, far, two[1], right),
            ):
                where = (i, done, at[0], cc)
                self.sends.arrived((i, part, phase, side, step), self.block(*where), source[1])
                if phase == 2:
                    self.forward((i, part, "f", side, step), *where)

    def received(self, item):
        for name, (i, done, at, cc) in self.forwards[item]:
            self.sends.arrived(name, self.block(i, done, at, cc, self.other), self.sibling)


class Exchange:
    def __init__(self, sends, key, bufs, lanes, jobs):
        self.sends, self.key, self.bufs, self.lanes, self.jobs = sends, key, bufs, lanes, jobs
        self.core, self.spot = position()
        self.other = 1 - self.core
        self.mine, self.theirs = (
            [pl.ds(pl.multiple_of(lane * 256 + core * 128, 128), 128) for lane in range(lanes)]
            for core in (self.core, self.other)
        )
        self.sibling = device(self.other, self.spot)
        self.near = neighbours(self.core, self.spot)

    def index(self, cols, axis=None, where=None):
        return tuple(pl.ds(where, 1) if a == axis else pl.ds(0, 4) for a in range(3)) + (slice(None), cols)

    def moves(self, stage, which):
        before, after = self.bufs[stage], self.bufs[stage + 1]
        away, stay = [], []
        if stage == 0:
            for lane in range(self.lanes):
                mine, theirs = self.index(self.mine[lane]), self.index(self.theirs[lane])
                away.append(((self.key, 0, lane), theirs, mine, self.sibling, theirs, self.sibling))
                stay.append(mine)
            return before, after, away, stay
        for number, (lo, width, first) in enumerate(self.jobs):
            if which is not None and number not in which:
                continue
            axis = (first + stage - 1) % 3
            cols = pl.ds(lo, width)
            here = self.index(cols, axis, self.spot[axis])
            for by in (2, 1, 3):
                there, target = self.near[axis, by]
                behind, source = self.near[axis, 4 - by]
                away.append(
                    (
                        (self.key, stage, number, by),
                        self.index(cols, axis, there[axis]),
                        here,
                        target,
                        self.index(cols, axis, behind[axis]),
                        source,
                    )
                )
            stay.append(here)
        return before, after, away, stay

    def launch(self, stage, which=None):
        before, after, away, stay = self.moves(stage, which)
        for name, src, dst, target, _, _ in away:
            self.sends.start(name, lambda src=src, dst=dst, target=target: (before.at[src], after.at[dst], target))
        for here in stay:
            after[here] = before[here]

    def land(self, stage, which=None):
        _, after, away, _ = self.moves(stage, which)
        for name, _, _, _, landing, source in away:
            self.sends.arrived(name, after.at[landing], source)

    def fill(self, lane, scratch, values):
        row = 0
        for value in values:
            for j in range(value.shape[1] // 128):
                scratch[pl.ds(row, N_DEV, stride=16), :] = value[:, j * 128 : (j + 1) * 128].astype(F32)
                row += 1
        blocks = scratch[...].reshape(4, 4, 4, 2, 16, 128)
        for core in range(2):
            at = lane * 256 + core * 128
            self.bufs[0][:, :, :, :, at : at + 128] = blocks[:, :, :, core].astype(BF)


BY_CORE = [(0, 128, 0), (128, 128, 1)]


class RowExchange:
    RADIX = {"x": 4, "z": 4, "y": 4, "c": 2}
    NATURAL = ("x", "z", "y", "c")

    def __init__(self, sends, key, src, dst):
        self.sends, self.key, self.src, self.dst = sends, key, src, dst
        self.core, self.spot = position()
        self.mine, self.theirs = pl.ds(2 * self.core, 2), pl.ds(2 * (1 - self.core), 2)
        self.sibling = device(1 - self.core, self.spot)
        self.near = neighbours(self.core, self.spot)

    def order(self, stage):
        lead = "c" if stage == 0 else AXES[stage - 1]
        return (lead,) + tuple(name for name in self.NATURAL if name != lead)

    def shuffle(self, new, old, rows):
        rest = lax.broadcasted_iota(jnp.int32, (N_DEV, N_DEV), 0)
        digit = {}
        for name in reversed(new):
            digit[name] = rest % self.RADIX[name]
            rest = rest // self.RADIX[name]
        index = 0
        for name in old:
            index = index * self.RADIX[name] + digit[name]
        onehot = (index == lax.broadcasted_iota(jnp.int32, (N_DEV, N_DEV), 1)).astype(BF)
        return dot(onehot, rows).astype(BF)

    def launch(self, stage, value=None):
        if stage == 0:
            self.src[0] = self.shuffle(self.order(0), self.NATURAL, value).reshape(4, 32, 128)
            self.sends.start(
                (self.key, 0), lambda: (self.src.at[0, self.theirs], self.dst.at[0, self.mine], self.sibling)
            )
            return
        rows = self.dst[stage - 1].reshape(N_DEV, 128)
        self.src[stage] = self.shuffle(self.order(stage), self.order(stage - 1), rows).reshape(4, 32, 128)
        axis = stage - 1
        for by in (2, 1, 3):
            there, target = self.near[axis, by]
            self.sends.start(
                (self.key, stage, by),
                lambda there=there, target=target: (
                    self.src.at[stage, there[axis]],
                    self.dst.at[stage, self.spot[axis]],
                    target,
                ),
            )

    def land(self, stage):
        if stage == 0:
            self.dst[0, self.mine] = self.src[0, self.mine]
            self.sends.arrived((self.key, 0), self.dst.at[0, self.theirs], self.sibling)
            return
        axis = stage - 1
        self.dst[stage, self.spot[axis]] = self.src[stage, self.spot[axis]]
        for by in (2, 1, 3):
            there, source = self.near[axis, 4 - by]
            self.sends.arrived((self.key, stage, by), self.dst.at[stage, there[axis]], source)

    def rows(self):
        return self.shuffle(self.NATURAL, self.order(3), self.dst[3].reshape(N_DEV, 128))


WALL = 768
TOKEN_ROWS = 32
WIDTHS = (4 * HCOLS + 7 * AR, D + FB + WALL, FB + WALL, FB + WALL)
FSTEPS = H
BLOCKS = FFP // FB


def forward_kernel(
    split_ref, sent_ref, rates_ref, gain1_ref, gain2_ref, mask_ref, place_ref, pers_ref,
    mine0, mine1, mine2, mine3,
    g0_ref, g1_ref, g2_ref, g3_ref, proj_ref, x_ref, h1_ref, lat_ref, wf_ref, lw_ref, back_ref, dz_ref, dmid_ref,
    grads_ref,
    rate_src, rate_dst, got, flat, d_ref, dec_ref, dect_ref, inc0, inc1, inc2, inc3, stage0, stage1, stage2, stage3,
    w_buf, up_buf, down_buf, z_ref, wup_buf, wd_buf, lead_buf,
    x2_ref, h2_ref, inv_ref, lat_out_ref, lat_up_ref, dl_down_ref, acc_ref, lat_acc_ref, dh_ref, dlat_ref,
    send_sem, recv_sem, local_sem, w_sem, j_sem, token_send, token_recv,
):
    step = pl.program_id(0)
    mine, inc = (mine0, mine1, mine2, mine3), (inc0, inc1, inc2, inc3)
    stage, outs = (stage0, stage1, stage2, stage3), (g0_ref, g1_ref, g2_ref, g3_ref)
    sends = Sends(send_sem, recv_sem)
    ring = Gather(sends, outs, WIDTHS)
    core, spot = ring.core, ring.spot
    other = 1 - core
    items = range(4)
    me = lax.axis_index("fsdp")
    decay_rows = RowExchange(sends, "rates", rate_src, rate_dst)

    def token_copy(k):
        target = (me + k) % N_DEV
        return pltpu.make_async_remote_copy(
            src_ref=sent_ref.at[target], dst_ref=got.at[me], send_sem=token_send.at[k], recv_sem=token_recv.at[k],
            device_id=(target,), device_id_type=MESH,
        )

    def head_loads(h, slot):
        half, place = h // 4, pl.multiple_of((h % 4) * HCOLS, 128)
        return (
            pltpu.make_async_copy(
                g0_ref.at[half, :, :, :, :, pl.ds(place, HCOLS)], w_buf.at[slot], w_sem.at[slot, 0]
            ),
            pltpu.make_async_copy(
                g0_ref.at[1, h // 2, pl.ds(2 * (h % 2), 2), :, :, pl.ds(4 * HCOLS, HCOLS)],
                up_buf.at[slot],
                w_sem.at[slot, 1],
            ),
        )

    def down_load():
        return pltpu.make_async_copy(
            g0_ref.at[0, :, :, :, :, pl.ds(4 * HCOLS, HCOLS)], down_buf, local_sem.at[0]
        )

    def lead_load():
        return pltpu.make_async_copy(g1_ref.at[:, :, :, :, :, pl.ds(0, D)], lead_buf, local_sem.at[0])

    def up_load(k):
        at = D if k == 0 else 0
        return pltpu.make_async_copy(
            outs[k + 1].at[:, :, :, :, :, pl.ds(at, FB)], wup_buf.at[k % 2], j_sem.at[k % 2, 0]
        )

    def wall_load(k):
        at = D + FB if k == 0 else FB
        return pltpu.make_async_copy(
            outs[k + 1].at[:, :, :, :, :, pl.ds(at, WALL)], wd_buf.at[k % 2], j_sem.at[k % 2, 1]
        )

    @pl.when(step == 0)
    def _():
        barrier = pltpu.get_barrier_semaphore()

        def signal(k, carry):
            pl.semaphore_signal(barrier, inc=1, device_id=((me + k) % N_DEV,), device_id_type=MESH)
            return carry

        lax.fori_loop(1, N_DEV, signal, 0)
        pl.semaphore_wait(barrier, N_DEV - 1)
        for i in items:
            sends.start(("pair", i), lambda i=i: (mine[i].at[other], inc[i], ring.sibling))
        own_copy = lambda i: pltpu.make_async_copy(
            stage[i], outs[i].at[core, spot[0], spot[1], spot[2]], local_sem.at[i]
        )
        for i in items:
            sends.arrived(("pair", i), inc[i], ring.sibling)
            own, theirs = mine[i][core], inc[i][...]
            first = jnp.where(core == 0, own, theirs)
            last = jnp.where(core == 0, theirs, own)
            stage[i][...] = jnp.concatenate([first, last], axis=0).astype(BF)
            own_copy(i).start()
        def send_tokens(k, carry):
            token_copy(k).start()
            return carry

        def take_tokens(k, carry):
            token_copy(k).wait()
            return carry

        def columns(first, count):
            return jnp.concatenate(
                [flat[pl.ds(first + c, N_DEV, stride=TOKEN_ROWS), :].astype(BF) for c in range(count)], axis=1
            )

        for i in items:
            own_copy(i).wait()
            ring.begin(i, 0)
        decay_rows.launch(0, rates_ref[...])
        lax.fori_loop(1, 43, send_tokens, 0)
        ring.finish(0, 0)
        ring.begin(0, 1)
        decay_rows.land(0)
        decay_rows.launch(1)
        lax.fori_loop(43, 85, send_tokens, 0)
        for i in items[1:]:
            ring.finish(i, 0)
        ring.relay(0, 1)
        decay_rows.land(1)
        decay_rows.launch(2)
        lax.fori_loop(85, N_DEV, send_tokens, 0)
        got[me] = sent_ref[me]
        ring.finish(0, 1)
        decay_rows.land(2)
        decay_rows.launch(3)
        ring.begin(0, 2)
        ring.begin(1, 1)
        lax.fori_loop(1, N_DEV, take_tokens, 0)
        flat[...] = got[...].astype(F32).reshape(N_DEV * TOKEN_ROWS, 128)
        decay_rows.land(3)
        rates = decay_rows.rows()
        for m in range(MB):
            s = slice(m * GROUP, (m + 1) * GROUP)
            x_ref[s, :] = dot(place_ref[m], columns(m * D // 128, D // 128), TN).astype(BF)
            d_ref[s, :] = dot(place_ref[m], columns((MB + m) * D // 128, D // 128), TN).astype(BF)
            sent = rates[:, m * 3 * H : (m + 1) * 3 * H]
            dec_ref[s, :] = dot(place_ref[m], sent, TN)
            dect_ref[:, s] = dot(sent, place_ref[m], TN)
        decay_kernel(split_ref, dec_ref, dect_ref, wf_ref, lw_ref)
        normed, _ = norm_fwd(x_ref[...].astype(F32), gain1_ref[...])
        h1_ref[...] = normed.astype(BF)
        ring.relay(0, 2)
        ring.relay(1, 1)
        for i in items[2:]:
            ring.begin(i, 1)
        ring.finish(0, 2)
        ring.finish(1, 1)
        ring.begin(1, 2)
        ring.received(0)
        for copy in head_loads(0, 0):
            copy.start()
        down_load().start()
        down_load().wait()
        latent = dot(h1_ref[...], down_buf[...].reshape(D, HCOLS))
        mask = mask_ref[...]
        for part in range(7):
            s = slice(part * AR, (part + 1) * AR)
            lat_ref[:, s] = (latent[:, s] * mask).astype(BF)

    @pl.when(step == 1)
    def _():
        for i in items[2:]:
            ring.relay(i, 1)

    @pl.when(step == 3)
    def _():
        ring.relay(1, 2)

    @pl.when(step == 6)
    def _():
        ring.finish(2, 1)
        ring.begin(2, 2)
        ring.finish(3, 1)

    @pl.when(step < FSTEPS)
    def _():
        slot = step % 2
        for copy in head_loads(step, slot):
            copy.wait()

        @pl.when(step + 1 < FSTEPS)
        def _():
            for copy in head_loads(step + 1, 1 - slot):
                copy.start()

        base = dot(h1_ref[...], w_buf[slot].reshape(D, HCOLS))
        up = up_buf[slot].reshape(HEAD, HCOLS)
        pieces = []
        for part in range(7):
            s = slice(part * AR, (part + 1) * AR)
            piece = base[:, part * HEAD : (part + 1) * HEAD] + dot(lat_ref[:, s], up[:, s], NT)
            proj_ref[:, part * HEAD : (part + 1) * HEAD] = piece
            pieces.append(piece)
        q, k, v = (pieces[i].astype(BF) for i in range(3))
        pk, pv = pers_ref[0, :, pl.ds(pl.multiple_of(step * HEAD, HEAD), HEAD)], pers_ref[
            1, :, pl.ds(pl.multiple_of(step * HEAD, HEAD), HEAD)
        ]
        near, far = attend(q, k, v, pk, pv, allowed_mask(split_ref))
        att = attend_out(near.astype(BF), far.astype(BF), v, pv)
        kn, _ = unit(pieces[3])
        qn, _ = unit(pieces[5])
        here = pl.ds(step, 1)
        mem = memory_out(memory_terms(kn, qn, pieces[4], wf_ref.at[here], lw_ref.at[here]))
        z_ref[:, pl.ds(pl.multiple_of(step * HEAD, HEAD), HEAD)] = (
            att + jax.nn.sigmoid(pieces[6]) * mem
        ).astype(BF)

    lead = lambda half, lo, hi: lead_buf[half, :, :, :, :, lo:hi].reshape(D, hi - lo)
    out_down = lambda: lead(0, 0, 128)
    up_down = lambda: lead(0, 128, 384)
    out_up = lambda: lead(0, 384, 512)
    down_up = lambda: lead(0, 512, 640)
    w_out = lambda: lead(1, 0, D)

    @pl.when(step == FSTEPS)
    def _():
        ring.finish(1, 2)
        ring.received(1)
        for copy in (lead_load(), up_load(0), wall_load(0)):
            copy.start()
        lead_load().wait()
        ring.relay(2, 2)
        ring.begin(3, 2)
        mask = mask_ref[...]
        z = z_ref[...]
        lat_out_ref[...] = (dot(z, out_down()) * mask).astype(BF)
        x2 = x_ref[...].astype(F32) + (dot(z, w_out()) + dot(lat_out_ref[...], out_up(), NT))
        x2_ref[...] = x2
        normed, inv = norm_fwd(x2, gain2_ref[...])
        inv_ref[...] = jnp.broadcast_to(inv, inv_ref.shape)
        h2_ref[...] = normed.astype(BF)
        latent = dot(h2_ref[...], up_down())
        lat_up_ref[:, :AR] = (latent[:, :AR] * mask).astype(BF)
        lat_up_ref[:, AR:] = (latent[:, AR:] * mask).astype(BF)
        dl_down_ref[...] = (dot(d_ref[...], down_up()) * mask).astype(BF)
        for ref in (acc_ref, lat_acc_ref, dh_ref, dlat_ref):
            ref[...] = jnp.zeros_like(ref)

    @pl.when(step == FSTEPS)
    def _():
        ring.finish(2, 2)
        ring.received(2)
        up_load(1).start()
        wall_load(1).start()

    @pl.when(step >= FSTEPS)
    def _():
        k = step - FSTEPS
        slot = k % 2
        h2 = h2_ref[...]
        d = d_ref[...]
        lat0, lat1 = lat_up_ref[:, :AR], lat_up_ref[:, AR:]
        wall = lambda half, lo, hi: wd_buf[slot, half, :, :, :, :, lo:hi].reshape(FB, hi - lo)
        pltpu.make_async_copy(wup_buf.at[slot], wup_buf.at[slot], j_sem.at[slot, 0]).wait()
        pltpu.make_async_copy(wd_buf.at[slot], wd_buf.at[slot], j_sem.at[slot, 1]).wait()
        w_gate, w_lift = (wup_buf[slot, half].reshape(D, FB) for half in range(2))
        wda, wdb = wall(0, 0, 768), wall(1, 0, 256)
        uu0, uu1, dd = wall(1, 256, 384), wall(1, 384, 512), wall(1, 512, 640)
        gate = dot(h2, w_gate) + dot(lat0, uu0, NT)
        lift = dot(h2, w_lift) + dot(lat1, uu1, NT)
        sig = jax.nn.sigmoid(gate)
        silu = gate * sig
        act = (silu * lift).astype(BF)
        d_act = dot(d[:, :768], wda, NT) + dot(d[:, 768:], wdb, NT) + dot(dl_down_ref[...], dd, NT)
        d_gate = (d_act * lift * (sig * (1.0 + gate * (1.0 - sig)))).astype(BF)
        d_lift = (d_act * silu).astype(BF)
        acc_ref[:, :768] += dot(act, wda)
        acc_ref[:, 768:] += dot(act, wdb)
        lat_acc_ref[...] += dot(act, dd)
        dh_ref[...] += dot(d_gate, w_gate, NT) + dot(d_lift, w_lift, NT)
        dlat_ref[:, :AR] += dot(d_gate, uu0)
        dlat_ref[:, AR:] += dot(d_lift, uu1)
        for half, at, term in (
            (0, k * 256, dot(d_gate, lat0, TN)),
            (0, k * 256 + AR, dot(d_lift, lat1, TN)),
            (1, k * AR, dot(act, dl_down_ref[...], TN)),
        ):
            at = pl.ds(pl.multiple_of(at, AR), AR)
            grads_ref[half, :, :, at] = term.reshape(64, 16, AR).astype(BF)

        @pl.when(k == 0)
        def _():
            ring.relay(3, 2)

        @pl.when(k == 1)
        def _():
            ring.finish(3, 2)
            ring.received(3)
            up_load(2).start()
            wall_load(2).start()

    @pl.when(step == FSTEPS + BLOCKS - 1)
    def _():
        mask = mask_ref[...]
        lat_down = (lat_acc_ref[...] * mask).astype(BF)
        out = (x2_ref[...] + acc_ref[...] + dot(lat_down, down_up(), NT)).astype(BF)
        for m in range(MB):
            s = slice(m * GROUP, (m + 1) * GROUP)
            back_ref[:, m * D : (m + 1) * D] = dot(place_ref[m], out[s]).astype(BF)
        d = d_ref[...]
        h2 = h2_ref[...]
        z = z_ref[...]

        def put(half, at, value):
            grads_ref[half, :, :, at : at + AR] = value.reshape(64, 16, AR).astype(BF)

        put(0, 768, dot(d, lat_down, TN))
        dlu0 = (dlat_ref[:, :AR] * mask).astype(BF)
        dlu1 = (dlat_ref[:, AR:] * mask).astype(BF)
        put(1, 640, dot(h2, dlu0, TN))
        put(1, 768, dot(h2, dlu1, TN))
        ud = up_down()
        dh = dh_ref[...] + (dot(dlu0, ud[:, :AR], NT) + dot(dlu1, ud[:, AR:], NT))
        dmid = d.astype(F32) + norm_bwd(dh, x2_ref[...], inv_ref[:, :1], gain2_ref[...])
        dmid_ref[...] = dmid
        dmb = dmid.astype(BF)
        dlo = (dot(dmb, out_up()) * mask).astype(BF)
        put(1, 384, dot(z, dlo, TN))
        put(1, 512, dot(dmb, lat_out_ref[...], TN))
        dz_ref[...] = (dot(dmb, w_out(), NT) + dot(dlo, out_down(), NT)).astype(BF)
        sends.drain()


def forward_call(split, sent, rates, gain1, gain2, mask, place, persistent, mine):
    once = pl.Buffered(1)
    whole = lambda *shape: pl.BlockSpec(shape, lambda s: (0,) * len(shape), pipeline_mode=once)
    hbm = pl.BlockSpec(memory_space=pl.ANY)
    slots = 4 * (1 + 3 * (3 + 2 * 6 + 7)) + 1 + 3 * 3
    return pl.pallas_call(
        forward_kernel,
        grid=(FSTEPS + BLOCKS,),
        out_shape=tuple(jax.ShapeDtypeStruct((2, 4, 4, 4, 16, width), BF) for width in WIDTHS)
        + (
            jax.ShapeDtypeStruct((ROWS, 7 * D), F32),
            jax.ShapeDtypeStruct((ROWS, D), BF),
            jax.ShapeDtypeStruct((ROWS, D), BF),
            jax.ShapeDtypeStruct((ROWS, 7 * AR), BF),
            jax.ShapeDtypeStruct((H, MB, GROUP, GROUP), F32),
            jax.ShapeDtypeStruct((H, MB, 8, GROUP), F32),
            jax.ShapeDtypeStruct((GROUP, MB * D), BF),
            jax.ShapeDtypeStruct((ROWS, D), BF),
            jax.ShapeDtypeStruct((ROWS, D), F32),
            jax.ShapeDtypeStruct((2, 64, 16, 896), BF),
        ),
        in_specs=[
            pl.BlockSpec(memory_space=pltpu.SMEM),
            whole(N_DEV, TOKEN_ROWS, 128),
            whole(N_DEV, 128),
            whole(1, D),
            whole(1, D),
            whole(ROWS, AR),
            whole(MB, GROUP, GROUP),
            whole(2, NP, D),
        ]
        + [whole(2, 8, width) for width in WIDTHS],
        out_specs=(hbm,) * 4
        + (
            pl.BlockSpec((ROWS, HCOLS), lambda s: (0, jnp.minimum(s, FSTEPS - 1))),
            whole(ROWS, D),
            whole(ROWS, D),
            whole(ROWS, 7 * AR),
            whole(H, MB, GROUP, GROUP),
            whole(H, MB, 8, GROUP),
            whole(GROUP, MB * D),
            whole(ROWS, D),
            whole(ROWS, D),
            whole(2, 64, 16, 896),
        ),
        scratch_shapes=[
            pltpu.VMEM((4, 4, 32, 128), BF),
            pltpu.VMEM((4, 4, 32, 128), BF),
            pltpu.VMEM((N_DEV, TOKEN_ROWS, 128), BF),
            pltpu.VMEM((N_DEV * TOKEN_ROWS, 128), F32),
            pltpu.VMEM((ROWS, D), BF),
            pltpu.VMEM((ROWS, 3 * H), F32),
            pltpu.VMEM((3 * H, ROWS), F32),
        ]
        + [pltpu.VMEM((8, width), F32) for width in WIDTHS]
        + [pltpu.VMEM((16, width), BF) for width in WIDTHS]
        + [
            pltpu.VMEM((2, 4, 4, 4, 16, HCOLS), BF),
            pltpu.VMEM((2, 2, 4, 16, HCOLS), BF),
            pltpu.VMEM((4, 4, 4, 16, HCOLS), BF),
            pltpu.VMEM((ROWS, D), BF),
            pltpu.VMEM((2, 2, 4, 4, 4, 16, FB), BF),
            pltpu.VMEM((2, 2, 4, 4, 4, 16, WALL), BF),
            pltpu.VMEM((2, 4, 4, 4, 16, D), BF),
            pltpu.VMEM((ROWS, D), F32),
            pltpu.VMEM((ROWS, D), BF),
            pltpu.VMEM((ROWS, 128), F32),
            pltpu.VMEM((ROWS, AR), BF),
            pltpu.VMEM((ROWS, 2 * AR), BF),
            pltpu.VMEM((ROWS, AR), BF),
            pltpu.VMEM((ROWS, D), F32),
            pltpu.VMEM((ROWS, AR), F32),
            pltpu.VMEM((ROWS, D), F32),
            pltpu.VMEM((ROWS, 2 * AR), F32),
            pltpu.SemaphoreType.DMA((slots,)),
            pltpu.SemaphoreType.DMA((slots,)),
            pltpu.SemaphoreType.DMA((4,)),
            pltpu.SemaphoreType.DMA((2, 2)),
            pltpu.SemaphoreType.DMA((2, 2)),
            pltpu.SemaphoreType.DMA((N_DEV,)),
            pltpu.SemaphoreType.DMA((N_DEV,)),
        ],
        compiler_params=pltpu.CompilerParams(
            collective_id=0, has_side_effects=True, vmem_limit_bytes=VMEM_LIMIT
        ),
        name="gather_forward",
    )(split, sent, rates, gain1, gain2, mask, place, persistent, *mine)


class Scatter:
    def __init__(self, sends, key, grads, out, inc0, total, inc1, inc2, inc3, t1, t2):
        self.sends, self.key, self.grads, self.out = sends, key, grads, out
        self.inc0, self.total, self.inc = inc0, total, (None, inc1, inc2, inc3)
        self.t1, self.t2 = t1, t2
        self.core, self.spot = position()
        self.other = 1 - self.core
        self.sibling = device(1 - self.core, self.spot)
        self.near = neighbours(self.core, self.spot)
        self.parts = [(part, pl.ds(*cols)) for part, cols in enumerate(cut(7, 3))]

    def peers(self):
        return [self.sibling] + [there[1] for there in self.near.values()]

    def pair(self):
        for x in range(4):
            self.sends.start(
                (self.key, "pair", x),
                lambda x=x: (
                    self.grads.at[self.other, pl.ds(16 * x, 16)],
                    self.inc0.at[x],
                    self.sibling,
                ),
            )

    def source(self, phase, part, at):
        axis = (part + phase - 1) % 3
        cs = self.parts[part][1]
        if phase == 1:
            index = tuple(at if a == axis else slice(None) for a in range(3))
            return self.total, index + (slice(None), cs)
        rest = [a for a in range(3) if a != part]
        if phase == 2:
            index = (at, slice(None)) if rest[0] == axis else (slice(None), at)
            return self.t1, index + (slice(None), cs)
        return self.t2, (at, slice(None), cs)

    def landing(self, phase, part, k):
        return (k,) + (slice(None),) * (4 - phase) + (self.parts[part][1],)

    def send(self, phase):
        for part, _ in self.parts:
            axis = (part + phase - 1) % 3
            for k, by in enumerate((2, 1, 3)):
                to = self.near[axis, by]

                def make(part=part, axis=axis, to=to, k=k):
                    ref, index = self.source(phase, part, to[0][axis])
                    return ref.at[index], self.inc[phase].at[self.landing(phase, part, k)], to[1]

                self.sends.start((self.key, part, phase, by), make)

    def add(self, phase):
        for part, cs in self.parts:
            axis = (part + phase - 1) % 3
            ref, index = self.source(phase, part, self.spot[axis])
            acc = ref[index].astype(F32)
            for k, by in enumerate((2, 1, 3)):
                here = self.landing(phase, part, k)
                source = self.near[axis, 4 - by][1]
                self.sends.arrived((self.key, part, phase, by), self.inc[phase].at[here], source)
                acc = acc + self.inc[phase][here].astype(F32)
            if phase == 1:
                self.t1[:, :, :, cs] = acc.astype(BF)
            elif phase == 2:
                self.t2[:, :, cs] = acc.astype(BF)
            else:
                self.out[self.core, :, cs] = acc

    def add_pair(self):
        for x in range(4):
            self.sends.arrived((self.key, "pair", x), self.inc0.at[x], self.sibling)
            both = self.grads[self.core, pl.ds(16 * x, 16)].astype(F32) + self.inc0[x].astype(F32)
            self.total[x] = both.reshape(4, 4, 16, 896).astype(BF)

    def swap(self):
        self.sends.start(
            (self.key, "last"), lambda: (self.out.at[self.core], self.out.at[self.core], self.sibling)
        )

    def swapped(self):
        self.sends.arrived((self.key, "last"), self.out.at[self.other], self.sibling)


def backward_kernel(
    split_ref, x_ref, gain_ref, mask_ref, place_ref, proj_ref, dz_ref, dmid_ref, h1_ref, lat_ref,
    w_ref, down_ref, up_ref, pers_ref, wf_ref, lw_ref, ffn_ref, back_ref,
    act_out, grad_out, ffn_out, heads_out,
    dh_ref, dlat_ref, dlat_half, grads_ref, *rest,
):
    step = pl.program_id(0)
    send_sem, recv_sem = rest[-2:]
    sends = Sends(send_sem, recv_sem)
    first_sums = Scatter(sends, 0, ffn_ref, *rest[:8])
    last_sums = Scatter(sends, 1, grads_ref, *rest[8:16])
    flat = rest[26]
    ex_act = Exchange(sends, "a", rest[16:21], 1, BY_CORE)
    ex_grad = Exchange(sends, "g", rest[21:26], 1, BY_CORE)

    def one_head():
        pieces = [proj_ref[:, p * HEAD : (p + 1) * HEAD] for p in range(7)]
        q, k, v = (pieces[i].astype(BF) for i in range(3))
        pk, pv = pers_ref[0], pers_ref[1]
        near, far = attend(q, k, v, pk, pv, allowed_mask(split_ref))
        near_half = near.astype(BF)
        dz = dz_ref[...]
        d_near = by_group(lambda s, g: dot(dz[s], v[s], NT))
        d_far = dot(dz, pv, NT)
        d_v = by_group(lambda s, g: dot(near_half[s], dz[s], TN))
        total = jnp.sum(d_near * near, axis=-1, keepdims=True) + jnp.sum(
            d_far * far, axis=-1, keepdims=True
        )
        ds_near = (near * (d_near - total) * SCALE).astype(BF)
        ds_far = (far * (d_far - total) * SCALE).astype(BF)
        d_q = by_group(lambda s, g: dot(ds_near[s], k[s])) + dot(ds_far, pk)
        d_k = by_group(lambda s, g: dot(ds_near[s], q[s], TN))

        dzf = dz.astype(F32)
        opening = jax.nn.sigmoid(pieces[6])
        kn, k_inv = unit(pieces[3])
        qn, q_inv = unit(pieces[5])
        kept = memory_terms(kn, qn, pieces[4], wf_ref, lw_ref, plain, dot1)
        mem = memory_out(kept, dot1)
        d_open = dzf * mem * (opening * (1.0 - opening))
        d_kn, d_qn, d_mv = memory_bwd(kept, dzf * opening)
        d_mk = unit_bwd(d_kn, pieces[3], k_inv)
        d_mq = unit_bwd(d_qn, pieces[5], q_inv)
        dy = [item.astype(BF) for item in (d_q, d_k, d_v, d_mk, d_mv, d_mq, d_open)]
        dh_ref[...] += dot(jnp.concatenate(dy, axis=1), w_ref[0], NT)
        first = pl.multiple_of(step * 8, 8)
        for part in range(7):
            s = slice(part * AR, (part + 1) * AR)
            dlat_ref[:, s] += dot(dy[part], up_ref[0, :, s])
            grads_ref[1, pl.ds(first, 8), :, s] = (
                dot(dy[part], lat_ref[:, s], TN).reshape(8, 16, AR).astype(BF)
            )

    @pl.when(step == 0)
    def _():
        greet(first_sums.peers())
        ex_act.fill(0, flat, [back_ref[...]])
        ex_act.launch(0)
        first_sums.pair()
        dh_ref[...] = jnp.zeros_like(dh_ref)
        dlat_ref[...] = jnp.zeros_like(dlat_ref)

    @pl.when(step == 1)
    def _():
        ex_act.land(0)
        ex_act.launch(1)

    @pl.when(step == 2)
    def _():
        first_sums.add_pair()
        first_sums.send(1)

    @pl.when(step == 3)
    def _():
        ex_act.land(1)
        ex_act.launch(2)

    @pl.when(step == 5)
    def _():
        first_sums.add(1)
        first_sums.send(2)
        ex_act.land(2)
        ex_act.launch(3)

    @pl.when(step == 6)
    def _():
        first_sums.add(2)
        first_sums.send(3)

    @pl.when(step == 7)
    def _():
        first_sums.add(3)
        first_sums.swap()
        ex_act.land(3)
        act_out[...] = ex_act.bufs[4][...]

    one_head()

    @pl.when(step == H - 1)
    def _():
        mask = mask_ref[...]
        for p in range(7):
            s = slice(p * AR, (p + 1) * AR)
            dlat_half[:, s] = (dlat_ref[:, s] * mask).astype(BF)
        grads_ref[0] = dot(h1_ref[...], dlat_half[...], TN).reshape(64, 16, 7 * AR).astype(BF)
        last_sums.pair()
        dh = dh_ref[...] + dot(dlat_half[...], down_ref[0], NT)
        x = x_ref[...].astype(F32)
        inv = lax.rsqrt(jnp.mean(x * x, axis=-1, keepdims=True) + EPS)
        dx = (dmid_ref[...] + norm_bwd(dh, x, inv, gain_ref[...])).astype(BF)
        ex_grad.fill(
            0, flat, [dot(place_ref[m], dx[m * GROUP : (m + 1) * GROUP]) for m in range(MB)]
        )
        ex_grad.launch(0)
        last_sums.add_pair()
        ex_grad.land(0)
        ex_grad.launch(1)
        last_sums.send(1)
        first_sums.swapped()
        ffn_out[...] = first_sums.out[...]
        ex_grad.land(1)
        ex_grad.launch(2)
        last_sums.add(1)
        last_sums.send(2)
        ex_grad.land(2)
        ex_grad.launch(3)
        last_sums.add(2)
        last_sums.send(3)
        ex_grad.land(3)
        grad_out[...] = ex_grad.bufs[4][...]
        last_sums.add(3)
        last_sums.swap()
        last_sums.swapped()
        heads_out[...] = last_sums.out[...]
        sends.drain()


def backward_call(split, x, gain, mask, place, proj, dz, dmid, h1, lat, a1, persistent, wf, lw, grads_ffn, back):
    once = pl.Buffered(1)
    whole = lambda *shape: pl.BlockSpec(shape, lambda s: (0,) * len(shape), pipeline_mode=once)
    head = lambda s: s
    buffers = [
        pltpu.VMEM((2, 16, 896), F32),
        pltpu.VMEM((4, 16, 16, 896), BF),
        pltpu.VMEM((4, 4, 4, 16, 896), BF),
        pltpu.VMEM((3, 4, 4, 16, 896), BF),
        pltpu.VMEM((3, 4, 16, 896), BF),
        pltpu.VMEM((3, 16, 896), BF),
        pltpu.VMEM((4, 4, 16, 896), BF),
        pltpu.VMEM((4, 16, 896), BF),
    ]
    slots = 2 * (4 + 3 * 9 + 1) + 2 * (1 + 3 * 6)
    return pl.pallas_call(
        backward_kernel,
        grid=(H,),
        out_shape=(
            jax.ShapeDtypeStruct((4, 4, 4, 16, 256), BF),
            jax.ShapeDtypeStruct((4, 4, 4, 16, 256), BF),
            jax.ShapeDtypeStruct((2, 16, 896), F32),
            jax.ShapeDtypeStruct((2, 16, 896), F32),
        ),
        in_specs=[
            pl.BlockSpec(memory_space=pltpu.SMEM),
            whole(ROWS, D),
            whole(1, D),
            whole(ROWS, AR),
            whole(MB, GROUP, GROUP),
            pl.BlockSpec((ROWS, HCOLS), lambda s: (0, head(s))),
            pl.BlockSpec((ROWS, HEAD), lambda s: (0, head(s))),
            whole(ROWS, D),
            whole(ROWS, D),
            whole(ROWS, 7 * AR),
            pl.BlockSpec((1, D, HCOLS), lambda s: (s // 4, 0, s % 4)),
            pl.BlockSpec((1, D, HCOLS), lambda s: (0, 0, 4), pipeline_mode=once),
            pl.BlockSpec((1, HEAD, HCOLS), lambda s: (1, head(s), 4)),
            pl.BlockSpec((2, NP, HEAD), lambda s: (0, 0, head(s))),
            pl.BlockSpec((1, MB, GROUP, GROUP), lambda s: (head(s), 0, 0, 0)),
            pl.BlockSpec((1, MB, 8, GROUP), lambda s: (head(s), 0, 0, 0)),
            pl.BlockSpec(memory_space=pltpu.VMEM),
            pl.BlockSpec(memory_space=pltpu.VMEM),
        ],
        out_specs=(
            whole(4, 4, 4, 16, 256),
            whole(4, 4, 4, 16, 256),
            pl.BlockSpec(memory_space=pltpu.VMEM),
            pl.BlockSpec(memory_space=pltpu.VMEM),
        ),
        scratch_shapes=[
            pltpu.VMEM((ROWS, D), F32),
            pltpu.VMEM((ROWS, 7 * AR), F32),
            pltpu.VMEM((ROWS, 7 * AR), BF),
            pltpu.VMEM((2, 64, 16, 896), BF),
        ]
        + buffers * 2
        + [pltpu.VMEM((4, 4, 4, 16, 256), BF)] * 10
        + [pltpu.VMEM((16 * N_DEV, 128), F32)]
        + [pltpu.SemaphoreType.DMA((slots,)), pltpu.SemaphoreType.DMA((slots,))],
        compiler_params=pltpu.CompilerParams(
            collective_id=1, has_side_effects=True, vmem_limit_bytes=VMEM_LIMIT
        ),
        name="backward_scatter",
    )(split, x, gain, mask, place, proj, dz, dmid, h1, lat, a1, a1, a1, persistent, wf, lw, grads_ffn, back)


def selector(parts):
    rows = lax.broadcasted_iota(jnp.int32, (parts * R, parts * AR), 0)
    cols = lax.broadcasted_iota(jnp.int32, (parts * R, parts * AR), 1)
    return (rows // R == cols // AR) & (rows % R == cols % R)


def adapter_of(shape):
    return (lax.broadcasted_iota(jnp.int32, shape, len(shape) - 1) % AR) // R


def pack_kernel(
    lengths_ref, ids_ref, route_ref, tok_ref, cot_ref, decays_ref,
    w_in, w_out, w_up, w_down, in_down, in_up, out_down, out_up, up_down, up_up, down_down, down_up,
    sent, rates_out, item0, item1, item2, item3, to_ref, place_ref, mask_ref, split_ref,
    flat, wide,
):
    me = lax.axis_index("fsdp")

    below = lax.broadcasted_iota(jnp.int32, (GROUP, GROUP), 0)
    along = lax.broadcasted_iota(jnp.int32, (GROUP, GROUP), 1)
    for m in range(MB):
        to = (below == route_ref[m, pl.ds(me, 1), :] // GROUP).astype(BF)
        to_ref[m] = to
        for ref, first in ((tok_ref, m * 8), (cot_ref, (MB + m) * 8)):
            value = dot(to, ref[m])
            for j in range(8):
                flat[pl.ds(first + j, N_DEV, stride=TOKEN_ROWS), :] = value[:, j * 128 : (j + 1) * 128]
    rates = [dot(to_ref[m], decays_ref[m], NT) for m in range(MB)]
    rates = jnp.concatenate(rates + [jnp.zeros((GROUP, 128 - MB * 3 * H), F32)], axis=1)
    rates_out[...] = rates.astype(BF)
    sent[...] = flat[...].reshape(N_DEV, TOKEN_ROWS, 128).astype(BF)

    for m in range(MB):
        blocks = route_ref[m]
        landing = jnp.sum(jnp.where(blocks // GROUP == me, blocks % GROUP, 0), axis=1, keepdims=True)
        place_ref[m] = (landing == along).astype(BF)
        early = lengths_ref[m, 0]
        row = lax.broadcasted_iota(jnp.int32, (GROUP, AR), 0)
        adapter = jnp.where(row < early, ids_ref[m, 0], ids_ref[m, 1])
        mask_ref[m * GROUP : (m + 1) * GROUP, :] = (adapter == adapter_of((GROUP, AR))).astype(F32)
        split_ref[m] = jnp.where(early < GROUP, 1.0, 0.0)

    select = selector(7).astype(BF)
    items = (item1, item2, item3)

    def ranks(ref, parts):
        cut_to = select[: parts * R, : parts * AR]
        rows = ref.shape[1]
        out = jnp.zeros((rows, parts * AR), F32)
        for a in range(NAD):
            out = out + jnp.where(adapter_of(out.shape) == a, dot(ref[a], cut_to), 0.0)
        return out

    def ranks_t(ref, parts):
        cut_to = select[: parts * R, : parts * AR]
        cols = ref.shape[2]
        out = jnp.zeros((cols, parts * AR), F32)
        for a in range(NAD):
            out = out + jnp.where(adapter_of(out.shape) == a, dot(ref[a], cut_to, TN), 0.0)
        return out

    def ranks_mid(ref, parts):
        rows = ref.shape[0]
        value = ref[...].astype(F32).reshape(rows * NAD, parts * R).astype(BF)
        value = dot(value, select[: parts * R, : parts * AR]).reshape(rows, NAD, parts * AR)
        mine = adapter_of(value.shape) == lax.broadcasted_iota(jnp.int32, value.shape, 1)
        return jnp.sum(jnp.where(mine, value, 0.0), axis=1)

    def tall(value):
        return jnp.concatenate([value, jnp.zeros((FF_PAD - FF_SHARD, value.shape[1]), F32)], axis=0)

    for h in range(H):
        for part in range(7):
            at = (h % 4) * HCOLS + part * HEAD
            item0[h // 4, :, at : at + HEAD] = w_in[:, part * D + h * HEAD : part * D + (h + 1) * HEAD].astype(F32)
    item0[0, :, 4 * HCOLS :] = ranks(in_down, 7)
    item0[1, :, 4 * HCOLS :] = ranks(in_up, 7)

    item1[0, :, 0:128] = ranks(out_down, 1)
    item1[0, :, 128:384] = ranks(up_down, 2)
    item1[0, :, 384:512] = ranks(out_up, 1)
    item1[0, :, 512:640] = ranks(down_up, 1)
    item1[0, :, 640:D] = jnp.zeros((8, D - 640), F32)
    item1[1, :, 0:D] = w_out[...].astype(F32)

    wide[...] = w_up[...].astype(F32)
    span = 8 * FF_SHARD
    rows = lax.broadcasted_iota(jnp.int32, (span, 3 * 64), 0)
    cols = lax.broadcasted_iota(jnp.int32, (span, 3 * 64), 1)
    unit_at = (cols // 64) * 8 + cols % 8
    spread = ((rows == (cols % 64) // 8 * FF_SHARD + unit_at) & (unit_at < FF_SHARD)).astype(BF)
    pieces = [wide[:, c * span : (c + 1) * span] for c in range(32)]
    moved_up = dot(jnp.concatenate(pieces, axis=0).astype(BF), spread)
    for c in range(32):
        half, chunk = c // 16, c % 16
        for k in range(3):
            at = (D if k == 0 else 0) + chunk * 64
            items[k][half, :, at : at + 64] = moved_up[c * 8 : (c + 1) * 8, k * 64 : (k + 1) * 64]
    down = tall(w_down[...].astype(F32))
    uu, dd = tall(ranks_mid(up_up, 2)), tall(ranks_t(down_down, 1))
    for k in range(3):
        at = (D if k == 0 else 0) + FB
        s = slice(k * 8, (k + 1) * 8)
        items[k][0, :, at : at + 768] = down[s, :768]
        items[k][1, :, at : at + 256] = down[s, 768:]
        items[k][1, :, at + 256 : at + 512] = uu[s]
        items[k][1, :, at + 512 : at + 640] = dd[s]
        items[k][1, :, at + 640 : at + 768] = jnp.zeros((8, 128), F32)


def pack_call(lengths, ids, route, tokens, cotangent, decays, weights):
    smem, vmem = pl.BlockSpec(memory_space=pltpu.SMEM), pl.BlockSpec(memory_space=pltpu.VMEM)
    return pl.pallas_call(
        pack_kernel,
        out_shape=(
            jax.ShapeDtypeStruct((N_DEV, TOKEN_ROWS, 128), BF),
            jax.ShapeDtypeStruct((N_DEV, 128), BF),
        )
        + tuple(jax.ShapeDtypeStruct((2, 8, width), F32) for width in WIDTHS)
        + (
            jax.ShapeDtypeStruct((MB, GROUP, GROUP), BF),
            jax.ShapeDtypeStruct((MB, GROUP, GROUP), BF),
            jax.ShapeDtypeStruct((ROWS, AR), F32),
            jax.ShapeDtypeStruct((MB,), F32),
        ),
        in_specs=[smem] * 2 + [vmem] * (4 + len(weights)),
        out_specs=(vmem,) * 9 + (smem,),
        scratch_shapes=[
            pltpu.VMEM((N_DEV * TOKEN_ROWS, 128), F32),
            pltpu.VMEM((8, 2 * FF), F32),
        ],
        compiler_params=pltpu.CompilerParams(vmem_limit_bytes=VMEM_LIMIT),
        name="pack",
    )(lengths, ids, route, tokens, cotangent, decays, *weights)


def unpack_kernel(
    core_ref, to_ref, act_ref, grad_ref, ffn_ref, heads_ref,
    out_ref, back_ref, in_down, in_up, out_down, out_up, up_down, up_up, down_down, down_up,
    flat,
):
    core = core_ref[0]
    for source, target in ((act_ref, out_ref), (grad_ref, back_ref)):
        got = [source[:, :, :, :, c * 128 : (c + 1) * 128].astype(F32) for c in range(2)]
        flat[...] = jnp.stack(got, axis=3).reshape(16 * N_DEV, 128)
        for m in range(MB):
            value = jnp.concatenate(
                [flat[pl.ds(m * 8 + j, N_DEV, stride=16), :].astype(BF) for j in range(8)], axis=1
            )
            target[m] = dot(to_ref[m], value, TN).astype(BF)
    own = pl.ds(pl.multiple_of(core * 8, 8), 8)
    heads = [heads_ref[half, own, :] for half in range(2)]
    ffn = [ffn_ref[half, own, :] for half in range(2)]
    select = selector(7).astype(F32)

    def tall(value, width):
        return jnp.concatenate([value[:, k * width : (k + 1) * width] for k in range(3)], axis=0)

    def put(ref, value, parts):
        rows, width = value.shape
        shape = (NAD, rows, width)
        mine = adapter_of(shape) == lax.broadcasted_iota(jnp.int32, shape, 0)
        apart = jnp.where(mine, value[None], 0.0).reshape(NAD * rows, width)
        ref[...] = exact(apart, select[: parts * R, :width], NT).reshape(NAD, rows, parts * R)

    put(in_down, heads[0], 7)
    put(in_up, heads[1], 7)
    put(out_down, ffn[1][:, 384:512], 1)
    put(out_up, ffn[1][:, 512:640], 1)
    put(up_down, ffn[1][:, 640:896], 2)
    put(down_up, ffn[0][:, 768:], 1)
    value = tall(ffn[0][:, :768], 256)
    shape = (FF_PAD, NAD, 2 * AR)
    mine = adapter_of(shape) == lax.broadcasted_iota(jnp.int32, shape, 1)
    apart = jnp.where(mine, jnp.broadcast_to(value[:, None, :], shape), 0.0).reshape(FF_PAD * NAD, 2 * AR)
    up_up[...] = exact(apart, select[: 2 * R, : 2 * AR], NT).reshape(FF_PAD, NAD, 2 * R)[:FF_SHARD]
    value = tall(ffn[1][:, :384], AR)
    for a in range(NAD):
        mine = jnp.where(adapter_of(value.shape) == a, value, 0.0)
        down_down[a] = exact(select[:R, :AR], mine, NT)[:, :FF_SHARD]


def unpack_call(core, to, act, grad, ffn_sums, heads_sums, shapes):
    smem, vmem = pl.BlockSpec(memory_space=pltpu.SMEM), pl.BlockSpec(memory_space=pltpu.VMEM)
    return pl.pallas_call(
        unpack_kernel,
        out_shape=(jax.ShapeDtypeStruct((MB, GROUP, D), BF),) * 2
        + tuple(jax.ShapeDtypeStruct(shape, F32) for shape in shapes),
        in_specs=[smem] + [vmem] * 5,
        out_specs=(vmem,) * (2 + len(shapes)),
        scratch_shapes=[pltpu.VMEM((16 * N_DEV, 128), F32)],
        compiler_params=pltpu.CompilerParams(vmem_limit_bytes=VMEM_LIMIT),
        name="unpack",
    )(core, to, act, grad, ffn_sums, heads_sums)


def body(
    tokens, cotangent, decays, route, lengths, adapter_ids, gain_mix, gain_ffn, persistent,
    w_in, w_out, w_up, w_down, in_down, in_up, out_down, out_up, up_down, up_up, down_down, down_up,
):
    me = lax.axis_index("fsdp").astype(jnp.int32)
    weights = (
        w_in, w_out, w_up, w_down, in_down, in_up, out_down, out_up, up_down, up_up, down_down, down_up,
    )
    turned = lambda value: jnp.swapaxes(value, 1, 2)
    views = (None,) * 5 + (turned, None, turned, None, lambda value: value.transpose(2, 0, 1), turned, turned)
    back_views = views[:9] + (lambda value: value.transpose(1, 2, 0), turned, turned)
    viewed = [item if view is None else view(item) for item, view in zip(weights, views)]
    sent, rates, *items, to, place, mask, split = pack_call(
        lengths[:, 0], adapter_ids[:, 0], route.reshape(MB, N_DEV, GROUP), tokens, cotangent, turned(decays), viewed
    )
    gain_mix, gain_ffn = gain_mix[None, :], gain_ffn[None, :]
    a1, _, _, _, proj, x, h1, lat, wf, lw, back, dz, dmid, grads_ffn = forward_call(
        split, sent, rates, gain_mix, gain_ffn, mask, place, persistent, items
    )
    act, grad, ffn_sums, heads_sums = backward_call(
        split, x, gain_mix, mask, place, proj, dz, dmid, h1, lat, a1.reshape(2, D, WIDTHS[0]), persistent, wf, lw,
        grads_ffn, back,
    )
    outs = unpack_call((me % 2)[None], to, act, grad, ffn_sums, heads_sums, [item.shape for item in viewed[4:]])
    grads = [item if view is None else view(item) for item, view in zip(outs[2:], back_views[4:])]
    return tuple(outs[:2]) + tuple(grads)


def solution(mesh):
    rows, cols = P(None, "fsdp", None), P(None, None, "fsdp")
    weight = P("fsdp", None)
    return jax.shard_map(
        body,
        mesh=mesh,
        in_specs=(rows, rows, rows, P(), rows, rows, P(), P(), P())
        + (weight,) * 4
        + (rows, cols) * 4,
        out_specs=(rows, rows) + (rows, cols) * 4,
        check_vma=False,
    )
```

```python
import functools
import math

import jax
import jax.numpy as jnp
from jax import lax
from jax.experimental import pallas as pl
from jax.experimental.pallas import tpu as pltpu
from jax.sharding import PartitionSpec as P

D = 1024
H = 8
HEAD = 128
FF = 2816
R = 16
NAD = 8
NP = 16
SPAN = 64
GROUP = 128
MB = 2
ROWS = MB * GROUP
N_DEV = 128
AR = NAD * R
HCOLS = 7 * HEAD
FF_SHARD = FF // N_DEV
FF_PAD = 24
FFP = FF_PAD * N_DEV
FB = 1024
EPS = 1e-05
SCALE = 1.0 / math.sqrt(HEAD)
VMEM_LIMIT = 60 * 1024 * 1024
BF = jnp.bfloat16
F32 = jnp.float32

NN = (((1,), (0,)), ((), ()))
NT = (((1,), (1,)), ((), ()))
TN = (((0,), (0,)), ((), ()))


def dot(left, right, dims=NN):
    return lax.dot_general(left, right, dims, preferred_element_type=F32)


def exact(left, right, dims=NN):
    return lax.dot_general(
        left, right, dims, precision=lax.Precision.HIGHEST, preferred_element_type=F32
    )


def halves(value):
    high = value.astype(BF)
    return high, (value - high.astype(F32)).astype(BF)


def dot3(left, right, dims=NN):
    lh, ll = left
    rh, rl = right
    return dot(lh, rh, dims) + (dot(lh, rl, dims) + dot(ll, rh, dims))


def norm_fwd(values, gain):
    inv = lax.rsqrt(jnp.mean(values * values, axis=-1, keepdims=True) + EPS)
    return values * inv * gain, inv


def norm_bwd(grad, values, inv, gain):
    scaled = grad * gain
    return inv * (scaled - values * (inv * inv * jnp.mean(values * scaled, axis=-1, keepdims=True)))


def decay_kernel(split_ref, dec_ref, dect_ref, wf_ref, lw_ref):
    rows = lax.broadcasted_iota(jnp.int32, (GROUP, GROUP), 0)
    cols = lax.broadcasted_iota(jnp.int32, (GROUP, GROUP), 1)
    lower = (rows >= cols) & ((rows >= SPAN) == (cols >= SPAN))
    tri = lower.astype(F32)
    second = rows >= SPAN
    for g in range(MB):
        keep = 1.0 - split_ref[g]
        here = dec_ref[g * GROUP : (g + 1) * GROUP, :]
        here_t = dect_ref[:, g * GROUP : (g + 1) * GROUP]
        run = exact(tri, jnp.log(here[:, : 2 * H]))
        run_t = exact(jnp.log(here_t[: 2 * H, :]), tri, NT)
        for h in range(H):
            gap = run[:, h : h + 1] - run_t[h : h + 1, :]
            retain = jnp.exp(jnp.where(lower, gap, -1e30))
            gap = run[:, H + h : H + h + 1] - run_t[H + h : H + h + 1, :]
            moment = jnp.exp(jnp.where(lower, gap, -1e30))
            pairs = exact(retain, moment)
            theta = here_t[2 * H + h : 2 * H + h + 1, :]
            moment_run = jnp.exp(run_t[H + h : H + h + 1, :])
            carry = jnp.sum(retain * moment_run, axis=1, keepdims=True)
            last_weight = pairs[SPAN - 1 : SPAN, :] * theta * keep
            last_moment = moment[SPAN - 1 : SPAN, :] * theta * keep
            across = jnp.exp(run[:, h : h + 1]) * last_weight + carry * last_moment
            wf_ref[h, g] = pairs * theta + jnp.where(second, across, 0.0)
            lw_ref[h, g] = jnp.broadcast_to(last_weight, (8, GROUP))


def allowed_mask(split_ref):
    rows = lax.broadcasted_iota(jnp.int32, (ROWS, GROUP), 0)
    cols = lax.broadcasted_iota(jnp.int32, (ROWS, GROUP), 1)
    local = rows % GROUP
    group = rows // GROUP
    split = jnp.where(group == 0, split_ref[0], split_ref[1]) > 0.5
    return (local >= cols) & jnp.logical_not(split & (local >= SPAN) & (cols < SPAN))


def by_group(make):
    return jnp.concatenate([make(slice(0, GROUP), 0), make(slice(GROUP, ROWS), 1)], axis=0)


def attend(q, k, v, pk, pv, allowed):
    near = by_group(lambda s, g: dot(q[s], k[s], NT))
    far = dot(q, pk, NT) * SCALE
    near = jnp.where(allowed, near * SCALE, -1000000000.0)
    top = jnp.maximum(
        jnp.max(near, axis=-1, keepdims=True), jnp.max(far, axis=-1, keepdims=True)
    )
    near = jnp.exp(near - top)
    far = jnp.exp(far - top)
    inv = 1.0 / (jnp.sum(near, axis=-1, keepdims=True) + jnp.sum(far, axis=-1, keepdims=True))
    near = near * inv
    far = far * inv
    return near, far


def attend_out(near_half, far_half, v, pv):
    return by_group(lambda s, g: dot(near_half[s], v[s])) + dot(far_half, pv)


def unit(values):
    inv = lax.rsqrt(jnp.mean(values * values, axis=-1, keepdims=True) + EPS)
    return values * (inv * SCALE), inv


def unit_bwd(grad, values, inv):
    return (inv * SCALE) * (
        grad - values * (inv * inv * jnp.mean(values * grad, axis=-1, keepdims=True))
    )


def plain(value):
    return (value.astype(BF),)


def dot1(left, right, dims=NN):
    return dot(left[0], right[0], dims)


def memory_terms(kn, qn, mv, wf_ref, lw_ref, halves=halves, dot3=dot3):
    second = lax.broadcasted_iota(jnp.int32, (GROUP, GROUP), 0) >= SPAN
    kept = []
    for g in range(MB):
        s = slice(g * GROUP, (g + 1) * GROUP)
        kh, qh = halves(kn[s]), halves(qn[s])
        wf = wf_ref[0, g]
        lw = jnp.where(second, lw_ref[0, g][0:1, :], 0.0)
        kk = dot3(kh, kh, NT) * lw
        qk = dot3(qh, kh, NT) * wf
        kk_half = halves(kk)
        mvh = halves(mv[s])
        err = mv[s] - dot3(kk_half, mvh)
        errh = halves(err)
        qk_half = halves(qk)
        kept.append((kh, qh, wf, lw, kk_half, qk_half, mvh, errh))
    return kept


def memory_out(kept, dot3=dot3):
    return jnp.concatenate([dot3(item[5], item[7]) for item in kept], axis=0)


def memory_bwd(kept, grad, halves=plain, dot3=dot1):
    grads_k, grads_q, grads_v = [], [], []
    for g in range(MB):
        kh, qh, wf, lw, kk_half, qk_half, mvh, errh = kept[g]
        gh = halves(grad[g * GROUP : (g + 1) * GROUP])
        d_qk = dot3(gh, errh, NT) * wf
        d_err = dot3(qk_half, gh, TN)
        deh = halves(d_err)
        d_v = d_err - dot3(kk_half, deh, TN)
        d_kk = dot3(deh, mvh, NT) * lw
        dqh = halves(d_qk)
        dkh = halves(d_kk)
        grads_q.append(dot3(dqh, kh))
        grads_k.append(dot3(dqh, qh, TN) - (dot3(dkh, kh) + dot3(dkh, kh, TN)))
        grads_v.append(d_v)
    return (
        jnp.concatenate(grads_k, axis=0),
        jnp.concatenate(grads_q, axis=0),
        jnp.concatenate(grads_v, axis=0),
    )


AXES = ("x", "z", "y")
MESH = pl.DeviceIdType.MESH


def position():
    me = lax.axis_index("fsdp")
    chip = me // 2
    return me % 2, (chip // 16, (chip // 4) % 4, chip % 4)


def device(core, spot):
    return (((spot[0] * 4 + spot[1]) * 4 + spot[2]) * 2 + core,)


def moved(spot, axis, by):
    return tuple((v + by + 4) % 4 if i == axis else v for i, v in enumerate(spot))


def cut(lanes, count, first=0):
    base, extra = divmod(lanes, count)
    runs, at = [], 0
    for i in range(count):
        size = base + (1 if (i - first) % count < extra else 0)
        runs.append((at * 128, size * 128))
        at += size
    return runs


def neighbours(core, spot):
    found = {}
    for axis in range(3):
        for by in (1, 2, 3):
            there = moved(spot, axis, by)
            found[axis, by] = (there, device(core, there))
    return found


class Sends:
    def __init__(self, send_sem, recv_sem):
        self.send_sem, self.recv_sem = send_sem, recv_sem
        self.slots, self.open = {}, []

    def copy(self, name, src, dst, target):
        slot = self.slots.setdefault(name, len(self.slots))
        return pltpu.make_async_remote_copy(
            src_ref=src, dst_ref=dst, send_sem=self.send_sem.at[slot], recv_sem=self.recv_sem.at[slot],
            device_id=target, device_id_type=MESH,
        )

    def start(self, name, make):
        self.copy(name, *make()).start()
        self.open.append((name, make))

    def arrived(self, name, ref, target):
        self.copy(name, ref, ref, target).wait_recv()

    def drain(self):
        for name, make in self.open:
            self.copy(name, *make()).wait_send()
        self.open = []


def greet(targets):
    barrier = pltpu.get_barrier_semaphore()
    for target in targets:
        pl.semaphore_signal(barrier, inc=1, device_id=target, device_id_type=MESH)
    pl.semaphore_wait(barrier, len(targets))


LONGER = (0, 2, 2, 1)
TURNED = {(2, 0), (2, 2), (3, 1)}


class Gather:
    def __init__(self, sends, outs, widths):
        self.sends, self.outs = sends, outs
        self.core, self.spot = position()
        self.other = 1 - self.core
        self.sibling = device(1 - self.core, self.spot)
        self.near = neighbours(self.core, self.spot)
        self.jobs = [
            [(i, part, cols) for part, cols in enumerate(cut(width // 128, 3, LONGER[i]))]
            for i, width in enumerate(widths)
        ]
        self.forwards = [[] for _ in widths]

    def peers(self):
        return [self.sibling] + [self.near[a, by][1] for a in range(3) for by in (1, 3)]

    def block(self, i, whole_axes, at, cols, half=None):
        index = [pl.ds(0, 4) if a in whole_axes else pl.ds(at[a], 1) for a in range(3)]
        half = self.core if half is None else half
        return self.outs[i].at[half, index[0], index[1], index[2], :, pl.ds(cols[0], cols[1])]

    def push(self, name, target, *where):
        def make():
            ref = self.block(*where)
            return ref, ref, target

        self.sends.start(name, make)

    def forward(self, name, *where):
        self.push(name, self.sibling, *where)
        self.forwards[where[0]].append((name, where))

    def plan(self, item, phase):
        for i, part, cols in self.jobs[item]:
            axis = (part + phase) % 3
            done = [(part + p) % 3 for p in range(phase)]
            sides = [self.near[axis, by] for by in (1, 3, 2)]
            halves_of = [(cols[0] + at, size) for at, size in cut(cols[1] // 128, 2, (i, part) in TURNED)]
            yield i, part, cols, done, sides, halves_of

    def begin(self, item, phase):
        for i, part, cols, done, (right, left, far), two in self.plan(item, phase):
            if phase == 0:
                for side, there in (("f", far), ("r", right), ("l", left)):
                    self.push((i, part, phase, side), there[1], i, done, self.spot, cols)
                continue
            for step, (a, b) in enumerate(((0, 1), (1, 0))):
                self.push((i, part, phase, "r", step), right[1], i, done, self.spot, two[a])
                self.push((i, part, phase, "l", step), left[1], i, done, self.spot, two[b])
            if phase == 2:
                self.forward((i, part, "f"), i, done, self.spot, cols)

    def relay(self, item, phase):
        for i, part, cols, done, (right, left, _), two in self.plan(item, phase):
            for side, source, target, cc in (("r", left, right, two[0]), ("l", right, left, two[1])):
                where = (i, done, source[0], cc)
                self.sends.arrived((i, part, phase, side, 0), self.block(*where), source[1])
                self.push((i, part, phase, side, 2), target[1], *where)
                if phase == 2:
                    self.forward((i, part, "f", side, 0), *where)

    def finish(self, item, phase):
        for i, part, cols, done, (right, left, far), two in self.plan(item, phase):
            if phase == 0:
                for side, source in (("r", left), ("l", right), ("f", far)):
                    self.sends.arrived((i, part, phase, side), self.block(i, done, source[0], cols), source[1])
                continue
            for side, step, at, cc, source in (
                ("r", 1, left, two[1], left),
                ("l", 1, right, two[0], right),
                ("r", 2, far, two[0], left),
                ("l", 2, far, two[1], right),
            ):
                where = (i, done, at[0], cc)
                self.sends.arrived((i, part, phase, side, step), self.block(*where), source[1])
                if phase == 2:
                    self.forward((i, part, "f", side, step), *where)

    def received(self, item):
        for name, (i, done, at, cc) in self.forwards[item]:
            self.sends.arrived(name, self.block(i, done, at, cc, self.other), self.sibling)


class Exchange:
    def __init__(self, sends, key, bufs, lanes, jobs):
        self.sends, self.key, self.bufs, self.lanes, self.jobs = sends, key, bufs, lanes, jobs
        self.core, self.spot = position()
        self.other = 1 - self.core
        self.mine, self.theirs = (
            [pl.ds(pl.multiple_of(lane * 256 + core * 128, 128), 128) for lane in range(lanes)]
            for core in (self.core, self.other)
        )
        self.sibling = device(self.other, self.spot)
        self.near = neighbours(self.core, self.spot)

    def index(self, cols, axis=None, where=None):
        return tuple(pl.ds(where, 1) if a == axis else pl.ds(0, 4) for a in range(3)) + (slice(None), cols)

    def moves(self, stage, which):
        before, after = self.bufs[stage], self.bufs[stage + 1]
        away, stay = [], []
        if stage == 0:
            for lane in range(self.lanes):
                mine, theirs = self.index(self.mine[lane]), self.index(self.theirs[lane])
                away.append(((self.key, 0, lane), theirs, mine, self.sibling, theirs, self.sibling))
                stay.append(mine)
            return before, after, away, stay
        for number, (lo, width, first) in enumerate(self.jobs):
            if which is not None and number not in which:
                continue
            axis = (first + stage - 1) % 3
            cols = pl.ds(lo, width)
            here = self.index(cols, axis, self.spot[axis])
            for by in (2, 1, 3):
                there, target = self.near[axis, by]
                behind, source = self.near[axis, 4 - by]
                away.append(
                    (
                        (self.key, stage, number, by),
                        self.index(cols, axis, there[axis]),
                        here,
                        target,
                        self.index(cols, axis, behind[axis]),
                        source,
                    )
                )
            stay.append(here)
        return before, after, away, stay

    def launch(self, stage, which=None):
        before, after, away, stay = self.moves(stage, which)
        for name, src, dst, target, _, _ in away:
            self.sends.start(name, lambda src=src, dst=dst, target=target: (before.at[src], after.at[dst], target))
        for here in stay:
            after[here] = before[here]

    def land(self, stage, which=None):
        _, after, away, _ = self.moves(stage, which)
        for name, _, _, _, landing, source in away:
            self.sends.arrived(name, after.at[landing], source)

    def fill(self, lane, scratch, values):
        row = 0
        for value in values:
            for j in range(value.shape[1] // 128):
                scratch[pl.ds(row, N_DEV, stride=16), :] = value[:, j * 128 : (j + 1) * 128].astype(F32)
                row += 1
        blocks = scratch[...].reshape(4, 4, 4, 2, 16, 128)
        for core in range(2):
            at = lane * 256 + core * 128
            self.bufs[0][:, :, :, :, at : at + 128] = blocks[:, :, :, core].astype(BF)


BY_CORE = [(0, 128, 0), (128, 128, 1)]


class RowExchange:
    RADIX = {"x": 4, "z": 4, "y": 4, "c": 2}
    NATURAL = ("x", "z", "y", "c")

    def __init__(self, sends, key, src, dst):
        self.sends, self.key, self.src, self.dst = sends, key, src, dst
        self.core, self.spot = position()
        self.mine, self.theirs = pl.ds(2 * self.core, 2), pl.ds(2 * (1 - self.core), 2)
        self.sibling = device(1 - self.core, self.spot)
        self.near = neighbours(self.core, self.spot)

    def order(self, stage):
        lead = "c" if stage == 0 else AXES[stage - 1]
        return (lead,) + tuple(name for name in self.NATURAL if name != lead)

    def shuffle(self, new, old, rows):
        rest = lax.broadcasted_iota(jnp.int32, (N_DEV, N_DEV), 0)
        digit = {}
        for name in reversed(new):
            digit[name] = rest % self.RADIX[name]
            rest = rest // self.RADIX[name]
        index = 0
        for name in old:
            index = index * self.RADIX[name] + digit[name]
        onehot = (index == lax.broadcasted_iota(jnp.int32, (N_DEV, N_DEV), 1)).astype(BF)
        return dot(onehot, rows).astype(BF)

    def launch(self, stage, value=None):
        if stage == 0:
            self.src[0] = self.shuffle(self.order(0), self.NATURAL, value).reshape(4, 32, 128)
            self.sends.start(
                (self.key, 0), lambda: (self.src.at[0, self.theirs], self.dst.at[0, self.mine], self.sibling)
            )
            return
        rows = self.dst[stage - 1].reshape(N_DEV, 128)
        self.src[stage] = self.shuffle(self.order(stage), self.order(stage - 1), rows).reshape(4, 32, 128)
        axis = stage - 1
        for by in (2, 1, 3):
            there, target = self.near[axis, by]
            self.sends.start(
                (self.key, stage, by),
                lambda there=there, target=target: (
                    self.src.at[stage, there[axis]],
                    self.dst.at[stage, self.spot[axis]],
                    target,
                ),
            )

    def land(self, stage):
        if stage == 0:
            self.dst[0, self.mine] = self.src[0, self.mine]
            self.sends.arrived((self.key, 0), self.dst.at[0, self.theirs], self.sibling)
            return
        axis = stage - 1
        self.dst[stage, self.spot[axis]] = self.src[stage, self.spot[axis]]
        for by in (2, 1, 3):
            there, source = self.near[axis, 4 - by]
            self.sends.arrived((self.key, stage, by), self.dst.at[stage, there[axis]], source)

    def rows(self):
        return self.shuffle(self.NATURAL, self.order(3), self.dst[3].reshape(N_DEV, 128))


WALL = 768
TOKEN_ROWS = 32
WIDTHS = (4 * HCOLS + 7 * AR, D + FB + WALL, FB + WALL, FB + WALL)
FSTEPS = H
BLOCKS = FFP // FB


def forward_kernel(
    split_ref, sent_ref, rates_ref, gain1_ref, gain2_ref, mask_ref, place_ref, pers_ref,
    mine0, mine1, mine2, mine3,
    g0_ref, g1_ref, g2_ref, g3_ref, proj_ref, x_ref, h1_ref, lat_ref, wf_ref, lw_ref, back_ref, dz_ref, dmid_ref,
    grads_ref,
    rate_src, rate_dst, got, flat, d_ref, dec_ref, dect_ref, inc0, inc1, inc2, inc3, stage0, stage1, stage2, stage3,
    w_buf, up_buf, down_buf, z_ref, wup_buf, wd_buf, lead_buf,
    x2_ref, h2_ref, inv_ref, lat_out_ref, lat_up_ref, dl_down_ref, acc_ref, lat_acc_ref, dh_ref, dlat_ref,
    send_sem, recv_sem, local_sem, w_sem, j_sem, token_send, token_recv,
):
    step = pl.program_id(0)
    mine, inc = (mine0, mine1, mine2, mine3), (inc0, inc1, inc2, inc3)
    stage, outs = (stage0, stage1, stage2, stage3), (g0_ref, g1_ref, g2_ref, g3_ref)
    sends = Sends(send_sem, recv_sem)
    ring = Gather(sends, outs, WIDTHS)
    core, spot = ring.core, ring.spot
    other = 1 - core
    items = range(4)
    me = lax.axis_index("fsdp")
    decay_rows = RowExchange(sends, "rates", rate_src, rate_dst)

    def token_copy(k):
        target = (me + k) % N_DEV
        return pltpu.make_async_remote_copy(
            src_ref=sent_ref.at[target], dst_ref=got.at[me], send_sem=token_send.at[k], recv_sem=token_recv.at[k],
            device_id=(target,), device_id_type=MESH,
        )

    def head_loads(h, slot):
        half, place = h // 4, pl.multiple_of((h % 4) * HCOLS, 128)
        return (
            pltpu.make_async_copy(
                g0_ref.at[half, :, :, :, :, pl.ds(place, HCOLS)], w_buf.at[slot], w_sem.at[slot, 0]
            ),
            pltpu.make_async_copy(
                g0_ref.at[1, h // 2, pl.ds(2 * (h % 2), 2), :, :, pl.ds(4 * HCOLS, HCOLS)],
                up_buf.at[slot],
                w_sem.at[slot, 1],
            ),
        )

    def down_load():
        return pltpu.make_async_copy(
            g0_ref.at[0, :, :, :, :, pl.ds(4 * HCOLS, HCOLS)], down_buf, local_sem.at[0]
        )

    def lead_load():
        return pltpu.make_async_copy(g1_ref.at[:, :, :, :, :, pl.ds(0, D)], lead_buf, local_sem.at[0])

    def up_load(k):
        at = D if k == 0 else 0
        return pltpu.make_async_copy(
            outs[k + 1].at[:, :, :, :, :, pl.ds(at, FB)], wup_buf.at[k % 2], j_sem.at[k % 2, 0]
        )

    def wall_load(k):
        at = D + FB if k == 0 else FB
        return pltpu.make_async_copy(
            outs[k + 1].at[:, :, :, :, :, pl.ds(at, WALL)], wd_buf.at[k % 2], j_sem.at[k % 2, 1]
        )

    @pl.when(step == 0)
    def _():
        barrier = pltpu.get_barrier_semaphore()

        def signal(k, carry):
            pl.semaphore_signal(barrier, inc=1, device_id=((me + k) % N_DEV,), device_id_type=MESH)
            return carry

        lax.fori_loop(1, N_DEV, signal, 0)
        pl.semaphore_wait(barrier, N_DEV - 1)
        for i in items:
            sends.start(("pair", i), lambda i=i: (mine[i].at[other], inc[i], ring.sibling))
        own_copy = lambda i: pltpu.make_async_copy(
            stage[i], outs[i].at[core, spot[0], spot[1], spot[2]], local_sem.at[i]
        )
        for i in items:
            sends.arrived(("pair", i), inc[i], ring.sibling)
            own, theirs = mine[i][core], inc[i][...]
            first = jnp.where(core == 0, own, theirs)
            last = jnp.where(core == 0, theirs, own)
            stage[i][...] = jnp.concatenate([first, last], axis=0).astype(BF)
            own_copy(i).start()
        def send_tokens(k, carry):
            token_copy(k).start()
            return carry

        def take_tokens(k, carry):
            token_copy(k).wait()
            return carry

        def columns(first, count):
            return jnp.concatenate(
                [flat[pl.ds(first + c, N_DEV, stride=TOKEN_ROWS), :].astype(BF) for c in range(count)], axis=1
            )

        for i in items:
            own_copy(i).wait()
            ring.begin(i, 0)
        decay_rows.launch(0, rates_ref[...])
        lax.fori_loop(1, 43, send_tokens, 0)
        ring.finish(0, 0)
        ring.begin(0, 1)
        decay_rows.land(0)
        decay_rows.launch(1)
        lax.fori_loop(43, 85, send_tokens, 0)
        for i in items[1:]:
            ring.finish(i, 0)
        ring.relay(0, 1)
        decay_rows.land(1)
        decay_rows.launch(2)
        lax.fori_loop(85, N_DEV, send_tokens, 0)
        got[me] = sent_ref[me]
        ring.finish(0, 1)
        decay_rows.land(2)
        decay_rows.launch(3)
        ring.begin(0, 2)
        ring.begin(1, 1)
        lax.fori_loop(1, N_DEV, take_tokens, 0)
        flat[...] = got[...].astype(F32).reshape(N_DEV * TOKEN_ROWS, 128)
        decay_rows.land(3)
        rates = decay_rows.rows()
        for m in range(MB):
            s = slice(m * GROUP, (m + 1) * GROUP)
            x_ref[s, :] = dot(place_ref[m], columns(m * D // 128, D // 128), TN).astype(BF)
            d_ref[s, :] = dot(place_ref[m], columns((MB + m) * D // 128, D // 128), TN).astype(BF)
            sent = rates[:, m * 3 * H : (m + 1) * 3 * H]
            dec_ref[s, :] = dot(place_ref[m], sent, TN)
            dect_ref[:, s] = dot(sent, place_ref[m], TN)
        decay_kernel(split_ref, dec_ref, dect_ref, wf_ref, lw_ref)
        normed, _ = norm_fwd(x_ref[...].astype(F32), gain1_ref[...])
        h1_ref[...] = normed.astype(BF)
        ring.relay(0, 2)
        ring.relay(1, 1)
        for i in items[2:]:
            ring.begin(i, 1)
        ring.finish(0, 2)
        ring.finish(1, 1)
        ring.begin(1, 2)
        ring.received(0)
        for copy in head_loads(0, 0):
            copy.start()
        down_load().start()
        down_load().wait()
        latent = dot(h1_ref[...], down_buf[...].reshape(D, HCOLS))
        mask = mask_ref[...]
        for part in range(7):
            s = slice(part * AR, (part + 1) * AR)
            lat_ref[:, s] = (latent[:, s] * mask).astype(BF)

    @pl.when(step == 1)
    def _():
        for i in items[2:]:
            ring.relay(i, 1)

    @pl.when(step == 3)
    def _():
        ring.relay(1, 2)

    @pl.when(step == 6)
    def _():
        ring.finish(2, 1)
        ring.begin(2, 2)
        ring.finish(3, 1)

    @pl.when(step < FSTEPS)
    def _():
        slot = step % 2
        for copy in head_loads(step, slot):
            copy.wait()

        @pl.when(step + 1 < FSTEPS)
        def _():
            for copy in head_loads(step + 1, 1 - slot):
                copy.start()

        base = dot(h1_ref[...], w_buf[slot].reshape(D, HCOLS))
        up = up_buf[slot].reshape(HEAD, HCOLS)
        pieces = []
        for part in range(7):
            s = slice(part * AR, (part + 1) * AR)
            piece = base[:, part * HEAD : (part + 1) * HEAD] + dot(lat_ref[:, s], up[:, s], NT)
            proj_ref[:, part * HEAD : (part + 1) * HEAD] = piece
            pieces.append(piece)
        q, k, v = (pieces[i].astype(BF) for i in range(3))
        pk, pv = pers_ref[0, :, pl.ds(pl.multiple_of(step * HEAD, HEAD), HEAD)], pers_ref[
            1, :, pl.ds(pl.multiple_of(step * HEAD, HEAD), HEAD)
        ]
        near, far = attend(q, k, v, pk, pv, allowed_mask(split_ref))
        att = attend_out(near.astype(BF), far.astype(BF), v, pv)
        kn, _ = unit(pieces[3])
        qn, _ = unit(pieces[5])
        here = pl.ds(step, 1)
        mem = memory_out(memory_terms(kn, qn, pieces[4], wf_ref.at[here], lw_ref.at[here]))
        z_ref[:, pl.ds(pl.multiple_of(step * HEAD, HEAD), HEAD)] = (
            att + jax.nn.sigmoid(pieces[6]) * mem
        ).astype(BF)

    lead = lambda half, lo, hi: lead_buf[half, :, :, :, :, lo:hi].reshape(D, hi - lo)
    out_down = lambda: lead(0, 0, 128)
    up_down = lambda: lead(0, 128, 384)
    out_up = lambda: lead(0, 384, 512)
    down_up = lambda: lead(0, 512, 640)
    w_out = lambda: lead(1, 0, D)

    @pl.when(step == FSTEPS)
    def _():
        ring.finish(1, 2)
        ring.received(1)
        for copy in (lead_load(), up_load(0), wall_load(0)):
            copy.start()
        lead_load().wait()
        ring.relay(2, 2)
        ring.begin(3, 2)
        mask = mask_ref[...]
        z = z_ref[...]
        lat_out_ref[...] = (dot(z, out_down()) * mask).astype(BF)
        x2 = x_ref[...].astype(F32) + (dot(z, w_out()) + dot(lat_out_ref[...], out_up(), NT))
        x2_ref[...] = x2
        normed, inv = norm_fwd(x2, gain2_ref[...])
        inv_ref[...] = jnp.broadcast_to(inv, inv_ref.shape)
        h2_ref[...] = normed.astype(BF)
        latent = dot(h2_ref[...], up_down())
        lat_up_ref[:, :AR] = (latent[:, :AR] * mask).astype(BF)
        lat_up_ref[:, AR:] = (latent[:, AR:] * mask).astype(BF)
        dl_down_ref[...] = (dot(d_ref[...], down_up()) * mask).astype(BF)
        for ref in (acc_ref, lat_acc_ref, dh_ref, dlat_ref):
            ref[...] = jnp.zeros_like(ref)

    @pl.when(step == FSTEPS)
    def _():
        ring.finish(2, 2)
        ring.received(2)
        up_load(1).start()
        wall_load(1).start()

    @pl.when(step >= FSTEPS)
    def _():
        k = step - FSTEPS
        slot = k % 2
        h2 = h2_ref[...]
        d = d_ref[...]
        lat0, lat1 = lat_up_ref[:, :AR], lat_up_ref[:, AR:]
        wall = lambda half, lo, hi: wd_buf[slot, half, :, :, :, :, lo:hi].reshape(FB, hi - lo)
        pltpu.make_async_copy(wup_buf.at[slot], wup_buf.at[slot], j_sem.at[slot, 0]).wait()
        pltpu.make_async_copy(wd_buf.at[slot], wd_buf.at[slot], j_sem.at[slot, 1]).wait()
        w_gate, w_lift = (wup_buf[slot, half].reshape(D, FB) for half in range(2))
        wda, wdb = wall(0, 0, 768), wall(1, 0, 256)
        uu0, uu1, dd = wall(1, 256, 384), wall(1, 384, 512), wall(1, 512, 640)
        gate = dot(h2, w_gate) + dot(lat0, uu0, NT)
        lift = dot(h2, w_lift) + dot(lat1, uu1, NT)
        sig = jax.nn.sigmoid(gate)
        silu = gate * sig
        act = (silu * lift).astype(BF)
        d_act = dot(d[:, :768], wda, NT) + dot(d[:, 768:], wdb, NT) + dot(dl_down_ref[...], dd, NT)
        d_gate = (d_act * lift * (sig * (1.0 + gate * (1.0 - sig)))).astype(BF)
        d_lift = (d_act * silu).astype(BF)
        acc_ref[:, :768] += dot(act, wda)
        acc_ref[:, 768:] += dot(act, wdb)
        lat_acc_ref[...] += dot(act, dd)
        dh_ref[...] += dot(d_gate, w_gate, NT) + dot(d_lift, w_lift, NT)
        dlat_ref[:, :AR] += dot(d_gate, uu0)
        dlat_ref[:, AR:] += dot(d_lift, uu1)
        for half, at, term in (
            (0, k * 256, dot(d_gate, lat0, TN)),
            (0, k * 256 + AR, dot(d_lift, lat1, TN)),
            (1, k * AR, dot(act, dl_down_ref[...], TN)),
        ):
            at = pl.ds(pl.multiple_of(at, AR), AR)
            grads_ref[half, :, :, at] = term.reshape(64, 16, AR).astype(BF)

        @pl.when(k == 0)
        def _():
            ring.relay(3, 2)

        @pl.when(k == 1)
        def _():
            ring.finish(3, 2)
            ring.received(3)
            up_load(2).start()
            wall_load(2).start()

    @pl.when(step == FSTEPS + BLOCKS - 1)
    def _():
        mask = mask_ref[...]
        lat_down = (lat_acc_ref[...] * mask).astype(BF)
        out = (x2_ref[...] + acc_ref[...] + dot(lat_down, down_up(), NT)).astype(BF)
        for m in range(MB):
            s = slice(m * GROUP, (m + 1) * GROUP)
            back_ref[:, m * D : (m + 1) * D] = dot(place_ref[m], out[s]).astype(BF)
        d = d_ref[...]
        h2 = h2_ref[...]
        z = z_ref[...]

        def put(half, at, value):
            grads_ref[half, :, :, at : at + AR] = value.reshape(64, 16, AR).astype(BF)

        put(0, 768, dot(d, lat_down, TN))
        dlu0 = (dlat_ref[:, :AR] * mask).astype(BF)
        dlu1 = (dlat_ref[:, AR:] * mask).astype(BF)
        put(1, 640, dot(h2, dlu0, TN))
        put(1, 768, dot(h2, dlu1, TN))
        ud = up_down()
        dh = dh_ref[...] + (dot(dlu0, ud[:, :AR], NT) + dot(dlu1, ud[:, AR:], NT))
        dmid = d.astype(F32) + norm_bwd(dh, x2_ref[...], inv_ref[:, :1], gain2_ref[...])
        dmid_ref[...] = dmid
        dmb = dmid.astype(BF)
        dlo = (dot(dmb, out_up()) * mask).astype(BF)
        put(1, 384, dot(z, dlo, TN))
        put(1, 512, dot(dmb, lat_out_ref[...], TN))
        dz_ref[...] = (dot(dmb, w_out(), NT) + dot(dlo, out_down(), NT)).astype(BF)
        sends.drain()


def forward_call(split, sent, rates, gain1, gain2, mask, place, persistent, mine):
    once = pl.Buffered(1)
    whole = lambda *shape: pl.BlockSpec(shape, lambda s: (0,) * len(shape), pipeline_mode=once)
    hbm = pl.BlockSpec(memory_space=pl.ANY)
    slots = 4 * (1 + 3 * (3 + 2 * 6 + 7)) + 1 + 3 * 3
    return pl.pallas_call(
        forward_kernel,
        grid=(FSTEPS + BLOCKS,),
        out_shape=tuple(jax.ShapeDtypeStruct((2, 4, 4, 4, 16, width), BF) for width in WIDTHS)
        + (
            jax.ShapeDtypeStruct((ROWS, 7 * D), F32),
            jax.ShapeDtypeStruct((ROWS, D), BF),
            jax.ShapeDtypeStruct((ROWS, D), BF),
            jax.ShapeDtypeStruct((ROWS, 7 * AR), BF),
            jax.ShapeDtypeStruct((H, MB, GROUP, GROUP), F32),
            jax.ShapeDtypeStruct((H, MB, 8, GROUP), F32),
            jax.ShapeDtypeStruct((GROUP, MB * D), BF),
            jax.ShapeDtypeStruct((ROWS, D), BF),
            jax.ShapeDtypeStruct((ROWS, D), F32),
            jax.ShapeDtypeStruct((2, 64, 16, 896), BF),
        ),
        in_specs=[
            pl.BlockSpec(memory_space=pltpu.SMEM),
            whole(N_DEV, TOKEN_ROWS, 128),
            whole(N_DEV, 128),
            whole(1, D),
            whole(1, D),
            whole(ROWS, AR),
            whole(MB, GROUP, GROUP),
            whole(2, NP, D),
        ]
        + [whole(2, 8, width) for width in WIDTHS],
        out_specs=(hbm,) * 4
        + (
            pl.BlockSpec((ROWS, HCOLS), lambda s: (0, jnp.minimum(s, FSTEPS - 1))),
            whole(ROWS, D),
            whole(ROWS, D),
            whole(ROWS, 7 * AR),
            whole(H, MB, GROUP, GROUP),
            whole(H, MB, 8, GROUP),
            whole(GROUP, MB * D),
            whole(ROWS, D),
            whole(ROWS, D),
            whole(2, 64, 16, 896),
        ),
        scratch_shapes=[
            pltpu.VMEM((4, 4, 32, 128), BF),
            pltpu.VMEM((4, 4, 32, 128), BF),
            pltpu.VMEM((N_DEV, TOKEN_ROWS, 128), BF),
            pltpu.VMEM((N_DEV * TOKEN_ROWS, 128), F32),
            pltpu.VMEM((ROWS, D), BF),
            pltpu.VMEM((ROWS, 3 * H), F32),
            pltpu.VMEM((3 * H, ROWS), F32),
        ]
        + [pltpu.VMEM((8, width), F32) for width in WIDTHS]
        + [pltpu.VMEM((16, width), BF) for width in WIDTHS]
        + [
            pltpu.VMEM((2, 4, 4, 4, 16, HCOLS), BF),
            pltpu.VMEM((2, 2, 4, 16, HCOLS), BF),
            pltpu.VMEM((4, 4, 4, 16, HCOLS), BF),
            pltpu.VMEM((ROWS, D), BF),
            pltpu.VMEM((2, 2, 4, 4, 4, 16, FB), BF),
            pltpu.VMEM((2, 2, 4, 4, 4, 16, WALL), BF),
            pltpu.VMEM((2, 4, 4, 4, 16, D), BF),
            pltpu.VMEM((ROWS, D), F32),
            pltpu.VMEM((ROWS, D), BF),
            pltpu.VMEM((ROWS, 128), F32),
            pltpu.VMEM((ROWS, AR), BF),
            pltpu.VMEM((ROWS, 2 * AR), BF),
            pltpu.VMEM((ROWS, AR), BF),
            pltpu.VMEM((ROWS, D), F32),
            pltpu.VMEM((ROWS, AR), F32),
            pltpu.VMEM((ROWS, D), F32),
            pltpu.VMEM((ROWS, 2 * AR), F32),
            pltpu.SemaphoreType.DMA((slots,)),
            pltpu.SemaphoreType.DMA((slots,)),
            pltpu.SemaphoreType.DMA((4,)),
            pltpu.SemaphoreType.DMA((2, 2)),
            pltpu.SemaphoreType.DMA((2, 2)),
            pltpu.SemaphoreType.DMA((N_DEV,)),
            pltpu.SemaphoreType.DMA((N_DEV,)),
        ],
        compiler_params=pltpu.CompilerParams(
            collective_id=0, has_side_effects=True, vmem_limit_bytes=VMEM_LIMIT
        ),
        name="gather_forward",
    )(split, sent, rates, gain1, gain2, mask, place, persistent, *mine)


class Scatter:
    def __init__(self, sends, key, grads, out, inc0, total, inc1, inc2, inc3, t1, t2):
        self.sends, self.key, self.grads, self.out = sends, key, grads, out
        self.inc0, self.total, self.inc = inc0, total, (None, inc1, inc2, inc3)
        self.t1, self.t2 = t1, t2
        self.core, self.spot = position()
        self.other = 1 - self.core
        self.sibling = device(1 - self.core, self.spot)
        self.near = neighbours(self.core, self.spot)
        self.parts = [(part, pl.ds(*cols)) for part, cols in enumerate(cut(7, 3))]
        self.slabs = [(by, self.slab(by)) for by in (2, 1, 3, 0)]

    def peers(self):
        return [self.sibling] + [there[1] for there in self.near.values()]

    def slab(self, by):
        return (self.spot[0] + by) % 4

    def pair(self):
        for by, x in self.slabs:
            self.sends.start(
                (self.key, "pair", by),
                lambda x=x: (
                    self.grads.at[self.other, pl.ds(pl.multiple_of(16 * x, 16), 16)],
                    self.inc0.at[x],
                    self.sibling,
                ),
            )

    def source(self, phase, part, at):
        axis = (part + phase - 1) % 3
        cs = self.parts[part][1]
        if phase == 1:
            index = tuple(at if a == axis else slice(None) for a in range(3))
            return self.total, index + (slice(None), cs)
        rest = [a for a in range(3) if a != part]
        if phase == 2:
            index = (at, slice(None)) if rest[0] == axis else (slice(None), at)
            return self.t1, index + (slice(None), cs)
        return self.t2, (at, slice(None), cs)

    def landing(self, phase, part, k):
        return (k,) + (slice(None),) * (4 - phase) + (self.parts[part][1],)

    def send_one(self, phase, part, by):
        axis = (part + phase - 1) % 3
        to = self.near[axis, by]
        k = (2, 1, 3).index(by)

        def make():
            ref, index = self.source(phase, part, to[0][axis])
            return ref.at[index], self.inc[phase].at[self.landing(phase, part, k)], to[1]

        self.sends.start((self.key, part, phase, by), make)

    def send(self, phase):
        for part, _ in self.parts:
            if phase == 1 and part == 0:
                continue
            for by in (2, 1, 3):
                self.send_one(phase, part, by)

    def add(self, phase):
        for part, cs in self.parts:
            axis = (part + phase - 1) % 3
            ref, index = self.source(phase, part, self.spot[axis])
            acc = ref[index].astype(F32)
            for k, by in enumerate((2, 1, 3)):
                here = self.landing(phase, part, k)
                source = self.near[axis, 4 - by][1]
                self.sends.arrived((self.key, part, phase, by), self.inc[phase].at[here], source)
                acc = acc + self.inc[phase][here].astype(F32)
            if phase == 1:
                self.t1[:, :, :, cs] = acc.astype(BF)
            elif phase == 2:
                self.t2[:, :, cs] = acc.astype(BF)
            else:
                self.out[self.core, :, cs] = acc

    def add_pair(self):
        for by, x in self.slabs:
            self.sends.arrived((self.key, "pair", by), self.inc0.at[x], self.sibling)
            mine = self.grads[self.core, pl.ds(pl.multiple_of(16 * x, 16), 16)]
            both = mine.astype(F32) + self.inc0[x].astype(F32)
            self.total[x] = both.reshape(4, 4, 16, 896).astype(BF)
            if by:
                self.send_one(1, 0, by)

    def swap(self):
        self.sends.start(
            (self.key, "last"), lambda: (self.out.at[self.core], self.out.at[self.core], self.sibling)
        )

    def swapped(self):
        self.sends.arrived((self.key, "last"), self.out.at[self.other], self.sibling)


def backward_kernel(
    split_ref, x_ref, gain_ref, mask_ref, place_ref, proj_ref, dz_ref, dmid_ref, h1_ref, lat_ref,
    w_ref, down_ref, up_ref, pers_ref, wf_ref, lw_ref, ffn_ref, back_ref,
    act_out, grad_out, ffn_out, heads_out,
    dh_ref, dlat_ref, dlat_half, grads_ref, *rest,
):
    step = pl.program_id(0)
    send_sem, recv_sem = rest[-2:]
    sends = Sends(send_sem, recv_sem)
    first_sums = Scatter(sends, 0, ffn_ref, *rest[:8])
    last_sums = Scatter(sends, 1, grads_ref, *rest[8:16])
    flat = rest[26]
    ex_act = Exchange(sends, "a", rest[16:21], 1, BY_CORE)
    ex_grad = Exchange(sends, "g", rest[21:26], 1, BY_CORE)

    def one_head():
        pieces = [proj_ref[:, p * HEAD : (p + 1) * HEAD] for p in range(7)]
        q, k, v = (pieces[i].astype(BF) for i in range(3))
        pk, pv = pers_ref[0], pers_ref[1]
        near, far = attend(q, k, v, pk, pv, allowed_mask(split_ref))
        near_half = near.astype(BF)
        dz = dz_ref[...]
        d_near = by_group(lambda s, g: dot(dz[s], v[s], NT))
        d_far = dot(dz, pv, NT)
        d_v = by_group(lambda s, g: dot(near_half[s], dz[s], TN))
        total = jnp.sum(d_near * near, axis=-1, keepdims=True) + jnp.sum(
            d_far * far, axis=-1, keepdims=True
        )
        ds_near = (near * (d_near - total) * SCALE).astype(BF)
        ds_far = (far * (d_far - total) * SCALE).astype(BF)
        d_q = by_group(lambda s, g: dot(ds_near[s], k[s])) + dot(ds_far, pk)
        d_k = by_group(lambda s, g: dot(ds_near[s], q[s], TN))

        dzf = dz.astype(F32)
        opening = jax.nn.sigmoid(pieces[6])
        kn, k_inv = unit(pieces[3])
        qn, q_inv = unit(pieces[5])
        kept = memory_terms(kn, qn, pieces[4], wf_ref, lw_ref, plain, dot1)
        mem = memory_out(kept, dot1)
        d_open = dzf * mem * (opening * (1.0 - opening))
        d_kn, d_qn, d_mv = memory_bwd(kept, dzf * opening)
        d_mk = unit_bwd(d_kn, pieces[3], k_inv)
        d_mq = unit_bwd(d_qn, pieces[5], q_inv)
        dy = [item.astype(BF) for item in (d_q, d_k, d_v, d_mk, d_mv, d_mq, d_open)]
        dh_ref[...] += dot(jnp.concatenate(dy, axis=1), w_ref[0], NT)
        first = pl.multiple_of(step * 8, 8)
        for part in range(7):
            s = slice(part * AR, (part + 1) * AR)
            dlat_ref[:, s] += dot(dy[part], up_ref[0, :, s])
            grads_ref[1, pl.ds(first, 8), :, s] = (
                dot(dy[part], lat_ref[:, s], TN).reshape(8, 16, AR).astype(BF)
            )

    @pl.when(step == 0)
    def _():
        greet(first_sums.peers())
        ex_act.fill(0, flat, [back_ref[...]])
        ex_act.launch(0)
        first_sums.pair()
        dh_ref[...] = jnp.zeros_like(dh_ref)
        dlat_ref[...] = jnp.zeros_like(dlat_ref)

    @pl.when(step == 1)
    def _():
        ex_act.land(0)
        ex_act.launch(1)

    @pl.when(step == 2)
    def _():
        first_sums.add_pair()
        first_sums.send(1)

    @pl.when(step == 3)
    def _():
        ex_act.land(1)
        ex_act.launch(2)

    @pl.when(step == 5)
    def _():
        first_sums.add(1)
        first_sums.send(2)
        ex_act.land(2)
        ex_act.launch(3)

    @pl.when(step == 6)
    def _():
        first_sums.add(2)
        first_sums.send(3)

    @pl.when(step == 7)
    def _():
        first_sums.add(3)
        first_sums.swap()
        ex_act.land(3)
        act_out[...] = ex_act.bufs[4][...]

    one_head()

    @pl.when(step == H - 1)
    def _():
        mask = mask_ref[...]
        for p in range(7):
            s = slice(p * AR, (p + 1) * AR)
            dlat_half[:, s] = (dlat_ref[:, s] * mask).astype(BF)
        grads_ref[0] = dot(h1_ref[...], dlat_half[...], TN).reshape(64, 16, 7 * AR).astype(BF)
        last_sums.pair()
        dh = dh_ref[...] + dot(dlat_half[...], down_ref[0], NT)
        x = x_ref[...].astype(F32)
        inv = lax.rsqrt(jnp.mean(x * x, axis=-1, keepdims=True) + EPS)
        dx = (dmid_ref[...] + norm_bwd(dh, x, inv, gain_ref[...])).astype(BF)
        ex_grad.fill(
            0, flat, [dot(place_ref[m], dx[m * GROUP : (m + 1) * GROUP]) for m in range(MB)]
        )
        ex_grad.launch(0)
        last_sums.add_pair()
        ex_grad.land(0)
        ex_grad.launch(1)
        last_sums.send(1)
        first_sums.swapped()
        ffn_out[...] = first_sums.out[...]
        ex_grad.land(1)
        ex_grad.launch(2)
        last_sums.add(1)
        last_sums.send(2)
        ex_grad.land(2)
        ex_grad.launch(3)
        last_sums.add(2)
        last_sums.send(3)
        ex_grad.land(3)
        grad_out[...] = ex_grad.bufs[4][...]
        last_sums.add(3)
        last_sums.swap()
        last_sums.swapped()
        heads_out[...] = last_sums.out[...]
        sends.drain()


def backward_call(split, x, gain, mask, place, proj, dz, dmid, h1, lat, a1, persistent, wf, lw, grads_ffn, back):
    once = pl.Buffered(1)
    whole = lambda *shape: pl.BlockSpec(shape, lambda s: (0,) * len(shape), pipeline_mode=once)
    head = lambda s: s
    buffers = [
        pltpu.VMEM((2, 16, 896), F32),
        pltpu.VMEM((4, 16, 16, 896), BF),
        pltpu.VMEM((4, 4, 4, 16, 896), BF),
        pltpu.VMEM((3, 4, 4, 16, 896), BF),
        pltpu.VMEM((3, 4, 16, 896), BF),
        pltpu.VMEM((3, 16, 896), BF),
        pltpu.VMEM((4, 4, 16, 896), BF),
        pltpu.VMEM((4, 16, 896), BF),
    ]
    slots = 2 * (4 + 3 * 9 + 1) + 2 * (1 + 3 * 6)
    return pl.pallas_call(
        backward_kernel,
        grid=(H,),
        out_shape=(
            jax.ShapeDtypeStruct((4, 4, 4, 16, 256), BF),
            jax.ShapeDtypeStruct((4, 4, 4, 16, 256), BF),
            jax.ShapeDtypeStruct((2, 16, 896), F32),
            jax.ShapeDtypeStruct((2, 16, 896), F32),
        ),
        in_specs=[
            pl.BlockSpec(memory_space=pltpu.SMEM),
            whole(ROWS, D),
            whole(1, D),
            whole(ROWS, AR),
            whole(MB, GROUP, GROUP),
            pl.BlockSpec((ROWS, HCOLS), lambda s: (0, head(s))),
            pl.BlockSpec((ROWS, HEAD), lambda s: (0, head(s))),
            whole(ROWS, D),
            whole(ROWS, D),
            whole(ROWS, 7 * AR),
            pl.BlockSpec((1, D, HCOLS), lambda s: (s // 4, 0, s % 4)),
            pl.BlockSpec((1, D, HCOLS), lambda s: (0, 0, 4), pipeline_mode=once),
            pl.BlockSpec((1, HEAD, HCOLS), lambda s: (1, head(s), 4)),
            pl.BlockSpec((2, NP, HEAD), lambda s: (0, 0, head(s))),
            pl.BlockSpec((1, MB, GROUP, GROUP), lambda s: (head(s), 0, 0, 0)),
            pl.BlockSpec((1, MB, 8, GROUP), lambda s: (head(s), 0, 0, 0)),
            pl.BlockSpec(memory_space=pltpu.VMEM),
            pl.BlockSpec(memory_space=pltpu.VMEM),
        ],
        out_specs=(
            whole(4, 4, 4, 16, 256),
            whole(4, 4, 4, 16, 256),
            pl.BlockSpec(memory_space=pltpu.VMEM),
            pl.BlockSpec(memory_space=pltpu.VMEM),
        ),
        scratch_shapes=[
            pltpu.VMEM((ROWS, D), F32),
            pltpu.VMEM((ROWS, 7 * AR), F32),
            pltpu.VMEM((ROWS, 7 * AR), BF),
            pltpu.VMEM((2, 64, 16, 896), BF),
        ]
        + buffers * 2
        + [pltpu.VMEM((4, 4, 4, 16, 256), BF)] * 10
        + [pltpu.VMEM((16 * N_DEV, 128), F32)]
        + [pltpu.SemaphoreType.DMA((slots,)), pltpu.SemaphoreType.DMA((slots,))],
        compiler_params=pltpu.CompilerParams(
            collective_id=1, has_side_effects=True, vmem_limit_bytes=VMEM_LIMIT
        ),
        name="backward_scatter",
    )(split, x, gain, mask, place, proj, dz, dmid, h1, lat, a1, a1, a1, persistent, wf, lw, grads_ffn, back)


def selector(parts):
    rows = lax.broadcasted_iota(jnp.int32, (parts * R, parts * AR), 0)
    cols = lax.broadcasted_iota(jnp.int32, (parts * R, parts * AR), 1)
    return (rows // R == cols // AR) & (rows % R == cols % R)


def adapter_of(shape):
    return (lax.broadcasted_iota(jnp.int32, shape, len(shape) - 1) % AR) // R


def pack_kernel(
    lengths_ref, ids_ref, route_ref, tok_ref, cot_ref, decays_ref,
    w_in, w_out, w_up, w_down, in_down, in_up, out_down, out_up, up_down, up_up, down_down, down_up,
    sent, rates_out, item0, item1, item2, item3, to_ref, place_ref, mask_ref, split_ref,
    flat, wide,
):
    me = lax.axis_index("fsdp")

    below = lax.broadcasted_iota(jnp.int32, (GROUP, GROUP), 0)
    along = lax.broadcasted_iota(jnp.int32, (GROUP, GROUP), 1)
    for m in range(MB):
        to = (below == route_ref[m, pl.ds(me, 1), :] // GROUP).astype(BF)
        to_ref[m] = to
        for ref, first in ((tok_ref, m * 8), (cot_ref, (MB + m) * 8)):
            value = dot(to, ref[m])
            for j in range(8):
                flat[pl.ds(first + j, N_DEV, stride=TOKEN_ROWS), :] = value[:, j * 128 : (j + 1) * 128]
    rates = [dot(to_ref[m], decays_ref[m], NT) for m in range(MB)]
    rates = jnp.concatenate(rates + [jnp.zeros((GROUP, 128 - MB * 3 * H), F32)], axis=1)
    rates_out[...] = rates.astype(BF)
    sent[...] = flat[...].reshape(N_DEV, TOKEN_ROWS, 128).astype(BF)

    for m in range(MB):
        blocks = route_ref[m]
        landing = jnp.sum(jnp.where(blocks // GROUP == me, blocks % GROUP, 0), axis=1, keepdims=True)
        place_ref[m] = (landing == along).astype(BF)
        early = lengths_ref[m, 0]
        row = lax.broadcasted_iota(jnp.int32, (GROUP, AR), 0)
        adapter = jnp.where(row < early, ids_ref[m, 0], ids_ref[m, 1])
        mask_ref[m * GROUP : (m + 1) * GROUP, :] = (adapter == adapter_of((GROUP, AR))).astype(F32)
        split_ref[m] = jnp.where(early < GROUP, 1.0, 0.0)

    select = selector(7).astype(BF)
    items = (item1, item2, item3)

    def ranks(ref, parts):
        cut_to = select[: parts * R, : parts * AR]
        rows = ref.shape[1]
        out = jnp.zeros((rows, parts * AR), F32)
        for a in range(NAD):
            out = out + jnp.where(adapter_of(out.shape) == a, dot(ref[a], cut_to), 0.0)
        return out

    def ranks_t(ref, parts):
        cut_to = select[: parts * R, : parts * AR]
        cols = ref.shape[2]
        out = jnp.zeros((cols, parts * AR), F32)
        for a in range(NAD):
            out = out + jnp.where(adapter_of(out.shape) == a, dot(ref[a], cut_to, TN), 0.0)
        return out

    def ranks_mid(ref, parts):
        rows = ref.shape[0]
        value = ref[...].astype(F32).reshape(rows * NAD, parts * R).astype(BF)
        value = dot(value, select[: parts * R, : parts * AR]).reshape(rows, NAD, parts * AR)
        mine = adapter_of(value.shape) == lax.broadcasted_iota(jnp.int32, value.shape, 1)
        return jnp.sum(jnp.where(mine, value, 0.0), axis=1)

    def tall(value):
        return jnp.concatenate([value, jnp.zeros((FF_PAD - FF_SHARD, value.shape[1]), F32)], axis=0)

    for h in range(H):
        for part in range(7):
            at = (h % 4) * HCOLS + part * HEAD
            item0[h // 4, :, at : at + HEAD] = w_in[:, part * D + h * HEAD : part * D + (h + 1) * HEAD].astype(F32)
    item0[0, :, 4 * HCOLS :] = ranks(in_down, 7)
    item0[1, :, 4 * HCOLS :] = ranks(in_up, 7)

    item1[0, :, 0:128] = ranks(out_down, 1)
    item1[0, :, 128:384] = ranks(up_down, 2)
    item1[0, :, 384:512] = ranks(out_up, 1)
    item1[0, :, 512:640] = ranks(down_up, 1)
    item1[0, :, 640:D] = jnp.zeros((8, D - 640), F32)
    item1[1, :, 0:D] = w_out[...].astype(F32)

    wide[...] = w_up[...].astype(F32)
    span = 8 * FF_SHARD
    rows = lax.broadcasted_iota(jnp.int32, (span, 3 * 64), 0)
    cols = lax.broadcasted_iota(jnp.int32, (span, 3 * 64), 1)
    unit_at = (cols // 64) * 8 + cols % 8
    spread = ((rows == (cols % 64) // 8 * FF_SHARD + unit_at) & (unit_at < FF_SHARD)).astype(BF)
    pieces = [wide[:, c * span : (c + 1) * span] for c in range(32)]
    moved_up = dot(jnp.concatenate(pieces, axis=0).astype(BF), spread)
    for c in range(32):
        half, chunk = c // 16, c % 16
        for k in range(3):
            at = (D if k == 0 else 0) + chunk * 64
            items[k][half, :, at : at + 64] = moved_up[c * 8 : (c + 1) * 8, k * 64 : (k + 1) * 64]
    down = tall(w_down[...].astype(F32))
    uu, dd = tall(ranks_mid(up_up, 2)), tall(ranks_t(down_down, 1))
    for k in range(3):
        at = (D if k == 0 else 0) + FB
        s = slice(k * 8, (k + 1) * 8)
        items[k][0, :, at : at + 768] = down[s, :768]
        items[k][1, :, at : at + 256] = down[s, 768:]
        items[k][1, :, at + 256 : at + 512] = uu[s]
        items[k][1, :, at + 512 : at + 640] = dd[s]
        items[k][1, :, at + 640 : at + 768] = jnp.zeros((8, 128), F32)


def pack_call(lengths, ids, route, tokens, cotangent, decays, weights):
    smem, vmem = pl.BlockSpec(memory_space=pltpu.SMEM), pl.BlockSpec(memory_space=pltpu.VMEM)
    return pl.pallas_call(
        pack_kernel,
        out_shape=(
            jax.ShapeDtypeStruct((N_DEV, TOKEN_ROWS, 128), BF),
            jax.ShapeDtypeStruct((N_DEV, 128), BF),
        )
        + tuple(jax.ShapeDtypeStruct((2, 8, width), F32) for width in WIDTHS)
        + (
            jax.ShapeDtypeStruct((MB, GROUP, GROUP), BF),
            jax.ShapeDtypeStruct((MB, GROUP, GROUP), BF),
            jax.ShapeDtypeStruct((ROWS, AR), F32),
            jax.ShapeDtypeStruct((MB,), F32),
        ),
        in_specs=[smem] * 2 + [vmem] * (4 + len(weights)),
        out_specs=(vmem,) * 9 + (smem,),
        scratch_shapes=[
            pltpu.VMEM((N_DEV * TOKEN_ROWS, 128), F32),
            pltpu.VMEM((8, 2 * FF), F32),
        ],
        compiler_params=pltpu.CompilerParams(vmem_limit_bytes=VMEM_LIMIT),
        name="pack",
    )(lengths, ids, route, tokens, cotangent, decays, *weights)


def unpack_kernel(
    core_ref, to_ref, act_ref, grad_ref, ffn_ref, heads_ref,
    out_ref, back_ref, in_down, in_up, out_down, out_up, up_down, up_up, down_down, down_up,
    flat,
):
    core = core_ref[0]
    for source, target in ((act_ref, out_ref), (grad_ref, back_ref)):
        got = [source[:, :, :, :, c * 128 : (c + 1) * 128].astype(F32) for c in range(2)]
        flat[...] = jnp.stack(got, axis=3).reshape(16 * N_DEV, 128)
        for m in range(MB):
            value = jnp.concatenate(
                [flat[pl.ds(m * 8 + j, N_DEV, stride=16), :].astype(BF) for j in range(8)], axis=1
            )
            target[m] = dot(to_ref[m], value, TN).astype(BF)
    own = pl.ds(pl.multiple_of(core * 8, 8), 8)
    heads = [heads_ref[half, own, :] for half in range(2)]
    ffn = [ffn_ref[half, own, :] for half in range(2)]
    select = selector(7).astype(F32)

    def tall(value, width):
        return jnp.concatenate([value[:, k * width : (k + 1) * width] for k in range(3)], axis=0)

    def put(ref, value, parts):
        rows, width = value.shape
        shape = (NAD, rows, width)
        mine = adapter_of(shape) == lax.broadcasted_iota(jnp.int32, shape, 0)
        apart = jnp.where(mine, value[None], 0.0).reshape(NAD * rows, width)
        ref[...] = exact(apart, select[: parts * R, :width], NT).reshape(NAD, rows, parts * R)

    put(in_down, heads[0], 7)
    put(in_up, heads[1], 7)
    put(out_down, ffn[1][:, 384:512], 1)
    put(out_up, ffn[1][:, 512:640], 1)
    put(up_down, ffn[1][:, 640:896], 2)
    put(down_up, ffn[0][:, 768:], 1)
    value = tall(ffn[0][:, :768], 256)
    shape = (FF_PAD, NAD, 2 * AR)
    mine = adapter_of(shape) == lax.broadcasted_iota(jnp.int32, shape, 1)
    apart = jnp.where(mine, jnp.broadcast_to(value[:, None, :], shape), 0.0).reshape(FF_PAD * NAD, 2 * AR)
    up_up[...] = exact(apart, select[: 2 * R, : 2 * AR], NT).reshape(FF_PAD, NAD, 2 * R)[:FF_SHARD]
    value = tall(ffn[1][:, :384], AR)
    for a in range(NAD):
        mine = jnp.where(adapter_of(value.shape) == a, value, 0.0)
        down_down[a] = exact(select[:R, :AR], mine, NT)[:, :FF_SHARD]


def unpack_call(core, to, act, grad, ffn_sums, heads_sums, shapes):
    smem, vmem = pl.BlockSpec(memory_space=pltpu.SMEM), pl.BlockSpec(memory_space=pltpu.VMEM)
    return pl.pallas_call(
        unpack_kernel,
        out_shape=(jax.ShapeDtypeStruct((MB, GROUP, D), BF),) * 2
        + tuple(jax.ShapeDtypeStruct(shape, F32) for shape in shapes),
        in_specs=[smem] + [vmem] * 5,
        out_specs=(vmem,) * (2 + len(shapes)),
        scratch_shapes=[pltpu.VMEM((16 * N_DEV, 128), F32)],
        compiler_params=pltpu.CompilerParams(vmem_limit_bytes=VMEM_LIMIT),
        name="unpack",
    )(core, to, act, grad, ffn_sums, heads_sums)


def body(
    tokens, cotangent, decays, route, lengths, adapter_ids, gain_mix, gain_ffn, persistent,
    w_in, w_out, w_up, w_down, in_down, in_up, out_down, out_up, up_down, up_up, down_down, down_up,
):
    me = lax.axis_index("fsdp").astype(jnp.int32)
    weights = (
        w_in, w_out, w_up, w_down, in_down, in_up, out_down, out_up, up_down, up_up, down_down, down_up,
    )
    turned = lambda value: jnp.swapaxes(value, 1, 2)
    views = (None,) * 5 + (turned, None, turned, None, lambda value: value.transpose(2, 0, 1), turned, turned)
    back_views = views[:9] + (lambda value: value.transpose(1, 2, 0), turned, turned)
    viewed = [item if view is None else view(item) for item, view in zip(weights, views)]
    sent, rates, *items, to, place, mask, split = pack_call(
        lengths[:, 0], adapter_ids[:, 0], route.reshape(MB, N_DEV, GROUP), tokens, cotangent, turned(decays), viewed
    )
    gain_mix, gain_ffn = gain_mix[None, :], gain_ffn[None, :]
    a1, _, _, _, proj, x, h1, lat, wf, lw, back, dz, dmid, grads_ffn = forward_call(
        split, sent, rates, gain_mix, gain_ffn, mask, place, persistent, items
    )
    act, grad, ffn_sums, heads_sums = backward_call(
        split, x, gain_mix, mask, place, proj, dz, dmid, h1, lat, a1.reshape(2, D, WIDTHS[0]), persistent, wf, lw,
        grads_ffn, back,
    )
    outs = unpack_call((me % 2)[None], to, act, grad, ffn_sums, heads_sums, [item.shape for item in viewed[4:]])
    grads = [item if view is None else view(item) for item, view in zip(outs[2:], back_views[4:])]
    return tuple(outs[:2]) + tuple(grads)


def solution(mesh):
    rows, cols = P(None, "fsdp", None), P(None, None, "fsdp")
    weight = P("fsdp", None)
    return jax.shard_map(
        body,
        mesh=mesh,
        in_specs=(rows, rows, rows, P(), rows, rows, P(), P(), P())
        + (weight,) * 4
        + (rows, cols) * 4,
        out_specs=(rows, rows) + (rows, cols) * 4,
        check_vma=False,
    )
```
